32 devices in a mesh: section: 2 (over core), dp: 4 (over z), ctx: 4 (over y, x).
Axes of the slice: x: 2, y: 2, z: 4, core: 2. Of those that a mesh axis runs over, the one named last changes fastest.
Arguments:
- inputs: bfloat16 [2, 4, 1024, 960], P(None, 'dp', 'ctx'), may hold values from -6 to 6
- segment_ids: int32 [2, 4, 1024], P(None, 'dp'), may hold values from 0 to 11, as said below
- cotangent: bfloat16 [2, 4, 1024, 960], P(None, 'dp', 'ctx'), may hold values from -6 to 6
- gain_attn: bfloat16 [960], replicated, may hold values from 0.099609375 to 1.8984375
- w_query: bfloat16 [960, 960], replicated, may hold values from -0.1875 to 0.1875
- w_key: bfloat16 [960, 320], replicated, may hold values from -0.1875 to 0.1875
- w_value: bfloat16 [960, 320], replicated, may hold values from -0.1875 to 0.1875
- w_out: bfloat16 [960, 960], replicated, may hold values from -0.75 to 0.75
- gain_ffn: bfloat16 [960], replicated, may hold values from 0.099609375 to 1.8984375
- w_gate: bfloat16 [960, 2560], replicated, may hold values from -0.1875 to 0.1875
- w_up: bfloat16 [960, 2560], replicated, may hold values from -0.1875 to 0.1875
- w_down: bfloat16 [2560, 960], replicated, may hold values from -0.125 to 0.125
Outputs:
- activations: bfloat16 [2, 2, 4, 1024, 960], P('section', None, 'dp', 'ctx')
- input_grads: float32 [2, 2, 4, 1024, 960], P('section', None, 'dp', 'ctx')
- grad_gain_attn: float32 [960], P('dp')
- grad_w_query: float32 [960, 960], P('dp')
- grad_w_key: float32 [960, 320], P('dp')
- grad_w_value: float32 [960, 320], P('dp')
- grad_w_out: float32 [960, 960], P('dp')
- grad_gain_ffn: float32 [960], P('dp')
- grad_w_gate: float32 [960, 2560], P('dp')
- grad_w_up: float32 [960, 2560], P('dp')
- grad_w_down: float32 [2560, 960], P('dp')
The draws below stay inside these ranges and needn't reach their ends.
Inputs may be any that keep to these rules, and one draw needn't show every extreme that they name: `segment_ids`: document numbers never fall along a row, start at 0. On each index of dp, one of its rows of the micro-batches, drawn from the seed, holds a document that begins within its first 256 tokens and ends within its last 256.
All inputs are finite; a program needn't handle non-finite values.
Results may differ from the reference program's by a relative error of at most 0.035.
Values may be sent and summed in bfloat16 or wider, within the bound.
A program may use at most 256 MiB of HBM per device.

```python
import jax
import jax.numpy as jnp
from jax import lax

HEADS = 15
KV_HEADS = 5
HEAD_DIM = 64
FF = 2560
D = 960
KVD = 320
MB = 2
ROWS_DEV = 1
CTX_TOK = 256
ROWS = 4
LEN = 1024


def draw_segment_ids(key, part):
    key = jax.random.fold_in(key, 7)
    slots = MB * ROWS_DEV
    groups = ROWS // ROWS_DEV
    stride = LEN // 12
    strata = jnp.arange(11, dtype=jnp.int32) * stride
    drawn = strata[None, None, :] + jax.random.randint(jax.random.fold_in(key, 1), (MB, ROWS, 11), 1, stride + 1)
    counts = jax.random.randint(jax.random.fold_in(key, 2), (MB, ROWS, 1), 3, 12)
    row_keys = jax.random.split(jax.random.fold_in(key, 3), MB * ROWS)
    ranks = jax.vmap(lambda one_key: jax.random.permutation(one_key, 11))(row_keys).reshape(MB, ROWS, 11)
    micro_index = jnp.arange(MB, dtype=jnp.int32)[:, None]
    row_index = jnp.arange(ROWS, dtype=jnp.int32)[None, :]
    slot_index = micro_index * ROWS_DEV + row_index % ROWS_DEV
    group_index = row_index // ROWS_DEV
    chosen = jax.random.randint(jax.random.fold_in(key, 4), (groups,), 0, slots)
    spanning = slot_index == chosen[group_index]
    filled = (group_index == 0) & (slot_index == (chosen[0] + 1) % slots)
    active = (ranks.astype(jnp.int32) < counts) | filled[:, :, None]
    drawn = jnp.where(active, drawn, LEN)
    first_bounds = jax.random.randint(jax.random.fold_in(key, 5), (MB, ROWS, 2), 1, CTX_TOK)
    last_bounds = jax.random.randint(jax.random.fold_in(key, 6), (MB, ROWS, 2), LEN - CTX_TOK + 1, LEN)
    unused = jnp.full((MB, ROWS, 7), LEN, jnp.int32)
    span_bounds = jnp.concatenate([first_bounds, last_bounds, unused], -1)
    bounds = jnp.where(spanning[:, :, None], span_bounds, drawn)
    positions = jnp.arange(LEN, dtype=jnp.int32)
    return jnp.sum((positions[None, None, :, None] >= bounds[:, :, None, :]).astype(jnp.int32), -1)


def steps_of(own_key, dims, cuts, low, high):
    factor_of, own = 1.0, jax.random.fold_in(own_key, 6)
    for position, parts in cuts:
        heights = jnp.exp(jax.random.uniform(jax.random.fold_in(own, position), (parts,), jnp.float32, low / len(cuts), high / len(cuts)))
        factor_of = factor_of * jnp.repeat(heights, dims[position] // parts).reshape([-1 if axis == position else 1 for axis in range(len(dims))])
    return factor_of


def noise(own_key, shape, scale, reach, pieces=(), held_as=jnp.bfloat16):
    result = jax.random.normal(own_key, shape, jnp.float32) * scale
    if len(pieces) > 0:
        result = steps_of(own_key, shape, pieces, -0.22, 0.18) * result
    return jnp.clip(result, min=-reach, max=reach).astype(held_as)


def setup_inputs(seed: int = 0) -> dict:
    splits = jax.random.split(jax.random.key(seed), 13)
    inputs = noise(splits[0], (MB, ROWS, LEN, D), 1.0, 6.0, ((1, 4), (2, 4)))
    segment_ids = draw_segment_ids(jax.random.fold_in(splits[12], 71), 0)
    cotangent = noise(splits[2], (MB, ROWS, LEN, D), 1.0, 6.0, ((1, 4), (2, 4)))
    gain_attn = jnp.clip(1.0 + 0.18 * jax.random.normal(splits[3], (D,), jnp.float32), 0.099609375, 1.8984375).astype(jnp.bfloat16)
    w_query = noise(splits[4], (D, D), D ** -0.5, 0.1875)
    w_key = noise(splits[5], (D, KVD), D ** -0.5, 0.1875)
    w_value = noise(splits[6], (D, KVD), D ** -0.5, 0.1875)
    w_out = noise(splits[7], (D, D), (D // 16) ** -0.5, 0.75)
    gain_ffn = jnp.clip(1.0 + 0.18 * jax.random.normal(splits[8], (D,), jnp.float32), 0.099609375, 1.8984375).astype(jnp.bfloat16)
    w_gate = noise(splits[9], (D, FF), D ** -0.5, 0.1875)
    w_up = noise(splits[10], (D, FF), D ** -0.5, 0.1875)
    w_down = noise(splits[11], (FF, D), FF ** -0.5, 0.125)
    return {"inputs": inputs, "segment_ids": segment_ids, "cotangent": cotangent, "gain_attn": gain_attn, "w_query": w_query, "w_key": w_key, "w_value": w_value, "w_out": w_out, "gain_ffn": gain_ffn, "w_gate": w_gate, "w_up": w_up, "w_down": w_down}


epsilon = 1e-05
score_scale = 0.125
mask_floor = -1e+30
highest = lax.Precision.HIGHEST

@jax.custom_vjp
def low(v):
    return lax.optimization_barrier(v.astype(jnp.bfloat16)).astype(jnp.float32)

@jax.custom_vjp
def low_back(v):
    return v

def low_keep(v):
    return (low(v), None)

def low_pass(kept, grad):
    return (grad,)

def back_keep(v):
    return (v, None)

def back_low(kept, grad):
    return (low(grad),)
low.defvjp(low_keep, low_pass)
low_back.defvjp(back_keep, back_low)

def rms_norm(values, gain_vec):
    return values * lax.rsqrt(lax.optimization_barrier(jnp.mean(values * values, -1, keepdims=True)) + epsilon) * gain_vec

def rotary_tables(positions):
    halfway = HEAD_DIM // 2
    frequency = 10000.0 ** (-2.0 * jnp.arange(halfway, dtype=jnp.float32) / HEAD_DIM)
    angles = positions.astype(jnp.float32)[:, None] * frequency[None, :]
    return (jnp.cos(angles), jnp.sin(angles))

def rotate(values, cos_table, sine_table):
    halfway = HEAD_DIM // 2
    former = values[..., :halfway]
    latter = values[..., halfway:]
    cos_part = cos_table[:, None, :]
    sine_part = sine_table[:, None, :]
    return jnp.concatenate([former * cos_part - latter * sine_part, latter * cos_part + former * sine_part], -1)

def attend_block(queries, query_seg, query_pos, key_rows, value_rows, key_seg, key_pos):
    product = jnp.einsum('bkgd,lkd->bkgl', queries, key_rows, precision=highest)
    scores = low_back(product * score_scale)
    allowed = (query_seg[:, None] == key_seg[None, :]) & (key_pos[None, :] <= query_pos[:, None])
    scores = jnp.where(allowed[:, None, None, :], scores, mask_floor)
    largest = lax.optimization_barrier(jnp.max(scores, -1, keepdims=True))
    weights = jnp.exp(scores - largest)
    softmax_out = weights / lax.optimization_barrier(jnp.sum(weights, -1, keepdims=True))
    return jnp.einsum('bkgl,lkd->bkgd', low(softmax_out), value_rows, precision=highest)

def layer(hidden, segments, params, cos_table, sine_table):
    gain_attn, w_query, w_key, w_value, w_out, gain_ffn, w_gate, w_up, w_down = params
    length = hidden.shape[0]
    groups = HEADS // KV_HEADS
    normed = low(rms_norm(hidden, gain_attn))
    query_pre = low_back(jnp.dot(normed, w_query, precision=highest))
    key_pre = low_back(jnp.dot(normed, w_key, precision=highest))
    value_pre = low_back(jnp.dot(normed, w_value, precision=highest))
    queries = low(rotate(query_pre.reshape(length, HEADS, HEAD_DIM), cos_table, sine_table))
    key_rows = low(rotate(key_pre.reshape(length, KV_HEADS, HEAD_DIM), cos_table, sine_table))
    value_rows = low(value_pre.reshape(length, KV_HEADS, HEAD_DIM))
    block_rows = min(512, length)
    block_count = length // block_rows
    positions = jnp.arange(length, dtype=jnp.int32)

    def one_block(query_block, seg_block, pos_block):
        return attend_block(query_block, seg_block, pos_block, key_rows, value_rows, segments, positions)
    checked = jax.checkpoint(one_block)

    def mapped(row_item):
        return checked(row_item[0], row_item[1], row_item[2])
    attended = lax.map(mapped, (queries.reshape(block_count, block_rows, KV_HEADS, groups, HEAD_DIM), segments.reshape(block_count, block_rows), positions.reshape(block_count, block_rows)))
    attended = low_back(low(attended.reshape(length, HEADS * HEAD_DIM)))
    middle = hidden + low_back(jnp.dot(attended, w_out, precision=highest))
    normed_ffn = low(rms_norm(middle, gain_ffn))
    gate_pre = low_back(jnp.dot(normed_ffn, w_gate, precision=highest))
    upward = low_back(jnp.dot(normed_ffn, w_up, precision=highest))
    inner_act = low(jax.nn.silu(gate_pre) * upward)
    return middle + low_back(jnp.dot(inner_act, w_down, precision=highest))

def reference(inputs, segment_ids, cotangent, gain_attn, w_query, w_key, w_value, w_out, gain_ffn, w_gate, w_up, w_down):
    params = tuple((weight.astype(jnp.float32) for weight in (gain_attn, w_query, w_key, w_value, w_out, gain_ffn, w_gate, w_up, w_down)))
    length = inputs.shape[2]
    model_width = inputs.shape[3]
    rows_in = inputs.reshape(-1, length, model_width).astype(jnp.float32)
    rows_seg = segment_ids.reshape(-1, length)
    rows_cot = cotangent.reshape(-1, length, model_width).astype(jnp.float32)
    cos_table, sine_table = rotary_tables(jnp.arange(length, dtype=jnp.int32))

    def per_row(running, row_item):
        row_in, row_seg, row_cot = row_item

        def closed(start_rows, boundary_probe, weights):
            first_out = layer(start_rows, row_seg, weights, cos_table, sine_table)
            passed = low_back(low(first_out)) + boundary_probe
            return (layer(passed, row_seg, weights, cos_table, sine_table), first_out)
        second, pullback, first_out = jax.vjp(closed, row_in, jnp.zeros_like(row_in), params, has_aux=True)
        grad_in, grad_mid, grad_weights = pullback(row_cot)
        running = jax.tree.map(lambda accumulated, addition: accumulated + addition, running, grad_weights)
        return (running, (first_out, second, grad_in, low(grad_mid)))
    zero_grads = tuple((jnp.zeros_like(weight) for weight in params))
    totals, outputs = lax.scan(per_row, zero_grads, (rows_in, rows_seg, rows_cot))
    firsts, seconds, grads_in, grads_mid = outputs
    out_shape = (2,) + inputs.shape
    activations = jnp.stack([firsts, seconds]).reshape(out_shape).astype(jnp.bfloat16)
    input_grads = jnp.stack([grads_in, grads_mid]).reshape(out_shape)
    return (activations, input_grads, totals[0], totals[1], totals[2], totals[3], totals[4], totals[5], totals[6], totals[7], totals[8])
```

```python
import math

import jax
import jax.numpy as jnp
from jax import lax
from jax.sharding import PartitionSpec as P

HEADS = 15
KV_HEADS = 5
HEAD_DIM = 64


epsilon = 1e-05
score_scale = 0.125
mask_floor = -1e30


def rms_forward(values, gain_vec):
    inverse = lax.rsqrt(jnp.mean(values * values, -1, keepdims=True) + epsilon)
    return (values * inverse * gain_vec, inverse)


def rms_backward(values, gain_vec, inverse, grad_normed):
    weighted = grad_normed * gain_vec
    grad_gain = jnp.sum(grad_normed * values * inverse, axis=(0, 1))
    cubed = inverse * inverse * inverse
    grad_values = inverse * weighted - values * cubed * jnp.mean(
        weighted * values, -1, keepdims=True
    )
    return (grad_values, grad_gain)


def rotate(values, cos_table, sine_table):
    halfway = values.shape[-1] // 2
    former = values[..., :halfway]
    latter = values[..., halfway:]
    cos_part = cos_table[None, :, None, :]
    sine_part = sine_table[None, :, None, :]
    return jnp.concatenate(
        [former * cos_part - latter * sine_part, latter * cos_part + former * sine_part], -1
    )


def block_scores(queries, key_part, query_seg, key_seg, query_pos, offset):
    block_rows = key_part.shape[1]
    scores = (
        jnp.einsum("rckgd,rnkd->rkgcn", queries, key_part, preferred_element_type=jnp.float32)
        * score_scale
    )
    key_pos = offset + jnp.arange(block_rows, dtype=jnp.int32)
    allowed = (query_seg[:, :, None] == key_seg[:, None, :]) & (
        key_pos[None, None, :] <= query_pos[None, :, None]
    )
    return (scores, allowed[:, None, None, :, :])


def body(
    inputs,
    segment_ids,
    cotangent,
    gain_attn,
    w_query,
    w_key,
    w_value,
    w_out,
    gain_ffn,
    w_gate,
    w_up,
    w_down,
):
    micro_count, row_count, tok_local, model_width = inputs.shape
    kv_width = w_key.shape[1]
    group_size = HEADS // KV_HEADS
    section_index = lax.axis_index("section")
    on_first = section_index == 0
    ctx_index = lax.axis_index("ctx")
    first_token = ctx_index * tok_local
    query_pos = first_token + jnp.arange(tok_local, dtype=jnp.int32)
    halfway = HEAD_DIM // 2
    frequency = 10000.0 ** (-2.0 * jnp.arange(halfway, dtype=jnp.float32) / HEAD_DIM)
    angles = query_pos.astype(jnp.float32)[:, None] * frequency[None, :]
    cos_table = jnp.cos(angles)
    sine_table = jnp.sin(angles)
    w_pair = jnp.concatenate([w_key, w_value], 1)
    head_shape = (row_count, tok_local, KV_HEADS, group_size, HEAD_DIM)
    state_shape = (row_count, KV_HEADS, group_size, tok_local)

    def front(hidden, segments):
        query_seg = lax.dynamic_slice_in_dim(segments, first_token, tok_local, 1)
        normed, inverse = rms_forward(hidden, gain_attn)
        normed_low = normed.astype(jnp.bfloat16)
        query_pre = jnp.einsum(
            "rcd,de->rce", normed_low, w_query, preferred_element_type=jnp.float32
        )
        pair_pre = jnp.einsum("rcd,de->rce", normed_low, w_pair, preferred_element_type=jnp.float32)
        queries = rotate(
            query_pre.reshape(row_count, tok_local, HEADS, HEAD_DIM), cos_table, sine_table
        )
        queries = queries.astype(jnp.bfloat16).reshape(head_shape)
        key_rot = rotate(
            pair_pre[..., :kv_width].reshape(row_count, tok_local, KV_HEADS, HEAD_DIM),
            cos_table,
            sine_table,
        )
        packed = jnp.concatenate(
            [key_rot.reshape(row_count, tok_local, kv_width), pair_pre[..., kv_width:]], -1
        )
        return (query_seg, inverse, normed_low, queries, packed.astype(jnp.bfloat16))

    def attend_forward(queries, arrived, segments, query_seg):
        start_state = (
            jnp.full(state_shape, mask_floor, jnp.float32),
            jnp.zeros(state_shape, jnp.float32),
            jnp.zeros(state_shape + (HEAD_DIM,), jnp.float32),
        )
        piece_rows = arrived.shape[1]
        block_rows = math.gcd(piece_rows, 512)

        def fold_inner_step(step_index, loop_state):
            run_max, run_sum, run_acc = loop_state
            offset = step_index * block_rows
            key_block = lax.dynamic_slice_in_dim(arrived, step_index * block_rows, block_rows, 1)
            key_part = key_block[..., :kv_width].reshape(row_count, block_rows, KV_HEADS, HEAD_DIM)
            value_part = key_block[..., kv_width:].reshape(
                row_count, block_rows, KV_HEADS, HEAD_DIM
            )
            key_seg = lax.dynamic_slice_in_dim(segments, offset, block_rows, 1)
            scores, allowed = block_scores(queries, key_part, query_seg, key_seg, query_pos, offset)
            masked = jnp.where(allowed, scores, mask_floor)
            new_max = jnp.maximum(run_max, jnp.max(masked, -1))
            weights = jnp.where(allowed, jnp.exp(masked - new_max[..., None]), 0.0)
            rescale = jnp.exp(run_max - new_max)
            run_sum = run_sum * rescale + jnp.sum(weights, -1)
            run_acc = run_acc * rescale[..., None] + jnp.einsum(
                "rkgcn,rnkd->rkgcd",
                weights.astype(jnp.bfloat16),
                value_part,
                preferred_element_type=jnp.float32,
            )
            return (new_max, run_sum, run_acc)

        run_max, run_sum, run_acc = lax.fori_loop(
            0, piece_rows // block_rows, fold_inner_step, start_state
        )
        return (run_acc / run_sum[..., None], run_max + jnp.log(run_sum))

    def rear(hidden, attended):
        attn_low = (
            attended.transpose(0, 3, 1, 2, 4)
            .reshape(row_count, tok_local, HEADS * HEAD_DIM)
            .astype(jnp.bfloat16)
        )
        middle = hidden + jnp.einsum(
            "rce,ed->rcd", attn_low, w_out, preferred_element_type=jnp.float32
        )
        normed_ffn, inverse_ffn = rms_forward(middle, gain_ffn)
        ffn_low = normed_ffn.astype(jnp.bfloat16)
        gate_pre = jnp.einsum("rcd,df->rcf", ffn_low, w_gate, preferred_element_type=jnp.float32)
        upward = jnp.einsum("rcd,df->rcf", ffn_low, w_up, preferred_element_type=jnp.float32)
        inner_act = (jax.nn.silu(gate_pre) * upward).astype(jnp.bfloat16)
        output = middle + jnp.einsum(
            "rcf,fd->rcd", inner_act, w_down, preferred_element_type=jnp.float32
        )
        return (output, (attn_low, middle, inverse_ffn, ffn_low, gate_pre, upward, inner_act))


    assert micro_count == lax.axis_size("section")

    def mine(stacked):
        return lax.dynamic_index_in_dim(stacked, section_index, 0, keepdims=False)

    segments = mine(segment_ids)

    def forward(hidden):
        query_seg, inverse, normed_low, queries, packed = front(hidden, segments)
        arrived = lax.all_gather(packed, "ctx", axis=1, tiled=True)
        attended, log_sum = attend_forward(queries, arrived, segments, query_seg)
        output, saved = rear(hidden, attended)
        return output.astype(jnp.bfloat16), (
            hidden, query_seg, inverse, normed_low, queries, arrived, attended, log_sum, saved
        )

    def backward(grad_out, kept):
        (
            hidden,
            backward_query_seg,
            backward_inverse,
            backward_normed_low,
            backward_queries,
            piece_arrived,
            backward_attended,
            log_sum,
            saved,
        ) = kept
        (
            backward_attn_low,
            backward_middle,
            backward_inverse_ffn,
            backward_ffn_low,
            backward_gate_pre,
            backward_upward,
            backward_inner_act,
        ) = saved
        grad_low = grad_out.astype(jnp.bfloat16)
        grad_inner = jnp.einsum("rcd,fd->rcf", grad_low, w_down, preferred_element_type=jnp.float32)
        backward_sum_down = jnp.einsum(
            "rcf,rcd->fd", backward_inner_act, grad_low, preferred_element_type=jnp.float32
        )
        sigmoid = jax.nn.sigmoid(backward_gate_pre)
        grad_gate = (
            grad_inner * backward_upward * sigmoid * (1.0 + backward_gate_pre * (1.0 - sigmoid))
        ).astype(jnp.bfloat16)
        grad_up = (grad_inner * backward_gate_pre * sigmoid).astype(jnp.bfloat16)
        backward_sum_gate = jnp.einsum(
            "rcd,rcf->df", backward_ffn_low, grad_gate, preferred_element_type=jnp.float32
        )
        backward_sum_up = jnp.einsum(
            "rcd,rcf->df", backward_ffn_low, grad_up, preferred_element_type=jnp.float32
        )
        grad_norm_ffn = jnp.einsum(
            "rcf,df->rcd", grad_gate, w_gate, preferred_element_type=jnp.float32
        ) + jnp.einsum("rcf,df->rcd", grad_up, w_up, preferred_element_type=jnp.float32)
        grad_mid_norm, backward_sum_gain_ffn = rms_backward(
            backward_middle, gain_ffn, backward_inverse_ffn, grad_norm_ffn
        )
        grad_middle = grad_out + grad_mid_norm
        grad_branch = grad_middle.astype(jnp.bfloat16)
        backward_sum_out = jnp.einsum(
            "rce,rcd->ed", backward_attn_low, grad_branch, preferred_element_type=jnp.float32
        )
        grad_attn = jnp.einsum(
            "rcd,ed->rce", grad_branch, w_out, preferred_element_type=jnp.float32
        ).astype(jnp.bfloat16)
        grad_heads = grad_attn.reshape(head_shape).transpose(0, 2, 3, 1, 4)
        row_delta = jnp.sum(grad_heads.astype(jnp.float32) * backward_attended, -1)
        query_start = jnp.zeros(state_shape + (HEAD_DIM,), jnp.float32)
        fold_grad_query = query_start
        grad_query = fold_grad_query
        piece_piece_rows = piece_arrived.shape[1]
        piece_block_rows = math.gcd(piece_piece_rows, 512)

        def piece_inner_step(step_index, loop_state):
            grad_query, local_pair = loop_state
            inside = step_index * piece_block_rows
            key_block = lax.dynamic_slice_in_dim(piece_arrived, inside, piece_block_rows, 1)
            key_part = key_block[..., :kv_width].reshape(
                row_count, piece_block_rows, KV_HEADS, HEAD_DIM
            )
            value_part = key_block[..., kv_width:].reshape(
                row_count, piece_block_rows, KV_HEADS, HEAD_DIM
            )
            key_seg = lax.dynamic_slice_in_dim(segments, inside, piece_block_rows, 1)
            scores, allowed = block_scores(
                backward_queries, key_part, backward_query_seg, key_seg, query_pos, inside
            )
            chances = jnp.where(
                allowed, jnp.exp(jnp.where(allowed, scores, mask_floor) - log_sum[..., None]), 0.0
            )
            grad_chance = jnp.einsum(
                "rkgcd,rnkd->rkgcn", grad_heads, value_part, preferred_element_type=jnp.float32
            )
            grad_scores = (chances * (grad_chance - row_delta[..., None])).astype(jnp.bfloat16)
            grad_query = grad_query + score_scale * jnp.einsum(
                "rkgcn,rnkd->rkgcd", grad_scores, key_part, preferred_element_type=jnp.float32
            )
            grad_key = score_scale * jnp.einsum(
                "rkgcn,rckgd->rnkd",
                grad_scores,
                backward_queries,
                preferred_element_type=jnp.float32,
            )
            grad_value = jnp.einsum(
                "rkgcn,rkgcd->rnkd",
                chances.astype(jnp.bfloat16),
                grad_heads,
                preferred_element_type=jnp.float32,
            )
            update = jnp.concatenate(
                [
                    grad_key.reshape(row_count, piece_block_rows, kv_width),
                    grad_value.reshape(row_count, piece_block_rows, kv_width),
                ],
                -1,
            )
            current = lax.dynamic_slice_in_dim(local_pair, inside, piece_block_rows, 1)
            local_pair = lax.dynamic_update_slice_in_dim(local_pair, current + update, inside, 1)
            return (grad_query, local_pair)

        local_start = jnp.zeros((row_count, piece_piece_rows, 2 * kv_width), jnp.float32)
        fold_grad_query, fold_local_pair = lax.fori_loop(
            0, piece_piece_rows // piece_block_rows, piece_inner_step, (grad_query, local_start)
        )
        grad_pair = fold_local_pair
        grad_query, grad_pair = (fold_grad_query, grad_pair)
        pair_share = lax.psum_scatter(
            grad_pair.astype(jnp.bfloat16), "ctx", scatter_dimension=1, tiled=True
        ).astype(jnp.float32)
        query_tok = grad_query.transpose(0, 3, 1, 2, 4).reshape(
            row_count, tok_local, HEADS, HEAD_DIM
        )
        query_back = rotate(query_tok, cos_table, -sine_table).reshape(
            row_count, tok_local, HEADS * HEAD_DIM
        )
        query_back = query_back.astype(jnp.bfloat16)
        key_back = rotate(
            pair_share[..., :kv_width].reshape(row_count, tok_local, KV_HEADS, HEAD_DIM),
            cos_table,
            -sine_table,
        )
        pair_low = jnp.concatenate(
            [key_back.reshape(row_count, tok_local, kv_width), pair_share[..., kv_width:]], -1
        )
        pair_low = pair_low.astype(jnp.bfloat16)
        backward_sum_query = jnp.einsum(
            "rcd,rce->de", backward_normed_low, query_back, preferred_element_type=jnp.float32
        )
        sum_pair = jnp.einsum(
            "rcd,rce->de", backward_normed_low, pair_low, preferred_element_type=jnp.float32
        )
        grad_normed = jnp.einsum(
            "rce,de->rcd", query_back, w_query, preferred_element_type=jnp.float32
        ) + jnp.einsum("rce,de->rcd", pair_low, w_pair, preferred_element_type=jnp.float32)
        grad_front, backward_sum_gain_attn = rms_backward(
            hidden, gain_attn, backward_inverse, grad_normed
        )
        tick_grads = (
            backward_sum_gain_attn,
            backward_sum_query,
            sum_pair[:, :kv_width],
            sum_pair[:, kv_width:],
            backward_sum_out,
            backward_sum_gain_ffn,
            backward_sum_gate,
            backward_sum_up,
            backward_sum_down,
        )
        return grad_middle + grad_front, tick_grads

    def exchange(for_first, for_last):
        kept = jnp.where(on_first, for_first, for_last)
        sent = jnp.where(on_first, for_last, for_first)
        got = lax.ppermute(sent, "section", [(0, 1), (1, 0)])
        return jnp.where(
            on_first, jnp.stack([kept, got]), jnp.stack([got, kept])
        )

    first_low, first_kept = forward(mine(inputs).astype(jnp.float32))
    second_low, second_kept = forward(first_low.astype(jnp.float32))
    grad_mid, second_grads = backward(mine(cotangent).astype(jnp.float32), second_kept)
    grad_mid_low = grad_mid.astype(jnp.bfloat16)
    grad_in, first_grads = backward(grad_mid_low.astype(jnp.float32), first_kept)
    (
        sum_gain_attn,
        sum_query,
        sum_key,
        sum_value,
        sum_out,
        sum_gain_ffn,
        sum_gate,
        sum_up,
        sum_down,
    ) = tuple(one + other for one, other in zip(second_grads, first_grads))
    shares = (
        lax.psum_scatter(
            sum_gain_attn.astype(jnp.bfloat16), "dp", scatter_dimension=0, tiled=True
        ).astype(jnp.float32),
        lax.psum_scatter(
            sum_query.astype(jnp.bfloat16), "dp", scatter_dimension=0, tiled=True
        ).astype(jnp.float32),
        lax.psum_scatter(
            sum_key.astype(jnp.bfloat16), "dp", scatter_dimension=0, tiled=True
        ).astype(jnp.float32),
        lax.psum_scatter(
            sum_value.astype(jnp.bfloat16), "dp", scatter_dimension=0, tiled=True
        ).astype(jnp.float32),
        lax.psum_scatter(
            sum_out.astype(jnp.bfloat16), "dp", scatter_dimension=0, tiled=True
        ).astype(jnp.float32),
        lax.psum_scatter(
            sum_gain_ffn.astype(jnp.bfloat16), "dp", scatter_dimension=0, tiled=True
        ).astype(jnp.float32),
        lax.psum_scatter(
            sum_gate.astype(jnp.bfloat16), "dp", scatter_dimension=0, tiled=True
        ).astype(jnp.float32),
        lax.psum_scatter(sum_up.astype(jnp.bfloat16), "dp", scatter_dimension=0, tiled=True).astype(
            jnp.float32
        ),
        lax.psum_scatter(
            sum_down.astype(jnp.bfloat16), "dp", scatter_dimension=0, tiled=True
        ).astype(jnp.float32),
    )
    totals = (
        lax.psum(shares[0].astype(jnp.bfloat16), ("section", "ctx")).astype(jnp.float32),
        lax.psum(shares[1].astype(jnp.bfloat16), ("section", "ctx")).astype(jnp.float32),
        lax.psum(shares[2].astype(jnp.bfloat16), ("section", "ctx")).astype(jnp.float32),
        lax.psum(shares[3].astype(jnp.bfloat16), ("section", "ctx")).astype(jnp.float32),
        lax.psum(shares[4].astype(jnp.bfloat16), ("section", "ctx")).astype(jnp.float32),
        lax.psum(shares[5].astype(jnp.bfloat16), ("section", "ctx")).astype(jnp.float32),
        lax.psum(shares[6].astype(jnp.bfloat16), ("section", "ctx")).astype(jnp.float32),
        lax.psum(shares[7].astype(jnp.bfloat16), ("section", "ctx")).astype(jnp.float32),
        lax.psum(shares[8].astype(jnp.bfloat16), ("section", "ctx")).astype(jnp.float32),
    )
    activations = exchange(first_low, second_low)[None]
    input_grads = exchange(grad_in.astype(jnp.bfloat16), grad_mid_low).astype(jnp.float32)[None]
    return (
        activations,
        input_grads,
        totals[0],
        totals[1],
        totals[2],
        totals[3],
        totals[4],
        totals[5],
        totals[6],
        totals[7],
        totals[8],
    )


def solution(mesh):
    placed = (
        P(None, "dp", "ctx", None),
        P(None, "dp", None),
        P(None, "dp", "ctx", None),
        P(),
        P(),
        P(),
        P(),
        P(),
        P(),
        P(),
        P(),
        P(),
    )
    return jax.shard_map(
        body,
        mesh=mesh,
        in_specs=placed,
        out_specs=(
            P("section", None, "dp", "ctx", None),
            P("section", None, "dp", "ctx", None),
            P("dp"),
            P("dp", None),
            P("dp", None),
            P("dp", None),
            P("dp", None),
            P("dp"),
            P("dp", None),
            P("dp", None),
            P("dp", None),
        ),
        check_vma=False,
    )
```

```python
import functools
import math

import jax
import jax.numpy as jnp
from jax import lax
from jax.experimental import pallas as pl
from jax.experimental.pallas import tpu as pltpu
from jax.sharding import PartitionSpec as P

HEADS = 15
KV_HEADS = 5
HEAD_DIM = 64
LANES = 128
MESH = pl.DeviceIdType.MESH


epsilon = 1e-05
score_scale = 0.125
mask_floor = -1e30


def rms_forward(values, gain_vec):
    inverse = lax.rsqrt(jnp.mean(values * values, -1, keepdims=True) + epsilon)
    return (values * inverse * gain_vec, inverse)


def rms_backward(values, gain_vec, inverse, grad_normed):
    weighted = grad_normed * gain_vec
    grad_gain = jnp.sum(grad_normed * values * inverse, axis=(0, 1))
    cubed = inverse * inverse * inverse
    grad_values = inverse * weighted - values * cubed * jnp.mean(
        weighted * values, -1, keepdims=True
    )
    return (grad_values, grad_gain)


def rotate(values, cos_table, sine_table):
    halfway = values.shape[-1] // 2
    former = values[..., :halfway]
    latter = values[..., halfway:]
    cos_part = cos_table[None, :, None, :]
    sine_part = sine_table[None, :, None, :]
    return jnp.concatenate(
        [former * cos_part - latter * sine_part, latter * cos_part + former * sine_part], -1
    )


def block_scores(queries, key_part, query_seg, key_seg, query_pos, offset):
    block_rows = key_part.shape[1]
    scores = (
        jnp.einsum("rckgd,rnkd->rkgcn", queries, key_part, preferred_element_type=jnp.float32)
        * score_scale
    )
    key_pos = offset + jnp.arange(block_rows, dtype=jnp.int32)
    allowed = (query_seg[:, :, None] == key_seg[:, None, :]) & (
        key_pos[None, None, :] <= query_pos[None, :, None]
    )
    return (scores, allowed[:, None, None, :, :])


def up_to(value, step):
    return -(-value // step) * step


class Plan:
    def __init__(self, dp, ctx, width, hidden, kv_width):
        self.dp, self.ctx = dp, ctx
        self.cx = 1 << (ctx.bit_length() // 2) if ctx & (ctx - 1) == 0 else ctx
        self.cy = ctx // self.cx
        self.low = max(dp // 2, 1)
        self.rows = up_to(width // dp, 16)
        self.down_rows = up_to(hidden // dp // 2, 16)
        self.up_tiles = hidden // LANES
        self.width_tiles = up_to(width, LANES) // LANES
        self.pair_tiles = (width + kv_width) // LANES
        chunks = []
        for kind, count, rows, step in (
            ("ffn", self.up_tiles, self.rows, 4),
            ("down", self.width_tiles, self.down_rows, 4),
            ("attn", self.width_tiles - 1, self.rows, 4),
            ("mixed", self.pair_tiles - self.width_tiles + 1, self.rows, 4),
        ):
            for start in range(0, count, step):
                tiles = min(step, count - start)
                extra = 16 if kind == "mixed" else 0
                piece = up_to(up_to(tiles * rows + extra, ctx) // ctx, 16)
                chunks.append((kind, start, tiles, rows, piece))
        self.chunks = chunks
        self.offsets = [sum(c[4] for c in chunks[:i]) for i in range(len(chunks))]
        self.total = sum(c[4] for c in chunks)

    def spans(self, index, first, count):
        piece = self.chunks[index][4]
        out, done = [], 0
        while done < count:
            at = first + done
            size = min(count - done, piece - at % piece)
            out.append((at // piece, self.offsets[index] + at % piece, done, size))
            done += size
        return out


def reduce_kernel(
    plan, ffn_x, ffn_dy, down_x, down_dy, attn_x, attn_dy, pair_dy, extra, out,
    sent, partner, own, rx1, ry1, rx2, ry2, rz,
    sem_ps, sem_pr, sem_x1, sem_y1, sem_x2, sem_y2, sem_z, sem_g, sem_f,
):
    dp, cx, cy, low = plan.dp, plan.cx, plan.cy, plan.low
    section, row, ctx = (lax.axis_index(name) for name in ("section", "dp", "ctx"))
    px, py = lax.rem(ctx, cx), lax.div(ctx, cx)
    mate = 1 - section
    chunks, count = plan.chunks, len(plan.chunks)

    def at(index):
        return pl.ds(plan.offsets[index], chunks[index][4])

    def turn(base, step, size):
        return lax.rem(base + step, size)

    barrier = pltpu.get_barrier_semaphore()
    friends = [(mate, row, ctx)]
    friends += [(section, turn(row, k, dp), ctx) for k in range(1, dp)]
    friends += [(section, row, turn(ctx, k, plan.ctx)) for k in range(1, plan.ctx)]
    for friend in friends:
        pl.semaphore_signal(barrier, 1, device_id=friend, device_id_type=MESH)
    pl.semaphore_wait(barrier, len(friends))

    def remote(source, target, sems, place, device):
        return pltpu.make_async_remote_copy(
            source, target, sems[0].at[place], sems[1].at[place], device_id=device, device_id_type=MESH
        )

    def products(index, half, finish):
        kind, start, tiles, rows, piece = chunks[index]

        def shard(j, carry):
            if kind == "ffn":
                value = jnp.dot(
                    ffn_x[j], ffn_dy[half, :, start * LANES : (start + tiles) * LANES],
                    preferred_element_type=jnp.float32,
                )
            elif kind == "down":
                value = jnp.dot(
                    down_x[half, j], down_dy[:, start * LANES : (start + tiles) * LANES],
                    preferred_element_type=jnp.float32,
                )
            elif kind == "attn":
                value = jnp.dot(
                    attn_x[half, j], attn_dy[half, :, start * LANES : (start + tiles) * LANES],
                    preferred_element_type=jnp.float32,
                )
            else:
                value = jnp.dot(
                    attn_x[0, j], pair_dy[half], preferred_element_type=jnp.float32
                )
                last = plan.width_tiles - 1
                mixed = jnp.dot(
                    attn_x[half, j], attn_dy[half, :, last * LANES :], preferred_element_type=jnp.float32
                )
                value = jnp.concatenate([value[:, :LANES] + mixed, value[:, LANES:]], 1)
            for tile in range(tiles):
                finish(j, tile * rows, value[:, tile * LANES : (tile + 1) * LANES])
            if kind == "mixed":
                finish(j, tiles * rows, extra[half, j])
            return carry

        lax.fori_loop(0, dp, shard, 0)

    def make_partner(index):
        if index >= 2:
            send_partner(index - 2).wait_send()
        slot = index % 2
        base = plan.offsets[index]

        def finish(j, first, value):
            for p, place, inside, size in plan.spans(index, first, value.shape[0]):
                sent[slot, j, p, place - base : place - base + size, :] = value[
                    inside : inside + size
                ].astype(jnp.bfloat16)

        products(index, mate, finish)
        send_partner(index).start()

    def send_partner(index):
        piece = chunks[index][4]
        return remote(
            sent.at[index % 2, :, :, pl.ds(0, piece)], partner.at[:, :, at(index)],
            (sem_ps, sem_pr), index, (mate, row, ctx),
        )

    def make_own(index):
        send_partner(index).wait_recv()

        def finish(j, first, value):
            for p, place, inside, size in plan.spans(index, first, value.shape[0]):
                rows = pl.ds(place, size)
                own[j, p // cx, p % cx, rows, :] = (
                    value[inside : inside + size] + partner[j, p, rows, :].astype(jnp.float32)
                ).astype(jnp.bfloat16)

        products(index, section, finish)
        for copy in first_copies(index):
            copy.start()

    def first_copies(index):
        rows, copies = at(index), []
        for k in range(1, cx):
            other = turn(px, k, cx)
            copies.append(remote(
                own.at[pl.ds(0, low), :, other, rows], rx1.at[k - 1, :, :, rows],
                (sem_x1.at[0], sem_x1.at[1]), (index, k - 1), (section, row, py * cx + other),
            ))
        if dp > low:
            for k in range(1, cy):
                other = turn(py, k, cy)
                copies.append(remote(
                    own.at[pl.ds(low, dp - low), other, :, rows], ry1.at[k - 1, :, :, rows],
                    (sem_y1.at[0], sem_y1.at[1]), (index, k - 1), (section, row, other * cx + px),
                ))
        return copies

    def second_copies(index):
        rows, copies = at(index), []
        for k in range(1, cy):
            other = turn(py, k, cy)
            copies.append(remote(
                own.at[pl.ds(0, low), other, px, rows], ry2.at[k - 1, :, rows],
                (sem_y2.at[0], sem_y2.at[1]), (index, k - 1), (section, row, other * cx + px),
            ))
        if dp > low:
            for k in range(1, cx):
                other = turn(px, k, cx)
                copies.append(remote(
                    own.at[pl.ds(low, dp - low), py, other, rows], rx2.at[k - 1, :, rows],
                    (sem_x2.at[0], sem_x2.at[1]), (index, k - 1), (section, row, py * cx + other),
                ))
        return copies

    def add_first(index):
        rows = at(index)
        for copy in first_copies(index):
            copy.wait()
        for j in range(low):
            for other in range(cy):
                total = own[j, other, px, rows, :].astype(jnp.float32)
                for k in range(cx - 1):
                    total = total + rx1[k, j, other, rows, :].astype(jnp.float32)
                own[j, other, px, rows, :] = total.astype(jnp.bfloat16)
        for j in range(low, dp):
            for other in range(cx):
                total = own[j, py, other, rows, :].astype(jnp.float32)
                for k in range(cy - 1):
                    total = total + ry1[k, j - low, other, rows, :].astype(jnp.float32)
                own[j, py, other, rows, :] = total.astype(jnp.bfloat16)
        for copy in second_copies(index):
            copy.start()

    def z_copies(index):
        rows, copies = at(index), []
        for k in range(1, dp):
            other = turn(row, k, dp)
            copies.append(remote(
                own.at[other, py, px, rows], rz.at[k - 1, rows],
                (sem_z.at[0], sem_z.at[1]), (index, k - 1), (section, other, ctx),
            ))
        return copies

    def add_second(index):
        rows = at(index)
        for copy in second_copies(index):
            copy.wait()
        for j in range(dp):
            total = own[j, py, px, rows, :].astype(jnp.float32)
            if j < low:
                for k in range(cy - 1):
                    total = total + ry2[k, j, rows, :].astype(jnp.float32)
            else:
                for k in range(cx - 1):
                    total = total + rx2[k, j - low, rows, :].astype(jnp.float32)
            own[j, py, px, rows, :] = total.astype(jnp.bfloat16)
        for copy in z_copies(index):
            copy.start()

    def gather_copies(index):
        rows, copies = at(index), []
        for k in range(1, plan.ctx):
            other = turn(ctx, k, plan.ctx)
            copies.append(remote(
                out.at[section, ctx, rows], out.at[section, ctx, rows],
                (sem_g.at[0], sem_g.at[1]), (index, k - 1), (section, row, other),
            ))
        return copies

    def forward_copy(index, k):
        rows = at(index)
        piece = turn(ctx, plan.ctx - k, plan.ctx)
        return remote(
            out.at[section, piece, rows], out.at[section, piece, rows],
            (sem_f.at[0], sem_f.at[1]), (index, k), (mate, row, ctx),
        )

    def add_last(index):
        rows = at(index)
        for copy in z_copies(index):
            copy.wait()
        total = own[row, py, px, rows, :].astype(jnp.float32)
        for k in range(dp - 1):
            total = total + rz[k, rows, :].astype(jnp.float32)
        out[section, ctx, rows, :] = total.astype(jnp.bfloat16)
        for copy in gather_copies(index):
            copy.start()
        forward_copy(index, 0).start()

    def pass_on(index):
        for k, copy in enumerate(gather_copies(index)):
            copy.wait()
            forward_copy(index, k + 1).start()

    def finish_all(index):
        for k in range(plan.ctx):
            forward_copy(index, k).wait()

    stages = (make_partner, make_own, add_first, add_second, add_last, pass_on, finish_all)
    for step in range(count + len(stages) - 1):
        for number, stage in enumerate(stages):
            if 0 <= step - number < count:
                stage(step - number)
    for index in range(max(count - 2, 0), count):
        send_partner(index).wait_send()


def reduce_grads(plan, *operands):
    dp, ctx, total = plan.dp, plan.ctx, plan.total
    low, high = plan.low, max(plan.dp - plan.low, 1)
    widest, count = max(c[4] for c in plan.chunks), len(plan.chunks)
    nx, ny, nz = max(plan.cx - 1, 1), max(plan.cy - 1, 1), max(dp - 1, 1)
    low_type = jnp.bfloat16
    dma = pltpu.SemaphoreType.DMA
    return pl.pallas_call(
        functools.partial(reduce_kernel, plan),
        out_shape=jax.ShapeDtypeStruct((2, ctx, total, LANES), low_type),
        in_specs=[pl.BlockSpec(memory_space=pltpu.VMEM)] * len(operands),
        out_specs=pl.BlockSpec(memory_space=pltpu.VMEM),
        scratch_shapes=[
            pltpu.VMEM((2, dp, ctx, widest, LANES), low_type),
            pltpu.VMEM((dp, ctx, total, LANES), low_type),
            pltpu.VMEM((dp, plan.cy, plan.cx, total, LANES), low_type),
            pltpu.VMEM((nx, low, plan.cy, total, LANES), low_type),
            pltpu.VMEM((ny, high, plan.cx, total, LANES), low_type),
            pltpu.VMEM((nx, high, total, LANES), low_type),
            pltpu.VMEM((ny, low, total, LANES), low_type),
            pltpu.VMEM((nz, total, LANES), low_type),
            dma((count,)),
            dma((count,)),
            dma((2, count, nx)),
            dma((2, count, ny)),
            dma((2, count, nx)),
            dma((2, count, ny)),
            dma((2, count, nz)),
            dma((2, count, max(ctx - 1, 1))),
            dma((2, count, ctx)),
        ],
        compiler_params=pltpu.CompilerParams(
            collective_id=0, has_side_effects=True, vmem_limit_bytes=64 << 20
        ),
        cost_estimate=pl.CostEstimate(flops=10**10, bytes_accessed=20 * 10**6, transcendentals=0),
    )(*operands)


def body(
    inputs,
    segment_ids,
    cotangent,
    gain_attn,
    w_query,
    w_key,
    w_value,
    w_out,
    gain_ffn,
    w_gate,
    w_up,
    w_down,
):
    micro_count, row_count, tok_local, model_width = inputs.shape
    kv_width = w_key.shape[1]
    group_size = HEADS // KV_HEADS
    section_index = lax.axis_index("section")
    on_first = section_index == 0
    ctx_index = lax.axis_index("ctx")
    first_token = ctx_index * tok_local
    query_pos = first_token + jnp.arange(tok_local, dtype=jnp.int32)
    halfway = HEAD_DIM // 2
    frequency = 10000.0 ** (-2.0 * jnp.arange(halfway, dtype=jnp.float32) / HEAD_DIM)
    angles = query_pos.astype(jnp.float32)[:, None] * frequency[None, :]
    cos_table = jnp.cos(angles)
    sine_table = jnp.sin(angles)
    w_pair = jnp.concatenate([w_key, w_value], 1)
    head_shape = (row_count, tok_local, KV_HEADS, group_size, HEAD_DIM)
    state_shape = (row_count, KV_HEADS, group_size, tok_local)

    def front(hidden, segments):
        query_seg = lax.dynamic_slice_in_dim(segments, first_token, tok_local, 1)
        normed, inverse = rms_forward(hidden, gain_attn)
        normed_low = normed.astype(jnp.bfloat16)
        query_pre = jnp.einsum(
            "rcd,de->rce", normed_low, w_query, preferred_element_type=jnp.float32
        )
        pair_pre = jnp.einsum("rcd,de->rce", normed_low, w_pair, preferred_element_type=jnp.float32)
        queries = rotate(
            query_pre.reshape(row_count, tok_local, HEADS, HEAD_DIM), cos_table, sine_table
        )
        queries = queries.astype(jnp.bfloat16).reshape(head_shape)
        key_rot = rotate(
            pair_pre[..., :kv_width].reshape(row_count, tok_local, KV_HEADS, HEAD_DIM),
            cos_table,
            sine_table,
        )
        packed = jnp.concatenate(
            [key_rot.reshape(row_count, tok_local, kv_width), pair_pre[..., kv_width:]], -1
        )
        return (query_seg, inverse, normed_low, queries, packed.astype(jnp.bfloat16))

    def attend_forward(queries, arrived, segments, query_seg):
        start_state = (
            jnp.full(state_shape, mask_floor, jnp.float32),
            jnp.zeros(state_shape, jnp.float32),
            jnp.zeros(state_shape + (HEAD_DIM,), jnp.float32),
        )
        piece_rows = arrived.shape[1]
        block_rows = math.gcd(piece_rows, 512)

        def fold_inner_step(step_index, loop_state):
            run_max, run_sum, run_acc = loop_state
            offset = step_index * block_rows
            key_block = lax.dynamic_slice_in_dim(arrived, step_index * block_rows, block_rows, 1)
            key_part = key_block[..., :kv_width].reshape(row_count, block_rows, KV_HEADS, HEAD_DIM)
            value_part = key_block[..., kv_width:].reshape(
                row_count, block_rows, KV_HEADS, HEAD_DIM
            )
            key_seg = lax.dynamic_slice_in_dim(segments, offset, block_rows, 1)
            scores, allowed = block_scores(queries, key_part, query_seg, key_seg, query_pos, offset)
            masked = jnp.where(allowed, scores, mask_floor)
            new_max = jnp.maximum(run_max, jnp.max(masked, -1))
            weights = jnp.where(allowed, jnp.exp(masked - new_max[..., None]), 0.0)
            rescale = jnp.exp(run_max - new_max)
            run_sum = run_sum * rescale + jnp.sum(weights, -1)
            run_acc = run_acc * rescale[..., None] + jnp.einsum(
                "rkgcn,rnkd->rkgcd",
                weights.astype(jnp.bfloat16),
                value_part,
                preferred_element_type=jnp.float32,
            )
            return (new_max, run_sum, run_acc)

        run_max, run_sum, run_acc = lax.fori_loop(
            0, piece_rows // block_rows, fold_inner_step, start_state
        )
        return (run_acc / run_sum[..., None], run_max + jnp.log(run_sum))

    def rear(hidden, attended):
        attn_low = (
            attended.transpose(0, 3, 1, 2, 4)
            .reshape(row_count, tok_local, HEADS * HEAD_DIM)
            .astype(jnp.bfloat16)
        )
        middle = hidden + jnp.einsum(
            "rce,ed->rcd", attn_low, w_out, preferred_element_type=jnp.float32
        )
        normed_ffn, inverse_ffn = rms_forward(middle, gain_ffn)
        ffn_low = normed_ffn.astype(jnp.bfloat16)
        gate_pre = jnp.einsum("rcd,df->rcf", ffn_low, w_gate, preferred_element_type=jnp.float32)
        upward = jnp.einsum("rcd,df->rcf", ffn_low, w_up, preferred_element_type=jnp.float32)
        inner_act = (jax.nn.silu(gate_pre) * upward).astype(jnp.bfloat16)
        output = middle + jnp.einsum(
            "rcf,fd->rcd", inner_act, w_down, preferred_element_type=jnp.float32
        )
        return (output, (attn_low, middle, inverse_ffn, ffn_low, gate_pre, upward, inner_act))


    assert micro_count == lax.axis_size("section")

    def mine(stacked):
        return lax.dynamic_index_in_dim(stacked, section_index, 0, keepdims=False)

    segments = mine(segment_ids)

    def forward(hidden):
        query_seg, inverse, normed_low, queries, packed = front(hidden, segments)
        arrived = lax.all_gather(packed, "ctx", axis=1, tiled=True)
        attended, log_sum = attend_forward(queries, arrived, segments, query_seg)
        output, saved = rear(hidden, attended)
        return output.astype(jnp.bfloat16), (
            hidden, query_seg, inverse, normed_low, queries, arrived, attended, log_sum, saved
        )

    def backward(grad_out, kept):
        (
            hidden,
            backward_query_seg,
            backward_inverse,
            backward_normed_low,
            backward_queries,
            piece_arrived,
            backward_attended,
            log_sum,
            saved,
        ) = kept
        (
            backward_attn_low,
            backward_middle,
            backward_inverse_ffn,
            backward_ffn_low,
            backward_gate_pre,
            backward_upward,
            backward_inner_act,
        ) = saved
        grad_low = grad_out.astype(jnp.bfloat16)
        grad_inner = jnp.einsum("rcd,fd->rcf", grad_low, w_down, preferred_element_type=jnp.float32)
        sigmoid = jax.nn.sigmoid(backward_gate_pre)
        grad_gate = (
            grad_inner * backward_upward * sigmoid * (1.0 + backward_gate_pre * (1.0 - sigmoid))
        ).astype(jnp.bfloat16)
        grad_up = (grad_inner * backward_gate_pre * sigmoid).astype(jnp.bfloat16)
        grad_norm_ffn = jnp.einsum(
            "rcf,df->rcd", grad_gate, w_gate, preferred_element_type=jnp.float32
        ) + jnp.einsum("rcf,df->rcd", grad_up, w_up, preferred_element_type=jnp.float32)
        grad_mid_norm, backward_sum_gain_ffn = rms_backward(
            backward_middle, gain_ffn, backward_inverse_ffn, grad_norm_ffn
        )
        grad_middle = grad_out + grad_mid_norm
        grad_branch = grad_middle.astype(jnp.bfloat16)
        grad_attn = jnp.einsum(
            "rcd,ed->rce", grad_branch, w_out, preferred_element_type=jnp.float32
        ).astype(jnp.bfloat16)
        grad_heads = grad_attn.reshape(head_shape).transpose(0, 2, 3, 1, 4)
        row_delta = jnp.sum(grad_heads.astype(jnp.float32) * backward_attended, -1)
        query_start = jnp.zeros(state_shape + (HEAD_DIM,), jnp.float32)
        fold_grad_query = query_start
        grad_query = fold_grad_query
        piece_piece_rows = piece_arrived.shape[1]
        piece_block_rows = math.gcd(piece_piece_rows, 512)

        def piece_inner_step(step_index, loop_state):
            grad_query, local_pair = loop_state
            inside = step_index * piece_block_rows
            key_block = lax.dynamic_slice_in_dim(piece_arrived, inside, piece_block_rows, 1)
            key_part = key_block[..., :kv_width].reshape(
                row_count, piece_block_rows, KV_HEADS, HEAD_DIM
            )
            value_part = key_block[..., kv_width:].reshape(
                row_count, piece_block_rows, KV_HEADS, HEAD_DIM
            )
            key_seg = lax.dynamic_slice_in_dim(segments, inside, piece_block_rows, 1)
            scores, allowed = block_scores(
                backward_queries, key_part, backward_query_seg, key_seg, query_pos, inside
            )
            chances = jnp.where(
                allowed, jnp.exp(jnp.where(allowed, scores, mask_floor) - log_sum[..., None]), 0.0
            )
            grad_chance = jnp.einsum(
                "rkgcd,rnkd->rkgcn", grad_heads, value_part, preferred_element_type=jnp.float32
            )
            grad_scores = (chances * (grad_chance - row_delta[..., None])).astype(jnp.bfloat16)
            grad_query = grad_query + score_scale * jnp.einsum(
                "rkgcn,rnkd->rkgcd", grad_scores, key_part, preferred_element_type=jnp.float32
            )
            grad_key = score_scale * jnp.einsum(
                "rkgcn,rckgd->rnkd",
                grad_scores,
                backward_queries,
                preferred_element_type=jnp.float32,
            )
            grad_value = jnp.einsum(
                "rkgcn,rkgcd->rnkd",
                chances.astype(jnp.bfloat16),
                grad_heads,
                preferred_element_type=jnp.float32,
            )
            update = jnp.concatenate(
                [
                    grad_key.reshape(row_count, piece_block_rows, kv_width),
                    grad_value.reshape(row_count, piece_block_rows, kv_width),
                ],
                -1,
            )
            current = lax.dynamic_slice_in_dim(local_pair, inside, piece_block_rows, 1)
            local_pair = lax.dynamic_update_slice_in_dim(local_pair, current + update, inside, 1)
            return (grad_query, local_pair)

        local_start = jnp.zeros((row_count, piece_piece_rows, 2 * kv_width), jnp.float32)
        fold_grad_query, fold_local_pair = lax.fori_loop(
            0, piece_piece_rows // piece_block_rows, piece_inner_step, (grad_query, local_start)
        )
        grad_pair = fold_local_pair
        grad_query, grad_pair = (fold_grad_query, grad_pair)
        pair_share = lax.psum_scatter(
            grad_pair.astype(jnp.bfloat16), "ctx", scatter_dimension=1, tiled=True
        ).astype(jnp.float32)
        query_tok = grad_query.transpose(0, 3, 1, 2, 4).reshape(
            row_count, tok_local, HEADS, HEAD_DIM
        )
        query_back = rotate(query_tok, cos_table, -sine_table).reshape(
            row_count, tok_local, HEADS * HEAD_DIM
        )
        query_back = query_back.astype(jnp.bfloat16)
        key_back = rotate(
            pair_share[..., :kv_width].reshape(row_count, tok_local, KV_HEADS, HEAD_DIM),
            cos_table,
            -sine_table,
        )
        pair_low = jnp.concatenate(
            [key_back.reshape(row_count, tok_local, kv_width), pair_share[..., kv_width:]], -1
        )
        pair_low = pair_low.astype(jnp.bfloat16)
        grad_normed = jnp.einsum(
            "rce,de->rcd", query_back, w_query, preferred_element_type=jnp.float32
        ) + jnp.einsum("rce,de->rcd", pair_low, w_pair, preferred_element_type=jnp.float32)
        grad_front, backward_sum_gain_attn = rms_backward(
            hidden, gain_attn, backward_inverse, grad_normed
        )
        factors = (
            backward_normed_low, backward_attn_low, backward_ffn_low, backward_inner_act,
            query_back, pair_low, grad_branch, grad_gate, grad_up, grad_low,
        )
        tick_grads = (backward_sum_gain_attn, backward_sum_gain_ffn, factors)
        return grad_middle + grad_front, tick_grads

    def exchange(for_first, for_last):
        kept = jnp.where(on_first, for_first, for_last)
        sent = jnp.where(on_first, for_last, for_first)
        got = lax.ppermute(sent, "section", [(0, 1), (1, 0)])
        return jnp.where(
            on_first, jnp.stack([kept, got]), jnp.stack([got, kept])
        )

    first_low, first_kept = forward(mine(inputs).astype(jnp.float32))
    second_low, second_kept = forward(first_low.astype(jnp.float32))
    grad_mid, second_grads = backward(mine(cotangent).astype(jnp.float32), second_kept)
    grad_mid_low = grad_mid.astype(jnp.bfloat16)
    grad_in, first_grads = backward(grad_mid_low.astype(jnp.float32), first_kept)
    plan = Plan(
        lax.axis_size("dp"), lax.axis_size("ctx"), model_width, w_gate.shape[1], kv_width
    )
    dp = plan.dp

    def stacked(one, other):
        return jnp.concatenate([one, other], 1).reshape(-1, one.shape[-1])

    normed, attn, ffn, inner, d_query, d_pair, d_branch, d_gate, d_up, d_out = (
        stacked(one, other) for one, other in zip(first_grads[2], second_grads[2])
    )
    tokens = normed.shape[0]

    def sides(values, rows):
        cut = values.reshape(tokens, dp, -1)
        cut = jnp.pad(cut, ((0, 0), (0, 0), (0, rows - cut.shape[2])))
        return cut.transpose(1, 2, 0)

    normed_t = sides(normed, plan.rows)
    halves = inner.reshape(tokens, dp, 2, -1)
    inner_t = jnp.stack([sides(halves[:, :, h], plan.down_rows) for h in range(2)])
    wide = plan.width_tiles * LANES
    spare = wide - model_width
    extra = jnp.stack([
        jnp.pad((one + other).reshape(dp, -1), ((0, 0), (0, 16 * LANES - model_width // dp)))
        for one, other in zip(first_grads[:2], second_grads[:2])
    ]).reshape(2, dp, 16, LANES)
    summed = reduce_grads(
        plan,
        sides(ffn, plan.rows),
        jnp.stack([d_gate, d_up]),
        inner_t,
        jnp.pad(d_out, ((0, 0), (0, spare))),
        jnp.stack([normed_t, sides(attn, plan.rows)]),
        jnp.pad(jnp.stack([d_query, d_branch]), ((0, 0), (0, 0), (0, spare))),
        jnp.pad(
            jnp.stack([d_pair[:, :kv_width], d_pair[:, kv_width:]]),
            ((0, 0), (0, 0), (LANES - spare, 0)),
        ),
        extra,
    )

    def tiles_of(kind):
        found = []
        for index, (name, start, tiles, rows, piece) in enumerate(plan.chunks):
            if name == kind:
                first = plan.offsets[index]
                flat = summed[:, :, first : first + piece].reshape(2, -1, LANES)
                found.append(flat[:, : tiles * rows].reshape(2, tiles, rows, LANES))
        return jnp.concatenate(found, 1)

    def joined(values, rows):
        values = values[:, :, :rows].transpose(0, 2, 1, 3)
        return values.reshape(2, rows, -1).astype(jnp.float32)

    ffn_sum = joined(tiles_of("ffn"), model_width // dp)
    down_sum = joined(tiles_of("down"), w_down.shape[0] // dp // 2)[:, :, :model_width]
    attn_sum = joined(
        jnp.concatenate([tiles_of("attn"), tiles_of("mixed")], 1), model_width // dp
    )
    kind, start, tiles, rows, piece = plan.chunks[-1]
    flat = summed[:, :, plan.offsets[-1] : plan.offsets[-1] + piece].reshape(2, -1)
    flat = flat[:, tiles * rows * LANES :][:, : model_width // dp].astype(jnp.float32)
    totals = (
        flat[0],
        attn_sum[0, :, :model_width],
        attn_sum[0, :, model_width:],
        attn_sum[1, :, model_width:],
        attn_sum[1, :, :model_width],
        flat[1],
        ffn_sum[0],
        ffn_sum[1],
        down_sum.reshape(-1, model_width),
    )
    activations = exchange(first_low, second_low)[None]
    input_grads = exchange(grad_in.astype(jnp.bfloat16), grad_mid_low).astype(jnp.float32)[None]
    return (
        activations,
        input_grads,
        totals[0],
        totals[1],
        totals[2],
        totals[3],
        totals[4],
        totals[5],
        totals[6],
        totals[7],
        totals[8],
    )


def solution(mesh):
    placed = (
        P(None, "dp", "ctx", None),
        P(None, "dp", None),
        P(None, "dp", "ctx", None),
        P(),
        P(),
        P(),
        P(),
        P(),
        P(),
        P(),
        P(),
        P(),
    )
    return jax.shard_map(
        body,
        mesh=mesh,
        in_specs=placed,
        out_specs=(
            P("section", None, "dp", "ctx", None),
            P("section", None, "dp", "ctx", None),
            P("dp"),
            P("dp", None),
            P("dp", None),
            P("dp", None),
            P("dp", None),
            P("dp"),
            P("dp", None),
            P("dp", None),
            P("dp", None),
        ),
        check_vma=False,
    )
```

```python
import functools
import math

import jax
import jax.numpy as jnp
import numpy as np
from jax import lax
from jax.experimental import pallas as pl
from jax.experimental.pallas import tpu as pltpu
from jax.sharding import PartitionSpec as P

HEADS = 15
KV_HEADS = 5
HEAD_DIM = 64
LANES = 128
MESH = pl.DeviceIdType.MESH


epsilon = 1e-05
score_scale = 0.125
score_unit = score_scale / math.log(2.0)
mask_floor = -1e30


def rms_forward(values, gain_vec):
    inverse = lax.rsqrt(jnp.mean(values * values, -1, keepdims=True) + epsilon)
    return (values * inverse * gain_vec, inverse)


def rms_backward(values, gain_vec, inverse, grad_normed):
    weighted = grad_normed * gain_vec
    grad_gain = jnp.sum(grad_normed * values * inverse, axis=(0, 1))
    cubed = inverse * inverse * inverse
    grad_values = inverse * weighted - values * cubed * jnp.mean(
        weighted * values, -1, keepdims=True
    )
    return (grad_values, grad_gain)


def rotate(values, cos_table, sine_table):
    halfway = values.shape[-1] // 2
    former = values[..., :halfway]
    latter = values[..., halfway:]
    cos_part = cos_table[None, :, None, :]
    sine_part = sine_table[None, :, None, :]
    return jnp.concatenate(
        [former * cos_part - latter * sine_part, latter * cos_part + former * sine_part], -1
    )


def block_scores(queries, key_part, query_seg, key_seg, query_pos, offset):
    block_rows = key_part.shape[1]
    scores = (
        jnp.einsum("rckgd,rnkd->rkgcn", queries, key_part, preferred_element_type=jnp.float32)
        * score_scale
    )
    key_pos = offset + jnp.arange(block_rows, dtype=jnp.int32)
    allowed = (query_seg[:, :, None] == key_seg[:, None, :]) & (
        key_pos[None, None, :] <= query_pos[None, :, None]
    )
    return (scores, allowed[:, None, None, :, :])


def up_to(value, step):
    return -(-value // step) * step


class Plan:
    def __init__(self, dp, ctx, width, hidden, kv_width):
        self.dp, self.ctx = dp, ctx
        self.cx = 1 << (ctx.bit_length() // 2) if ctx & (ctx - 1) == 0 else ctx
        self.cy = ctx // self.cx
        self.low = max(dp // 2, 1)
        self.rows = up_to(width // dp, 16)
        self.down_rows = up_to(hidden // dp // 2, 16)
        self.up_tiles = hidden // LANES
        self.width_tiles = up_to(width, LANES) // LANES
        self.pair_tiles = (width + kv_width) // LANES
        chunks = []
        for kind, count, rows, step in (
            ("ffn", self.up_tiles, self.rows, 4),
            ("down", self.width_tiles, self.down_rows, 4),
            ("attn", self.width_tiles - 1, self.rows, 4),
            ("mixed", self.pair_tiles - self.width_tiles + 1, self.rows, 4),
        ):
            for start in range(0, count, step):
                tiles = min(step, count - start)
                extra = 16 if kind == "mixed" else 0
                piece = up_to(up_to(tiles * rows + extra, ctx) // ctx, 16)
                chunks.append((kind, start, tiles, rows, piece))
        self.chunks = chunks
        self.offsets = [sum(c[4] for c in chunks[:i]) for i in range(len(chunks))]
        self.total = sum(c[4] for c in chunks)

    def spans(self, index, first, count):
        piece = self.chunks[index][4]
        out, done = [], 0
        while done < count:
            at = first + done
            size = min(count - done, piece - at % piece)
            out.append((at // piece, self.offsets[index] + at % piece, done, size))
            done += size
        return out


def reduce_kernel(
    plan, ffn_x, ffn_dy, down_x, down_dy, attn_x, attn_dy, pair_dy, extra, out,
    sent, partner, own, rx1, ry1, rx2, ry2, rz,
    sem_ps, sem_pr, sem_x1, sem_y1, sem_x2, sem_y2, sem_z, sem_g, sem_f,
):
    dp, cx, cy, low = plan.dp, plan.cx, plan.cy, plan.low
    section, row, ctx = (lax.axis_index(name) for name in ("section", "dp", "ctx"))
    px, py = lax.rem(ctx, cx), lax.div(ctx, cx)
    mate = 1 - section
    chunks, count = plan.chunks, len(plan.chunks)

    def at(index):
        return pl.ds(plan.offsets[index], chunks[index][4])

    def turn(base, step, size):
        return lax.rem(base + step, size)

    barrier = pltpu.get_barrier_semaphore()
    friends = [(mate, row, ctx)]
    friends += [(section, turn(row, k, dp), ctx) for k in range(1, dp)]
    friends += [(section, row, turn(ctx, k, plan.ctx)) for k in range(1, plan.ctx)]
    for friend in friends:
        pl.semaphore_signal(barrier, 1, device_id=friend, device_id_type=MESH)
    pl.semaphore_wait(barrier, len(friends))

    def remote(source, target, sems, place, device):
        return pltpu.make_async_remote_copy(
            source, target, sems[0].at[place], sems[1].at[place], device_id=device, device_id_type=MESH
        )

    def products(index, half, finish):
        kind, start, tiles, rows, piece = chunks[index]

        def shard(j, carry):
            if kind == "ffn":
                value = jnp.dot(
                    ffn_x[j], ffn_dy[half, :, start * LANES : (start + tiles) * LANES],
                    preferred_element_type=jnp.float32,
                )
            elif kind == "down":
                value = jnp.dot(
                    down_x[2 * j + half], down_dy[:, start * LANES : (start + tiles) * LANES],
                    preferred_element_type=jnp.float32,
                )
            elif kind == "attn":
                value = jnp.dot(
                    attn_x[half, j], attn_dy[half, :, start * LANES : (start + tiles) * LANES],
                    preferred_element_type=jnp.float32,
                )
            else:
                value = jnp.dot(
                    attn_x[0, j], pair_dy[half], preferred_element_type=jnp.float32
                )
                last = plan.width_tiles - 1
                mixed = jnp.dot(
                    attn_x[half, j], attn_dy[half, :, last * LANES :], preferred_element_type=jnp.float32
                )
                value = jnp.concatenate([value[:, :LANES] + mixed, value[:, LANES:]], 1)
            for tile in range(tiles):
                finish(j, tile * rows, value[:, tile * LANES : (tile + 1) * LANES])
            if kind == "mixed":
                finish(j, tiles * rows, extra[half, j])
            return carry

        lax.fori_loop(0, dp, shard, 0)

    def make_partner(index):
        if index >= 2:
            send_partner(index - 2).wait_send()
        slot = index % 2
        base = plan.offsets[index]

        def finish(j, first, value):
            for p, place, inside, size in plan.spans(index, first, value.shape[0]):
                sent[slot, j, p, place - base : place - base + size, :] = value[
                    inside : inside + size
                ].astype(jnp.bfloat16)

        products(index, mate, finish)
        send_partner(index).start()

    def send_partner(index):
        piece = chunks[index][4]
        return remote(
            sent.at[index % 2, :, :, pl.ds(0, piece)], partner.at[:, :, at(index)],
            (sem_ps, sem_pr), index, (mate, row, ctx),
        )

    def make_own(index):
        send_partner(index).wait_recv()

        def finish(j, first, value):
            for p, place, inside, size in plan.spans(index, first, value.shape[0]):
                rows = pl.ds(place, size)
                own[j, p // cx, p % cx, rows, :] = (
                    value[inside : inside + size] + partner[j, p, rows, :].astype(jnp.float32)
                ).astype(jnp.bfloat16)

        products(index, section, finish)
        for copy in first_copies(index):
            copy.start()

    def first_copies(index):
        rows, copies = at(index), []
        for k in range(1, cx):
            other = turn(px, k, cx)
            copies.append(remote(
                own.at[pl.ds(0, low), :, other, rows], rx1.at[k - 1, :, :, rows],
                (sem_x1.at[0], sem_x1.at[1]), (index, k - 1), (section, row, py * cx + other),
            ))
        if dp > low:
            for k in range(1, cy):
                other = turn(py, k, cy)
                copies.append(remote(
                    own.at[pl.ds(low, dp - low), other, :, rows], ry1.at[k - 1, :, :, rows],
                    (sem_y1.at[0], sem_y1.at[1]), (index, k - 1), (section, row, other * cx + px),
                ))
        return copies

    def second_copies(index):
        rows, copies = at(index), []
        for k in range(1, cy):
            other = turn(py, k, cy)
            copies.append(remote(
                own.at[pl.ds(0, low), other, px, rows], ry2.at[k - 1, :, rows],
                (sem_y2.at[0], sem_y2.at[1]), (index, k - 1), (section, row, other * cx + px),
            ))
        if dp > low:
            for k in range(1, cx):
                other = turn(px, k, cx)
                copies.append(remote(
                    own.at[pl.ds(low, dp - low), py, other, rows], rx2.at[k - 1, :, rows],
                    (sem_x2.at[0], sem_x2.at[1]), (index, k - 1), (section, row, py * cx + other),
                ))
        return copies

    def add_first(index):
        rows = at(index)
        for copy in first_copies(index):
            copy.wait()
        for j in range(low):
            for other in range(cy):
                total = own[j, other, px, rows, :].astype(jnp.float32)
                for k in range(cx - 1):
                    total = total + rx1[k, j, other, rows, :].astype(jnp.float32)
                own[j, other, px, rows, :] = total.astype(jnp.bfloat16)
        for j in range(low, dp):
            for other in range(cx):
                total = own[j, py, other, rows, :].astype(jnp.float32)
                for k in range(cy - 1):
                    total = total + ry1[k, j - low, other, rows, :].astype(jnp.float32)
                own[j, py, other, rows, :] = total.astype(jnp.bfloat16)
        for copy in second_copies(index):
            copy.start()

    def z_copies(index):
        rows, copies = at(index), []
        for k in range(1, dp):
            other = turn(row, k, dp)
            copies.append(remote(
                own.at[other, py, px, rows], rz.at[k - 1, rows],
                (sem_z.at[0], sem_z.at[1]), (index, k - 1), (section, other, ctx),
            ))
        return copies

    def add_second(index):
        rows = at(index)
        for copy in second_copies(index):
            copy.wait()
        for j in range(dp):
            total = own[j, py, px, rows, :].astype(jnp.float32)
            if j < low:
                for k in range(cy - 1):
                    total = total + ry2[k, j, rows, :].astype(jnp.float32)
            else:
                for k in range(cx - 1):
                    total = total + rx2[k, j - low, rows, :].astype(jnp.float32)
            own[j, py, px, rows, :] = total.astype(jnp.bfloat16)
        for copy in z_copies(index):
            copy.start()

    def gather_copies(index):
        rows, copies = at(index), []
        for k in range(1, plan.ctx):
            other = turn(ctx, k, plan.ctx)
            copies.append(remote(
                out.at[section, ctx, rows], out.at[section, ctx, rows],
                (sem_g.at[0], sem_g.at[1]), (index, k - 1), (section, row, other),
            ))
        return copies

    def forward_copy(index, k):
        rows = at(index)
        piece = turn(ctx, plan.ctx - k, plan.ctx)
        return remote(
            out.at[section, piece, rows], out.at[section, piece, rows],
            (sem_f.at[0], sem_f.at[1]), (index, k), (mate, row, ctx),
        )

    def add_last(index):
        rows = at(index)
        for copy in z_copies(index):
            copy.wait()
        total = own[row, py, px, rows, :].astype(jnp.float32)
        for k in range(dp - 1):
            total = total + rz[k, rows, :].astype(jnp.float32)
        out[section, ctx, rows, :] = total.astype(jnp.bfloat16)
        for copy in gather_copies(index):
            copy.start()
        forward_copy(index, 0).start()

    def pass_on(index):
        for k, copy in enumerate(gather_copies(index)):
            copy.wait()
            forward_copy(index, k + 1).start()

    def finish_all(index):
        for k in range(plan.ctx):
            forward_copy(index, k).wait()

    stages = (make_partner, make_own, add_first, add_second, add_last, pass_on, finish_all)
    for step in range(count + len(stages) - 1):
        for number, stage in enumerate(stages):
            if 0 <= step - number < count:
                stage(step - number)
    for index in range(max(count - 2, 0), count):
        send_partner(index).wait_send()


def reduce_grads(plan, *operands):
    dp, ctx, total = plan.dp, plan.ctx, plan.total
    low, high = plan.low, max(plan.dp - plan.low, 1)
    widest, count = max(c[4] for c in plan.chunks), len(plan.chunks)
    nx, ny, nz = max(plan.cx - 1, 1), max(plan.cy - 1, 1), max(dp - 1, 1)
    low_type = jnp.bfloat16
    dma = pltpu.SemaphoreType.DMA
    return pl.pallas_call(
        functools.partial(reduce_kernel, plan),
        out_shape=jax.ShapeDtypeStruct((2, ctx, total, LANES), low_type),
        in_specs=[pl.BlockSpec(memory_space=pltpu.VMEM)] * len(operands),
        out_specs=pl.BlockSpec(memory_space=pltpu.VMEM),
        scratch_shapes=[
            pltpu.VMEM((2, dp, ctx, widest, LANES), low_type),
            pltpu.VMEM((dp, ctx, total, LANES), low_type),
            pltpu.VMEM((dp, plan.cy, plan.cx, total, LANES), low_type),
            pltpu.VMEM((nx, low, plan.cy, total, LANES), low_type),
            pltpu.VMEM((ny, high, plan.cx, total, LANES), low_type),
            pltpu.VMEM((nx, high, total, LANES), low_type),
            pltpu.VMEM((ny, low, total, LANES), low_type),
            pltpu.VMEM((nz, total, LANES), low_type),
            dma((count,)),
            dma((count,)),
            dma((2, count, nx)),
            dma((2, count, ny)),
            dma((2, count, nx)),
            dma((2, count, ny)),
            dma((2, count, nz)),
            dma((2, count, max(ctx - 1, 1))),
            dma((2, count, ctx)),
        ],
        compiler_params=pltpu.CompilerParams(
            collective_id=0, has_side_effects=True, vmem_limit_bytes=64 << 20
        ),
        cost_estimate=pl.CostEstimate(flops=10**10, bytes_accessed=20 * 10**6, transcendentals=0),
    )(*operands)


class Block:
    def __init__(self, tokens, length, width, hidden, kv_width, ctx):
        self.tokens, self.length, self.width, self.hidden = tokens, length, width, hidden
        self.kv_width, self.ctx = kv_width, ctx
        self.kv_heads = kv_width // HEAD_DIM
        self.group = width // kv_width
        self.step = 512


def dot(one, other, over=(1, 0)):
    return lax.dot_general(
        one, other, (((over[0],), (over[1],)), ((), ())), preferred_element_type=jnp.float32
    )


def block_kernel(
    size, inputs, cotangent, segments, cos_q, sin_q, cos_kv, sin_kv, gain_attn, gain_ffn,
    wq_in, wk_in, wv_in, wo_in, wg_in, wu_in, wd_in,
    acts, grad_mid, grad_in, x_attn, n2_t, inner_t, d_attn, d_pair, d_ffn, d_out, gain_sums,
    wq, wk, wv, wo, wg, wu, wd, xin, cot, mid, q_t, kv, kv_send, kv_recv, lse, o_t, do_t, dq_t, bias, accum, dmid,
    sem_w, sem_k, sem_d,
):
    tokens, ctx_count, groups, group = size.tokens, size.ctx, size.kv_heads, size.group
    low_type = jnp.bfloat16
    section, row, ctx = (lax.axis_index(name) for name in ("section", "dp", "ctx"))
    loads = [
        pltpu.make_async_copy(source, target, sem_w.at[number])
        for number, (source, target) in enumerate((
            (inputs.at[section], xin.at[0]), (wk_in, wk), (wv_in, wv), (wq_in, wq), (wo_in, wo),
            (wg_in, wg), (wu_in, wu), (wd_in, wd), (cotangent.at[section], cot),
        ))
    ]
    for load in loads:
        load.start()
    barrier = pltpu.get_barrier_semaphore()
    for k in range(1, ctx_count):
        pl.semaphore_signal(
            barrier, 1, device_id=(section, row, lax.rem(ctx + k, ctx_count)), device_id_type=MESH
        )
    pl.semaphore_wait(barrier, ctx_count - 1)

    lane = lax.broadcasted_iota(jnp.int32, (tokens, LANES), 1)
    lower = lane < HEAD_DIM
    turn_up = (lane % HEAD_DIM) < HEAD_DIM // 2

    key_seg = jnp.broadcast_to(segments[section].astype(jnp.float32), (LANES, size.length)).T
    key_pos = lax.broadcasted_iota(jnp.int32, (size.length, LANES), 0)
    query_seg = segments[section, :, pl.ds(pl.multiple_of(ctx * tokens, tokens), tokens)]
    for part in range(tokens // LANES):
        cols = slice(part * LANES, (part + 1) * LANES)
        query_pos = (
            lax.broadcasted_iota(jnp.int32, (size.length, LANES), 1) + part * LANES + ctx * tokens
        )
        allowed = (key_seg == query_seg[:, cols].astype(jnp.float32)) & (key_pos <= query_pos)
        bias[:, cols] = jnp.where(allowed, 0.0, mask_floor)

    for k in range(1, ctx_count):
        @pl.when(ctx + k < ctx_count)
        def _():
            rows = pl.ds(pl.multiple_of((ctx + k) * tokens, tokens), tokens)
            for app in range(2):
                kv[app, :, rows, :] = jnp.zeros((groups, tokens, LANES), low_type)

    own_rows = pl.ds(pl.multiple_of(ctx * tokens, tokens), tokens)

    def kv_copy(app, g, k):
        return pltpu.make_async_remote_copy(
            kv.at[app, g, own_rows], kv.at[app, g, own_rows],
            sem_k.at[0, app, g, k - 1], sem_k.at[1, app, g, k - 1],
            device_id=(section, row, jnp.minimum(ctx + k, ctx_count - 1)), device_id_type=MESH,
        )

    def grad_copy(app, g, k):
        owner = jnp.maximum(ctx - k, 0)
        rows = pl.ds(pl.multiple_of(owner * tokens, tokens), tokens)
        return pltpu.make_async_remote_copy(
            kv_send.at[app, g, rows], kv_recv.at[app, k - 1, g],
            sem_d.at[0, app, g, k - 1], sem_d.at[1, app, g, k - 1],
            device_id=(section, row, owner), device_id_type=MESH,
        )

    def norm(values):
        return lax.rsqrt(jnp.mean(values * values, -1, keepdims=True) + epsilon)

    def norm_back(values, gain_vec, grad_normed):
        inverse = norm(values)
        weighted = grad_normed * gain_vec
        gain_grad = jnp.sum(grad_normed * values * inverse, axis=0, keepdims=True)
        cubed = inverse * inverse * inverse
        return inverse * weighted - values * cubed * jnp.mean(
            weighted * values, -1, keepdims=True
        ), gain_grad

    def rope_lanes(tile, sine):
        partner = jnp.where(turn_up, pltpu.roll(tile, 96, 1), pltpu.roll(tile, 32, 1))
        return tile * cos_kv[...] + partner * sine

    def rope_rows(values, sign):
        half = HEAD_DIM // 2
        out = []
        for start in range(0, values.shape[0], HEAD_DIM):
            former = values[start : start + half]
            latter = values[start + half : start + HEAD_DIM]
            out.append(former * cos_q[...] - latter * (sign * sin_q[...]))
            out.append(latter * cos_q[...] + former * (sign * sin_q[...]))
        return jnp.concatenate(out, 0)

    def half_tiles(values):
        spare = (-values.shape[1]) % LANES
        if spare:
            values = jnp.concatenate([values, jnp.zeros((values.shape[0], spare), values.dtype)], 1)
        out = []
        for g in range(groups):
            tile = values[:, g // 2 * LANES : (g // 2 + 1) * LANES]
            turned = pltpu.roll(tile, HEAD_DIM, 1)
            out.append((tile, turned) if g % 2 == 0 else (turned, tile))
        return out

    def app_tokens(app):
        return slice(app * tokens, (app + 1) * tokens)

    def forward(app):
        x = xin[app].astype(jnp.float32)
        normed = (x * norm(x) * gain_attn[...]).astype(low_type)
        if app == 0:
            loads[1].wait()
            loads[2].wait()
        keys = half_tiles(dot(normed, wk[...]))
        values = half_tiles(dot(normed, wv[...]))
        for g in range(groups):
            tile = rope_lanes(jnp.where(lower, keys[g][0], values[g][1]), sin_kv[...])
            kv[app, g, own_rows, :] = tile.astype(low_type)
            for k in range(1, ctx_count):
                @pl.when(ctx + k < ctx_count)
                def _():
                    kv_copy(app, g, k).start()
        x_attn[0, :, app_tokens(app)] = normed.T
        if app == 0:
            loads[3].wait()
        for start in range(0, size.width, LANES):
            stop = min(start + LANES, size.width)
            tile = dot(normed, wq[:, start:stop])
            q_t[app, start:stop, :] = rope_rows(tile.T, 1.0).astype(low_type)

        def heads(g, carry):
            for k in range(1, ctx_count):
                @pl.when(ctx - k >= 0)
                def _():
                    kv_copy(app, g, k).wait_recv()
            kv_g = kv[app, g]
            v_t = kv_g.T[HEAD_DIM:]
            for h in range(group):
                rows = pl.ds(pl.multiple_of((g * group + h) * HEAD_DIM, HEAD_DIM), HEAD_DIM)
                query = q_t[app, rows, :]
                query = jnp.concatenate([query, jnp.zeros_like(query)], 0)
                scores = dot(kv_g, query) * score_unit + bias[...]
                largest = jnp.max(scores, 0, keepdims=True)
                weights = jnp.exp2(scores - largest)
                total = jnp.sum(weights, 0, keepdims=True)
                out = dot(v_t, weights.astype(low_type)) / total
                lse[app, g, h : h + 1, :] = largest + jnp.log(total) * (1.0 / math.log(2.0))
                o_t[app, rows, :] = out
                x_attn[1, rows, app_tokens(app)] = out.astype(low_type)
            return carry

        lax.fori_loop(0, groups, heads, 0)
        if app == 0:
            loads[4].wait()
        x = xin[app].astype(jnp.float32)
        middle = x + dot(x_attn[1, :, app_tokens(app)], wo[...], (0, 0))
        mid[app] = middle
        ffn = (middle * norm(middle) * gain_ffn[...]).astype(low_type)
        n2_t[:, app_tokens(app)] = ffn.T
        if app == 0:
            for load in loads[5:8]:
                load.wait()
        accum[...] = middle

        def chunk(i, carry):
            cols = pl.ds(pl.multiple_of(i * size.step, size.step), size.step)
            gate = dot(ffn, wg[:, cols])
            upward = dot(ffn, wu[:, cols])
            inner = (gate / (1.0 + jnp.exp(-gate)) * upward).astype(low_type)
            d_ffn[0, app_tokens(app), cols] = gate.astype(low_type)
            d_ffn[1, app_tokens(app), cols] = upward.astype(low_type)
            inner_t[cols, app_tokens(app)] = inner.T
            accum[...] += dot(inner, wd[cols, :])
            return carry

        lax.fori_loop(0, size.hidden // size.step, chunk, 0)
        acts[app] = accum[...].astype(low_type)
        if app == 0:
            xin[1] = accum[...].astype(low_type)

    def backward(app, grad_low):
        d_out[app_tokens(app), : size.width] = grad_low
        d_out[app_tokens(app), size.width :] = jnp.zeros(
            (tokens, d_out.shape[1] - size.width), low_type
        )
        accum[...] = jnp.zeros_like(accum)

        def chunk(i, carry):
            cols = pl.ds(pl.multiple_of(i * size.step, size.step), size.step)
            gate = d_ffn[0, app_tokens(app), cols].astype(jnp.float32)
            upward = d_ffn[1, app_tokens(app), cols].astype(jnp.float32)
            grad_inner = dot(d_out[app_tokens(app), : size.width], wd[cols, :], (1, 1))
            sigmoid = 1.0 / (1.0 + jnp.exp(-gate))
            scaled = grad_inner * sigmoid
            grad_gate = (scaled * upward * (1.0 + gate * (1.0 - sigmoid))).astype(low_type)
            grad_up = (scaled * gate).astype(low_type)
            d_ffn[0, app_tokens(app), cols] = grad_gate
            d_ffn[1, app_tokens(app), cols] = grad_up
            accum[...] += dot(grad_gate, wg[:, cols], (1, 1)) + dot(grad_up, wu[:, cols], (1, 1))
            return carry

        lax.fori_loop(0, size.hidden // size.step, chunk, 0)
        grad, gain_grad = norm_back(mid[app], gain_ffn[...], accum[...])
        gain_sums[1:2] += gain_grad
        dmid[...] = d_out[app_tokens(app), : size.width].astype(jnp.float32) + grad
        branch = dmid[...].astype(low_type)
        d_attn[1, app_tokens(app), : size.width] = branch
        do_t[...] = dot(wo[...], branch, (1, 1)).astype(low_type)

        def heads(g, carry):
            kv_g = kv[app, g]
            k_t = kv_g.T[:HEAD_DIM]
            total = jnp.zeros((size.length, LANES), jnp.float32)
            for h in range(group):
                rows = pl.ds(pl.multiple_of((g * group + h) * HEAD_DIM, HEAD_DIM), HEAD_DIM)
                query, grad_head = q_t[app, rows, :], do_t[rows, :]
                empty = jnp.zeros_like(query)
                grad_pad = jnp.concatenate([empty, grad_head], 0)
                scores = dot(kv_g, jnp.concatenate([query, empty], 0)) * score_unit + bias[...]
                chances = jnp.exp2(scores - lse[app, g, h : h + 1, :])
                delta = jnp.sum(
                    grad_head.astype(jnp.float32) * o_t[app, rows, :], 0, keepdims=True
                )
                grad_scores = (chances * (dot(kv_g, grad_pad) - delta)).astype(low_type)
                small = (query.astype(jnp.float32) * score_scale).astype(low_type)
                total = total + dot(
                    grad_scores, jnp.concatenate([small, empty], 0), (1, 1)
                ) + dot(chances.astype(low_type), grad_pad, (1, 1))
                dq_t[rows, :] = dot(k_t, grad_scores) * score_scale
            kv_send[app, g] = total.astype(low_type)
            for k in range(1, ctx_count):
                @pl.when(ctx - k >= 0)
                def _():
                    grad_copy(app, g, k).start()
            return carry

        lax.fori_loop(0, groups, heads, 0)
        for start in range(0, size.width, LANES):
            stop = min(start + LANES, size.width)
            tile = rope_rows(dq_t[start:stop, :], -1.0)
            d_attn[0, app_tokens(app), start:stop] = tile.astype(low_type).T
        d_attn[:, app_tokens(app), size.width :] = jnp.zeros(
            (2, tokens, d_attn.shape[2] - size.width), low_type
        )
        turned = []
        for g in range(groups):
            tile = kv_send[app, g, own_rows, :].astype(jnp.float32)
            for k in range(1, ctx_count):
                @pl.when(ctx + k < ctx_count)
                def _():
                    grad_copy(app, g, k).wait_recv()
                tile = tile + jnp.where(
                    ctx + k < ctx_count, kv_recv[app, k - 1, g].astype(jnp.float32), 0.0
                )
            tile = rope_lanes(tile, -sin_kv[...])
            turned.append((tile, pltpu.roll(tile, HEAD_DIM, 1)))
        empty = jnp.zeros((tokens, LANES), jnp.float32)
        pairs = []
        for half in range(2):
            pieces = [(one, other) if half == 0 else (other, one) for one, other in turned]
            tiles = [jnp.where(lower, 0.0, pieces[0][1])]
            for g in range(1, groups, 2):
                tiles.append(jnp.where(lower, pieces[g][0], pieces[g + 1][1]))
            for number, tile in enumerate(tiles):
                d_pair[half, app_tokens(app), number * LANES : (number + 1) * LANES] = tile.astype(
                    low_type
                )
            straight = [
                jnp.where(lower, pieces[g][0], pieces[g + 1][1] if g + 1 < groups else empty)
                for g in range(0, groups, 2)
            ]
            pairs.append(
                jnp.concatenate(straight, 1)[:, : size.kv_width].astype(low_type)
            )
        grad_normed = (
            dot(d_attn[0, app_tokens(app), : size.width], wq[...], (1, 1))
            + dot(pairs[0], wk[...], (1, 1))
            + dot(pairs[1], wv[...], (1, 1))
        )
        grad, gain_grad = norm_back(xin[app].astype(jnp.float32), gain_attn[...], grad_normed)
        gain_sums[0:1] += gain_grad
        return dmid[...] + grad

    gain_sums[...] = jnp.zeros_like(gain_sums)
    loads[0].wait()
    forward(0)
    forward(1)
    loads[8].wait()
    low = backward(1, cot[...]).astype(low_type)
    grad_mid[...] = low
    grad_in[...] = backward(0, low)

    def drain(g, carry):
        for app in range(2):
            for k in range(1, ctx_count):
                @pl.when(ctx + k < ctx_count)
                def _():
                    kv_copy(app, g, k).wait_send()

                @pl.when(ctx - k >= 0)
                def _():
                    grad_copy(app, g, k).wait_send()
        return carry

    lax.fori_loop(0, groups, drain, 0)


def run_block(size, plan, *operands):
    tokens, width, hidden, groups = size.tokens, size.width, size.hidden, size.kv_heads
    low, full = jnp.bfloat16, jnp.float32
    wide, kv_wide = plan.width_tiles * LANES, (plan.pair_tiles - plan.width_tiles + 1) * LANES
    both = 2 * tokens
    vmem = pl.BlockSpec(memory_space=pltpu.VMEM)
    far = pl.BlockSpec(memory_space=pl.ANY)
    dma = pltpu.SemaphoreType.DMA
    others = max(size.ctx - 1, 1)
    shapes = [
        ((2, tokens, width), low),
        ((tokens, width), low),
        ((tokens, width), full),
        ((2, width, both), low),
        ((width, both), low),
        ((hidden, both), low),
        ((2, both, wide), low),
        ((2, both, kv_wide), low),
        ((2, both, hidden), low),
        ((both, wide), low),
        ((2, width), full),
    ]
    scratch = [
        ((width, width), low),
        ((width, size.kv_width), low),
        ((width, size.kv_width), low),
        ((width, width), low),
        ((width, hidden), low),
        ((width, hidden), low),
        ((hidden, width), low),
        ((2, tokens, width), low),
        ((tokens, width), low),
        ((2, tokens, width), full),
        ((2, width, tokens), low),
        ((2, groups, size.length, LANES), low),
        ((2, groups, size.length, LANES), low),
        ((2, others, groups, tokens, LANES), low),
        ((2, groups, 8, tokens), full),
        ((2, width, tokens), full),
        ((width, tokens), low),
        ((width, tokens), full),
        ((size.length, tokens), full),
        ((tokens, width), full),
        ((tokens, width), full),
    ]
    return pl.pallas_call(
        functools.partial(block_kernel, size),
        out_shape=[jax.ShapeDtypeStruct(*shape) for shape in shapes],
        in_specs=[far, far] + [vmem] * 7 + [far] * 7,
        out_specs=[vmem] * len(shapes),
        scratch_shapes=[pltpu.VMEM(*shape) for shape in scratch] + [
            dma((9,)), dma((2, 2, groups, others)), dma((2, 2, groups, others)),
        ],
        compiler_params=pltpu.CompilerParams(
            collective_id=1, has_side_effects=True, vmem_limit_bytes=64 << 20
        ),
        cost_estimate=pl.CostEstimate(
            flops=4 * 10**10, bytes_accessed=40 * 10**6, transcendentals=3 * 10**7
        ),
    )(*operands)


def rotary(length):
    half = HEAD_DIM // 2
    frequency = 10000.0 ** (-2.0 * np.arange(half) / HEAD_DIM)
    angles = np.arange(length)[:, None] * frequency[None, :]
    cos, sine = np.cos(angles), np.sin(angles)
    kept, none = np.ones((length, HEAD_DIM)), np.zeros((length, HEAD_DIM))
    cos_kv = np.concatenate([cos, cos, kept], 1)
    sin_kv = np.concatenate([-sine, sine, none], 1)
    return [np.asarray(table, np.float32) for table in (cos, sine, cos_kv, sin_kv)]


def plain_block(
    plan, inputs, segment_ids, cotangent,
    gain_attn, w_query, w_key, w_value, w_out, gain_ffn, w_gate, w_up, w_down,
):
    micro_count, row_count, tok_local, model_width = inputs.shape
    kv_width = w_key.shape[1]
    group_size = HEADS // KV_HEADS
    section_index = lax.axis_index("section")
    on_first = section_index == 0
    ctx_index = lax.axis_index("ctx")
    first_token = ctx_index * tok_local
    query_pos = first_token + jnp.arange(tok_local, dtype=jnp.int32)
    halfway = HEAD_DIM // 2
    frequency = 10000.0 ** (-2.0 * jnp.arange(halfway, dtype=jnp.float32) / HEAD_DIM)
    angles = query_pos.astype(jnp.float32)[:, None] * frequency[None, :]
    cos_table = jnp.cos(angles)
    sine_table = jnp.sin(angles)
    w_pair = jnp.concatenate([w_key, w_value], 1)
    head_shape = (row_count, tok_local, KV_HEADS, group_size, HEAD_DIM)
    state_shape = (row_count, KV_HEADS, group_size, tok_local)

    def front(hidden, segments):
        query_seg = lax.dynamic_slice_in_dim(segments, first_token, tok_local, 1)
        normed, inverse = rms_forward(hidden, gain_attn)
        normed_low = normed.astype(jnp.bfloat16)
        query_pre = jnp.einsum(
            "rcd,de->rce", normed_low, w_query, preferred_element_type=jnp.float32
        )
        pair_pre = jnp.einsum("rcd,de->rce", normed_low, w_pair, preferred_element_type=jnp.float32)
        queries = rotate(
            query_pre.reshape(row_count, tok_local, HEADS, HEAD_DIM), cos_table, sine_table
        )
        queries = queries.astype(jnp.bfloat16).reshape(head_shape)
        key_rot = rotate(
            pair_pre[..., :kv_width].reshape(row_count, tok_local, KV_HEADS, HEAD_DIM),
            cos_table,
            sine_table,
        )
        packed = jnp.concatenate(
            [key_rot.reshape(row_count, tok_local, kv_width), pair_pre[..., kv_width:]], -1
        )
        return (query_seg, inverse, normed_low, queries, packed.astype(jnp.bfloat16))

    def attend_forward(queries, arrived, segments, query_seg):
        start_state = (
            jnp.full(state_shape, mask_floor, jnp.float32),
            jnp.zeros(state_shape, jnp.float32),
            jnp.zeros(state_shape + (HEAD_DIM,), jnp.float32),
        )
        piece_rows = arrived.shape[1]
        block_rows = math.gcd(piece_rows, 512)

        def fold_inner_step(step_index, loop_state):
            run_max, run_sum, run_acc = loop_state
            offset = step_index * block_rows
            key_block = lax.dynamic_slice_in_dim(arrived, step_index * block_rows, block_rows, 1)
            key_part = key_block[..., :kv_width].reshape(row_count, block_rows, KV_HEADS, HEAD_DIM)
            value_part = key_block[..., kv_width:].reshape(
                row_count, block_rows, KV_HEADS, HEAD_DIM
            )
            key_seg = lax.dynamic_slice_in_dim(segments, offset, block_rows, 1)
            scores, allowed = block_scores(queries, key_part, query_seg, key_seg, query_pos, offset)
            masked = jnp.where(allowed, scores, mask_floor)
            new_max = jnp.maximum(run_max, jnp.max(masked, -1))
            weights = jnp.where(allowed, jnp.exp(masked - new_max[..., None]), 0.0)
            rescale = jnp.exp(run_max - new_max)
            run_sum = run_sum * rescale + jnp.sum(weights, -1)
            run_acc = run_acc * rescale[..., None] + jnp.einsum(
                "rkgcn,rnkd->rkgcd",
                weights.astype(jnp.bfloat16),
                value_part,
                preferred_element_type=jnp.float32,
            )
            return (new_max, run_sum, run_acc)

        run_max, run_sum, run_acc = lax.fori_loop(
            0, piece_rows // block_rows, fold_inner_step, start_state
        )
        return (run_acc / run_sum[..., None], run_max + jnp.log(run_sum))

    def rear(hidden, attended):
        attn_low = (
            attended.transpose(0, 3, 1, 2, 4)
            .reshape(row_count, tok_local, HEADS * HEAD_DIM)
            .astype(jnp.bfloat16)
        )
        middle = hidden + jnp.einsum(
            "rce,ed->rcd", attn_low, w_out, preferred_element_type=jnp.float32
        )
        normed_ffn, inverse_ffn = rms_forward(middle, gain_ffn)
        ffn_low = normed_ffn.astype(jnp.bfloat16)
        gate_pre = jnp.einsum("rcd,df->rcf", ffn_low, w_gate, preferred_element_type=jnp.float32)
        upward = jnp.einsum("rcd,df->rcf", ffn_low, w_up, preferred_element_type=jnp.float32)
        inner_act = (jax.nn.silu(gate_pre) * upward).astype(jnp.bfloat16)
        output = middle + jnp.einsum(
            "rcf,fd->rcd", inner_act, w_down, preferred_element_type=jnp.float32
        )
        return (output, (attn_low, middle, inverse_ffn, ffn_low, gate_pre, upward, inner_act))


    assert micro_count == lax.axis_size("section")

    def mine(stacked):
        return lax.dynamic_index_in_dim(stacked, section_index, 0, keepdims=False)

    segments = mine(segment_ids)

    def forward(hidden):
        query_seg, inverse, normed_low, queries, packed = front(hidden, segments)
        arrived = lax.all_gather(packed, "ctx", axis=1, tiled=True)
        attended, log_sum = attend_forward(queries, arrived, segments, query_seg)
        output, saved = rear(hidden, attended)
        return output.astype(jnp.bfloat16), (
            hidden, query_seg, inverse, normed_low, queries, arrived, attended, log_sum, saved
        )

    def backward(grad_out, kept):
        (
            hidden,
            backward_query_seg,
            backward_inverse,
            backward_normed_low,
            backward_queries,
            piece_arrived,
            backward_attended,
            log_sum,
            saved,
        ) = kept
        (
            backward_attn_low,
            backward_middle,
            backward_inverse_ffn,
            backward_ffn_low,
            backward_gate_pre,
            backward_upward,
            backward_inner_act,
        ) = saved
        grad_low = grad_out.astype(jnp.bfloat16)
        grad_inner = jnp.einsum("rcd,fd->rcf", grad_low, w_down, preferred_element_type=jnp.float32)
        sigmoid = jax.nn.sigmoid(backward_gate_pre)
        grad_gate = (
            grad_inner * backward_upward * sigmoid * (1.0 + backward_gate_pre * (1.0 - sigmoid))
        ).astype(jnp.bfloat16)
        grad_up = (grad_inner * backward_gate_pre * sigmoid).astype(jnp.bfloat16)
        grad_norm_ffn = jnp.einsum(
            "rcf,df->rcd", grad_gate, w_gate, preferred_element_type=jnp.float32
        ) + jnp.einsum("rcf,df->rcd", grad_up, w_up, preferred_element_type=jnp.float32)
        grad_mid_norm, backward_sum_gain_ffn = rms_backward(
            backward_middle, gain_ffn, backward_inverse_ffn, grad_norm_ffn
        )
        grad_middle = grad_out + grad_mid_norm
        grad_branch = grad_middle.astype(jnp.bfloat16)
        grad_attn = jnp.einsum(
            "rcd,ed->rce", grad_branch, w_out, preferred_element_type=jnp.float32
        ).astype(jnp.bfloat16)
        grad_heads = grad_attn.reshape(head_shape).transpose(0, 2, 3, 1, 4)
        row_delta = jnp.sum(grad_heads.astype(jnp.float32) * backward_attended, -1)
        query_start = jnp.zeros(state_shape + (HEAD_DIM,), jnp.float32)
        fold_grad_query = query_start
        grad_query = fold_grad_query
        piece_piece_rows = piece_arrived.shape[1]
        piece_block_rows = math.gcd(piece_piece_rows, 512)

        def piece_inner_step(step_index, loop_state):
            grad_query, local_pair = loop_state
            inside = step_index * piece_block_rows
            key_block = lax.dynamic_slice_in_dim(piece_arrived, inside, piece_block_rows, 1)
            key_part = key_block[..., :kv_width].reshape(
                row_count, piece_block_rows, KV_HEADS, HEAD_DIM
            )
            value_part = key_block[..., kv_width:].reshape(
                row_count, piece_block_rows, KV_HEADS, HEAD_DIM
            )
            key_seg = lax.dynamic_slice_in_dim(segments, inside, piece_block_rows, 1)
            scores, allowed = block_scores(
                backward_queries, key_part, backward_query_seg, key_seg, query_pos, inside
            )
            chances = jnp.where(
                allowed, jnp.exp(jnp.where(allowed, scores, mask_floor) - log_sum[..., None]), 0.0
            )
            grad_chance = jnp.einsum(
                "rkgcd,rnkd->rkgcn", grad_heads, value_part, preferred_element_type=jnp.float32
            )
            grad_scores = (chances * (grad_chance - row_delta[..., None])).astype(jnp.bfloat16)
            grad_query = grad_query + score_scale * jnp.einsum(
                "rkgcn,rnkd->rkgcd", grad_scores, key_part, preferred_element_type=jnp.float32
            )
            grad_key = score_scale * jnp.einsum(
                "rkgcn,rckgd->rnkd",
                grad_scores,
                backward_queries,
                preferred_element_type=jnp.float32,
            )
            grad_value = jnp.einsum(
                "rkgcn,rkgcd->rnkd",
                chances.astype(jnp.bfloat16),
                grad_heads,
                preferred_element_type=jnp.float32,
            )
            update = jnp.concatenate(
                [
                    grad_key.reshape(row_count, piece_block_rows, kv_width),
                    grad_value.reshape(row_count, piece_block_rows, kv_width),
                ],
                -1,
            )
            current = lax.dynamic_slice_in_dim(local_pair, inside, piece_block_rows, 1)
            local_pair = lax.dynamic_update_slice_in_dim(local_pair, current + update, inside, 1)
            return (grad_query, local_pair)

        local_start = jnp.zeros((row_count, piece_piece_rows, 2 * kv_width), jnp.float32)
        fold_grad_query, fold_local_pair = lax.fori_loop(
            0, piece_piece_rows // piece_block_rows, piece_inner_step, (grad_query, local_start)
        )
        grad_pair = fold_local_pair
        grad_query, grad_pair = (fold_grad_query, grad_pair)
        pair_share = lax.psum_scatter(
            grad_pair.astype(jnp.bfloat16), "ctx", scatter_dimension=1, tiled=True
        ).astype(jnp.float32)
        query_tok = grad_query.transpose(0, 3, 1, 2, 4).reshape(
            row_count, tok_local, HEADS, HEAD_DIM
        )
        query_back = rotate(query_tok, cos_table, -sine_table).reshape(
            row_count, tok_local, HEADS * HEAD_DIM
        )
        query_back = query_back.astype(jnp.bfloat16)
        key_back = rotate(
            pair_share[..., :kv_width].reshape(row_count, tok_local, KV_HEADS, HEAD_DIM),
            cos_table,
            -sine_table,
        )
        pair_low = jnp.concatenate(
            [key_back.reshape(row_count, tok_local, kv_width), pair_share[..., kv_width:]], -1
        )
        pair_low = pair_low.astype(jnp.bfloat16)
        grad_normed = jnp.einsum(
            "rce,de->rcd", query_back, w_query, preferred_element_type=jnp.float32
        ) + jnp.einsum("rce,de->rcd", pair_low, w_pair, preferred_element_type=jnp.float32)
        grad_front, backward_sum_gain_attn = rms_backward(
            hidden, gain_attn, backward_inverse, grad_normed
        )
        factors = (
            backward_normed_low, backward_attn_low, backward_ffn_low, backward_inner_act,
            query_back, pair_low, grad_branch, grad_gate, grad_up, grad_low,
        )
        tick_grads = (backward_sum_gain_attn, backward_sum_gain_ffn, factors)
        return grad_middle + grad_front, tick_grads

    first_low, first_kept = forward(mine(inputs).astype(jnp.float32))
    second_low, second_kept = forward(first_low.astype(jnp.float32))
    grad_mid, second_grads = backward(mine(cotangent).astype(jnp.float32), second_kept)
    grad_mid_low = grad_mid.astype(jnp.bfloat16)
    grad_in, first_grads = backward(grad_mid_low.astype(jnp.float32), first_kept)
    dp = plan.dp

    def stacked(one, other):
        return jnp.concatenate([one, other], 1).reshape(-1, one.shape[-1])

    normed, attn, ffn, inner, d_query, d_pair, d_branch, d_gate, d_up, d_out = (
        stacked(one, other) for one, other in zip(first_grads[2], second_grads[2])
    )
    tokens = normed.shape[0]

    def sides(values, rows):
        cut = values.reshape(tokens, dp, -1)
        cut = jnp.pad(cut, ((0, 0), (0, 0), (0, rows - cut.shape[2])))
        return cut.transpose(1, 2, 0)

    halves = inner.reshape(tokens, dp, 2, -1)
    inner_t = jnp.stack([sides(halves[:, :, h], plan.down_rows) for h in range(2)], 1)
    spare = plan.width_tiles * LANES - model_width
    gain_sums = jnp.stack([one + other for one, other in zip(first_grads[:2], second_grads[:2])])
    factors = (
        sides(ffn, plan.rows),
        jnp.stack([d_gate, d_up]),
        inner_t.reshape(2 * dp, plan.down_rows, tokens),
        jnp.pad(d_out, ((0, 0), (0, spare))),
        jnp.stack([sides(normed, plan.rows), sides(attn, plan.rows)]),
        jnp.pad(jnp.stack([d_query, d_branch]), ((0, 0), (0, 0), (0, spare))),
        jnp.pad(
            jnp.stack([d_pair[:, :kv_width], d_pair[:, kv_width:]]),
            ((0, 0), (0, 0), (LANES - spare, 0)),
        ),
    )
    acts = (first_low, second_low)
    return acts, (grad_in, grad_mid_low), gain_sums, factors


def fused_block(
    size, plan, inputs, segment_ids, cotangent,
    gain_attn, w_query, w_key, w_value, w_out, gain_ffn, w_gate, w_up, w_down,
):
    tokens, width, dp = size.tokens, size.width, plan.dp
    first_token = lax.axis_index("ctx") * tokens
    cos_q, sin_q, cos_kv, sin_kv = (
        lax.dynamic_slice_in_dim(jnp.asarray(table), first_token, tokens, 0)
        for table in rotary(size.length)
    )
    (
        acts, grad_mid, grad_in, x_attn, n2_t, inner_t, d_attn, d_pair, d_ffn, d_out, gain_sums
    ) = run_block(
        size, plan, inputs[:, 0], cotangent[:, 0], segment_ids, cos_q.T, sin_q.T, cos_kv, sin_kv,
        gain_attn.astype(jnp.float32)[None], gain_ffn.astype(jnp.float32)[None],
        w_query, w_key, w_value, w_out, w_gate, w_up, w_down,
    )
    factors = (
        n2_t.reshape(dp, plan.rows, -1),
        d_ffn,
        inner_t.reshape(2 * dp, plan.down_rows, -1),
        d_out,
        x_attn.reshape(2, dp, plan.rows, -1),
        d_attn,
        d_pair,
    )
    return (acts[0][None], acts[1][None]), (grad_in[None], grad_mid[None]), gain_sums, factors


def body(
    inputs,
    segment_ids,
    cotangent,
    gain_attn,
    w_query,
    w_key,
    w_value,
    w_out,
    gain_ffn,
    w_gate,
    w_up,
    w_down,
):
    micro_count, row_count, tok_local, model_width = inputs.shape
    kv_width, hidden = w_key.shape[1], w_gate.shape[1]
    assert micro_count == lax.axis_size("section")
    on_first = lax.axis_index("section") == 0
    plan = Plan(lax.axis_size("dp"), lax.axis_size("ctx"), model_width, hidden, kv_width)
    dp = plan.dp
    size = Block(tok_local, segment_ids.shape[2], model_width, hidden, kv_width, plan.ctx)
    fits = (
        row_count == 1
        and size.length <= 1024
        and tok_local % LANES == 0
        and plan.rows * dp == model_width
        and plan.down_rows * dp * 2 == hidden
    )
    run = functools.partial(fused_block, size) if fits else plain_block
    acts, grads, gain_sums, factors = run(
        plan, inputs, segment_ids, cotangent,
        gain_attn, w_query, w_key, w_value, w_out, gain_ffn, w_gate, w_up, w_down,
    )
    extra = jnp.pad(
        gain_sums.reshape(2, dp, -1), ((0, 0), (0, 0), (0, 16 * LANES - model_width // dp))
    ).reshape(2, dp, 16, LANES)
    summed = reduce_grads(plan, *factors, extra)

    def exchange(for_first, for_last):
        kept = jnp.where(on_first, for_first, for_last)
        sent = jnp.where(on_first, for_last, for_first)
        got = lax.ppermute(sent, "section", [(0, 1), (1, 0)])
        return jnp.where(
            on_first, jnp.stack([kept, got]), jnp.stack([got, kept])
        )

    def tiles_of(kind):
        found = []
        for index, (name, start, tiles, rows, piece) in enumerate(plan.chunks):
            if name == kind:
                first = plan.offsets[index]
                flat = summed[:, :, first : first + piece].reshape(2, -1, LANES)
                found.append(flat[:, : tiles * rows].reshape(2, tiles, rows, LANES))
        return jnp.concatenate(found, 1)

    def joined(values, rows):
        values = values[:, :, :rows].transpose(0, 2, 1, 3)
        return values.reshape(2, rows, -1).astype(jnp.float32)

    ffn_sum = joined(tiles_of("ffn"), model_width // dp)
    down_sum = joined(tiles_of("down"), w_down.shape[0] // dp // 2)[:, :, :model_width]
    attn_sum = joined(
        jnp.concatenate([tiles_of("attn"), tiles_of("mixed")], 1), model_width // dp
    )
    kind, start, tiles, rows, piece = plan.chunks[-1]
    flat = summed[:, :, plan.offsets[-1] : plan.offsets[-1] + piece].reshape(2, -1)
    flat = flat[:, tiles * rows * LANES :][:, : model_width // dp].astype(jnp.float32)
    totals = (
        flat[0],
        attn_sum[0, :, :model_width],
        attn_sum[0, :, model_width:],
        attn_sum[1, :, model_width:],
        attn_sum[1, :, :model_width],
        flat[1],
        ffn_sum[0],
        ffn_sum[1],
        down_sum.reshape(-1, model_width),
    )
    activations = exchange(*acts)[None]
    input_grads = exchange(grads[0].astype(jnp.bfloat16), grads[1]).astype(jnp.float32)[None]
    return (
        activations,
        input_grads,
        totals[0],
        totals[1],
        totals[2],
        totals[3],
        totals[4],
        totals[5],
        totals[6],
        totals[7],
        totals[8],
    )


def solution(mesh):
    placed = (
        P(None, "dp", "ctx", None),
        P(None, "dp", None),
        P(None, "dp", "ctx", None),
        P(),
        P(),
        P(),
        P(),
        P(),
        P(),
        P(),
        P(),
        P(),
    )
    return jax.shard_map(
        body,
        mesh=mesh,
        in_specs=placed,
        out_specs=(
            P("section", None, "dp", "ctx", None),
            P("section", None, "dp", "ctx", None),
            P("dp"),
            P("dp", None),
            P("dp", None),
            P("dp", None),
            P("dp", None),
            P("dp"),
            P("dp", None),
            P("dp", None),
            P("dp", None),
        ),
        check_vma=False,
    )
```

```python
import functools
import math

import jax
import jax.numpy as jnp
import numpy as np
from jax import lax
from jax.experimental import pallas as pl
from jax.experimental.pallas import tpu as pltpu
from jax.sharding import PartitionSpec as P

HEADS = 15
KV_HEADS = 5
HEAD_DIM = 64
LANES = 128
MESH = pl.DeviceIdType.MESH


epsilon = 1e-05
score_scale = 0.125
score_unit = score_scale / math.log(2.0)
mask_floor = -1e30


def rms_forward(values, gain_vec):
    inverse = lax.rsqrt(jnp.mean(values * values, -1, keepdims=True) + epsilon)
    return (values * inverse * gain_vec, inverse)


def rms_backward(values, gain_vec, inverse, grad_normed):
    weighted = grad_normed * gain_vec
    grad_gain = jnp.sum(grad_normed * values * inverse, axis=(0, 1))
    cubed = inverse * inverse * inverse
    grad_values = inverse * weighted - values * cubed * jnp.mean(
        weighted * values, -1, keepdims=True
    )
    return (grad_values, grad_gain)


def rotate(values, cos_table, sine_table):
    halfway = values.shape[-1] // 2
    former = values[..., :halfway]
    latter = values[..., halfway:]
    cos_part = cos_table[None, :, None, :]
    sine_part = sine_table[None, :, None, :]
    return jnp.concatenate(
        [former * cos_part - latter * sine_part, latter * cos_part + former * sine_part], -1
    )


def block_scores(queries, key_part, query_seg, key_seg, query_pos, offset):
    block_rows = key_part.shape[1]
    scores = (
        jnp.einsum("rckgd,rnkd->rkgcn", queries, key_part, preferred_element_type=jnp.float32)
        * score_scale
    )
    key_pos = offset + jnp.arange(block_rows, dtype=jnp.int32)
    allowed = (query_seg[:, :, None] == key_seg[:, None, :]) & (
        key_pos[None, None, :] <= query_pos[None, :, None]
    )
    return (scores, allowed[:, None, None, :, :])


def up_to(value, step):
    return -(-value // step) * step


class Plan:
    def __init__(self, dp, ctx, width, hidden, kv_width):
        self.dp, self.ctx = dp, ctx
        self.cx = 1 << (ctx.bit_length() // 2) if ctx & (ctx - 1) == 0 else ctx
        self.cy = ctx // self.cx
        self.low = max(dp // 2, 1)
        self.shard = width // dp
        self.rows = up_to(width // dp, 16)
        self.down_rows = up_to(width // 2, 16)
        self.down_tiles = up_to(hidden // dp, LANES) // LANES
        self.up_tiles = hidden // LANES
        self.width_tiles = up_to(width, LANES) // LANES
        self.pair_tiles = (width + kv_width) // LANES
        chunks = []
        for kind, count, rows, step in (
            ("ffn", self.up_tiles, self.rows, 4),
            ("down", self.down_tiles, self.down_rows, 2),
            ("attn", self.width_tiles - 1, self.rows, 4),
            ("mixed", self.pair_tiles - self.width_tiles + 1, self.rows, 4),
        ):
            for start in range(0, count, step):
                tiles = min(step, count - start)
                extra = 16 if kind == "mixed" else 0
                piece = up_to(up_to(tiles * rows + extra, ctx) // ctx, 16)
                chunks.append((kind, start, tiles, rows, piece))
        self.chunks = chunks
        self.offsets = [sum(c[4] for c in chunks[:i]) for i in range(len(chunks))]
        self.total = sum(c[4] for c in chunks)

    def spans(self, index, first, count):
        piece = self.chunks[index][4]
        out, done = [], 0
        while done < count:
            at = first + done
            size = min(count - done, piece - at % piece)
            out.append((at // piece, self.offsets[index] + at % piece, done, size))
            done += size
        return out


def reduce_kernel(
    plan, ffn_x, ffn_dy, down_x, down_dy, attn_x, attn_dy, pair_dy, gain_sums, out,
    extra, sent, partner, own, rx1, ry1, rx2, ry2, rz,
    sem_ps, sem_pr, sem_x1, sem_y1, sem_x2, sem_y2, sem_z, sem_g, sem_f,
):
    dp, cx, cy, low = plan.dp, plan.cx, plan.cy, plan.low
    section, row, ctx = (lax.axis_index(name) for name in ("section", "dp", "ctx"))
    px, py = lax.rem(ctx, cx), lax.div(ctx, cx)
    mate = 1 - section
    chunks, count = plan.chunks, len(plan.chunks)

    def at(index):
        return pl.ds(plan.offsets[index], chunks[index][4])

    def turn(base, step, size):
        return lax.rem(base + step, size)

    barrier = pltpu.get_barrier_semaphore()
    friends = [(mate, row, ctx)]
    friends += [(section, turn(row, k, dp), ctx) for k in range(1, dp)]
    friends += [(section, row, turn(ctx, k, plan.ctx)) for k in range(1, plan.ctx)]
    for friend in friends:
        pl.semaphore_signal(barrier, 1, device_id=friend, device_id_type=MESH)
    pl.semaphore_wait(barrier, len(friends))

    for half in range(2):
        for j in range(dp):
            for number in range(-(-plan.shard // LANES)):
                start = j * plan.shard + number * LANES
                extra[half, j, number : number + 1, :] = gain_sums[
                    half : half + 1, start : start + LANES
                ]

    def remote(source, target, sems, place, device):
        return pltpu.make_async_remote_copy(
            source, target, sems[0].at[place], sems[1].at[place], device_id=device, device_id_type=MESH
        )

    def products(index, half, finish):
        kind, start, tiles, rows, piece = chunks[index]

        def shard(j, carry):
            if kind == "ffn":
                value = jnp.dot(
                    ffn_x[j], ffn_dy[half, :, start * LANES : (start + tiles) * LANES],
                    preferred_element_type=jnp.float32,
                )
            elif kind == "down":
                first = pl.multiple_of(j * (plan.down_tiles * LANES) + start * LANES, LANES)
                value = jnp.dot(
                    down_x[half], down_dy[:, pl.ds(first, tiles * LANES)],
                    preferred_element_type=jnp.float32,
                )
            elif kind == "attn":
                value = jnp.dot(
                    attn_x[half, j], attn_dy[half, :, start * LANES : (start + tiles) * LANES],
                    preferred_element_type=jnp.float32,
                )
            else:
                value = jnp.dot(
                    attn_x[0, j], pair_dy[half], preferred_element_type=jnp.float32
                )
                last = plan.width_tiles - 1
                mixed = jnp.dot(
                    attn_x[half, j], attn_dy[half, :, last * LANES :], preferred_element_type=jnp.float32
                )
                value = jnp.concatenate([value[:, :LANES] + mixed, value[:, LANES:]], 1)
            for tile in range(tiles):
                finish(j, tile * rows, value[:, tile * LANES : (tile + 1) * LANES])
            if kind == "mixed":
                finish(j, tiles * rows, extra[half, j])
            return carry

        lax.fori_loop(0, dp, shard, 0)

    def make_partner(index):
        if index >= 2:
            send_partner(index - 2).wait_send()
        slot = index % 2
        base = plan.offsets[index]

        def finish(j, first, value):
            for p, place, inside, size in plan.spans(index, first, value.shape[0]):
                sent[slot, j, p, place - base : place - base + size, :] = value[
                    inside : inside + size
                ].astype(jnp.bfloat16)

        products(index, mate, finish)
        send_partner(index).start()

    def send_partner(index):
        piece = chunks[index][4]
        return remote(
            sent.at[index % 2, :, :, pl.ds(0, piece)], partner.at[:, :, at(index)],
            (sem_ps, sem_pr), index, (mate, row, ctx),
        )

    def make_own(index):
        send_partner(index).wait_recv()

        def finish(j, first, value):
            for p, place, inside, size in plan.spans(index, first, value.shape[0]):
                rows = pl.ds(place, size)
                own[j, p // cx, p % cx, rows, :] = (
                    value[inside : inside + size] + partner[j, p, rows, :].astype(jnp.float32)
                ).astype(jnp.bfloat16)

        products(index, section, finish)
        for copy in first_copies(index):
            copy.start()

    def first_copies(index):
        rows, copies = at(index), []
        for k in range(1, cx):
            other = turn(px, k, cx)
            copies.append(remote(
                own.at[pl.ds(0, low), :, other, rows], rx1.at[k - 1, :, :, rows],
                (sem_x1.at[0], sem_x1.at[1]), (index, k - 1), (section, row, py * cx + other),
            ))
        if dp > low:
            for k in range(1, cy):
                other = turn(py, k, cy)
                copies.append(remote(
                    own.at[pl.ds(low, dp - low), other, :, rows], ry1.at[k - 1, :, :, rows],
                    (sem_y1.at[0], sem_y1.at[1]), (index, k - 1), (section, row, other * cx + px),
                ))
        return copies

    def second_copies(index):
        rows, copies = at(index), []
        for k in range(1, cy):
            other = turn(py, k, cy)
            copies.append(remote(
                own.at[pl.ds(0, low), other, px, rows], ry2.at[k - 1, :, rows],
                (sem_y2.at[0], sem_y2.at[1]), (index, k - 1), (section, row, other * cx + px),
            ))
        if dp > low:
            for k in range(1, cx):
                other = turn(px, k, cx)
                copies.append(remote(
                    own.at[pl.ds(low, dp - low), py, other, rows], rx2.at[k - 1, :, rows],
                    (sem_x2.at[0], sem_x2.at[1]), (index, k - 1), (section, row, py * cx + other),
                ))
        return copies

    def add_first(index):
        rows = at(index)
        for copy in first_copies(index):
            copy.wait()
        for j in range(low):
            for other in range(cy):
                total = own[j, other, px, rows, :].astype(jnp.float32)
                for k in range(cx - 1):
                    total = total + rx1[k, j, other, rows, :].astype(jnp.float32)
                own[j, other, px, rows, :] = total.astype(jnp.bfloat16)
        for j in range(low, dp):
            for other in range(cx):
                total = own[j, py, other, rows, :].astype(jnp.float32)
                for k in range(cy - 1):
                    total = total + ry1[k, j - low, other, rows, :].astype(jnp.float32)
                own[j, py, other, rows, :] = total.astype(jnp.bfloat16)
        for copy in second_copies(index):
            copy.start()

    def z_copies(index):
        rows, copies = at(index), []
        for k in range(1, dp):
            other = turn(row, k, dp)
            copies.append(remote(
                own.at[other, py, px, rows], rz.at[k - 1, rows],
                (sem_z.at[0], sem_z.at[1]), (index, k - 1), (section, other, ctx),
            ))
        return copies

    def add_second(index):
        rows = at(index)
        for copy in second_copies(index):
            copy.wait()
        for j in range(dp):
            total = own[j, py, px, rows, :].astype(jnp.float32)
            if j < low:
                for k in range(cy - 1):
                    total = total + ry2[k, j, rows, :].astype(jnp.float32)
            else:
                for k in range(cx - 1):
                    total = total + rx2[k, j - low, rows, :].astype(jnp.float32)
            own[j, py, px, rows, :] = total.astype(jnp.bfloat16)
        for copy in z_copies(index):
            copy.start()

    def gather_copies(index):
        rows, copies = at(index), []
        for k in range(1, plan.ctx):
            other = turn(ctx, k, plan.ctx)
            copies.append(remote(
                out.at[section, ctx, rows], out.at[section, ctx, rows],
                (sem_g.at[0], sem_g.at[1]), (index, k - 1), (section, row, other),
            ))
        return copies

    def forward_copy(index, k):
        rows = at(index)
        piece = turn(ctx, plan.ctx - k, plan.ctx)
        return remote(
            out.at[section, piece, rows], out.at[section, piece, rows],
            (sem_f.at[0], sem_f.at[1]), (index, k), (mate, row, ctx),
        )

    def add_last(index):
        rows = at(index)
        for copy in z_copies(index):
            copy.wait()
        total = own[row, py, px, rows, :].astype(jnp.float32)
        for k in range(dp - 1):
            total = total + rz[k, rows, :].astype(jnp.float32)
        out[section, ctx, rows, :] = total.astype(jnp.bfloat16)
        for copy in gather_copies(index):
            copy.start()
        forward_copy(index, 0).start()

    def pass_on(index):
        for k, copy in enumerate(gather_copies(index)):
            copy.wait()
            forward_copy(index, k + 1).start()

    def finish_all(index):
        for k in range(plan.ctx):
            forward_copy(index, k).wait()

    stages = (make_partner, make_own, add_first, add_second, add_last, pass_on, finish_all)
    for step in range(count + len(stages) - 1):
        for number, stage in enumerate(stages):
            if 0 <= step - number < count:
                stage(step - number)
    for index in range(max(count - 2, 0), count):
        send_partner(index).wait_send()


def reduce_grads(plan, *operands):
    dp, ctx, total = plan.dp, plan.ctx, plan.total
    low, high = plan.low, max(plan.dp - plan.low, 1)
    widest, count = max(c[4] for c in plan.chunks), len(plan.chunks)
    nx, ny, nz = max(plan.cx - 1, 1), max(plan.cy - 1, 1), max(dp - 1, 1)
    low_type = jnp.bfloat16
    dma = pltpu.SemaphoreType.DMA
    return pl.pallas_call(
        functools.partial(reduce_kernel, plan),
        out_shape=jax.ShapeDtypeStruct((2, ctx, total, LANES), low_type),
        in_specs=[pl.BlockSpec(memory_space=pltpu.VMEM)] * len(operands),
        out_specs=pl.BlockSpec(memory_space=pltpu.VMEM),
        scratch_shapes=[
            pltpu.VMEM((2, dp, 16, LANES), jnp.float32),
            pltpu.VMEM((2, dp, ctx, widest, LANES), low_type),
            pltpu.VMEM((dp, ctx, total, LANES), low_type),
            pltpu.VMEM((dp, plan.cy, plan.cx, total, LANES), low_type),
            pltpu.VMEM((nx, low, plan.cy, total, LANES), low_type),
            pltpu.VMEM((ny, high, plan.cx, total, LANES), low_type),
            pltpu.VMEM((nx, high, total, LANES), low_type),
            pltpu.VMEM((ny, low, total, LANES), low_type),
            pltpu.VMEM((nz, total, LANES), low_type),
            dma((count,)),
            dma((count,)),
            dma((2, count, nx)),
            dma((2, count, ny)),
            dma((2, count, nx)),
            dma((2, count, ny)),
            dma((2, count, nz)),
            dma((2, count, max(ctx - 1, 1))),
            dma((2, count, ctx)),
        ],
        compiler_params=pltpu.CompilerParams(
            collective_id=0, has_side_effects=True, vmem_limit_bytes=64 << 20
        ),
        cost_estimate=pl.CostEstimate(flops=10**10, bytes_accessed=20 * 10**6, transcendentals=0),
    )(*operands)


class Block:
    def __init__(self, tokens, length, width, hidden, kv_width, ctx):
        self.tokens, self.length, self.width, self.hidden = tokens, length, width, hidden
        self.kv_width, self.ctx = kv_width, ctx
        self.kv_heads = kv_width // HEAD_DIM
        self.group = width // kv_width
        self.step = 512


def dot(one, other, over=(1, 0)):
    return lax.dot_general(
        one, other, (((over[0],), (over[1],)), ((), ())), preferred_element_type=jnp.float32
    )


def fold_rows(values, combine):
    return combine(values.reshape(values.shape[0] // 8, 8, values.shape[1]), 0)


def block_kernel(
    size, inputs, cotangent, segments, cos_in, sin_in, gains,
    wq_in, wk_in, wv_in, wo_in, wg_in, wu_in, wd_in,
    acts, grads, x_attn, n2_t, df_t, inner, d_attn, d_pair, d_ffn, gain_sums,
    wq, wk, wv, wo, wg, wu, wd, cos_q, sin_q, columns, xin, cot, last, grad_stage, mid, q_t,
    kv, kv_send, kv_recv, lse, do_t, bias, accum, dmid, natural, scores, chances, grad_scores,
    sem_w, sem_k, sem_d, sem_e,
):
    tokens, ctx_count, groups, group = size.tokens, size.ctx, size.kv_heads, size.group
    width, low_type, full = size.width, jnp.bfloat16, jnp.float32
    section, row, ctx = (lax.axis_index(name) for name in ("section", "dp", "ctx"))
    mate = (1 - section, row, ctx)
    own_rows = pl.ds(pl.multiple_of(ctx * tokens, tokens), tokens)
    loads = [
        pltpu.make_async_copy(source, target, sem_w.at[number])
        for number, (source, target) in enumerate((
            (inputs.at[section], xin.at[0]), (cos_in.at[:, own_rows], cos_q),
            (sin_in.at[:, own_rows], sin_q), (wk_in, wk), (wv_in, wv), (wq_in, wq), (wo_in, wo),
            (wg_in, wg), (wu_in, wu), (wd_in, wd), (cotangent.at[section], cot),
        ))
    ]
    for load in loads:
        load.start()
    barrier = pltpu.get_barrier_semaphore()
    friends = [mate] + [(section, row, lax.rem(ctx + k, ctx_count)) for k in range(1, ctx_count)]
    for friend in friends:
        pl.semaphore_signal(barrier, 1, device_id=friend, device_id_type=MESH)

    for which in range(2):
        for start in range(0, width, LANES):
            rows = min(LANES, width - start)
            tile = jnp.broadcast_to(gains[which : which + 1, start : start + LANES], (LANES, LANES))
            columns[which, start : start + rows, :] = tile.T[:rows]
    query_seg = segments[section, :, own_rows].astype(full)
    query_pos = lax.broadcasted_iota(jnp.int32, (1, tokens), 1) + ctx * tokens
    for start in range(0, size.length, LANES):
        key_seg = jnp.broadcast_to(
            segments[section, :, start : start + LANES].astype(full), (LANES, LANES)
        ).T
        key_pos = lax.broadcasted_iota(jnp.int32, (LANES, tokens), 0) + start
        key_seg = jnp.concatenate([key_seg] * (tokens // LANES), 1)
        allowed = (key_seg == query_seg) & (key_pos <= query_pos)
        bias[start : start + LANES, :] = jnp.where(allowed, 0.0, mask_floor)
    for k in range(1, ctx_count):
        @pl.when(ctx + k < ctx_count)
        def _():
            rows = pl.ds(pl.multiple_of((ctx + k) * tokens, tokens), tokens)
            for app in range(2):
                kv[app, :, rows, :] = jnp.zeros((groups, tokens, LANES), low_type)
    pl.semaphore_wait(barrier, len(friends))

    def kv_copy(app, g, k):
        return pltpu.make_async_remote_copy(
            kv.at[app, g, own_rows], kv.at[app, g, own_rows],
            sem_k.at[0, app, g, k - 1], sem_k.at[1, app, g, k - 1],
            device_id=(section, row, jnp.minimum(ctx + k, ctx_count - 1)), device_id_type=MESH,
        )

    def grad_copy(app, g, k):
        owner = jnp.maximum(ctx - k, 0)
        rows = pl.ds(pl.multiple_of(owner * tokens, tokens), tokens)
        return pltpu.make_async_remote_copy(
            kv_send.at[app, g, rows], kv_recv.at[app, k - 1, g],
            sem_d.at[0, app, g, k - 1], sem_d.at[1, app, g, k - 1],
            device_id=(section, row, owner), device_id_type=MESH,
        )

    act_copies = [
        pltpu.make_async_remote_copy(
            source, acts.at[section], sem_e.at[0], sem_e.at[1], device_id=mate, device_id_type=MESH
        )
        for source in (xin.at[1], last)
    ]
    back_copy = pltpu.make_async_remote_copy(
        grad_stage, grads.at[section], sem_e.at[2], sem_e.at[3], device_id=mate, device_id_type=MESH
    )

    def wide(which):
        return jnp.concatenate([columns[which]] * (tokens // LANES), 1)

    def norm(values):
        return lax.rsqrt(jnp.mean(values * values, 0, keepdims=True) + epsilon)

    def norm_back(values, which, grad_normed):
        inverse = norm(values)
        product = grad_normed * values * inverse
        folded = product[:, :LANES]
        for start in range(LANES, tokens, LANES):
            folded = folded + product[:, start : start + LANES]
        for start in range(0, width, LANES):
            stop = min(start + LANES, width)
            part = folded[start:stop]
            if stop - start < LANES:
                part = jnp.concatenate([part, jnp.zeros((LANES - stop + start, LANES), full)], 0)
            gain_sums[which : which + 1, start : start + LANES] += jnp.sum(part.T, 0, keepdims=True)
        weighted = grad_normed * wide(which)
        cubed = inverse * inverse * inverse
        return inverse * weighted - values * (
            cubed * jnp.mean(weighted * values, 0, keepdims=True)
        )

    def rope(values, sign):
        half = HEAD_DIM // 2
        cos, sine = cos_q[...], sin_q[...] * sign
        out = []
        for start in range(0, values.shape[0], HEAD_DIM):
            former = values[start : start + half]
            latter = values[start + half : start + HEAD_DIM]
            out += [former * cos - latter * sine, latter * cos + former * sine]
        return jnp.concatenate(out, 0)

    def app_tokens(app):
        return slice(app * tokens, (app + 1) * tokens)

    def head_rows(g, h):
        return pl.ds(pl.multiple_of((g * group + h) * HEAD_DIM, HEAD_DIM), HEAD_DIM)

    def forward(app):
        x = xin[app].astype(full)
        normed = (x * norm(x) * wide(0)).astype(low_type)
        x_attn[0, :, app_tokens(app)] = normed
        if app == 0:
            for load in loads[1:5]:
                load.wait()
        keys = rope(dot(wk[...], normed), 1.0).astype(low_type)
        values = dot(wv[...], normed).astype(low_type)
        for g in range(groups):
            piece = slice(g * HEAD_DIM, (g + 1) * HEAD_DIM)
            kv[app, g, own_rows, :] = jnp.concatenate([keys[piece], values[piece]], 0).T
            for k in range(1, ctx_count):
                @pl.when(ctx + k < ctx_count)
                def _():
                    kv_copy(app, g, k).start()
        if app == 0:
            loads[5].wait()
        for start in range(0, width, 2 * LANES):
            stop = min(start + 2 * LANES, width)
            tile = dot(wq[:, start:stop], normed, (0, 0))
            q_t[app, start:stop, :] = rope(tile, 1.0).astype(low_type)

        def heads(g, carry):
            for k in range(1, ctx_count):
                @pl.when(ctx - k >= 0)
                def _():
                    kv_copy(app, g, k).wait_recv()
            v_t = kv[app, g].T[HEAD_DIM:]
            for h in range(group):
                query = q_t[app, head_rows(g, h), :]
                query = jnp.concatenate([query, jnp.zeros_like(query)], 0)
                largest = None
                for start in range(0, size.length, 256):
                    keys_at = slice(start, start + 256)
                    part = dot(kv[app, g, keys_at, :], query) * score_unit + bias[keys_at, :]
                    scores[h, keys_at, :] = part
                    most = fold_rows(part, jnp.max)
                    largest = most if largest is None else jnp.maximum(largest, most)
                largest = jnp.max(largest, 0, keepdims=True)
                total = jnp.zeros((8, tokens), full)
                for start in range(0, size.length, 64):
                    keys_at = slice(start, start + 64)
                    weights = jnp.exp2(scores[h, keys_at, :] - largest)
                    total = total + fold_rows(weights, jnp.sum)
                    chances[keys_at, h * tokens : (h + 1) * tokens] = weights.astype(low_type)
                total = jnp.sum(total, 0, keepdims=True)
                out = dot(v_t, chances[:, h * tokens : (h + 1) * tokens]) / total
                lse[app, g, h : h + 1, :] = largest + jnp.log(total) * (1.0 / math.log(2.0))
                x_attn[1, head_rows(g, h), app_tokens(app)] = out.astype(low_type)
            return carry

        lax.fori_loop(0, groups, heads, 0)
        if app == 0:
            loads[6].wait()
        middle = xin[app].astype(full) + dot(wo[...], x_attn[1, :, app_tokens(app)], (0, 0))
        mid[app] = middle
        ffn = (middle * norm(middle) * wide(1)).astype(low_type)
        n2_t[:, app_tokens(app)] = ffn
        natural[...] = ffn.T
        if app == 0:
            for load in loads[7:10]:
                load.wait()
        accum[...] = middle

        def chunk(i, carry):
            cols = pl.ds(pl.multiple_of(i * size.step, size.step), size.step)
            gate = dot(natural[...], wg[:, cols])
            upward = dot(natural[...], wu[:, cols])
            hidden = (gate / (1.0 + jnp.exp(-gate)) * upward).astype(low_type)
            d_ffn[0, app_tokens(app), cols] = gate.astype(low_type)
            d_ffn[1, app_tokens(app), cols] = upward.astype(low_type)
            inner[app_tokens(app), cols] = hidden
            accum[...] += dot(wd[:, cols], hidden, (1, 1))
            return carry

        lax.fori_loop(0, size.hidden // size.step, chunk, 0)
        output = accum[...].astype(low_type)
        if app == 0:
            xin[1] = output
        else:
            last[...] = output

        @pl.when(section == app)
        def _():
            acts[section] = output

        @pl.when(section != app)
        def _():
            act_copies[app].start()

    def backward(app, grad_low):
        df_t[:, app_tokens(app)] = grad_low
        natural[...] = grad_low.T
        accum[...] = jnp.zeros_like(accum)

        def chunk(i, carry):
            cols = pl.ds(pl.multiple_of(i * size.step, size.step), size.step)
            gate = d_ffn[0, app_tokens(app), cols].astype(full)
            upward = d_ffn[1, app_tokens(app), cols].astype(full)
            sigmoid = 1.0 / (1.0 + jnp.exp(-gate))
            scaled = dot(natural[...], wd[:, cols]) * sigmoid
            grad_gate = (scaled * upward * (1.0 + gate * (1.0 - sigmoid))).astype(low_type)
            grad_up = (scaled * gate).astype(low_type)
            d_ffn[0, app_tokens(app), cols] = grad_gate
            d_ffn[1, app_tokens(app), cols] = grad_up
            accum[...] += dot(wg[:, cols], grad_gate, (1, 1)) + dot(wu[:, cols], grad_up, (1, 1))
            return carry

        lax.fori_loop(0, size.hidden // size.step, chunk, 0)
        grad_middle = grad_low.astype(full) + norm_back(mid[app], 1, accum[...])
        dmid[...] = grad_middle
        branch = grad_middle.astype(low_type)
        d_attn[1, app_tokens(app), :width] = branch.T
        do_t[...] = dot(wo[...], branch).astype(low_type)

        def heads(g, carry):
            k_t = kv[app, g].T[:HEAD_DIM]
            sides = []
            for h in range(group):
                rows, cols = head_rows(g, h), slice(h * tokens, (h + 1) * tokens)
                query, grad_head = q_t[app, rows, :], do_t[rows, :]
                empty = jnp.zeros_like(query)
                query = jnp.concatenate([query, empty], 0)
                grad_pad = jnp.concatenate([empty, grad_head], 0)
                delta = jnp.sum(
                    grad_head.astype(full) * x_attn[1, rows, app_tokens(app)].astype(full),
                    0, keepdims=True,
                )
                log_sum = lse[app, g, h : h + 1, :]
                for start in range(0, size.length, 256):
                    keys_at = slice(start, start + 256)
                    part = dot(kv[app, g, keys_at, :], query) * score_unit + bias[keys_at, :]
                    chance = jnp.exp2(part - log_sum)
                    chances[keys_at, cols] = chance.astype(low_type)
                    change = dot(kv[app, g, keys_at, :], grad_pad) - delta
                    grad_scores[keys_at, cols] = (chance * change).astype(low_type)
                sides.append(((query.astype(full) * score_scale).astype(low_type), grad_pad))
                accum[rows, :] = dot(k_t, grad_scores[:, cols]) * score_scale
            small, grad_pad = (jnp.concatenate(side, 1) for side in zip(*sides))
            kv_send[app, g] = (
                dot(grad_scores[...], small, (1, 1)) + dot(chances[...], grad_pad, (1, 1))
            ).astype(low_type)
            for k in range(1, ctx_count):
                @pl.when(ctx - k >= 0)
                def _():
                    grad_copy(app, g, k).start()
            return carry

        lax.fori_loop(0, groups, heads, 0)
        for start in range(0, width, 2 * LANES):
            stop = min(start + 2 * LANES, width)
            tile = rope(accum[start:stop, :], -1.0).astype(low_type)
            natural[:, start:stop] = tile.T
            do_t[start:stop, :] = tile
        d_attn[0, app_tokens(app), :width] = natural[...]
        pairs = [[], []]
        for g in range(groups):
            tile = kv_send[app, g, own_rows, :].astype(full)
            for k in range(1, ctx_count):
                @pl.when(ctx + k < ctx_count)
                def _():
                    grad_copy(app, g, k).wait_recv()
                tile = tile + jnp.where(
                    ctx + k < ctx_count, kv_recv[app, k - 1, g].astype(full), 0.0
                )
            tile = tile.T
            pairs[0].append(rope(tile[:HEAD_DIM], -1.0).astype(low_type))
            pairs[1].append(tile[HEAD_DIM:].astype(low_type))
        spare = d_pair.shape[2] - size.kv_width
        for half in range(2):
            pairs[half] = jnp.concatenate(pairs[half], 0)
            d_pair[half, app_tokens(app), :] = jnp.concatenate(
                [jnp.zeros((spare, tokens), low_type), pairs[half]], 0
            ).T
        grad_normed = (
            dot(wq[...], do_t[...])
            + dot(wk[...], pairs[0], (0, 0))
            + dot(wv[...], pairs[1], (0, 0))
        )
        return dmid[...] + norm_back(xin[app].astype(full), 0, grad_normed)

    def keep_grad(app, value):
        @pl.when(section == app)
        def _():
            grads[section] = value

        @pl.when(section != app)
        def _():
            grad_stage[...] = value
            back_copy.start()

    gain_sums[...] = jnp.zeros_like(gain_sums)
    d_attn[:, :, width:] = jnp.zeros((2, 2 * tokens, d_attn.shape[2] - width), low_type)
    loads[0].wait()
    forward(0)
    forward(1)
    loads[10].wait()
    low = backward(1, cot[...]).astype(low_type)
    keep_grad(1, low.astype(full))
    keep_grad(0, backward(0, low))

    def drain(g, carry):
        for app in range(2):
            for k in range(1, ctx_count):
                @pl.when(ctx + k < ctx_count)
                def _():
                    kv_copy(app, g, k).wait_send()

                @pl.when(ctx - k >= 0)
                def _():
                    grad_copy(app, g, k).wait_send()
        return carry

    lax.fori_loop(0, groups, drain, 0)
    act_copies[0].wait()
    back_copy.wait()


def run_block(size, plan, *operands):
    tokens, width, hidden, groups = size.tokens, size.width, size.hidden, size.kv_heads
    low, full = jnp.bfloat16, jnp.float32
    padded, kv_wide = plan.width_tiles * LANES, (plan.pair_tiles - plan.width_tiles + 1) * LANES
    both = 2 * tokens
    vmem = pl.BlockSpec(memory_space=pltpu.VMEM)
    far = pl.BlockSpec(memory_space=pl.ANY)
    dma = pltpu.SemaphoreType.DMA
    others = max(size.ctx - 1, 1)
    shapes = [
        ((2, width, tokens), low),
        ((2, width, tokens), full),
        ((2, width, both), low),
        ((width, both), low),
        ((width, both), low),
        ((both, hidden), low),
        ((2, both, padded), low),
        ((2, both, kv_wide), low),
        ((2, both, hidden), low),
        ((8, padded), full),
    ]
    scratch = [
        ((width, width), low),
        ((size.kv_width, width), low),
        ((size.kv_width, width), low),
        ((width, width), low),
        ((width, hidden), low),
        ((width, hidden), low),
        ((width, hidden), low),
        ((HEAD_DIM // 2, tokens), full),
        ((HEAD_DIM // 2, tokens), full),
        ((2, width, LANES), full),
        ((2, width, tokens), low),
        ((width, tokens), low),
        ((width, tokens), low),
        ((width, tokens), full),
        ((2, width, tokens), full),
        ((2, width, tokens), low),
        ((2, groups, size.length, LANES), low),
        ((2, groups, size.length, LANES), low),
        ((2, others, groups, tokens, LANES), low),
        ((2, groups, 8, tokens), full),
        ((width, tokens), low),
        ((size.length, tokens), full),
        ((width, tokens), full),
        ((width, tokens), full),
        ((tokens, width), low),
        ((size.group, size.length, tokens), full),
        ((size.length, size.group * tokens), low),
        ((size.length, size.group * tokens), low),
    ]
    return pl.pallas_call(
        functools.partial(block_kernel, size),
        out_shape=[jax.ShapeDtypeStruct(*shape) for shape in shapes],
        in_specs=[far, far, vmem, far, far, vmem] + [far] * 7,
        out_specs=[vmem] * len(shapes),
        scratch_shapes=[pltpu.VMEM(*shape) for shape in scratch] + [
            dma((11,)), dma((2, 2, groups, others)), dma((2, 2, groups, others)), dma((4,)),
        ],
        compiler_params=pltpu.CompilerParams(
            collective_id=1, has_side_effects=True, vmem_limit_bytes=64 << 20
        ),
        cost_estimate=pl.CostEstimate(
            flops=4 * 10**10, bytes_accessed=40 * 10**6, transcendentals=3 * 10**7
        ),
    )(*operands)


def rotary(length):
    half = HEAD_DIM // 2
    frequency = 10000.0 ** (-2.0 * np.arange(half) / HEAD_DIM)
    angles = frequency[:, None] * np.arange(length)[None, :]
    return np.asarray(np.cos(angles), np.float32), np.asarray(np.sin(angles), np.float32)


def unpack_kernel(plan, sizes, *refs):
    width, hidden, kv_width, through = sizes
    summed, refs = refs[0], refs[1:]
    (query, key_t, value_t, out, gate, up, down_t, *gains), rest = refs[through : through + 9], refs[through + 9 :]
    for source, target in zip(refs[:through], rest):
        target[...] = source[...]
    full, rows, half_width = jnp.float32, width // plan.dp, width // 2

    def tile(half, index, first, count):
        parts = [
            summed[half, p, place : place + size, :]
            for p, place, inside, size in plan.spans(index, first, count)
        ]
        return (parts[0] if len(parts) == 1 else jnp.concatenate(parts, 0)).astype(full)

    def put(target, at, cols, value):
        count = min(LANES, target.shape[1] - cols)
        target[at : at + value.shape[0], cols : cols + count] = value[:, :count]

    for index, (kind, start, tiles, height, piece) in enumerate(plan.chunks):
        for half in range(2):
            for number in range(tiles):
                value = tile(half, index, number * height, height)
                cols = (start + number) * LANES
                if kind == "ffn":
                    put((gate, up)[half], 0, cols, value[:rows])
                elif kind == "down":
                    put(down_t, half * half_width, cols, value[:half_width])
                elif kind == "attn":
                    put((query, out)[half], 0, cols, value[:rows])
                else:
                    spare = plan.width_tiles * LANES - width
                    if number == 0:
                        put((query, out)[half], 0, width + spare - LANES, value[:rows])
                    pair_t = value.T[:, :rows]
                    first = number * LANES - LANES + spare
                    if first < 0:
                        pair_t = pair_t[LANES - spare :]
                        first = 0
                    (key_t, value_t)[half][first : first + pair_t.shape[0], :] = pair_t
            if kind == "mixed":
                lines = tile(half, index, tiles * height, 16)
                for number in range(-(-rows // LANES)):
                    put(gains[half], 0, number * LANES, lines[number : number + 1])


def unpack(plan, sizes, summed, *through):
    width, hidden, kv_width = sizes
    rows, full = width // plan.dp, jnp.float32
    shapes = [
        (rows, width), (kv_width, rows), (kv_width, rows), (rows, width),
        (rows, hidden), (rows, hidden), (width, hidden // plan.dp), (1, rows), (1, rows),
    ]
    vmem = pl.BlockSpec(memory_space=pltpu.VMEM)
    return pl.pallas_call(
        functools.partial(unpack_kernel, plan, (*sizes, len(through))),
        out_shape=[jax.ShapeDtypeStruct(shape, full) for shape in shapes]
        + [jax.ShapeDtypeStruct(value.shape, value.dtype) for value in through],
        in_specs=[vmem] * (1 + len(through)),
        out_specs=[vmem] * (len(shapes) + len(through)),
        compiler_params=pltpu.CompilerParams(vmem_limit_bytes=60 << 20),
    )(summed, *through)


def plain_block(
    plan, inputs, segment_ids, cotangent,
    gain_attn, w_query, w_key, w_value, w_out, gain_ffn, w_gate, w_up, w_down,
):
    micro_count, row_count, tok_local, model_width = inputs.shape
    kv_width = w_key.shape[1]
    group_size = HEADS // KV_HEADS
    section_index = lax.axis_index("section")
    on_first = section_index == 0
    ctx_index = lax.axis_index("ctx")
    first_token = ctx_index * tok_local
    query_pos = first_token + jnp.arange(tok_local, dtype=jnp.int32)
    halfway = HEAD_DIM // 2
    frequency = 10000.0 ** (-2.0 * jnp.arange(halfway, dtype=jnp.float32) / HEAD_DIM)
    angles = query_pos.astype(jnp.float32)[:, None] * frequency[None, :]
    cos_table = jnp.cos(angles)
    sine_table = jnp.sin(angles)
    w_pair = jnp.concatenate([w_key, w_value], 1)
    head_shape = (row_count, tok_local, KV_HEADS, group_size, HEAD_DIM)
    state_shape = (row_count, KV_HEADS, group_size, tok_local)

    def front(hidden, segments):
        query_seg = lax.dynamic_slice_in_dim(segments, first_token, tok_local, 1)
        normed, inverse = rms_forward(hidden, gain_attn)
        normed_low = normed.astype(jnp.bfloat16)
        query_pre = jnp.einsum(
            "rcd,de->rce", normed_low, w_query, preferred_element_type=jnp.float32
        )
        pair_pre = jnp.einsum("rcd,de->rce", normed_low, w_pair, preferred_element_type=jnp.float32)
        queries = rotate(
            query_pre.reshape(row_count, tok_local, HEADS, HEAD_DIM), cos_table, sine_table
        )
        queries = queries.astype(jnp.bfloat16).reshape(head_shape)
        key_rot = rotate(
            pair_pre[..., :kv_width].reshape(row_count, tok_local, KV_HEADS, HEAD_DIM),
            cos_table,
            sine_table,
        )
        packed = jnp.concatenate(
            [key_rot.reshape(row_count, tok_local, kv_width), pair_pre[..., kv_width:]], -1
        )
        return (query_seg, inverse, normed_low, queries, packed.astype(jnp.bfloat16))

    def attend_forward(queries, arrived, segments, query_seg):
        start_state = (
            jnp.full(state_shape, mask_floor, jnp.float32),
            jnp.zeros(state_shape, jnp.float32),
            jnp.zeros(state_shape + (HEAD_DIM,), jnp.float32),
        )
        piece_rows = arrived.shape[1]
        block_rows = math.gcd(piece_rows, 512)

        def fold_inner_step(step_index, loop_state):
            run_max, run_sum, run_acc = loop_state
            offset = step_index * block_rows
            key_block = lax.dynamic_slice_in_dim(arrived, step_index * block_rows, block_rows, 1)
            key_part = key_block[..., :kv_width].reshape(row_count, block_rows, KV_HEADS, HEAD_DIM)
            value_part = key_block[..., kv_width:].reshape(
                row_count, block_rows, KV_HEADS, HEAD_DIM
            )
            key_seg = lax.dynamic_slice_in_dim(segments, offset, block_rows, 1)
            scores, allowed = block_scores(queries, key_part, query_seg, key_seg, query_pos, offset)
            masked = jnp.where(allowed, scores, mask_floor)
            new_max = jnp.maximum(run_max, jnp.max(masked, -1))
            weights = jnp.where(allowed, jnp.exp(masked - new_max[..., None]), 0.0)
            rescale = jnp.exp(run_max - new_max)
            run_sum = run_sum * rescale + jnp.sum(weights, -1)
            run_acc = run_acc * rescale[..., None] + jnp.einsum(
                "rkgcn,rnkd->rkgcd",
                weights.astype(jnp.bfloat16),
                value_part,
                preferred_element_type=jnp.float32,
            )
            return (new_max, run_sum, run_acc)

        run_max, run_sum, run_acc = lax.fori_loop(
            0, piece_rows // block_rows, fold_inner_step, start_state
        )
        return (run_acc / run_sum[..., None], run_max + jnp.log(run_sum))

    def rear(hidden, attended):
        attn_low = (
            attended.transpose(0, 3, 1, 2, 4)
            .reshape(row_count, tok_local, HEADS * HEAD_DIM)
            .astype(jnp.bfloat16)
        )
        middle = hidden + jnp.einsum(
            "rce,ed->rcd", attn_low, w_out, preferred_element_type=jnp.float32
        )
        normed_ffn, inverse_ffn = rms_forward(middle, gain_ffn)
        ffn_low = normed_ffn.astype(jnp.bfloat16)
        gate_pre = jnp.einsum("rcd,df->rcf", ffn_low, w_gate, preferred_element_type=jnp.float32)
        upward = jnp.einsum("rcd,df->rcf", ffn_low, w_up, preferred_element_type=jnp.float32)
        inner_act = (jax.nn.silu(gate_pre) * upward).astype(jnp.bfloat16)
        output = middle + jnp.einsum(
            "rcf,fd->rcd", inner_act, w_down, preferred_element_type=jnp.float32
        )
        return (output, (attn_low, middle, inverse_ffn, ffn_low, gate_pre, upward, inner_act))


    assert micro_count == lax.axis_size("section")

    def mine(stacked):
        return lax.dynamic_index_in_dim(stacked, section_index, 0, keepdims=False)

    segments = mine(segment_ids)

    def forward(hidden):
        query_seg, inverse, normed_low, queries, packed = front(hidden, segments)
        arrived = lax.all_gather(packed, "ctx", axis=1, tiled=True)
        attended, log_sum = attend_forward(queries, arrived, segments, query_seg)
        output, saved = rear(hidden, attended)
        return output.astype(jnp.bfloat16), (
            hidden, query_seg, inverse, normed_low, queries, arrived, attended, log_sum, saved
        )

    def backward(grad_out, kept):
        (
            hidden,
            backward_query_seg,
            backward_inverse,
            backward_normed_low,
            backward_queries,
            piece_arrived,
            backward_attended,
            log_sum,
            saved,
        ) = kept
        (
            backward_attn_low,
            backward_middle,
            backward_inverse_ffn,
            backward_ffn_low,
            backward_gate_pre,
            backward_upward,
            backward_inner_act,
        ) = saved
        grad_low = grad_out.astype(jnp.bfloat16)
        grad_inner = jnp.einsum("rcd,fd->rcf", grad_low, w_down, preferred_element_type=jnp.float32)
        sigmoid = jax.nn.sigmoid(backward_gate_pre)
        grad_gate = (
            grad_inner * backward_upward * sigmoid * (1.0 + backward_gate_pre * (1.0 - sigmoid))
        ).astype(jnp.bfloat16)
        grad_up = (grad_inner * backward_gate_pre * sigmoid).astype(jnp.bfloat16)
        grad_norm_ffn = jnp.einsum(
            "rcf,df->rcd", grad_gate, w_gate, preferred_element_type=jnp.float32
        ) + jnp.einsum("rcf,df->rcd", grad_up, w_up, preferred_element_type=jnp.float32)
        grad_mid_norm, backward_sum_gain_ffn = rms_backward(
            backward_middle, gain_ffn, backward_inverse_ffn, grad_norm_ffn
        )
        grad_middle = grad_out + grad_mid_norm
        grad_branch = grad_middle.astype(jnp.bfloat16)
        grad_attn = jnp.einsum(
            "rcd,ed->rce", grad_branch, w_out, preferred_element_type=jnp.float32
        ).astype(jnp.bfloat16)
        grad_heads = grad_attn.reshape(head_shape).transpose(0, 2, 3, 1, 4)
        row_delta = jnp.sum(grad_heads.astype(jnp.float32) * backward_attended, -1)
        query_start = jnp.zeros(state_shape + (HEAD_DIM,), jnp.float32)
        fold_grad_query = query_start
        grad_query = fold_grad_query
        piece_piece_rows = piece_arrived.shape[1]
        piece_block_rows = math.gcd(piece_piece_rows, 512)

        def piece_inner_step(step_index, loop_state):
            grad_query, local_pair = loop_state
            inside = step_index * piece_block_rows
            key_block = lax.dynamic_slice_in_dim(piece_arrived, inside, piece_block_rows, 1)
            key_part = key_block[..., :kv_width].reshape(
                row_count, piece_block_rows, KV_HEADS, HEAD_DIM
            )
            value_part = key_block[..., kv_width:].reshape(
                row_count, piece_block_rows, KV_HEADS, HEAD_DIM
            )
            key_seg = lax.dynamic_slice_in_dim(segments, inside, piece_block_rows, 1)
            scores, allowed = block_scores(
                backward_queries, key_part, backward_query_seg, key_seg, query_pos, inside
            )
            chances = jnp.where(
                allowed, jnp.exp(jnp.where(allowed, scores, mask_floor) - log_sum[..., None]), 0.0
            )
            grad_chance = jnp.einsum(
                "rkgcd,rnkd->rkgcn", grad_heads, value_part, preferred_element_type=jnp.float32
            )
            grad_scores = (chances * (grad_chance - row_delta[..., None])).astype(jnp.bfloat16)
            grad_query = grad_query + score_scale * jnp.einsum(
                "rkgcn,rnkd->rkgcd", grad_scores, key_part, preferred_element_type=jnp.float32
            )
            grad_key = score_scale * jnp.einsum(
                "rkgcn,rckgd->rnkd",
                grad_scores,
                backward_queries,
                preferred_element_type=jnp.float32,
            )
            grad_value = jnp.einsum(
                "rkgcn,rkgcd->rnkd",
                chances.astype(jnp.bfloat16),
                grad_heads,
                preferred_element_type=jnp.float32,
            )
            update = jnp.concatenate(
                [
                    grad_key.reshape(row_count, piece_block_rows, kv_width),
                    grad_value.reshape(row_count, piece_block_rows, kv_width),
                ],
                -1,
            )
            current = lax.dynamic_slice_in_dim(local_pair, inside, piece_block_rows, 1)
            local_pair = lax.dynamic_update_slice_in_dim(local_pair, current + update, inside, 1)
            return (grad_query, local_pair)

        local_start = jnp.zeros((row_count, piece_piece_rows, 2 * kv_width), jnp.float32)
        fold_grad_query, fold_local_pair = lax.fori_loop(
            0, piece_piece_rows // piece_block_rows, piece_inner_step, (grad_query, local_start)
        )
        grad_pair = fold_local_pair
        grad_query, grad_pair = (fold_grad_query, grad_pair)
        pair_share = lax.psum_scatter(
            grad_pair.astype(jnp.bfloat16), "ctx", scatter_dimension=1, tiled=True
        ).astype(jnp.float32)
        query_tok = grad_query.transpose(0, 3, 1, 2, 4).reshape(
            row_count, tok_local, HEADS, HEAD_DIM
        )
        query_back = rotate(query_tok, cos_table, -sine_table).reshape(
            row_count, tok_local, HEADS * HEAD_DIM
        )
        query_back = query_back.astype(jnp.bfloat16)
        key_back = rotate(
            pair_share[..., :kv_width].reshape(row_count, tok_local, KV_HEADS, HEAD_DIM),
            cos_table,
            -sine_table,
        )
        pair_low = jnp.concatenate(
            [key_back.reshape(row_count, tok_local, kv_width), pair_share[..., kv_width:]], -1
        )
        pair_low = pair_low.astype(jnp.bfloat16)
        grad_normed = jnp.einsum(
            "rce,de->rcd", query_back, w_query, preferred_element_type=jnp.float32
        ) + jnp.einsum("rce,de->rcd", pair_low, w_pair, preferred_element_type=jnp.float32)
        grad_front, backward_sum_gain_attn = rms_backward(
            hidden, gain_attn, backward_inverse, grad_normed
        )
        factors = (
            backward_normed_low, backward_attn_low, backward_ffn_low, backward_inner_act,
            query_back, pair_low, grad_branch, grad_gate, grad_up, grad_low,
        )
        tick_grads = (backward_sum_gain_attn, backward_sum_gain_ffn, factors)
        return grad_middle + grad_front, tick_grads

    first_low, first_kept = forward(mine(inputs).astype(jnp.float32))
    second_low, second_kept = forward(first_low.astype(jnp.float32))
    grad_mid, second_grads = backward(mine(cotangent).astype(jnp.float32), second_kept)
    grad_mid_low = grad_mid.astype(jnp.bfloat16)
    grad_in, first_grads = backward(grad_mid_low.astype(jnp.float32), first_kept)
    dp = plan.dp

    def stacked(one, other):
        return jnp.concatenate([one, other], 1).reshape(-1, one.shape[-1])

    normed, attn, ffn, inner, d_query, d_pair, d_branch, d_gate, d_up, d_out = (
        stacked(one, other) for one, other in zip(first_grads[2], second_grads[2])
    )
    tokens = normed.shape[0]

    def sides(values, rows):
        cut = values.reshape(tokens, dp, -1)
        cut = jnp.pad(cut, ((0, 0), (0, 0), (0, rows - cut.shape[2])))
        return cut.transpose(1, 2, 0)

    inner = inner.reshape(tokens, dp, -1)
    inner = jnp.pad(
        inner, ((0, 0), (0, 0), (0, plan.down_tiles * LANES - inner.shape[2]))
    ).reshape(tokens, -1)
    spare = plan.width_tiles * LANES - model_width
    gain_sums = jnp.stack([one + other for one, other in zip(first_grads[:2], second_grads[:2])])
    gain_sums = jnp.pad(gain_sums, ((0, 6), (0, plan.width_tiles * LANES - model_width)))
    factors = (
        sides(ffn, plan.rows),
        jnp.stack([d_gate, d_up]),
        d_out.T.reshape(2, plan.down_rows, tokens),
        inner,
        jnp.stack([sides(normed, plan.rows), sides(attn, plan.rows)]),
        jnp.pad(jnp.stack([d_query, d_branch]), ((0, 0), (0, 0), (0, spare))),
        jnp.pad(
            jnp.stack([d_pair[:, :kv_width], d_pair[:, kv_width:]]),
            ((0, 0), (0, 0), (LANES - spare, 0)),
        ),
    )
    acts = (first_low, second_low)
    return acts, (grad_in, grad_mid_low), gain_sums, factors


def fused_block(
    size, plan, inputs, segment_ids, cotangent,
    gain_attn, w_query, w_key, w_value, w_out, gain_ffn, w_gate, w_up, w_down,
):
    tokens, width, dp = size.tokens, size.width, plan.dp
    cos_in, sin_in = rotary(size.length)
    gains = jnp.stack([gain_attn, gain_ffn]).astype(jnp.float32)
    gains = jnp.pad(gains, ((0, 0), (0, plan.width_tiles * LANES - width)))
    acts, grads, x_attn, n2_t, df_t, inner, d_attn, d_pair, d_ffn, gain_sums = run_block(
        size, plan, inputs[:, 0].swapaxes(1, 2), cotangent[:, 0].swapaxes(1, 2), segment_ids,
        cos_in, sin_in, gains, w_query, w_key.T, w_value.T, w_out, w_gate, w_up, w_down.T,
    )
    factors = (
        n2_t.reshape(dp, plan.rows, -1),
        d_ffn,
        df_t.reshape(2, plan.down_rows, -1),
        inner,
        x_attn.reshape(2, dp, plan.rows, -1),
        d_attn,
        d_pair,
    )
    return acts, grads, gain_sums, factors


def body(
    inputs,
    segment_ids,
    cotangent,
    gain_attn,
    w_query,
    w_key,
    w_value,
    w_out,
    gain_ffn,
    w_gate,
    w_up,
    w_down,
):
    micro_count, row_count, tok_local, model_width = inputs.shape
    kv_width, hidden = w_key.shape[1], w_gate.shape[1]
    assert micro_count == lax.axis_size("section")
    on_first = lax.axis_index("section") == 0
    plan = Plan(lax.axis_size("dp"), lax.axis_size("ctx"), model_width, hidden, kv_width)
    dp = plan.dp
    size = Block(tok_local, segment_ids.shape[2], model_width, hidden, kv_width, plan.ctx)
    fits = (
        row_count == 1
        and size.length <= 1024
        and tok_local % LANES == 0
        and plan.rows * dp == model_width
        and plan.down_tiles * LANES * dp == hidden
    )
    run = functools.partial(fused_block, size) if fits else plain_block
    acts, grads, gain_sums, factors = run(
        plan, inputs, segment_ids, cotangent,
        gain_attn, w_query, w_key, w_value, w_out, gain_ffn, w_gate, w_up, w_down,
    )
    summed = reduce_grads(plan, *factors, gain_sums)
    sizes = (model_width, hidden, kv_width)

    def exchange(for_first, for_last):
        kept = jnp.where(on_first, for_first, for_last)
        sent = jnp.where(on_first, for_last, for_first)
        got = lax.ppermute(sent, "section", [(0, 1), (1, 0)])
        return jnp.where(
            on_first, jnp.stack([kept, got]), jnp.stack([got, kept])
        )

    def turned(values):
        return values[None, :, None].swapaxes(3, 4)

    if fits:
        *parts, acts, grads = unpack(plan, sizes, summed, acts, grads)
        activations, input_grads = turned(acts), turned(grads)
    else:
        parts = unpack(plan, sizes, summed)
        activations = exchange(*acts)[None]
        input_grads = exchange(grads[0].astype(jnp.bfloat16), grads[1]).astype(jnp.float32)[None]
    query, key_t, value_t, out, gate, up, down_t, gain_one, gain_two = parts
    return (
        activations,
        input_grads,
        gain_one.reshape(-1),
        query,
        key_t.T,
        value_t.T,
        out,
        gain_two.reshape(-1),
        gate,
        up,
        down_t.T,
    )


def solution(mesh):
    placed = (
        P(None, "dp", "ctx", None),
        P(None, "dp", None),
        P(None, "dp", "ctx", None),
        P(),
        P(),
        P(),
        P(),
        P(),
        P(),
        P(),
        P(),
        P(),
    )
    return jax.shard_map(
        body,
        mesh=mesh,
        in_specs=placed,
        out_specs=(
            P("section", None, "dp", "ctx", None),
            P("section", None, "dp", "ctx", None),
            P("dp"),
            P("dp", None),
            P("dp", None),
            P("dp", None),
            P("dp", None),
            P("dp"),
            P("dp", None),
            P("dp", None),
            P("dp", None),
        ),
        check_vma=False,
    )
```

```python
import functools
import math
import types

import jax
import jax.numpy as jnp
import numpy as np
from jax import lax
from jax.experimental import pallas as pl
from jax.experimental.pallas import tpu as pltpu
from jax.sharding import PartitionSpec as P

HEADS = 15
KV_HEADS = 5
HEAD_DIM = 64
LANES = 128
Z_CHUNKS = 3
Z_LAG = 2
OWN_SLOTS = 8
PARTNER_SLOTS = 3
MESH = pl.DeviceIdType.MESH


epsilon = 1e-05
score_scale = 0.125
score_unit = score_scale / math.log(2.0)
mask_floor = -1e30


def rms_forward(values, gain_vec):
    inverse = lax.rsqrt(jnp.mean(values * values, -1, keepdims=True) + epsilon)
    return (values * inverse * gain_vec, inverse)


def rms_backward(values, gain_vec, inverse, grad_normed):
    weighted = grad_normed * gain_vec
    grad_gain = jnp.sum(grad_normed * values * inverse, axis=(0, 1))
    cubed = inverse * inverse * inverse
    grad_values = inverse * weighted - values * cubed * jnp.mean(
        weighted * values, -1, keepdims=True
    )
    return (grad_values, grad_gain)


def rotate(values, cos_table, sine_table):
    halfway = values.shape[-1] // 2
    former = values[..., :halfway]
    latter = values[..., halfway:]
    cos_part = cos_table[None, :, None, :]
    sine_part = sine_table[None, :, None, :]
    return jnp.concatenate(
        [former * cos_part - latter * sine_part, latter * cos_part + former * sine_part], -1
    )


def block_scores(queries, key_part, query_seg, key_seg, query_pos, offset):
    block_rows = key_part.shape[1]
    scores = (
        jnp.einsum("rckgd,rnkd->rkgcn", queries, key_part, preferred_element_type=jnp.float32)
        * score_scale
    )
    key_pos = offset + jnp.arange(block_rows, dtype=jnp.int32)
    allowed = (query_seg[:, :, None] == key_seg[:, None, :]) & (
        key_pos[None, None, :] <= query_pos[None, :, None]
    )
    return (scores, allowed[:, None, None, :, :])


def up_to(value, step):
    return -(-value // step) * step


TAIL_ORDER = (
    8, 0, -1, 24, 9, -1, 1, 25, 32, -1, 40, 33, 41, -1, -1, 48, 26, 34, -2, -3,
    -3, -3, 42, 49, 16, -3, 35, 27, 10, 17, -3, 56, 43, 57, 50, 2, 11, 36, -4, 64,
    58, 3, 37, 12, 65, 4, 59, 72, 51, 73, 66, 28, 80, 18, 81, 67, 74, 44, 82, 75,
    19, 60, 68, 45, 83, 29, 52, 5, 13, 76, 53, 30, 6, 69, 14, 20, 84, 46, 54, 31,
    77, 38, 61, 70, 85, 78, 21, 62, 47, 55, 71, 86, 39, 22, 7, 79, 63, 87, 15, 23,
)


class Plan:
    def __init__(self, dp, ctx, width, hidden, kv_width):
        self.dp, self.ctx = dp, ctx
        self.cx = 1 << (ctx.bit_length() // 2) if ctx & (ctx - 1) == 0 else ctx
        self.cy = ctx // self.cx
        self.low = max(dp // 2, 1)
        self.shard = width // dp
        self.rows = up_to(width // dp, 16)
        self.down_rows = up_to(width // 2, 16)
        self.down_tiles = up_to(hidden // dp, LANES) // LANES
        self.up_tiles = hidden // LANES
        self.width_tiles = up_to(width, LANES) // LANES
        self.pair_tiles = (width + kv_width) // LANES
        self.step = 4
        chunks = []
        for kind, count, rows, step in (
            ("down", self.down_tiles, self.down_rows, 2),
            ("ffn", self.up_tiles, self.rows, self.step),
            ("attn", self.width_tiles - 1, self.rows, 4),
            ("mixed", self.pair_tiles - self.width_tiles + 1, self.rows, 4),
        ):
            for start in range(0, count, step):
                tiles = min(step, count - start)
                extra = 16 if kind == "mixed" else 0
                piece = up_to(up_to(tiles * rows + extra, ctx) // ctx, 16)
                mode = "z" if len(chunks) < Z_CHUNKS else "xy"
                chunks.append((kind, start, tiles, rows, piece, mode))
        self.chunks = chunks
        self.offsets = [sum(c[4] for c in chunks[:i]) for i in range(len(chunks))]
        self.total = sum(c[4] for c in chunks)
        self.widest = max(c[4] for c in chunks)

    def of(self, kind):
        return [i for i, chunk in enumerate(self.chunks) if chunk[0] == kind]

    def spans(self, index, first, count):
        piece = self.chunks[index][4]
        out, done = [], 0
        while done < count:
            at = first + done
            size = min(count - done, piece - at % piece)
            out.append((at // piece, at % piece, done, size))
            done += size
        return out

    def scratch(self):
        dp, cy, cx, low = self.dp, self.cy, self.cx, self.low
        nx, ny, nz, high = max(cx - 1, 1), max(cy - 1, 1), max(dp - 1, 1), max(dp - low, 1)
        count = len(self.chunks)

        def buffer(*shape):
            return pltpu.VMEM((*shape, LANES), jnp.bfloat16)

        found = [
            buffer(2, dp, cy, cx, self.widest),
            buffer(PARTNER_SLOTS, dp, cy, cx, self.widest),
            buffer(OWN_SLOTS, dp, cy, cx, self.widest),
        ]
        for kind, start, tiles, rows, piece, mode in self.chunks:
            head = up_to(piece // 2, 16)
            rest = max(piece - head, 16)
            if mode == "xy":
                found += [
                    buffer(nz, piece), buffer(nx, low, cy, piece), buffer(ny, high, cx, piece),
                    buffer(nx, high, piece), buffer(ny, low, piece), buffer(piece),
                ]
            else:
                found += [
                    buffer(nz, cy, cx, piece), buffer(nx, cy, head), buffer(ny, cx, rest),
                    buffer(nx, rest), buffer(ny, head), buffer(piece),
                ]
        dma = pltpu.SemaphoreType.DMA
        return found + [
            dma((2, count)), dma((2, count, nx)), dma((2, count, ny)), dma((2, count, nx)),
            dma((2, count, ny)), dma((2, count, nz)), dma((2, count, nx)), dma((2, count, ny)),
            dma((2, count, nx)), dma((2, count, ny)), dma((2, count)), dma((count,)),
            pltpu.SemaphoreType.REGULAR,
        ]


class Reduction:
    def __init__(self, plan, products, out, refs, turns=None):
        self.plan, self.products, self.out = plan, products, out
        count = len(plan.chunks)
        self.turns = list(range(count)) if turns is None else turns
        self.sent, self.partner, self.own_ring = refs[:3]
        self.parts = [refs[3 + 6 * i : 9 + 6 * i] for i in range(count)]
        (
            self.sem_p, self.sem_x1, self.sem_y1, self.sem_x2, self.sem_y2, self.sem_z,
            self.sem_gx, self.sem_gy, self.sem_hx, self.sem_hy, self.sem_m, self.sem_o, self.credit,
        ) = refs[3 + 6 * count :]
        self.section, self.row, self.ctx = (
            lax.axis_index(name) for name in ("section", "dp", "ctx")
        )
        self.px, self.py = lax.rem(self.ctx, plan.cx), lax.div(self.ctx, plan.cx)
        self.mate = (1 - self.section, self.row, self.ctx)
        self.done = [0] * count

    def friends(self):
        plan = self.plan
        found = [self.mate]
        found += [(self.section, lax.rem(self.row + k, plan.dp), self.ctx) for k in range(1, plan.dp)]
        return found + [
            (self.section, self.row, lax.rem(self.ctx + k, plan.ctx)) for k in range(1, plan.ctx)
        ]

    def remote(self, source, target, sems, place, device):
        return pltpu.make_async_remote_copy(
            source, target, sems.at[(0, *place)], sems.at[(1, *place)],
            device_id=device, device_id_type=MESH,
        )

    def x_peers(self):
        for k in range(1, self.plan.cx):
            other = lax.rem(self.px + k, self.plan.cx)
            yield k - 1, other, (self.section, self.row, self.py * self.plan.cx + other)

    def y_peers(self):
        for k in range(1, self.plan.cy):
            other = lax.rem(self.py + k, self.plan.cy)
            yield k - 1, other, (self.section, self.row, other * self.plan.cx + self.px)

    def z_peers(self):
        for k in range(1, self.plan.dp):
            other = lax.rem(self.row + k, self.plan.dp)
            yield k - 1, other, (self.section, other, self.ctx)

    def turn(self, index):
        return self.turns.index(index)

    def own(self, index):
        return self.own_ring.at[self.turn(index) % OWN_SLOTS]

    def at(self, index):
        return pl.ds(self.plan.offsets[index], self.plan.chunks[index][4])

    def head(self, index):
        piece = self.plan.chunks[index][4]
        return up_to(piece // 2, 16)

    def partner_copy(self, index):
        rows = pl.ds(0, self.plan.chunks[index][4])
        return self.remote(
            self.sent.at[self.turn(index) % 2, :, :, :, rows],
            self.partner.at[self.turn(index) % PARTNER_SLOTS, :, :, :, rows],
            self.sem_p, (index,), self.mate,
        )

    def make_partner(self, index):
        turn, cx = self.turn(index), self.plan.cx
        if turn >= 2:
            self.partner_copy(self.turns[turn - 2]).wait_send()
        if turn >= PARTNER_SLOTS:
            pl.semaphore_wait(self.credit, 1)

        def finish(j, first, value):
            for p, place, inside, size in self.plan.spans(index, first, value.shape[0]):
                self.sent[turn % 2, j, p // cx, p % cx, place : place + size, :] = value[
                    inside : inside + size
                ].astype(jnp.bfloat16)

        self.products(index, 1 - self.section, finish)
        self.partner_copy(index).start()

    def make_own(self, index):
        turn = self.turn(index)
        assert turn < OWN_SLOTS or self.done[self.turns[turn - OWN_SLOTS]] > 4
        self.partner_copy(index).wait_recv()
        cx, slot, own = self.plan.cx, turn % PARTNER_SLOTS, self.own(index)

        def finish(j, first, value):
            for p, place, inside, size in self.plan.spans(index, first, value.shape[0]):
                rows = slice(place, place + size)
                other = self.partner[slot, j, p // cx, p % cx, rows, :].astype(jnp.float32)
                own[j, p // cx, p % cx, rows, :] = (
                    value[inside : inside + size] + other
                ).astype(jnp.bfloat16)

        self.products(index, self.section, finish)
        if turn + PARTNER_SLOTS < len(self.plan.chunks):
            pl.semaphore_signal(self.credit, 1, device_id=self.mate, device_id_type=MESH)
        self.start(self.z_copies(index) if self.is_z(index) else self.first_copies(index))

    def is_z(self, index):
        return self.plan.chunks[index][5] == "z"

    def start(self, copies):
        for copy in copies:
            copy.start()

    def wait(self, copies):
        for copy in copies:
            copy.wait()

    def z_copies(self, index):
        own, into = self.own(index), self.parts[index][0]
        piece = pl.ds(0, self.plan.chunks[index][4])
        found = []
        for slot, other, device in self.z_peers():
            if self.is_z(index):
                source = own.at[other, :, :, piece]
            else:
                source = own.at[other, self.py, self.px, piece]
            found.append(self.remote(source, into.at[slot], self.sem_z, (index, slot), device))
        return found

    def halves(self, index):
        plan, piece = self.plan, self.plan.chunks[index][4]
        if self.is_z(index):
            head = self.head(index)
            return (pl.ds(self.row, 1), pl.ds(0, head)), (pl.ds(self.row, 1), pl.ds(head, piece - head))
        rows = pl.ds(0, piece)
        return (pl.ds(0, plan.low), rows), (pl.ds(plan.low, plan.dp - plan.low), rows)

    def has_rest(self, index):
        if self.is_z(index):
            return self.plan.chunks[index][4] > self.head(index)
        return self.plan.dp > self.plan.low

    def first_copies(self, index):
        own = self.own(index)
        (j_x, rows_x), (j_y, rows_y) = self.halves(index)
        _, rx1, ry1, _, _, _ = self.parts[index]
        if self.is_z(index):
            j_x = j_y = self.row
        found = [
            self.remote(own.at[j_x, :, other, rows_x], rx1.at[slot], self.sem_x1, (index, slot), device)
            for slot, other, device in self.x_peers()
        ]
        if self.has_rest(index):
            found += [
                self.remote(
                    own.at[j_y, other, :, rows_y], ry1.at[slot], self.sem_y1, (index, slot), device
                )
                for slot, other, device in self.y_peers()
            ]
        return found

    def second_copies(self, index):
        own = self.own(index)
        (j_x, rows_x), (j_y, rows_y) = self.halves(index)
        _, _, _, rx2, ry2, _ = self.parts[index]
        if self.is_z(index):
            j_x = j_y = self.row
        found = [
            self.remote(
                own.at[j_x, other, self.px, rows_x], ry2.at[slot], self.sem_y2, (index, slot), device
            )
            for slot, other, device in self.y_peers()
        ]
        if self.has_rest(index):
            found += [
                self.remote(
                    own.at[j_y, self.py, other, rows_y], rx2.at[slot], self.sem_x2, (index, slot), device
                )
                for slot, other, device in self.x_peers()
            ]
        return found

    def add_all_z(self, index):
        plan, own, into = self.plan, self.own(index), self.parts[index][0]
        piece = slice(0, plan.chunks[index][4])
        self.wait(self.z_copies(index))
        for y in range(plan.cy):
            for x in range(plan.cx):
                total = own[self.row, y, x, piece, :].astype(jnp.float32)
                for k in range(plan.dp - 1):
                    total = total + into[k, y, x].astype(jnp.float32)
                own[self.row, y, x, piece, :] = total.astype(jnp.bfloat16)
        self.start(self.first_copies(index))

    def add_first(self, index):
        plan, own = self.plan, self.own(index)
        _, rx1, ry1, _, _, _ = self.parts[index]
        piece, is_z = plan.chunks[index][4], self.is_z(index)
        head = self.head(index)
        self.wait(self.first_copies(index))
        places = [(self.row, 0, 0)] if is_z else [(j, j, j - plan.low) for j in range(plan.dp)]
        for j, at_x, at_y in places:
            if is_z or at_x < plan.low:
                rows = slice(0, head) if is_z else slice(0, piece)
                for y in range(plan.cy):
                    total = own[j, y, self.px, rows, :].astype(jnp.float32)
                    for k in range(plan.cx - 1):
                        part = rx1[k, y] if is_z else rx1[k, at_x, y]
                        total = total + part.astype(jnp.float32)
                    own[j, y, self.px, rows, :] = total.astype(jnp.bfloat16)
            if (is_z and piece > head) or (not is_z and at_y >= 0):
                rows = slice(head, piece) if is_z else slice(0, piece)
                for x in range(plan.cx):
                    total = own[j, self.py, x, rows, :].astype(jnp.float32)
                    for k in range(plan.cy - 1):
                        part = ry1[k, x] if is_z else ry1[k, at_y, x]
                        total = total + part.astype(jnp.float32)
                    own[j, self.py, x, rows, :] = total.astype(jnp.bfloat16)
        self.start(self.second_copies(index))

    def add_second(self, index):
        plan, own = self.plan, self.own(index)
        _, _, _, rx2, ry2, _ = self.parts[index]
        piece = slice(0, plan.chunks[index][4])
        self.wait(self.second_copies(index))
        for j in range(plan.dp):
            total = own[j, self.py, self.px, piece, :].astype(jnp.float32)
            if j < plan.low:
                for k in range(plan.cy - 1):
                    total = total + ry2[k, j].astype(jnp.float32)
            else:
                for k in range(plan.cx - 1):
                    total = total + rx2[k, j - plan.low].astype(jnp.float32)
            own[j, self.py, self.px, piece, :] = total.astype(jnp.bfloat16)
        self.start(self.z_copies(index))

    def add_last(self, index):
        plan, own = self.plan, self.own(index)
        rz, _, _, rx2, ry2, final = self.parts[index]
        piece, head = plan.chunks[index][4], self.head(index)
        if self.is_z(index):
            self.wait(self.second_copies(index))
            total = own[self.row, self.py, self.px, 0:head, :].astype(jnp.float32)
            for k in range(plan.cy - 1):
                total = total + ry2[k].astype(jnp.float32)
            final[0:head, :] = total.astype(jnp.bfloat16)
            if piece > head:
                total = own[self.row, self.py, self.px, head:piece, :].astype(jnp.float32)
                for k in range(plan.cx - 1):
                    total = total + rx2[k].astype(jnp.float32)
                final[head:piece, :] = total.astype(jnp.bfloat16)
        else:
            self.wait(self.z_copies(index))
            total = own[self.row, self.py, self.px, 0:piece, :].astype(jnp.float32)
            for k in range(plan.dp - 1):
                total = total + rz[k].astype(jnp.float32)
            final[...] = total.astype(jnp.bfloat16)
        self.place_copy(index).start()
        self.start(self.gather_one(index))

    def place_copy(self, index):
        target = self.out.at[self.section, self.py, self.px, self.at(index)]
        return pltpu.make_async_copy(self.parts[index][5], target, self.sem_o.at[index])

    def gather_parts(self, index):
        offset, piece, head = self.plan.offsets[index], self.plan.chunks[index][4], self.head(index)
        return pl.ds(offset, head), pl.ds(offset + head, piece - head), piece > head

    def gather_one(self, index):
        final, out = self.parts[index][5], self.out
        rows_x, rows_y, rest = self.gather_parts(index)
        head, piece = self.head(index), self.plan.chunks[index][4]
        found = [
            self.remote(
                final.at[pl.ds(0, head)], out.at[self.section, self.py, self.px, rows_x],
                self.sem_gx, (index, slot), device,
            )
            for slot, other, device in self.x_peers()
        ]
        if rest:
            found += [
                self.remote(
                    final.at[pl.ds(head, piece - head)], out.at[self.section, self.py, self.px, rows_y],
                    self.sem_gy, (index, slot), device,
                )
                for slot, other, device in self.y_peers()
            ]
        return found

    def gather_two(self, index):
        out = self.out
        rows_x, rows_y, rest = self.gather_parts(index)
        found = []
        for slot, other, device in self.y_peers():
            region = out.at[self.section, self.py, :, rows_x]
            found.append(self.remote(region, region, self.sem_hy, (index, slot), device))
        if rest:
            for slot, other, device in self.x_peers():
                region = out.at[self.section, :, self.px, rows_y]
                found.append(self.remote(region, region, self.sem_hx, (index, slot), device))
        return found

    def gather_on(self, index):
        self.place_copy(index).wait()
        self.wait(self.gather_one(index))
        self.start(self.gather_two(index))

    def mate_copy(self, index):
        region = self.out.at[self.section, :, :, self.at(index)]
        return self.remote(region, region, self.sem_m, (index,), self.mate)

    def pass_on(self, index):
        self.wait(self.gather_two(index))
        self.mate_copy(index).start()

    def finish(self, index):
        self.mate_copy(index).wait()

    def stages(self, index):
        middle = (self.add_all_z, self.add_first) if self.is_z(index) else (self.add_first, self.add_second)
        return (
            self.make_partner, self.make_own, *middle, self.add_last, self.gather_on, self.pass_on, self.finish
        )

    def advance(self, index, upto=None):
        stages = self.stages(index)
        while self.done[index] < len(stages):
            if upto is not None and self.done[index] >= upto:
                return
            stages[self.done[index]](index)
            self.done[index] += 1
            if upto is None:
                return

    def drain(self):
        todo = []
        for index in range(len(self.done)):
            for stage in range(self.done[index], len(self.stages(index))):
                late = Z_LAG if self.is_z(index) and stage >= 2 else 0
                todo.append((index + stage + late, stage, index))
        for step, stage, index in sorted(todo):
            self.advance(index)
        for index in self.turns[-2:]:
            self.partner_copy(index).wait_send()


def greet(friends):
    barrier = pltpu.get_barrier_semaphore()
    for friend in friends:
        pl.semaphore_signal(barrier, 1, device_id=friend, device_id_type=MESH)
    pl.semaphore_wait(barrier, len(friends))


def shard_products(plan, index, half, finish, sources):
    kind, start, tiles, rows, piece, mode = plan.chunks[index]
    shards = range(plan.dp)

    def give(value, first):
        for j in shards:
            part = value[j * rows : (j + 1) * rows]
            for tile in range(value.shape[1] // LANES):
                finish(j, (first + tile) * rows, part[:, tile * LANES : (tile + 1) * LANES])

    if kind == "down":
        rows_of = pl.ds(pl.multiple_of(half * plan.down_rows, 16), plan.down_rows)
        for j in shards:
            first = (j * plan.down_tiles + start) * LANES
            value = dot(sources.down_x[rows_of, :], sources.down_dy[:, first : first + tiles * LANES])
            for tile in range(tiles):
                finish(j, tile * rows, value[:, tile * LANES : (tile + 1) * LANES])
        return
    if kind == "mixed":
        last = plan.width_tiles - 1
        give(
            dot(sources.attn_x[0], sources.pair_dy[half, :, :LANES])
            + dot(sources.attn_x[half], sources.attn_dy[half, :, last * LANES :]),
            0,
        )
    for first in range(1 if kind == "mixed" else 0, tiles, 2):
        count = min(2, tiles - first)
        if kind == "mixed":
            value = dot(sources.attn_x[0], sources.pair_dy[half, :, first * LANES : (first + count) * LANES])
        else:
            cols = slice((start + first) * LANES, (start + first + count) * LANES)
            if kind == "ffn":
                value = dot(sources.ffn_x[...], sources.ffn_dy(half, index, first * LANES, cols))
            else:
                value = dot(sources.attn_x[half], sources.attn_dy[half, :, cols])
        give(value, first)
    if kind == "mixed":
        for j in shards:
            finish(j, tiles * rows, sources.extra[half, j])


def spread_gains(plan, gain_sums, extra):
    for half in range(2):
        for j in range(plan.dp):
            for number in range(-(-plan.shard // LANES)):
                start = j * plan.shard + number * LANES
                extra[half, j, number : number + 1, :] = gain_sums[
                    half : half + 1, start : start + LANES
                ]


def reduce_kernel(
    plan, ffn_x, ffn_dy, down_x, down_dy, attn_x, attn_dy, pair_dy, gain_sums, out, extra, *refs
):
    sources = types.SimpleNamespace(
        ffn_x=ffn_x, ffn_dy=lambda half, index, inside, cols: ffn_dy[half, :, cols],
        down_x=down_x, down_dy=down_dy,
        attn_x=attn_x, attn_dy=attn_dy, pair_dy=pair_dy, extra=extra,
    )
    reduction = Reduction(
        plan, lambda *place: shard_products(plan, *place, sources), out, refs
    )
    greet(reduction.friends())
    spread_gains(plan, gain_sums, extra)
    reduction.drain()


def reduce_grads(plan, *operands):
    return pl.pallas_call(
        functools.partial(reduce_kernel, plan),
        out_shape=jax.ShapeDtypeStruct((2, plan.cy, plan.cx, plan.total, LANES), jnp.bfloat16),
        in_specs=[pl.BlockSpec(memory_space=pltpu.VMEM)] * len(operands),
        out_specs=pl.BlockSpec(memory_space=pl.ANY),
        scratch_shapes=[pltpu.VMEM((2, plan.dp, 16, LANES), jnp.float32), *plan.scratch()],
        compiler_params=pltpu.CompilerParams(
            collective_id=0, has_side_effects=True, vmem_limit_bytes=64 << 20
        ),
        cost_estimate=pl.CostEstimate(flops=10**10, bytes_accessed=20 * 10**6, transcendentals=0),
    )(*operands)


class Block:
    def __init__(self, tokens, length, width, hidden, kv_width, ctx):
        self.tokens, self.length, self.width, self.hidden = tokens, length, width, hidden
        self.kv_width, self.ctx = kv_width, ctx
        self.kv_heads = kv_width // HEAD_DIM
        self.group = width // kv_width
        self.step = 512


def dot(one, other, over=(1, 0)):
    return lax.dot_general(
        one, other, (((over[0],), (over[1],)), ((), ())), preferred_element_type=jnp.float32
    )


def fold_rows(values, combine):
    return combine(values.reshape(values.shape[0] // 8, 8, values.shape[1]), 0)


def norm(values):
    return lax.rsqrt(jnp.mean(values * values, 0, keepdims=True) + epsilon)


def app_tokens(size, app):
    return slice(app * size.tokens, (app + 1) * size.tokens)


def head_rows(size, g, h):
    return pl.ds(pl.multiple_of((g * size.group + h) * HEAD_DIM, HEAD_DIM), HEAD_DIM)


def wide_gain(env, which):
    return jnp.concatenate([env.columns[which]] * (env.size.tokens // LANES), 1)


def spread_columns(size, gains, columns):
    for which in range(2):
        for start in range(0, size.width, LANES):
            rows = min(LANES, size.width - start)
            tile = jnp.broadcast_to(gains[which : which + 1, start : start + LANES], (LANES, LANES))
            columns[which, start : start + rows, :] = tile.T[:rows]


def norm_back(env, values, which, grad_normed):
    size = env.size
    inverse = norm(values)
    product = grad_normed * values * inverse
    folded = product[:, :LANES]
    for start in range(LANES, size.tokens, LANES):
        folded = folded + product[:, start : start + LANES]
    for start in range(0, size.width, LANES):
        stop = min(start + LANES, size.width)
        part = folded[start:stop]
        if stop - start < LANES:
            part = jnp.concatenate([part, jnp.zeros((LANES - stop + start, LANES), jnp.float32)], 0)
        env.gain_sums[which : which + 1, start : start + LANES] += jnp.sum(part.T, 0, keepdims=True)
    weighted = grad_normed * wide_gain(env, which)
    cubed = inverse * inverse * inverse
    return inverse * weighted - values * (cubed * jnp.mean(weighted * values, 0, keepdims=True))


def rope(env, values, sign):
    half = HEAD_DIM // 2
    cos, sine = env.cos_q[...], env.sin_q[...] * sign
    out = []
    for start in range(0, values.shape[0], HEAD_DIM):
        former = values[start : start + half]
        latter = values[start + half : start + HEAD_DIM]
        out += [former * cos - latter * sine, latter * cos + former * sine]
    return jnp.concatenate(out, 0)


def ffn_back(env, gate_ref, up_ref, rows, cols, wd, wg, wu):
    gate = gate_ref[rows, cols].astype(jnp.float32)
    upward = up_ref[rows, cols].astype(jnp.float32)
    sigmoid = 1.0 / (1.0 + jnp.exp(-gate))
    scaled = dot(env.natural[...], wd) * sigmoid
    grad_gate = (scaled * upward * (1.0 + gate * (1.0 - sigmoid))).astype(jnp.bfloat16)
    grad_up = (scaled * gate).astype(jnp.bfloat16)
    gate_ref[rows, cols] = grad_gate
    up_ref[rows, cols] = grad_up
    env.accum[...] += dot(wg, grad_gate, (1, 1)) + dot(wu, grad_up, (1, 1))


def middle_back(env, grad_low, mid):
    grad_middle = grad_low.astype(jnp.float32) + norm_back(env, mid, 1, env.accum[...])
    env.dmid[...] = grad_middle
    branch = grad_middle.astype(jnp.bfloat16)
    env.d_attn[1, : env.size.tokens, : env.size.width] = branch.T
    env.do_t[...] = dot(env.wo[...], branch).astype(jnp.bfloat16)


def grad_copy(env, g, k):
    owner = jnp.maximum(env.ctx - k, 0)
    rows = pl.ds(pl.multiple_of(owner * env.size.tokens, env.size.tokens), env.size.tokens)
    return pltpu.make_async_remote_copy(
        env.kv_send.at[g, rows], env.kv_recv.at[k - 1, g],
        env.sem_d.at[0, g, k - 1], env.sem_d.at[1, g, k - 1],
        device_id=(env.section, env.row, owner), device_id_type=MESH,
    )


def attend_back(env, at, g):
    size, low_type = env.size, jnp.bfloat16
    k_t = env.kv[g].T[:HEAD_DIM]
    sides = []
    for h in range(size.group):
        rows, cols = head_rows(size, g, h), slice(h * size.tokens, (h + 1) * size.tokens)
        query, grad_head = env.q_t[rows, :], env.do_t[rows, :]
        empty = jnp.zeros_like(query)
        query = jnp.concatenate([query, empty], 0)
        grad_pad = jnp.concatenate([empty, grad_head], 0)
        delta = jnp.sum(
            grad_head.astype(jnp.float32) * env.x_attn[1, rows, at].astype(jnp.float32),
            0, keepdims=True,
        )
        log_sum = env.lse[g, h : h + 1, :]
        for start in range(0, size.length, 256):
            keys_at = slice(start, start + 256)
            part = dot(env.kv[g, keys_at, :], query) * score_unit + env.bias[keys_at, :]
            chance = jnp.exp2(part - log_sum)
            env.chances[keys_at, cols] = chance.astype(low_type)
            change = dot(env.kv[g, keys_at, :], grad_pad) - delta
            env.grad_scores[keys_at, cols] = (chance * change).astype(low_type)
        sides.append(((query.astype(jnp.float32) * score_scale).astype(low_type), grad_pad))
        env.accum[rows, :] = dot(k_t, env.grad_scores[:, cols]) * score_scale
    small, grad_pad = (jnp.concatenate(side, 1) for side in zip(*sides))
    env.kv_send[g] = (
        dot(env.grad_scores[...], small, (1, 1)) + dot(env.chances[...], grad_pad, (1, 1))
    ).astype(low_type)
    for k in range(1, size.ctx):
        @pl.when(env.ctx - k >= 0)
        def _():
            grad_copy(env, g, k).start()


def project_back(env):
    size, low_type = env.size, jnp.bfloat16
    tokens, width = size.tokens, size.width
    for start in range(0, width, 2 * LANES):
        stop = min(start + 2 * LANES, width)
        tile = rope(env, env.accum[start:stop, :], -1.0).astype(low_type)
        env.natural[:, start:stop] = tile.T
        env.do_t[start:stop, :] = tile
    env.d_attn[0, :tokens, :width] = env.natural[...]
    own_rows = pl.ds(pl.multiple_of(env.ctx * tokens, tokens), tokens)
    pairs = [[], []]
    for g in range(size.kv_heads):
        tile = env.kv_send[g, own_rows, :].astype(jnp.float32)
        for k in range(1, size.ctx):
            @pl.when(env.ctx + k < size.ctx)
            def _():
                grad_copy(env, g, k).wait_recv()
            tile = tile + jnp.where(
                env.ctx + k < size.ctx, env.kv_recv[k - 1, g].astype(jnp.float32), 0.0
            )
        tile = tile.T
        pairs[0].append(rope(env, tile[:HEAD_DIM], -1.0).astype(low_type))
        pairs[1].append(tile[HEAD_DIM:].astype(low_type))
    spare = env.d_pair.shape[2] - size.kv_width
    for half in range(2):
        pairs[half] = jnp.concatenate(pairs[half], 0)
        env.d_pair[half, :tokens, :] = jnp.concatenate(
            [jnp.zeros((spare, tokens), low_type), pairs[half]], 0
        ).T
    grad_normed = (
        dot(env.wq[...], env.do_t[...])
        + dot(env.wk[...], pairs[0], (0, 0))
        + dot(env.wv[...], pairs[1], (0, 0))
    )
    return env.dmid[...] + norm_back(env, env.x[...].astype(jnp.float32), 0, grad_normed)


def drain_grad_copies(env):
    def one(g, carry):
        for k in range(1, env.size.ctx):
            @pl.when(env.ctx - k >= 0)
            def _():
                grad_copy(env, g, k).wait_send()
        return carry

    lax.fori_loop(0, env.size.kv_heads, one, 0)


def front_kernel(
    size, inputs, cotangent, segments, cos_in, sin_in, gains,
    wq_in, wk_in, wv_in, wo_in, wg_in, wu_in, wd_in,
    acts, n2_out, df_out, inner_out, attn_out, d_attn_out, d_pair_out, d_ffn_out,
    mid_out, q_out, kv_out, lse_out, bias_out, gain_out,
    wq, wk, wv, wo, wg, wu, wd, n2_t, df_t, inner, x_attn, d_attn, d_pair, d_ffn, gain_sums,
    cos_q, sin_q, columns, xin, cot, last, mid, q_t,
    kv, kv_send, kv_recv, lse, do_t, bias, accum, dmid, natural, scores, chances, grad_scores,
    sem_w, sem_k, sem_d, sem_e, sem_o,
):
    tokens, ctx_count, groups, group = size.tokens, size.ctx, size.kv_heads, size.group
    width, low_type, full = size.width, jnp.bfloat16, jnp.float32
    section, row, ctx = (lax.axis_index(name) for name in ("section", "dp", "ctx"))
    mate = (1 - section, row, ctx)
    own_rows = pl.ds(pl.multiple_of(ctx * tokens, tokens), tokens)
    env = types.SimpleNamespace(
        size=size, section=section, row=row, ctx=ctx, columns=columns, gain_sums=gain_sums,
        cos_q=cos_q, sin_q=sin_q, natural=natural, accum=accum, dmid=dmid, do_t=do_t,
        d_attn=d_attn, d_pair=d_pair, x_attn=x_attn, bias=bias, chances=chances,
        grad_scores=grad_scores, kv=kv.at[1], q_t=q_t.at[1], lse=lse.at[1], x=xin.at[1],
        kv_send=kv_send, kv_recv=kv_recv, sem_d=sem_d, wq=wq, wk=wk, wv=wv, wo=wo,
    )
    loads = [
        pltpu.make_async_copy(source, target, sem_w.at[number])
        for number, (source, target) in enumerate((
            (inputs.at[section], xin.at[0]), (cos_in.at[:, own_rows], cos_q),
            (sin_in.at[:, own_rows], sin_q), (wk_in, wk), (wv_in, wv), (wq_in, wq), (wo_in, wo),
            (wg_in, wg), (wu_in, wu), (wd_in, wd), (cotangent.at[section], cot),
        ))
    ]
    for load in loads:
        load.start()
    stores = []

    def store(source, target):
        copy = pltpu.make_async_copy(source, target, sem_o.at[len(stores)])
        copy.start()
        stores.append(copy)

    barrier = pltpu.get_barrier_semaphore()
    friends = [mate] + [(section, row, lax.rem(ctx + k, ctx_count)) for k in range(1, ctx_count)]
    for friend in friends:
        pl.semaphore_signal(barrier, 1, device_id=friend, device_id_type=MESH)
    spread_columns(size, gains, columns)
    query_seg = segments[section, :, own_rows].astype(full)
    query_pos = lax.broadcasted_iota(jnp.int32, (1, tokens), 1) + ctx * tokens
    for start in range(0, size.length, LANES):
        key_seg = jnp.broadcast_to(
            segments[section, :, start : start + LANES].astype(full), (LANES, LANES)
        ).T
        key_pos = lax.broadcasted_iota(jnp.int32, (LANES, tokens), 0) + start
        key_seg = jnp.concatenate([key_seg] * (tokens // LANES), 1)
        allowed = (key_seg == query_seg) & (key_pos <= query_pos)
        bias[start : start + LANES, :] = jnp.where(allowed, 0.0, mask_floor)
    store(bias, bias_out)
    for k in range(1, ctx_count):
        @pl.when(ctx + k < ctx_count)
        def _():
            rows = pl.ds(pl.multiple_of((ctx + k) * tokens, tokens), tokens)
            for app in range(2):
                kv[app, :, rows, :] = jnp.zeros((groups, tokens, LANES), low_type)
    pl.semaphore_wait(barrier, len(friends))

    def kv_copy(app, g, k):
        return pltpu.make_async_remote_copy(
            kv.at[app, g, own_rows], kv.at[app, g, own_rows],
            sem_k.at[0, app, g, k - 1], sem_k.at[1, app, g, k - 1],
            device_id=(section, row, jnp.minimum(ctx + k, ctx_count - 1)), device_id_type=MESH,
        )

    outputs = (xin.at[1], last)
    act_copies = [
        pltpu.make_async_remote_copy(
            source, acts.at[section], sem_e.at[0], sem_e.at[1], device_id=mate, device_id_type=MESH
        )
        for source in outputs
    ]
    act_stores = [
        pltpu.make_async_copy(source, acts.at[section], sem_e.at[2]) for source in outputs
    ]

    def forward(app):
        at = app_tokens(size, app)
        x = xin[app].astype(full)
        normed = (x * norm(x) * wide_gain(env, 0)).astype(low_type)
        x_attn[0, :, at] = normed
        if app == 0:
            for load in loads[1:5]:
                load.wait()
        keys = rope(env, dot(wk[...], normed), 1.0).astype(low_type)
        values = dot(wv[...], normed).astype(low_type)
        for g in range(groups):
            piece = slice(g * HEAD_DIM, (g + 1) * HEAD_DIM)
            kv[app, g, own_rows, :] = jnp.concatenate([keys[piece], values[piece]], 0).T
            for k in range(1, ctx_count):
                @pl.when(ctx + k < ctx_count)
                def _():
                    kv_copy(app, g, k).start()
        if app == 0:
            loads[5].wait()
        for start in range(0, width, 2 * LANES):
            stop = min(start + 2 * LANES, width)
            tile = dot(wq[:, start:stop], normed, (0, 0))
            q_t[app, start:stop, :] = rope(env, tile, 1.0).astype(low_type)
        if app == 0:
            store(q_t.at[0], q_out)

        def heads(g, carry):
            for k in range(1, ctx_count):
                @pl.when(ctx - k >= 0)
                def _():
                    kv_copy(app, g, k).wait_recv()
            v_t = kv[app, g].T[HEAD_DIM:]
            for h in range(group):
                query = q_t[app, head_rows(size, g, h), :]
                query = jnp.concatenate([query, jnp.zeros_like(query)], 0)
                largest = None
                for start in range(0, size.length, 256):
                    keys_at = slice(start, start + 256)
                    part = dot(kv[app, g, keys_at, :], query) * score_unit + bias[keys_at, :]
                    scores[h, keys_at, :] = part
                    most = fold_rows(part, jnp.max)
                    largest = most if largest is None else jnp.maximum(largest, most)
                largest = jnp.max(largest, 0, keepdims=True)
                total = jnp.zeros((8, tokens), full)
                for start in range(0, size.length, 64):
                    keys_at = slice(start, start + 64)
                    weights = jnp.exp2(scores[h, keys_at, :] - largest)
                    total = total + fold_rows(weights, jnp.sum)
                    chances[keys_at, h * tokens : (h + 1) * tokens] = weights.astype(low_type)
                total = jnp.sum(total, 0, keepdims=True)
                out = dot(v_t, chances[:, h * tokens : (h + 1) * tokens]) / total
                lse[app, g, h : h + 1, :] = largest + jnp.log(total) * (1.0 / math.log(2.0))
                x_attn[1, head_rows(size, g, h), at] = out.astype(low_type)
            return carry

        lax.fori_loop(0, groups, heads, 0)
        if app == 0:
            store(kv.at[0], kv_out)
            store(lse.at[0], lse_out)
            loads[6].wait()
        else:
            store(x_attn, attn_out)
        middle = xin[app].astype(full) + dot(wo[...], x_attn[1, :, at], (0, 0))
        mid[app] = middle
        ffn = (middle * norm(middle) * wide_gain(env, 1)).astype(low_type)
        n2_t[:, at] = ffn
        natural[...] = ffn.T
        if app == 0:
            store(mid.at[0], mid_out)
            for load in loads[7:10]:
                load.wait()
        else:
            store(n2_t, n2_out)
        accum[...] = middle

        def chunk(i, carry):
            cols = pl.ds(pl.multiple_of(i * size.step, size.step), size.step)
            gate = dot(natural[...], wg[:, cols])
            upward = dot(natural[...], wu[:, cols])
            hidden = (gate / (1.0 + jnp.exp(-gate)) * upward).astype(low_type)
            d_ffn[0, at, cols] = gate.astype(low_type)
            d_ffn[1, at, cols] = upward.astype(low_type)
            inner[at, cols] = hidden
            accum[...] += dot(wd[:, cols], hidden, (1, 1))
            return carry

        lax.fori_loop(0, size.hidden // size.step, chunk, 0)
        outputs[app][...] = accum[...].astype(low_type)

        @pl.when(section == app)
        def _():
            act_stores[app].start()

        @pl.when(section != app)
        def _():
            act_copies[app].start()

    gain_sums[...] = jnp.zeros_like(gain_sums)
    d_attn[:, :, width:] = jnp.zeros((2, tokens, d_attn.shape[2] - width), low_type)
    loads[0].wait()
    forward(0)
    forward(1)
    store(inner, inner_out)
    loads[10].wait()
    grad_low = cot[...]
    at = app_tokens(size, 1)
    df_t[:, at] = grad_low
    natural[...] = grad_low.T
    accum[...] = jnp.zeros_like(accum)

    def chunk(i, carry):
        cols = pl.ds(pl.multiple_of(i * size.step, size.step), size.step)
        ffn_back(env, d_ffn.at[0], d_ffn.at[1], at, cols, wd[:, cols], wg[:, cols], wu[:, cols])
        return carry

    lax.fori_loop(0, size.hidden // size.step, chunk, 0)
    store(d_ffn, d_ffn_out)
    middle_back(env, grad_low, mid[1])
    lax.fori_loop(0, groups, lambda g, carry: attend_back(env, at, g), None)
    df_t[:, app_tokens(size, 0)] = project_back(env).astype(low_type)
    for source, target in (
        (df_t, df_out), (d_attn, d_attn_out), (d_pair, d_pair_out), (gain_sums, gain_out)
    ):
        store(source, target)

    def drain(g, carry):
        for app in range(2):
            for k in range(1, ctx_count):
                @pl.when(ctx + k < ctx_count)
                def _():
                    kv_copy(app, g, k).wait_send()
        return carry

    lax.fori_loop(0, groups, drain, 0)
    drain_grad_copies(env)
    act_copies[0].wait()
    act_stores[0].wait()
    for copy in stores:
        copy.wait()


def front_shapes(size, plan):
    tokens, width, hidden, groups = size.tokens, size.width, size.hidden, size.kv_heads
    low, full, both = jnp.bfloat16, jnp.float32, 2 * size.tokens
    return [
        ((width, both), low),
        ((width, both), low),
        ((both, hidden), low),
        ((2, width, both), low),
        ((2, tokens, plan.width_tiles * LANES), low),
        ((2, tokens, (plan.pair_tiles - plan.width_tiles + 1) * LANES), low),
        ((2, both, hidden), low),
        ((width, tokens), full),
        ((width, tokens), low),
        ((groups, size.length, LANES), low),
        ((groups, 8, tokens), full),
        ((size.length, tokens), full),
        ((8, plan.width_tiles * LANES), full),
    ]


def run_front(size, plan, *operands):
    tokens, width, hidden, groups = size.tokens, size.width, size.hidden, size.kv_heads
    low, full = jnp.bfloat16, jnp.float32
    vmem = pl.BlockSpec(memory_space=pltpu.VMEM)
    far = pl.BlockSpec(memory_space=pl.ANY)
    dma = pltpu.SemaphoreType.DMA
    others = max(size.ctx - 1, 1)
    kept = front_shapes(size, plan)
    shapes = [((2, width, tokens), low)] + kept
    scratch = [
        ((width, width), low),
        ((size.kv_width, width), low),
        ((size.kv_width, width), low),
        ((width, width), low),
        ((width, hidden), low),
        ((width, hidden), low),
        ((width, hidden), low),
        *kept[:7],
        kept[12],
        ((HEAD_DIM // 2, tokens), full),
        ((HEAD_DIM // 2, tokens), full),
        ((2, width, LANES), full),
        ((2, width, tokens), low),
        ((width, tokens), low),
        ((width, tokens), low),
        ((2, width, tokens), full),
        ((2, width, tokens), low),
        ((2, groups, size.length, LANES), low),
        ((groups, size.length, LANES), low),
        ((others, groups, tokens, LANES), low),
        ((2, groups, 8, tokens), full),
        ((width, tokens), low),
        ((size.length, tokens), full),
        ((width, tokens), full),
        ((width, tokens), full),
        ((tokens, width), low),
        ((size.group, size.length, tokens), full),
        ((size.length, size.group * tokens), low),
        ((size.length, size.group * tokens), low),
    ]
    return pl.pallas_call(
        functools.partial(front_kernel, size),
        out_shape=[jax.ShapeDtypeStruct(*shape) for shape in shapes],
        in_specs=[far, far, vmem, far, far, vmem] + [far] * 7,
        out_specs=[far] * len(shapes),
        scratch_shapes=[pltpu.VMEM(*shape) for shape in scratch] + [
            dma((11,)), dma((2, 2, groups, others)), dma((2, groups, others)), dma((3,)),
            dma((len(kept),)),
        ],
        compiler_params=pltpu.CompilerParams(
            collective_id=1, has_side_effects=True, vmem_limit_bytes=64 << 20
        ),
        cost_estimate=pl.CostEstimate(
            flops=3 * 10**10, bytes_accessed=40 * 10**6, transcendentals=3 * 10**7
        ),
    )(*operands)


def tail_kernel(
    size, plan, inputs, cos_in, sin_in, gains, n2_in, df_in, inner_in, attn_in, d_attn_in, d_pair_in,
    d_ffn_in, mid_in, q_in, kv_in, lse_in, bias_in, gain_in,
    wq_in, wk_in, wv_in, wo_in, wg_in, wu_in, wd_in,
    out, grads,
    n2_t, df_t, inner, x_attn, d_attn, d_pair, d_ffn, mid, q_t, kv, lse, bias, gain_sums,
    wq, wk, wv, wo, blocks, cos_q, sin_q, columns, xin, kv_send, kv_recv, do_t, accum, natural,
    chances, grad_scores, stage, extra, sem_l, sem_b, sem_d, sem_e, *refs,
):
    tokens, width, low_type, full = size.tokens, size.width, jnp.bfloat16, jnp.float32
    section, row, ctx = (lax.axis_index(name) for name in ("section", "dp", "ctx"))
    mate = (1 - section, row, ctx)
    own_rows = pl.ds(pl.multiple_of(ctx * tokens, tokens), tokens)
    first_ffn, ffn_count = plan.of("ffn")[0], len(plan.of("ffn"))
    env = types.SimpleNamespace(
        size=size, section=section, row=row, ctx=ctx, columns=columns, gain_sums=gain_sums,
        cos_q=cos_q, sin_q=sin_q, natural=natural, accum=accum, dmid=mid, do_t=do_t,
        d_attn=d_attn, d_pair=d_pair, x_attn=x_attn, bias=bias, chances=chances,
        grad_scores=grad_scores, kv=kv, q_t=q_t, lse=lse, x=xin,
        kv_send=kv_send, kv_recv=kv_recv, sem_d=sem_d, wq=wq, wk=wk, wv=wv, wo=wo,
    )
    sources = types.SimpleNamespace(
        ffn_x=n2_t, ffn_dy=lambda half, index, inside, cols: d_ffn[
            (index - first_ffn) % 3, half, :, inside : inside + cols.stop - cols.start
        ],
        down_x=df_t, down_dy=inner, attn_x=x_attn, attn_dy=d_attn, pair_dy=d_pair, extra=extra,
    )
    count = len(plan.chunks)
    turns = [step // 8 for step in TAIL_ORDER if step >= 0 and step % 8 == 0]
    reduction = Reduction(
        plan, lambda *place: shard_products(plan, *place, sources), out, refs, turns
    )

    def block_loads(i):
        cols = pl.ds(i * size.step, size.step)
        pairs = [(wd_in, 0), (wg_in, 1), (wu_in, 2)]
        return [
            pltpu.make_async_copy(weight.at[:, cols], blocks.at[i % 2, n], sem_b.at[i % 2, n])
            for weight, n in pairs
        ] + [pltpu.make_async_copy(d_ffn_in.at[:, :, cols], d_ffn.at[i % 3], sem_b.at[i % 2, 3])]

    later = pl.ds(tokens, tokens)
    names = (
        "df", "inner", "mid", "n2", "wo", "cos", "sin", "q", "kv", "lse", "bias", "attn", "d_attn",
        "d_pair", "x", "wq", "wk", "wv", "gain",
    )
    loads = dict(zip(names, (
        pltpu.make_async_copy(source, target, sem_l.at[number])
        for number, (source, target) in enumerate((
            (df_in, df_t), (inner_in, inner), (mid_in, mid), (n2_in, n2_t), (wo_in, wo),
            (cos_in.at[:, own_rows], cos_q), (sin_in.at[:, own_rows], sin_q),
            (q_in, q_t), (kv_in, kv), (lse_in, lse), (bias_in, bias), (attn_in, x_attn),
            (d_attn_in, d_attn.at[:, later]), (d_pair_in, d_pair.at[:, later]),
            (inputs.at[section], xin), (wq_in, wq), (wk_in, wk), (wv_in, wv), (gain_in, gain_sums),
        ))
    )))

    def ready(*names):
        for name in names:
            if name in loads:
                loads.pop(name).wait()

    for name in ("df", "inner"):
        loads[name].start()
    for load in block_loads(0):
        load.start()
    for name in names[2:]:
        loads[name].start()
    greet(reduction.friends())
    spread_columns(size, gains, columns)
    d_attn[:, :tokens, width:] = jnp.zeros((2, tokens, d_attn.shape[2] - width), low_type)

    back_copy = pltpu.make_async_remote_copy(
        stage, grads.at[section], sem_e.at[0], sem_e.at[1], device_id=mate, device_id_type=MESH
    )
    back_store = pltpu.make_async_copy(stage, grads.at[section], sem_e.at[2])

    def keep(app, value):
        stage[...] = value

        @pl.when(section == app)
        def _():
            back_store.start()

        @pl.when(section != app)
        def _():
            back_copy.start()

    def kept(app):
        @pl.when(section == app)
        def _():
            back_store.wait()

        @pl.when(section != app)
        def _():
            back_copy.wait_send()

    ready("df", "inner")
    grad_low = df_t[:, :tokens]
    keep(1, grad_low.astype(full))
    natural[...] = grad_low.T
    accum[...] = jnp.zeros_like(accum)

    def ffn_step(i):
        for load in block_loads(i):
            load.wait()
        if i + 1 < ffn_count:
            assert i < 2 or reduction.done[first_ffn + i - 2] >= 2
            for load in block_loads(i + 1):
                load.start()
        ffn_back(
            env, d_ffn.at[i % 3, 0], d_ffn.at[i % 3, 1], slice(0, tokens), slice(0, size.step),
            blocks[i % 2, 0], blocks[i % 2, 1], blocks[i % 2, 2],
        )

    taken = {-1: 0, -2: 0, -3: 0, -4: 0}
    for step in TAIL_ORDER:
        if step >= 0:
            if plan.chunks[step // 8][0] == "ffn" and step % 8 < 2:
                ready("n2")
                assert taken[-1] > step // 8 - first_ffn
            assert reduction.done[step // 8] == step % 8
            reduction.advance(step // 8)
            continue
        number, taken[step] = taken[step], taken[step] + 1
        if step == -1:
            ffn_step(number)
        elif step == -2:
            assert taken[-1] == ffn_count
            ready("mid", "wo", "gain")
            middle_back(env, grad_low, mid[...])
        elif step == -3:
            ready("q", "kv", "lse", "bias", "attn")
            attend_back(env, app_tokens(size, 0), number)
        else:
            assert taken[-3] == size.kv_heads
            ready("cos", "sin", "d_attn", "d_pair", "x", "wq", "wk", "wv")
            grad_in = project_back(env)
            kept(1)
            keep(0, grad_in)
            spread_gains(plan, gain_sums, extra)
    reduction.drain()
    drain_grad_copies(env)
    kept(0)
    back_copy.wait_recv()


def run_tail(size, plan, *operands):
    tokens, width, groups = size.tokens, size.width, size.kv_heads
    low, full, both = jnp.bfloat16, jnp.float32, 2 * size.tokens
    vmem = pl.BlockSpec(memory_space=pltpu.VMEM)
    far = pl.BlockSpec(memory_space=pl.ANY)
    dma = pltpu.SemaphoreType.DMA
    others = max(size.ctx - 1, 1)
    kept = front_shapes(size, plan)
    scratch = kept[:4] + [
        ((2, both, kept[4][0][2]), low),
        ((2, both, kept[5][0][2]), low),
        ((3, 2, both, size.step), low),
        *kept[7:],
        ((width, width), low),
        ((size.kv_width, width), low),
        ((size.kv_width, width), low),
        ((width, width), low),
        ((2, 3, width, size.step), low),
        ((HEAD_DIM // 2, tokens), full),
        ((HEAD_DIM // 2, tokens), full),
        ((2, width, LANES), full),
        ((width, tokens), low),
        ((groups, size.length, LANES), low),
        ((others, groups, tokens, LANES), low),
        ((width, tokens), low),
        ((width, tokens), full),
        ((tokens, width), low),
        ((size.length, size.group * tokens), low),
        ((size.length, size.group * tokens), low),
        ((width, tokens), full),
        ((2, plan.dp, 16, LANES), full),
    ]
    return pl.pallas_call(
        functools.partial(tail_kernel, size, plan),
        out_shape=[
            jax.ShapeDtypeStruct((2, plan.cy, plan.cx, plan.total, LANES), low),
            jax.ShapeDtypeStruct((2, width, tokens), full),
        ],
        in_specs=[far, far, far, vmem] + [far] * (len(operands) - 4),
        out_specs=[far, far],
        scratch_shapes=[pltpu.VMEM(*shape) for shape in scratch] + [
            dma((19,)), dma((2, 4)), dma((2, groups, others)), dma((3,)), *plan.scratch(),
        ],
        compiler_params=pltpu.CompilerParams(
            collective_id=2, has_side_effects=True, vmem_limit_bytes=64 << 20
        ),
        cost_estimate=pl.CostEstimate(
            flops=3 * 10**10, bytes_accessed=40 * 10**6, transcendentals=10**7
        ),
    )(*operands)


def rotary(length):
    half = HEAD_DIM // 2
    frequency = 10000.0 ** (-2.0 * np.arange(half) / HEAD_DIM)
    angles = frequency[:, None] * np.arange(length)[None, :]
    return np.asarray(np.cos(angles), np.float32), np.asarray(np.sin(angles), np.float32)


def unpack_kernel(plan, sizes, *refs):
    width, hidden, kv_width, through = sizes
    summed, refs = refs[0], refs[1:]
    (query, key_t, value_t, out, gate, up, down_t, *gains), rest = refs[through : through + 9], refs[through + 9 :]
    for source, target in zip(refs[:through], rest):
        target[...] = source[...]
    full, rows, half_width = jnp.float32, width // plan.dp, width // 2

    def tile(half, index, first, count):
        parts = [
            summed[half, p // plan.cx, p % plan.cx, pl.ds(plan.offsets[index] + place, size), :]
            for p, place, inside, size in plan.spans(index, first, count)
        ]
        return (parts[0] if len(parts) == 1 else jnp.concatenate(parts, 0)).astype(full)

    def put(target, at, cols, value):
        count = min(LANES, target.shape[1] - cols)
        target[at : at + value.shape[0], cols : cols + count] = value[:, :count]

    for index, (kind, start, tiles, height, piece, mode) in enumerate(plan.chunks):
        for half in range(2):
            for number in range(tiles):
                value = tile(half, index, number * height, height)
                cols = (start + number) * LANES
                if kind == "ffn":
                    put((gate, up)[half], 0, cols, value[:rows])
                elif kind == "down":
                    put(down_t, half * half_width, cols, value[:half_width])
                elif kind == "attn":
                    put((query, out)[half], 0, cols, value[:rows])
                else:
                    spare = plan.width_tiles * LANES - width
                    if number == 0:
                        put((query, out)[half], 0, width + spare - LANES, value[:rows])
                    pair_t = value.T[:, :rows]
                    first = number * LANES - LANES + spare
                    if first < 0:
                        pair_t = pair_t[LANES - spare :]
                        first = 0
                    (key_t, value_t)[half][first : first + pair_t.shape[0], :] = pair_t
            if kind == "mixed":
                lines = tile(half, index, tiles * height, 16)
                for number in range(-(-rows // LANES)):
                    put(gains[half], 0, number * LANES, lines[number : number + 1])


def unpack(plan, sizes, summed, *through):
    width, hidden, kv_width = sizes
    rows, full = width // plan.dp, jnp.float32
    shapes = [
        (rows, width), (kv_width, rows), (kv_width, rows), (rows, width),
        (rows, hidden), (rows, hidden), (width, hidden // plan.dp), (1, rows), (1, rows),
    ]
    vmem = pl.BlockSpec(memory_space=pltpu.VMEM)
    return pl.pallas_call(
        functools.partial(unpack_kernel, plan, (*sizes, len(through))),
        out_shape=[jax.ShapeDtypeStruct(shape, full) for shape in shapes]
        + [jax.ShapeDtypeStruct(value.shape, value.dtype) for value in through],
        in_specs=[vmem] * (1 + len(through)),
        out_specs=[vmem] * (len(shapes) + len(through)),
        compiler_params=pltpu.CompilerParams(vmem_limit_bytes=60 << 20),
    )(summed, *through)


def plain_block(
    plan, inputs, segment_ids, cotangent,
    gain_attn, w_query, w_key, w_value, w_out, gain_ffn, w_gate, w_up, w_down,
):
    micro_count, row_count, tok_local, model_width = inputs.shape
    kv_width = w_key.shape[1]
    group_size = HEADS // KV_HEADS
    section_index = lax.axis_index("section")
    on_first = section_index == 0
    ctx_index = lax.axis_index("ctx")
    first_token = ctx_index * tok_local
    query_pos = first_token + jnp.arange(tok_local, dtype=jnp.int32)
    halfway = HEAD_DIM // 2
    frequency = 10000.0 ** (-2.0 * jnp.arange(halfway, dtype=jnp.float32) / HEAD_DIM)
    angles = query_pos.astype(jnp.float32)[:, None] * frequency[None, :]
    cos_table = jnp.cos(angles)
    sine_table = jnp.sin(angles)
    w_pair = jnp.concatenate([w_key, w_value], 1)
    head_shape = (row_count, tok_local, KV_HEADS, group_size, HEAD_DIM)
    state_shape = (row_count, KV_HEADS, group_size, tok_local)

    def front(hidden, segments):
        query_seg = lax.dynamic_slice_in_dim(segments, first_token, tok_local, 1)
        normed, inverse = rms_forward(hidden, gain_attn)
        normed_low = normed.astype(jnp.bfloat16)
        query_pre = jnp.einsum(
            "rcd,de->rce", normed_low, w_query, preferred_element_type=jnp.float32
        )
        pair_pre = jnp.einsum("rcd,de->rce", normed_low, w_pair, preferred_element_type=jnp.float32)
        queries = rotate(
            query_pre.reshape(row_count, tok_local, HEADS, HEAD_DIM), cos_table, sine_table
        )
        queries = queries.astype(jnp.bfloat16).reshape(head_shape)
        key_rot = rotate(
            pair_pre[..., :kv_width].reshape(row_count, tok_local, KV_HEADS, HEAD_DIM),
            cos_table,
            sine_table,
        )
        packed = jnp.concatenate(
            [key_rot.reshape(row_count, tok_local, kv_width), pair_pre[..., kv_width:]], -1
        )
        return (query_seg, inverse, normed_low, queries, packed.astype(jnp.bfloat16))

    def attend_forward(queries, arrived, segments, query_seg):
        start_state = (
            jnp.full(state_shape, mask_floor, jnp.float32),
            jnp.zeros(state_shape, jnp.float32),
            jnp.zeros(state_shape + (HEAD_DIM,), jnp.float32),
        )
        piece_rows = arrived.shape[1]
        block_rows = math.gcd(piece_rows, 512)

        def fold_inner_step(step_index, loop_state):
            run_max, run_sum, run_acc = loop_state
            offset = step_index * block_rows
            key_block = lax.dynamic_slice_in_dim(arrived, step_index * block_rows, block_rows, 1)
            key_part = key_block[..., :kv_width].reshape(row_count, block_rows, KV_HEADS, HEAD_DIM)
            value_part = key_block[..., kv_width:].reshape(
                row_count, block_rows, KV_HEADS, HEAD_DIM
            )
            key_seg = lax.dynamic_slice_in_dim(segments, offset, block_rows, 1)
            scores, allowed = block_scores(queries, key_part, query_seg, key_seg, query_pos, offset)
            masked = jnp.where(allowed, scores, mask_floor)
            new_max = jnp.maximum(run_max, jnp.max(masked, -1))
            weights = jnp.where(allowed, jnp.exp(masked - new_max[..., None]), 0.0)
            rescale = jnp.exp(run_max - new_max)
            run_sum = run_sum * rescale + jnp.sum(weights, -1)
            run_acc = run_acc * rescale[..., None] + jnp.einsum(
                "rkgcn,rnkd->rkgcd",
                weights.astype(jnp.bfloat16),
                value_part,
                preferred_element_type=jnp.float32,
            )
            return (new_max, run_sum, run_acc)

        run_max, run_sum, run_acc = lax.fori_loop(
            0, piece_rows // block_rows, fold_inner_step, start_state
        )
        return (run_acc / run_sum[..., None], run_max + jnp.log(run_sum))

    def rear(hidden, attended):
        attn_low = (
            attended.transpose(0, 3, 1, 2, 4)
            .reshape(row_count, tok_local, HEADS * HEAD_DIM)
            .astype(jnp.bfloat16)
        )
        middle = hidden + jnp.einsum(
            "rce,ed->rcd", attn_low, w_out, preferred_element_type=jnp.float32
        )
        normed_ffn, inverse_ffn = rms_forward(middle, gain_ffn)
        ffn_low = normed_ffn.astype(jnp.bfloat16)
        gate_pre = jnp.einsum("rcd,df->rcf", ffn_low, w_gate, preferred_element_type=jnp.float32)
        upward = jnp.einsum("rcd,df->rcf", ffn_low, w_up, preferred_element_type=jnp.float32)
        inner_act = (jax.nn.silu(gate_pre) * upward).astype(jnp.bfloat16)
        output = middle + jnp.einsum(
            "rcf,fd->rcd", inner_act, w_down, preferred_element_type=jnp.float32
        )
        return (output, (attn_low, middle, inverse_ffn, ffn_low, gate_pre, upward, inner_act))


    assert micro_count == lax.axis_size("section")

    def mine(stacked):
        return lax.dynamic_index_in_dim(stacked, section_index, 0, keepdims=False)

    segments = mine(segment_ids)

    def forward(hidden):
        query_seg, inverse, normed_low, queries, packed = front(hidden, segments)
        arrived = lax.all_gather(packed, "ctx", axis=1, tiled=True)
        attended, log_sum = attend_forward(queries, arrived, segments, query_seg)
        output, saved = rear(hidden, attended)
        return output.astype(jnp.bfloat16), (
            hidden, query_seg, inverse, normed_low, queries, arrived, attended, log_sum, saved
        )

    def backward(grad_out, kept):
        (
            hidden,
            backward_query_seg,
            backward_inverse,
            backward_normed_low,
            backward_queries,
            piece_arrived,
            backward_attended,
            log_sum,
            saved,
        ) = kept
        (
            backward_attn_low,
            backward_middle,
            backward_inverse_ffn,
            backward_ffn_low,
            backward_gate_pre,
            backward_upward,
            backward_inner_act,
        ) = saved
        grad_low = grad_out.astype(jnp.bfloat16)
        grad_inner = jnp.einsum("rcd,fd->rcf", grad_low, w_down, preferred_element_type=jnp.float32)
        sigmoid = jax.nn.sigmoid(backward_gate_pre)
        grad_gate = (
            grad_inner * backward_upward * sigmoid * (1.0 + backward_gate_pre * (1.0 - sigmoid))
        ).astype(jnp.bfloat16)
        grad_up = (grad_inner * backward_gate_pre * sigmoid).astype(jnp.bfloat16)
        grad_norm_ffn = jnp.einsum(
            "rcf,df->rcd", grad_gate, w_gate, preferred_element_type=jnp.float32
        ) + jnp.einsum("rcf,df->rcd", grad_up, w_up, preferred_element_type=jnp.float32)
        grad_mid_norm, backward_sum_gain_ffn = rms_backward(
            backward_middle, gain_ffn, backward_inverse_ffn, grad_norm_ffn
        )
        grad_middle = grad_out + grad_mid_norm
        grad_branch = grad_middle.astype(jnp.bfloat16)
        grad_attn = jnp.einsum(
            "rcd,ed->rce", grad_branch, w_out, preferred_element_type=jnp.float32
        ).astype(jnp.bfloat16)
        grad_heads = grad_attn.reshape(head_shape).transpose(0, 2, 3, 1, 4)
        row_delta = jnp.sum(grad_heads.astype(jnp.float32) * backward_attended, -1)
        query_start = jnp.zeros(state_shape + (HEAD_DIM,), jnp.float32)
        fold_grad_query = query_start
        grad_query = fold_grad_query
        piece_piece_rows = piece_arrived.shape[1]
        piece_block_rows = math.gcd(piece_piece_rows, 512)

        def piece_inner_step(step_index, loop_state):
            grad_query, local_pair = loop_state
            inside = step_index * piece_block_rows
            key_block = lax.dynamic_slice_in_dim(piece_arrived, inside, piece_block_rows, 1)
            key_part = key_block[..., :kv_width].reshape(
                row_count, piece_block_rows, KV_HEADS, HEAD_DIM
            )
            value_part = key_block[..., kv_width:].reshape(
                row_count, piece_block_rows, KV_HEADS, HEAD_DIM
            )
            key_seg = lax.dynamic_slice_in_dim(segments, inside, piece_block_rows, 1)
            scores, allowed = block_scores(
                backward_queries, key_part, backward_query_seg, key_seg, query_pos, inside
            )
            chances = jnp.where(
                allowed, jnp.exp(jnp.where(allowed, scores, mask_floor) - log_sum[..., None]), 0.0
            )
            grad_chance = jnp.einsum(
                "rkgcd,rnkd->rkgcn", grad_heads, value_part, preferred_element_type=jnp.float32
            )
            grad_scores = (chances * (grad_chance - row_delta[..., None])).astype(jnp.bfloat16)
            grad_query = grad_query + score_scale * jnp.einsum(
                "rkgcn,rnkd->rkgcd", grad_scores, key_part, preferred_element_type=jnp.float32
            )
            grad_key = score_scale * jnp.einsum(
                "rkgcn,rckgd->rnkd",
                grad_scores,
                backward_queries,
                preferred_element_type=jnp.float32,
            )
            grad_value = jnp.einsum(
                "rkgcn,rkgcd->rnkd",
                chances.astype(jnp.bfloat16),
                grad_heads,
                preferred_element_type=jnp.float32,
            )
            update = jnp.concatenate(
                [
                    grad_key.reshape(row_count, piece_block_rows, kv_width),
                    grad_value.reshape(row_count, piece_block_rows, kv_width),
                ],
                -1,
            )
            current = lax.dynamic_slice_in_dim(local_pair, inside, piece_block_rows, 1)
            local_pair = lax.dynamic_update_slice_in_dim(local_pair, current + update, inside, 1)
            return (grad_query, local_pair)

        local_start = jnp.zeros((row_count, piece_piece_rows, 2 * kv_width), jnp.float32)
        fold_grad_query, fold_local_pair = lax.fori_loop(
            0, piece_piece_rows // piece_block_rows, piece_inner_step, (grad_query, local_start)
        )
        grad_pair = fold_local_pair
        grad_query, grad_pair = (fold_grad_query, grad_pair)
        pair_share = lax.psum_scatter(
            grad_pair.astype(jnp.bfloat16), "ctx", scatter_dimension=1, tiled=True
        ).astype(jnp.float32)
        query_tok = grad_query.transpose(0, 3, 1, 2, 4).reshape(
            row_count, tok_local, HEADS, HEAD_DIM
        )
        query_back = rotate(query_tok, cos_table, -sine_table).reshape(
            row_count, tok_local, HEADS * HEAD_DIM
        )
        query_back = query_back.astype(jnp.bfloat16)
        key_back = rotate(
            pair_share[..., :kv_width].reshape(row_count, tok_local, KV_HEADS, HEAD_DIM),
            cos_table,
            -sine_table,
        )
        pair_low = jnp.concatenate(
            [key_back.reshape(row_count, tok_local, kv_width), pair_share[..., kv_width:]], -1
        )
        pair_low = pair_low.astype(jnp.bfloat16)
        grad_normed = jnp.einsum(
            "rce,de->rcd", query_back, w_query, preferred_element_type=jnp.float32
        ) + jnp.einsum("rce,de->rcd", pair_low, w_pair, preferred_element_type=jnp.float32)
        grad_front, backward_sum_gain_attn = rms_backward(
            hidden, gain_attn, backward_inverse, grad_normed
        )
        factors = (
            backward_normed_low, backward_attn_low, backward_ffn_low, backward_inner_act,
            query_back, pair_low, grad_branch, grad_gate, grad_up, grad_low,
        )
        tick_grads = (backward_sum_gain_attn, backward_sum_gain_ffn, factors)
        return grad_middle + grad_front, tick_grads

    first_low, first_kept = forward(mine(inputs).astype(jnp.float32))
    second_low, second_kept = forward(first_low.astype(jnp.float32))
    grad_mid, second_grads = backward(mine(cotangent).astype(jnp.float32), second_kept)
    grad_mid_low = grad_mid.astype(jnp.bfloat16)
    grad_in, first_grads = backward(grad_mid_low.astype(jnp.float32), first_kept)
    dp = plan.dp

    def stacked(one, other):
        return jnp.concatenate([one, other], 1).reshape(-1, one.shape[-1])

    normed, attn, ffn, inner, d_query, d_pair, d_branch, d_gate, d_up, d_out = (
        stacked(one, other) for one, other in zip(first_grads[2], second_grads[2])
    )
    tokens = normed.shape[0]

    def sides(values, rows):
        cut = values.reshape(tokens, dp, -1)
        cut = jnp.pad(cut, ((0, 0), (0, 0), (0, rows - cut.shape[2])))
        return cut.transpose(1, 2, 0).reshape(dp * rows, tokens)

    inner = inner.reshape(tokens, dp, -1)
    inner = jnp.pad(
        inner, ((0, 0), (0, 0), (0, plan.down_tiles * LANES - inner.shape[2]))
    ).reshape(tokens, -1)
    spare = plan.width_tiles * LANES - model_width
    gain_sums = jnp.stack([one + other for one, other in zip(first_grads[:2], second_grads[:2])])
    gain_sums = jnp.pad(gain_sums, ((0, 6), (0, plan.width_tiles * LANES - model_width)))
    factors = (
        sides(ffn, plan.rows),
        jnp.stack([d_gate, d_up]),
        d_out.T,
        inner,
        jnp.stack([sides(normed, plan.rows), sides(attn, plan.rows)]),
        jnp.pad(jnp.stack([d_query, d_branch]), ((0, 0), (0, 0), (0, spare))),
        jnp.pad(
            jnp.stack([d_pair[:, :kv_width], d_pair[:, kv_width:]]),
            ((0, 0), (0, 0), (LANES - spare, 0)),
        ),
    )
    acts = (first_low, second_low)
    return acts, (grad_in, grad_mid_low), gain_sums, factors


def fused_block(
    size, plan, inputs, segment_ids, cotangent,
    gain_attn, w_query, w_key, w_value, w_out, gain_ffn, w_gate, w_up, w_down,
):
    cos_in, sin_in = rotary(size.length)
    gains = jnp.stack([gain_attn, gain_ffn]).astype(jnp.float32)
    gains = jnp.pad(gains, ((0, 0), (0, plan.width_tiles * LANES - size.width)))
    hidden = inputs[:, 0].swapaxes(1, 2)
    weights = (w_query, w_key.T, w_value.T, w_out, w_gate, w_up, w_down.T)
    acts, *kept = run_front(
        size, plan, hidden, cotangent[:, 0].swapaxes(1, 2), segment_ids, cos_in, sin_in, gains, *weights
    )
    summed, grads = run_tail(size, plan, hidden, cos_in, sin_in, gains, *kept, *weights)
    return acts, grads, summed


def body(
    inputs,
    segment_ids,
    cotangent,
    gain_attn,
    w_query,
    w_key,
    w_value,
    w_out,
    gain_ffn,
    w_gate,
    w_up,
    w_down,
):
    micro_count, row_count, tok_local, model_width = inputs.shape
    kv_width, hidden = w_key.shape[1], w_gate.shape[1]
    assert micro_count == lax.axis_size("section")
    on_first = lax.axis_index("section") == 0
    plan = Plan(lax.axis_size("dp"), lax.axis_size("ctx"), model_width, hidden, kv_width)
    dp = plan.dp
    size = Block(tok_local, segment_ids.shape[2], model_width, hidden, kv_width, plan.ctx)
    fits = (
        row_count == 1
        and size.length <= 1024
        and tok_local % LANES == 0
        and plan.rows * dp == model_width
        and plan.down_tiles * LANES * dp == hidden
        and len(plan.chunks) == 11
    )
    params = (gain_attn, w_query, w_key, w_value, w_out, gain_ffn, w_gate, w_up, w_down)
    if fits:
        acts, grads, summed = fused_block(size, plan, inputs, segment_ids, cotangent, *params)
    else:
        acts, grads, gain_sums, factors = plain_block(
            plan, inputs, segment_ids, cotangent, *params
        )
        summed = reduce_grads(plan, *factors, gain_sums)
    sizes = (model_width, hidden, kv_width)

    def exchange(for_first, for_last):
        kept = jnp.where(on_first, for_first, for_last)
        sent = jnp.where(on_first, for_last, for_first)
        got = lax.ppermute(sent, "section", [(0, 1), (1, 0)])
        return jnp.where(
            on_first, jnp.stack([kept, got]), jnp.stack([got, kept])
        )

    def turned(values):
        return values[None, :, None].swapaxes(3, 4)

    if fits:
        *parts, acts, grads = unpack(plan, sizes, summed, acts, grads)
        activations, input_grads = turned(acts), turned(grads)
    else:
        parts = unpack(plan, sizes, summed)
        activations = exchange(*acts)[None]
        input_grads = exchange(grads[0].astype(jnp.bfloat16), grads[1]).astype(jnp.float32)[None]
    query, key_t, value_t, out, gate, up, down_t, gain_one, gain_two = parts
    return (
        activations,
        input_grads,
        gain_one.reshape(-1),
        query,
        key_t.T,
        value_t.T,
        out,
        gain_two.reshape(-1),
        gate,
        up,
        down_t.T,
    )


def solution(mesh):
    placed = (
        P(None, "dp", "ctx", None),
        P(None, "dp", None),
        P(None, "dp", "ctx", None),
        P(),
        P(),
        P(),
        P(),
        P(),
        P(),
        P(),
        P(),
        P(),
    )
    return jax.shard_map(
        body,
        mesh=mesh,
        in_specs=placed,
        out_specs=(
            P("section", None, "dp", "ctx", None),
            P("section", None, "dp", "ctx", None),
            P("dp"),
            P("dp", None),
            P("dp", None),
            P("dp", None),
            P("dp", None),
            P("dp"),
            P("dp", None),
            P("dp", None),
            P("dp", None),
        ),
        check_vma=False,
    )
```

```python
import functools
import math
import types

import jax
import jax.numpy as jnp
import numpy as np
from jax import lax
from jax.experimental import pallas as pl
from jax.experimental.pallas import tpu as pltpu
from jax.sharding import PartitionSpec as P

HEADS = 15
KV_HEADS = 5
HEAD_DIM = 64
LANES = 128
Z_CHUNKS = 3
Z_LAG = 2
OWN_SLOTS = 8
PARTNER_SLOTS = 3
MESH = pl.DeviceIdType.MESH


epsilon = 1e-05
score_scale = 0.125
score_unit = score_scale / math.log(2.0)
mask_floor = -1e30


def rms_forward(values, gain_vec):
    inverse = lax.rsqrt(jnp.mean(values * values, -1, keepdims=True) + epsilon)
    return (values * inverse * gain_vec, inverse)


def rms_backward(values, gain_vec, inverse, grad_normed):
    weighted = grad_normed * gain_vec
    grad_gain = jnp.sum(grad_normed * values * inverse, axis=(0, 1))
    cubed = inverse * inverse * inverse
    grad_values = inverse * weighted - values * cubed * jnp.mean(
        weighted * values, -1, keepdims=True
    )
    return (grad_values, grad_gain)


def rotate(values, cos_table, sine_table):
    halfway = values.shape[-1] // 2
    former = values[..., :halfway]
    latter = values[..., halfway:]
    cos_part = cos_table[None, :, None, :]
    sine_part = sine_table[None, :, None, :]
    return jnp.concatenate(
        [former * cos_part - latter * sine_part, latter * cos_part + former * sine_part], -1
    )


def block_scores(queries, key_part, query_seg, key_seg, query_pos, offset):
    block_rows = key_part.shape[1]
    scores = (
        jnp.einsum("rckgd,rnkd->rkgcn", queries, key_part, preferred_element_type=jnp.float32)
        * score_scale
    )
    key_pos = offset + jnp.arange(block_rows, dtype=jnp.int32)
    allowed = (query_seg[:, :, None] == key_seg[:, None, :]) & (
        key_pos[None, None, :] <= query_pos[None, :, None]
    )
    return (scores, allowed[:, None, None, :, :])


def up_to(value, step):
    return -(-value // step) * step


TAIL_ORDER = (
    0, 8, -1, 24, -1, 1, 16, 9, 25, 32, -1, 40, 17, 33, -1, 41, -1, -2, 26, -3,
    48, 2, 49, 56, -4, 3, 42, 4, 57, 64, 34, 58, 10, 72, 43, 27, 18, 65, 19, 11,
    59, 50, 20, 12, 35, 73, 66, 21, 51, 28, 44, 80, 81, 74, 5, 60, 67, 29, 75, 82,
    30, 52, 13, 36, 83, 61, 53, 22, 68, 45, 31, 76, 69, 84, 54, 62, 37, 46, 23, 77,
    6, 85, 70, 38, 63, 14, 78, 86, 39, 55, 71, 47, 15, 7, 79, 87,
)


class Plan:
    def __init__(self, dp, ctx, width, hidden, kv_width):
        self.dp, self.ctx = dp, ctx
        self.cx = 1 << (ctx.bit_length() // 2) if ctx & (ctx - 1) == 0 else ctx
        self.cy = ctx // self.cx
        self.low = max(dp // 2, 1)
        self.shard = width // dp
        self.rows = up_to(width // dp, 16)
        self.down_rows = up_to(width // 2, 16)
        self.down_tiles = up_to(hidden // dp, LANES) // LANES
        self.up_tiles = hidden // LANES
        self.width_tiles = up_to(width, LANES) // LANES
        self.pair_tiles = (width + kv_width) // LANES
        self.step = 4
        chunks = []
        for kind, count, rows, step in (
            ("down", self.down_tiles, self.down_rows, 2),
            ("ffn", self.up_tiles, self.rows, self.step),
            ("attn", self.width_tiles - 1, self.rows, 4),
            ("mixed", self.pair_tiles - self.width_tiles + 1, self.rows, 4),
        ):
            for start in range(0, count, step):
                tiles = min(step, count - start)
                extra = 16 if kind == "mixed" else 0
                piece = up_to(up_to(tiles * rows + extra, ctx) // ctx, 16)
                mode = "z" if len(chunks) < Z_CHUNKS else "xy"
                chunks.append((kind, start, tiles, rows, piece, mode))
        self.chunks = chunks
        self.offsets = [sum(c[4] for c in chunks[:i]) for i in range(len(chunks))]
        self.total = sum(c[4] for c in chunks)
        self.widest = max(c[4] for c in chunks)

    def of(self, kind):
        return [i for i, chunk in enumerate(self.chunks) if chunk[0] == kind]

    def spans(self, index, first, count):
        piece = self.chunks[index][4]
        out, done = [], 0
        while done < count:
            at = first + done
            size = min(count - done, piece - at % piece)
            out.append((at // piece, at % piece, done, size))
            done += size
        return out

    def scratch(self):
        dp, cy, cx, low = self.dp, self.cy, self.cx, self.low
        nx, ny, nz, high = max(cx - 1, 1), max(cy - 1, 1), max(dp - 1, 1), max(dp - low, 1)
        count = len(self.chunks)

        def buffer(*shape):
            return pltpu.VMEM((*shape, LANES), jnp.bfloat16)

        found = [
            buffer(2, dp, cy, cx, self.widest),
            buffer(PARTNER_SLOTS, dp, cy, cx, self.widest),
            buffer(OWN_SLOTS, dp, cy, cx, self.widest),
        ]
        for kind, start, tiles, rows, piece, mode in self.chunks:
            head = up_to(piece // 2, 16)
            rest = max(piece - head, 16)
            if mode == "xy":
                found += [
                    buffer(nz, piece), buffer(nx, low, cy, piece), buffer(ny, high, cx, piece),
                    buffer(nx, high, piece), buffer(ny, low, piece), buffer(piece),
                ]
            else:
                found += [
                    buffer(nz, cy, cx, piece), buffer(nx, cy, head), buffer(ny, cx, rest),
                    buffer(nx, rest), buffer(ny, head), buffer(piece),
                ]
        dma = pltpu.SemaphoreType.DMA
        return found + [
            dma((2, count)), dma((2, count, nx)), dma((2, count, ny)), dma((2, count, nx)),
            dma((2, count, ny)), dma((2, count, nz)), dma((2, count, nx)), dma((2, count, ny)),
            dma((2, count, nx)), dma((2, count, ny)), dma((2, count)), dma((count,)),
            pltpu.SemaphoreType.REGULAR,
        ]


class Reduction:
    def __init__(self, plan, products, out, refs, turns=None):
        self.plan, self.products, self.out = plan, products, out
        count = len(plan.chunks)
        self.turns = list(range(count)) if turns is None else turns
        self.sent, self.partner, self.own_ring = refs[:3]
        self.parts = [refs[3 + 6 * i : 9 + 6 * i] for i in range(count)]
        (
            self.sem_p, self.sem_x1, self.sem_y1, self.sem_x2, self.sem_y2, self.sem_z,
            self.sem_gx, self.sem_gy, self.sem_hx, self.sem_hy, self.sem_m, self.sem_o, self.credit,
        ) = refs[3 + 6 * count :]
        self.section, self.row, self.ctx = (
            lax.axis_index(name) for name in ("section", "dp", "ctx")
        )
        self.px, self.py = lax.rem(self.ctx, plan.cx), lax.div(self.ctx, plan.cx)
        self.mate = (1 - self.section, self.row, self.ctx)
        self.done = [0] * count

    def friends(self):
        plan = self.plan
        found = [self.mate]
        found += [(self.section, lax.rem(self.row + k, plan.dp), self.ctx) for k in range(1, plan.dp)]
        return found + [
            (self.section, self.row, lax.rem(self.ctx + k, plan.ctx)) for k in range(1, plan.ctx)
        ]

    def remote(self, source, target, sems, place, device):
        return pltpu.make_async_remote_copy(
            source, target, sems.at[(0, *place)], sems.at[(1, *place)],
            device_id=device, device_id_type=MESH,
        )

    def x_peers(self):
        for k in range(1, self.plan.cx):
            other = lax.rem(self.px + k, self.plan.cx)
            yield k - 1, other, (self.section, self.row, self.py * self.plan.cx + other)

    def y_peers(self):
        for k in range(1, self.plan.cy):
            other = lax.rem(self.py + k, self.plan.cy)
            yield k - 1, other, (self.section, self.row, other * self.plan.cx + self.px)

    def z_peers(self):
        for k in range(1, self.plan.dp):
            other = lax.rem(self.row + k, self.plan.dp)
            yield k - 1, other, (self.section, other, self.ctx)

    def turn(self, index):
        return self.turns.index(index)

    def own(self, index):
        return self.own_ring.at[self.turn(index) % OWN_SLOTS]

    def at(self, index):
        return pl.ds(self.plan.offsets[index], self.plan.chunks[index][4])

    def head(self, index):
        piece = self.plan.chunks[index][4]
        return up_to(piece // 2, 16)

    def partner_copy(self, index):
        rows = pl.ds(0, self.plan.chunks[index][4])
        return self.remote(
            self.sent.at[self.turn(index) % 2, :, :, :, rows],
            self.partner.at[self.turn(index) % PARTNER_SLOTS, :, :, :, rows],
            self.sem_p, (index,), self.mate,
        )

    def make_partner(self, index):
        turn, cx = self.turn(index), self.plan.cx
        if turn >= 2:
            self.partner_copy(self.turns[turn - 2]).wait_send()
        if turn >= PARTNER_SLOTS:
            pl.semaphore_wait(self.credit, 1)

        def finish(j, first, value):
            for p, place, inside, size in self.plan.spans(index, first, value.shape[0]):
                self.sent[turn % 2, j, p // cx, p % cx, place : place + size, :] = value[
                    inside : inside + size
                ].astype(jnp.bfloat16)

        self.products(index, 1 - self.section, finish)
        self.partner_copy(index).start()

    def make_own(self, index):
        turn = self.turn(index)
        assert turn < OWN_SLOTS or self.done[self.turns[turn - OWN_SLOTS]] > 4
        self.partner_copy(index).wait_recv()
        cx, slot, own = self.plan.cx, turn % PARTNER_SLOTS, self.own(index)

        def finish(j, first, value):
            for p, place, inside, size in self.plan.spans(index, first, value.shape[0]):
                rows = slice(place, place + size)
                other = self.partner[slot, j, p // cx, p % cx, rows, :].astype(jnp.float32)
                own[j, p // cx, p % cx, rows, :] = (
                    value[inside : inside + size] + other
                ).astype(jnp.bfloat16)

        self.products(index, self.section, finish)
        if turn + PARTNER_SLOTS < len(self.plan.chunks):
            pl.semaphore_signal(self.credit, 1, device_id=self.mate, device_id_type=MESH)
        self.start(self.z_copies(index) if self.is_z(index) else self.first_copies(index))

    def is_z(self, index):
        return self.plan.chunks[index][5] == "z"

    def start(self, copies):
        for copy in copies:
            copy.start()

    def wait(self, copies):
        for copy in copies:
            copy.wait()

    def z_copies(self, index):
        own, into = self.own(index), self.parts[index][0]
        piece = pl.ds(0, self.plan.chunks[index][4])
        found = []
        for slot, other, device in self.z_peers():
            if self.is_z(index):
                source = own.at[other, :, :, piece]
            else:
                source = own.at[other, self.py, self.px, piece]
            found.append(self.remote(source, into.at[slot], self.sem_z, (index, slot), device))
        return found

    def halves(self, index):
        plan, piece = self.plan, self.plan.chunks[index][4]
        if self.is_z(index):
            head = self.head(index)
            return (pl.ds(self.row, 1), pl.ds(0, head)), (pl.ds(self.row, 1), pl.ds(head, piece - head))
        rows = pl.ds(0, piece)
        return (pl.ds(0, plan.low), rows), (pl.ds(plan.low, plan.dp - plan.low), rows)

    def has_rest(self, index):
        if self.is_z(index):
            return self.plan.chunks[index][4] > self.head(index)
        return self.plan.dp > self.plan.low

    def first_copies(self, index):
        own = self.own(index)
        (j_x, rows_x), (j_y, rows_y) = self.halves(index)
        _, rx1, ry1, _, _, _ = self.parts[index]
        if self.is_z(index):
            j_x = j_y = self.row
        found = [
            self.remote(own.at[j_x, :, other, rows_x], rx1.at[slot], self.sem_x1, (index, slot), device)
            for slot, other, device in self.x_peers()
        ]
        if self.has_rest(index):
            found += [
                self.remote(
                    own.at[j_y, other, :, rows_y], ry1.at[slot], self.sem_y1, (index, slot), device
                )
                for slot, other, device in self.y_peers()
            ]
        return found

    def second_copies(self, index):
        own = self.own(index)
        (j_x, rows_x), (j_y, rows_y) = self.halves(index)
        _, _, _, rx2, ry2, _ = self.parts[index]
        if self.is_z(index):
            j_x = j_y = self.row
        found = [
            self.remote(
                own.at[j_x, other, self.px, rows_x], ry2.at[slot], self.sem_y2, (index, slot), device
            )
            for slot, other, device in self.y_peers()
        ]
        if self.has_rest(index):
            found += [
                self.remote(
                    own.at[j_y, self.py, other, rows_y], rx2.at[slot], self.sem_x2, (index, slot), device
                )
                for slot, other, device in self.x_peers()
            ]
        return found

    def add_all_z(self, index):
        plan, own, into = self.plan, self.own(index), self.parts[index][0]
        piece = slice(0, plan.chunks[index][4])
        self.wait(self.z_copies(index))
        for y in range(plan.cy):
            for x in range(plan.cx):
                total = own[self.row, y, x, piece, :].astype(jnp.float32)
                for k in range(plan.dp - 1):
                    total = total + into[k, y, x].astype(jnp.float32)
                own[self.row, y, x, piece, :] = total.astype(jnp.bfloat16)
        self.start(self.first_copies(index))

    def add_first(self, index):
        plan, own = self.plan, self.own(index)
        _, rx1, ry1, _, _, _ = self.parts[index]
        piece, is_z = plan.chunks[index][4], self.is_z(index)
        head = self.head(index)
        self.wait(self.first_copies(index))
        places = [(self.row, 0, 0)] if is_z else [(j, j, j - plan.low) for j in range(plan.dp)]
        for j, at_x, at_y in places:
            if is_z or at_x < plan.low:
                rows = slice(0, head) if is_z else slice(0, piece)
                for y in range(plan.cy):
                    total = own[j, y, self.px, rows, :].astype(jnp.float32)
                    for k in range(plan.cx - 1):
                        part = rx1[k, y] if is_z else rx1[k, at_x, y]
                        total = total + part.astype(jnp.float32)
                    own[j, y, self.px, rows, :] = total.astype(jnp.bfloat16)
            if (is_z and piece > head) or (not is_z and at_y >= 0):
                rows = slice(head, piece) if is_z else slice(0, piece)
                for x in range(plan.cx):
                    total = own[j, self.py, x, rows, :].astype(jnp.float32)
                    for k in range(plan.cy - 1):
                        part = ry1[k, x] if is_z else ry1[k, at_y, x]
                        total = total + part.astype(jnp.float32)
                    own[j, self.py, x, rows, :] = total.astype(jnp.bfloat16)
        self.start(self.second_copies(index))

    def add_second(self, index):
        plan, own = self.plan, self.own(index)
        _, _, _, rx2, ry2, _ = self.parts[index]
        piece = slice(0, plan.chunks[index][4])
        self.wait(self.second_copies(index))
        for j in range(plan.dp):
            total = own[j, self.py, self.px, piece, :].astype(jnp.float32)
            if j < plan.low:
                for k in range(plan.cy - 1):
                    total = total + ry2[k, j].astype(jnp.float32)
            else:
                for k in range(plan.cx - 1):
                    total = total + rx2[k, j - plan.low].astype(jnp.float32)
            own[j, self.py, self.px, piece, :] = total.astype(jnp.bfloat16)
        self.start(self.z_copies(index))

    def add_last(self, index):
        plan, own = self.plan, self.own(index)
        rz, _, _, rx2, ry2, final = self.parts[index]
        piece, head = plan.chunks[index][4], self.head(index)
        if self.is_z(index):
            self.wait(self.second_copies(index))
            total = own[self.row, self.py, self.px, 0:head, :].astype(jnp.float32)
            for k in range(plan.cy - 1):
                total = total + ry2[k].astype(jnp.float32)
            final[0:head, :] = total.astype(jnp.bfloat16)
            if piece > head:
                total = own[self.row, self.py, self.px, head:piece, :].astype(jnp.float32)
                for k in range(plan.cx - 1):
                    total = total + rx2[k].astype(jnp.float32)
                final[head:piece, :] = total.astype(jnp.bfloat16)
        else:
            self.wait(self.z_copies(index))
            total = own[self.row, self.py, self.px, 0:piece, :].astype(jnp.float32)
            for k in range(plan.dp - 1):
                total = total + rz[k].astype(jnp.float32)
            final[...] = total.astype(jnp.bfloat16)
        self.place_copy(index).start()
        self.start(self.gather_one(index))

    def place_copy(self, index):
        target = self.out.at[self.section, self.py, self.px, self.at(index)]
        return pltpu.make_async_copy(self.parts[index][5], target, self.sem_o.at[index])

    def gather_parts(self, index):
        offset, piece, head = self.plan.offsets[index], self.plan.chunks[index][4], self.head(index)
        return pl.ds(offset, head), pl.ds(offset + head, piece - head), piece > head

    def gather_one(self, index):
        final, out = self.parts[index][5], self.out
        rows_x, rows_y, rest = self.gather_parts(index)
        head, piece = self.head(index), self.plan.chunks[index][4]
        found = [
            self.remote(
                final.at[pl.ds(0, head)], out.at[self.section, self.py, self.px, rows_x],
                self.sem_gx, (index, slot), device,
            )
            for slot, other, device in self.x_peers()
        ]
        if rest:
            found += [
                self.remote(
                    final.at[pl.ds(head, piece - head)], out.at[self.section, self.py, self.px, rows_y],
                    self.sem_gy, (index, slot), device,
                )
                for slot, other, device in self.y_peers()
            ]
        return found

    def gather_two(self, index):
        out = self.out
        rows_x, rows_y, rest = self.gather_parts(index)
        found = []
        for slot, other, device in self.y_peers():
            region = out.at[self.section, self.py, :, rows_x]
            found.append(self.remote(region, region, self.sem_hy, (index, slot), device))
        if rest:
            for slot, other, device in self.x_peers():
                region = out.at[self.section, :, self.px, rows_y]
                found.append(self.remote(region, region, self.sem_hx, (index, slot), device))
        return found

    def gather_on(self, index):
        self.place_copy(index).wait()
        self.wait(self.gather_one(index))
        self.start(self.gather_two(index))

    def mate_copy(self, index):
        region = self.out.at[self.section, :, :, self.at(index)]
        return self.remote(region, region, self.sem_m, (index,), self.mate)

    def pass_on(self, index):
        self.wait(self.gather_two(index))
        self.mate_copy(index).start()

    def finish(self, index):
        self.mate_copy(index).wait()

    def stages(self, index):
        middle = (self.add_all_z, self.add_first) if self.is_z(index) else (self.add_first, self.add_second)
        return (
            self.make_partner, self.make_own, *middle, self.add_last, self.gather_on, self.pass_on, self.finish
        )

    def advance(self, index, upto=None):
        stages = self.stages(index)
        while self.done[index] < len(stages):
            if upto is not None and self.done[index] >= upto:
                return
            stages[self.done[index]](index)
            self.done[index] += 1
            if upto is None:
                return

    def drain(self):
        todo = []
        for index in range(len(self.done)):
            for stage in range(self.done[index], len(self.stages(index))):
                late = Z_LAG if self.is_z(index) and stage >= 2 else 0
                todo.append((index + stage + late, stage, index))
        for step, stage, index in sorted(todo):
            self.advance(index)
        for index in self.turns[-2:]:
            self.partner_copy(index).wait_send()


def greet(friends):
    barrier = pltpu.get_barrier_semaphore()
    for friend in friends:
        pl.semaphore_signal(barrier, 1, device_id=friend, device_id_type=MESH)
    pl.semaphore_wait(barrier, len(friends))


def shard_products(plan, index, half, finish, sources):
    kind, start, tiles, rows, piece, mode = plan.chunks[index]
    cols = slice(start * LANES, (start + tiles) * LANES)

    def shard(j, carry):
        own = pl.ds(pl.multiple_of(j * plan.rows, 16), plan.rows)
        if kind == "ffn":
            value = dot(sources.ffn_x[own, :], sources.ffn_dy(half, index, 0, cols))
        elif kind == "down":
            first = pl.multiple_of(j * (plan.down_tiles * LANES) + start * LANES, LANES)
            rows_of = pl.ds(pl.multiple_of(half * plan.down_rows, 16), plan.down_rows)
            value = dot(sources.down_x[rows_of, :], sources.down_dy[:, pl.ds(first, tiles * LANES)])
        elif kind == "attn":
            value = dot(sources.attn_x[half, own, :], sources.attn_dy[half, :, cols])
        else:
            value = dot(sources.attn_x[0, own, :], sources.pair_dy[half])
            last = plan.width_tiles - 1
            mixed = dot(sources.attn_x[half, own, :], sources.attn_dy[half, :, last * LANES :])
            value = jnp.concatenate([value[:, :LANES] + mixed, value[:, LANES:]], 1)
        for tile in range(tiles):
            finish(j, tile * rows, value[:, tile * LANES : (tile + 1) * LANES])
        if kind == "mixed":
            finish(j, tiles * rows, sources.extra[half, j])
        return carry

    lax.fori_loop(0, plan.dp, shard, 0)


def spread_gains(plan, gain_sums, extra):
    for half in range(2):
        for j in range(plan.dp):
            for number in range(-(-plan.shard // LANES)):
                start = j * plan.shard + number * LANES
                extra[half, j, number : number + 1, :] = gain_sums[
                    half : half + 1, start : start + LANES
                ]


def reduce_kernel(
    plan, ffn_x, ffn_dy, down_x, down_dy, attn_x, attn_dy, pair_dy, gain_sums, out, extra, *refs
):
    sources = types.SimpleNamespace(
        ffn_x=ffn_x, ffn_dy=lambda half, index, inside, cols: ffn_dy[half, :, cols],
        down_x=down_x, down_dy=down_dy,
        attn_x=attn_x, attn_dy=attn_dy, pair_dy=pair_dy, extra=extra,
    )
    reduction = Reduction(
        plan, lambda *place: shard_products(plan, *place, sources), out, refs
    )
    greet(reduction.friends())
    spread_gains(plan, gain_sums, extra)
    reduction.drain()


def reduce_grads(plan, *operands):
    return pl.pallas_call(
        functools.partial(reduce_kernel, plan),
        out_shape=jax.ShapeDtypeStruct((2, plan.cy, plan.cx, plan.total, LANES), jnp.bfloat16),
        in_specs=[pl.BlockSpec(memory_space=pltpu.VMEM)] * len(operands),
        out_specs=pl.BlockSpec(memory_space=pl.ANY),
        scratch_shapes=[pltpu.VMEM((2, plan.dp, 16, LANES), jnp.float32), *plan.scratch()],
        compiler_params=pltpu.CompilerParams(
            collective_id=0, has_side_effects=True, vmem_limit_bytes=64 << 20
        ),
        cost_estimate=pl.CostEstimate(flops=10**10, bytes_accessed=20 * 10**6, transcendentals=0),
    )(*operands)


class Block:
    def __init__(self, tokens, length, width, hidden, kv_width, ctx):
        self.tokens, self.length, self.width, self.hidden = tokens, length, width, hidden
        self.kv_width, self.ctx = kv_width, ctx
        self.kv_heads = kv_width // HEAD_DIM
        self.group = width // kv_width
        self.step = 512


def dot(one, other, over=(1, 0)):
    return lax.dot_general(
        one, other, (((over[0],), (over[1],)), ((), ())), preferred_element_type=jnp.float32
    )


def fold_rows(values, combine):
    return combine(values.reshape(values.shape[0] // 8, 8, values.shape[1]), 0)


def norm(values):
    return lax.rsqrt(jnp.mean(values * values, 0, keepdims=True) + epsilon)


def app_tokens(size, app):
    return slice(app * size.tokens, (app + 1) * size.tokens)


def head_rows(size, g, h):
    return pl.ds(pl.multiple_of((g * size.group + h) * HEAD_DIM, HEAD_DIM), HEAD_DIM)


def wide_gain(env, which):
    return jnp.concatenate([env.columns[which]] * (env.size.tokens // LANES), 1)


def spread_columns(size, gains, columns):
    for which in range(2):
        for start in range(0, size.width, LANES):
            rows = min(LANES, size.width - start)
            tile = jnp.broadcast_to(gains[which : which + 1, start : start + LANES], (LANES, LANES))
            columns[which, start : start + rows, :] = tile.T[:rows]


def norm_back(env, values, which, grad_normed):
    size = env.size
    inverse = norm(values)
    product = grad_normed * values * inverse
    folded = product[:, :LANES]
    for start in range(LANES, size.tokens, LANES):
        folded = folded + product[:, start : start + LANES]
    for start in range(0, size.width, LANES):
        stop = min(start + LANES, size.width)
        part = folded[start:stop]
        if stop - start < LANES:
            part = jnp.concatenate([part, jnp.zeros((LANES - stop + start, LANES), jnp.float32)], 0)
        env.gain_sums[which : which + 1, start : start + LANES] += jnp.sum(part.T, 0, keepdims=True)
    weighted = grad_normed * wide_gain(env, which)
    cubed = inverse * inverse * inverse
    return inverse * weighted - values * (cubed * jnp.mean(weighted * values, 0, keepdims=True))


def rope(env, values, sign):
    half = HEAD_DIM // 2
    cos, sine = env.cos_q[...], env.sin_q[...] * sign
    out = []
    for start in range(0, values.shape[0], HEAD_DIM):
        former = values[start : start + half]
        latter = values[start + half : start + HEAD_DIM]
        out += [former * cos - latter * sine, latter * cos + former * sine]
    return jnp.concatenate(out, 0)


def ffn_back(env, gate_ref, up_ref, rows, cols, wd, wg, wu):
    gate = gate_ref[rows, cols].astype(jnp.float32)
    upward = up_ref[rows, cols].astype(jnp.float32)
    sigmoid = 1.0 / (1.0 + jnp.exp(-gate))
    scaled = dot(env.natural[...], wd) * sigmoid
    grad_gate = (scaled * upward * (1.0 + gate * (1.0 - sigmoid))).astype(jnp.bfloat16)
    grad_up = (scaled * gate).astype(jnp.bfloat16)
    gate_ref[rows, cols] = grad_gate
    up_ref[rows, cols] = grad_up
    env.accum[...] += dot(wg, grad_gate, (1, 1)) + dot(wu, grad_up, (1, 1))


def middle_back(env, grad_low, mid):
    grad_middle = grad_low.astype(jnp.float32) + norm_back(env, mid, 1, env.accum[...])
    env.dmid[...] = grad_middle
    branch = grad_middle.astype(jnp.bfloat16)
    env.d_attn[1, : env.size.tokens, : env.size.width] = branch.T
    env.do_t[...] = dot(env.wo[...], branch).astype(jnp.bfloat16)


def grad_copy(env, g, k):
    owner = jnp.maximum(env.ctx - k, 0)
    rows = pl.ds(pl.multiple_of(owner * env.size.tokens, env.size.tokens), env.size.tokens)
    return pltpu.make_async_remote_copy(
        env.kv_send.at[g, rows], env.kv_recv.at[k - 1, g],
        env.sem_d.at[0, g, k - 1], env.sem_d.at[1, g, k - 1],
        device_id=(env.section, env.row, owner), device_id_type=MESH,
    )


def attend_back(env, at, g):
    size, low_type = env.size, jnp.bfloat16
    k_t = env.kv[g].T[:HEAD_DIM]
    sides = []
    for h in range(size.group):
        rows, cols = head_rows(size, g, h), slice(h * size.tokens, (h + 1) * size.tokens)
        query, grad_head = env.q_t[rows, :], env.do_t[rows, :]
        empty = jnp.zeros_like(query)
        query = jnp.concatenate([query, empty], 0)
        grad_pad = jnp.concatenate([empty, grad_head], 0)
        delta = jnp.sum(
            grad_head.astype(jnp.float32) * env.x_attn[1, rows, at].astype(jnp.float32),
            0, keepdims=True,
        )
        log_sum = env.lse[g, h : h + 1, :]
        for start in range(0, size.length, 256):
            keys_at = slice(start, start + 256)
            part = dot(env.kv[g, keys_at, :], query) * score_unit + env.bias[keys_at, :]
            chance = jnp.exp2(part - log_sum)
            env.chances[keys_at, cols] = chance.astype(low_type)
            change = dot(env.kv[g, keys_at, :], grad_pad) - delta
            env.grad_scores[keys_at, cols] = (chance * change).astype(low_type)
        sides.append(((query.astype(jnp.float32) * score_scale).astype(low_type), grad_pad))
        env.accum[rows, :] = dot(k_t, env.grad_scores[:, cols]) * score_scale
    small, grad_pad = (jnp.concatenate(side, 1) for side in zip(*sides))
    env.kv_send[g] = (
        dot(env.grad_scores[...], small, (1, 1)) + dot(env.chances[...], grad_pad, (1, 1))
    ).astype(low_type)
    for k in range(1, size.ctx):
        @pl.when(env.ctx - k >= 0)
        def _():
            grad_copy(env, g, k).start()


def project_back(env):
    size, low_type = env.size, jnp.bfloat16
    tokens, width = size.tokens, size.width
    for start in range(0, width, 2 * LANES):
        stop = min(start + 2 * LANES, width)
        tile = rope(env, env.accum[start:stop, :], -1.0).astype(low_type)
        env.natural[:, start:stop] = tile.T
        env.do_t[start:stop, :] = tile
    env.d_attn[0, :tokens, :width] = env.natural[...]
    own_rows = pl.ds(pl.multiple_of(env.ctx * tokens, tokens), tokens)
    pairs = [[], []]
    for g in range(size.kv_heads):
        tile = env.kv_send[g, own_rows, :].astype(jnp.float32)
        for k in range(1, size.ctx):
            @pl.when(env.ctx + k < size.ctx)
            def _():
                grad_copy(env, g, k).wait_recv()
            tile = tile + jnp.where(
                env.ctx + k < size.ctx, env.kv_recv[k - 1, g].astype(jnp.float32), 0.0
            )
        tile = tile.T
        pairs[0].append(rope(env, tile[:HEAD_DIM], -1.0).astype(low_type))
        pairs[1].append(tile[HEAD_DIM:].astype(low_type))
    spare = env.d_pair.shape[2] - size.kv_width
    for half in range(2):
        pairs[half] = jnp.concatenate(pairs[half], 0)
        env.d_pair[half, :tokens, :] = jnp.concatenate(
            [jnp.zeros((spare, tokens), low_type), pairs[half]], 0
        ).T
    grad_normed = (
        dot(env.wq[...], env.do_t[...])
        + dot(env.wk[...], pairs[0], (0, 0))
        + dot(env.wv[...], pairs[1], (0, 0))
    )
    return env.dmid[...] + norm_back(env, env.x[...].astype(jnp.float32), 0, grad_normed)


def drain_grad_copies(env):
    def one(g, carry):
        for k in range(1, env.size.ctx):
            @pl.when(env.ctx - k >= 0)
            def _():
                grad_copy(env, g, k).wait_send()
        return carry

    lax.fori_loop(0, env.size.kv_heads, one, 0)


def front_kernel(
    size, inputs, cotangent, segments, cos_in, sin_in, gains,
    wq_in, wk_in, wv_in, wo_in, wg_in, wu_in, wd_in,
    acts, n2_out, df_out, inner_out, attn_out, d_attn_out, d_pair_out, d_ffn_out,
    mid_out, q_out, kv_out, lse_out, bias_out, gain_out,
    wq, wk, wv, wo, wg, wu, wd, n2_t, df_t, inner, x_attn, d_attn, d_pair, d_ffn, gain_sums,
    cos_q, sin_q, columns, xin, cot, mid, q_t,
    kv, kv_send, kv_recv, lse, do_t, bias, accum, dmid, natural, scores, chances, grad_scores,
    sem_w, sem_k, sem_d, sem_e, sem_o,
):
    tokens, ctx_count, groups, group = size.tokens, size.ctx, size.kv_heads, size.group
    width, low_type, full = size.width, jnp.bfloat16, jnp.float32
    section, row, ctx = (lax.axis_index(name) for name in ("section", "dp", "ctx"))
    mate = (1 - section, row, ctx)
    own_rows = pl.ds(pl.multiple_of(ctx * tokens, tokens), tokens)
    env = types.SimpleNamespace(
        size=size, section=section, row=row, ctx=ctx, columns=columns, gain_sums=gain_sums,
        cos_q=cos_q, sin_q=sin_q, natural=natural, accum=accum, dmid=dmid, do_t=do_t,
        d_attn=d_attn, d_pair=d_pair, x_attn=x_attn, bias=bias, chances=chances,
        grad_scores=grad_scores, kv=kv.at[1], q_t=q_t.at[1], lse=lse.at[1], x=xin.at[1],
        kv_send=kv_send, kv_recv=kv_recv, sem_d=sem_d, wq=wq, wk=wk, wv=wv, wo=wo,
    )
    loads = [
        pltpu.make_async_copy(source, target, sem_w.at[number])
        for number, (source, target) in enumerate((
            (inputs.at[section], xin.at[0]), (cos_in.at[:, own_rows], cos_q),
            (sin_in.at[:, own_rows], sin_q), (wk_in, wk), (wv_in, wv), (wq_in, wq), (wo_in, wo),
            (wg_in, wg), (wu_in, wu), (wd_in, wd), (cotangent.at[section], cot),
        ))
    ]
    for load in loads:
        load.start()
    stores = []

    def store(source, target):
        copy = pltpu.make_async_copy(source, target, sem_o.at[len(stores)])
        copy.start()
        stores.append(copy)

    barrier = pltpu.get_barrier_semaphore()
    friends = [mate] + [(section, row, lax.rem(ctx + k, ctx_count)) for k in range(1, ctx_count)]
    for friend in friends:
        pl.semaphore_signal(barrier, 1, device_id=friend, device_id_type=MESH)
    spread_columns(size, gains, columns)
    query_seg = segments[section, :, own_rows].astype(full)
    query_pos = lax.broadcasted_iota(jnp.int32, (1, tokens), 1) + ctx * tokens
    for start in range(0, size.length, LANES):
        key_seg = jnp.broadcast_to(
            segments[section, :, start : start + LANES].astype(full), (LANES, LANES)
        ).T
        key_pos = lax.broadcasted_iota(jnp.int32, (LANES, tokens), 0) + start
        key_seg = jnp.concatenate([key_seg] * (tokens // LANES), 1)
        allowed = (key_seg == query_seg) & (key_pos <= query_pos)
        bias[start : start + LANES, :] = jnp.where(allowed, 0.0, mask_floor)
    store(bias, bias_out)
    for k in range(1, ctx_count):
        @pl.when(ctx + k < ctx_count)
        def _():
            rows = pl.ds(pl.multiple_of((ctx + k) * tokens, tokens), tokens)
            for app in range(2):
                kv[app, :, rows, :] = jnp.zeros((groups, tokens, LANES), low_type)
    pl.semaphore_wait(barrier, len(friends))

    def kv_copy(app, g, k):
        return pltpu.make_async_remote_copy(
            kv.at[app, g, own_rows], kv.at[app, g, own_rows],
            sem_k.at[0, app, g, k - 1], sem_k.at[1, app, g, k - 1],
            device_id=(section, row, jnp.minimum(ctx + k, ctx_count - 1)), device_id_type=MESH,
        )

    def act_copy(app):
        return pltpu.make_async_remote_copy(
            xin.at[app + 1], acts.at[section], sem_e.at[0], sem_e.at[1],
            device_id=mate, device_id_type=MESH,
        )

    def act_store(app):
        return pltpu.make_async_copy(xin.at[app + 1], acts.at[section], sem_e.at[2])

    early = [
        pltpu.make_async_copy(source, target, sem_o.at[number])
        for number, (source, target) in enumerate((
            (q_t.at[0], q_out), (kv.at[0], kv_out), (lse.at[0], lse_out), (mid.at[0], mid_out)
        ))
    ]
    stores += early

    def forward(app, carry):
        at = pl.ds(pl.multiple_of(app * tokens, tokens), tokens)
        x = xin[app].astype(full)
        normed = (x * norm(x) * wide_gain(env, 0)).astype(low_type)
        x_attn[0, :, at] = normed

        @pl.when(app == 0)
        def _():
            for load in loads[1:6]:
                load.wait()

        keys = rope(env, dot(wk[...], normed), 1.0).astype(low_type)
        values = dot(wv[...], normed).astype(low_type)
        for g in range(groups):
            piece = slice(g * HEAD_DIM, (g + 1) * HEAD_DIM)
            kv[app, g, own_rows, :] = jnp.concatenate([keys[piece], values[piece]], 0).T
            for k in range(1, ctx_count):
                @pl.when(ctx + k < ctx_count)
                def _():
                    kv_copy(app, g, k).start()
        for start in range(0, width, 2 * LANES):
            stop = min(start + 2 * LANES, width)
            tile = dot(wq[:, start:stop], normed, (0, 0))
            q_t[app, start:stop, :] = rope(env, tile, 1.0).astype(low_type)

        def heads(g, carry):
            for k in range(1, ctx_count):
                @pl.when(ctx - k >= 0)
                def _():
                    kv_copy(app, g, k).wait_recv()
            v_t = kv[app, g].T[HEAD_DIM:]
            for h in range(group):
                query = q_t[app, head_rows(size, g, h), :]
                query = jnp.concatenate([query, jnp.zeros_like(query)], 0)
                largest = None
                for start in range(0, size.length, 256):
                    keys_at = slice(start, start + 256)
                    part = dot(kv[app, g, keys_at, :], query) * score_unit + bias[keys_at, :]
                    scores[h, keys_at, :] = part
                    most = fold_rows(part, jnp.max)
                    largest = most if largest is None else jnp.maximum(largest, most)
                largest = jnp.max(largest, 0, keepdims=True)
                total = jnp.zeros((8, tokens), full)
                for start in range(0, size.length, 64):
                    keys_at = slice(start, start + 64)
                    weights = jnp.exp2(scores[h, keys_at, :] - largest)
                    total = total + fold_rows(weights, jnp.sum)
                    chances[keys_at, h * tokens : (h + 1) * tokens] = weights.astype(low_type)
                total = jnp.sum(total, 0, keepdims=True)
                out = dot(v_t, chances[:, h * tokens : (h + 1) * tokens]) / total
                lse[app, g, h : h + 1, :] = largest + jnp.log(total) * (1.0 / math.log(2.0))
                x_attn[1, head_rows(size, g, h), at] = out.astype(low_type)
            return carry

        lax.fori_loop(0, groups, heads, 0)

        @pl.when(app == 0)
        def _():
            for copy in early[:3]:
                copy.start()
            loads[6].wait()

        middle = xin[app].astype(full) + dot(wo[...], x_attn[1, :, at], (0, 0))
        mid[app] = middle
        ffn = (middle * norm(middle) * wide_gain(env, 1)).astype(low_type)
        n2_t[:, at] = ffn
        natural[...] = ffn.T

        @pl.when(app == 0)
        def _():
            early[3].start()
            for load in loads[7:10]:
                load.wait()

        accum[...] = middle

        def chunk(i, carry):
            cols = pl.ds(pl.multiple_of(i * size.step, size.step), size.step)
            gate = dot(natural[...], wg[:, cols])
            upward = dot(natural[...], wu[:, cols])
            hidden = (gate / (1.0 + jnp.exp(-gate)) * upward).astype(low_type)
            d_ffn[0, at, cols] = gate.astype(low_type)
            d_ffn[1, at, cols] = upward.astype(low_type)
            inner[at, cols] = hidden
            accum[...] += dot(wd[:, cols], hidden, (1, 1))
            return carry

        lax.fori_loop(0, size.hidden // size.step, chunk, 0)
        xin[app + 1] = accum[...].astype(low_type)

        @pl.when(section == app)
        def _():
            act_store(app).start()

        @pl.when(section != app)
        def _():
            act_copy(app).start()

        return carry

    gain_sums[...] = jnp.zeros_like(gain_sums)
    d_attn[:, :, width:] = jnp.zeros((2, tokens, d_attn.shape[2] - width), low_type)
    loads[0].wait()
    lax.fori_loop(0, 2, forward, 0)
    for source, target in ((x_attn, attn_out), (n2_t, n2_out), (inner, inner_out)):
        store(source, target)
    loads[10].wait()
    grad_low = cot[...]
    at = app_tokens(size, 1)
    df_t[:, at] = grad_low
    natural[...] = grad_low.T
    accum[...] = jnp.zeros_like(accum)

    def chunk(i, carry):
        cols = pl.ds(pl.multiple_of(i * size.step, size.step), size.step)
        ffn_back(env, d_ffn.at[0], d_ffn.at[1], at, cols, wd[:, cols], wg[:, cols], wu[:, cols])
        return carry

    lax.fori_loop(0, size.hidden // size.step, chunk, 0)
    store(d_ffn, d_ffn_out)
    middle_back(env, grad_low, mid[1])
    lax.fori_loop(0, groups, lambda g, carry: attend_back(env, at, g), None)
    df_t[:, app_tokens(size, 0)] = project_back(env).astype(low_type)
    for source, target in (
        (df_t, df_out), (d_attn, d_attn_out), (d_pair, d_pair_out), (gain_sums, gain_out)
    ):
        store(source, target)

    def drain(g, carry):
        for app in range(2):
            for k in range(1, ctx_count):
                @pl.when(ctx + k < ctx_count)
                def _():
                    kv_copy(app, g, k).wait_send()
        return carry

    lax.fori_loop(0, groups, drain, 0)
    drain_grad_copies(env)
    act_copy(0).wait()
    act_store(0).wait()
    for copy in stores:
        copy.wait()


def front_shapes(size, plan):
    tokens, width, hidden, groups = size.tokens, size.width, size.hidden, size.kv_heads
    low, full, both = jnp.bfloat16, jnp.float32, 2 * size.tokens
    return [
        ((width, both), low),
        ((width, both), low),
        ((both, hidden), low),
        ((2, width, both), low),
        ((2, tokens, plan.width_tiles * LANES), low),
        ((2, tokens, (plan.pair_tiles - plan.width_tiles + 1) * LANES), low),
        ((2, both, hidden), low),
        ((width, tokens), full),
        ((width, tokens), low),
        ((groups, size.length, LANES), low),
        ((groups, 8, tokens), full),
        ((size.length, tokens), full),
        ((8, plan.width_tiles * LANES), full),
    ]


def run_front(size, plan, *operands):
    tokens, width, hidden, groups = size.tokens, size.width, size.hidden, size.kv_heads
    low, full = jnp.bfloat16, jnp.float32
    vmem = pl.BlockSpec(memory_space=pltpu.VMEM)
    far = pl.BlockSpec(memory_space=pl.ANY)
    dma = pltpu.SemaphoreType.DMA
    others = max(size.ctx - 1, 1)
    kept = front_shapes(size, plan)
    shapes = [((2, width, tokens), low)] + kept
    scratch = [
        ((width, width), low),
        ((size.kv_width, width), low),
        ((size.kv_width, width), low),
        ((width, width), low),
        ((width, hidden), low),
        ((width, hidden), low),
        ((width, hidden), low),
        *kept[:7],
        kept[12],
        ((HEAD_DIM // 2, tokens), full),
        ((HEAD_DIM // 2, tokens), full),
        ((2, width, LANES), full),
        ((3, width, tokens), low),
        ((width, tokens), low),
        ((2, width, tokens), full),
        ((2, width, tokens), low),
        ((2, groups, size.length, LANES), low),
        ((groups, size.length, LANES), low),
        ((others, groups, tokens, LANES), low),
        ((2, groups, 8, tokens), full),
        ((width, tokens), low),
        ((size.length, tokens), full),
        ((width, tokens), full),
        ((width, tokens), full),
        ((tokens, width), low),
        ((size.group, size.length, tokens), full),
        ((size.length, size.group * tokens), low),
        ((size.length, size.group * tokens), low),
    ]
    return pl.pallas_call(
        functools.partial(front_kernel, size),
        out_shape=[jax.ShapeDtypeStruct(*shape) for shape in shapes],
        in_specs=[far, far, vmem, far, far, vmem] + [far] * 7,
        out_specs=[far] * len(shapes),
        scratch_shapes=[pltpu.VMEM(*shape) for shape in scratch] + [
            dma((11,)), dma((2, 2, groups, others)), dma((2, groups, others)), dma((3,)),
            dma((len(kept),)),
        ],
        compiler_params=pltpu.CompilerParams(
            collective_id=1, has_side_effects=True, vmem_limit_bytes=64 << 20
        ),
        cost_estimate=pl.CostEstimate(
            flops=3 * 10**10, bytes_accessed=40 * 10**6, transcendentals=3 * 10**7
        ),
    )(*operands)


def tail_kernel(
    size, plan, inputs, cos_in, sin_in, gains, n2_in, df_in, inner_in, attn_in, d_attn_in, d_pair_in,
    d_ffn_in, mid_in, q_in, kv_in, lse_in, bias_in, gain_in,
    wq_in, wk_in, wv_in, wo_in, wg_in, wu_in, wd_in,
    out, grads,
    n2_t, df_t, inner, x_attn, d_attn, d_pair, d_ffn, mid, q_t, kv, lse, bias, gain_sums,
    wq, wk, wv, wo, blocks, cos_q, sin_q, columns, xin, kv_send, kv_recv, do_t, accum, natural,
    chances, grad_scores, stage, extra, sem_l, sem_b, sem_d, sem_e, *refs,
):
    tokens, width, low_type, full = size.tokens, size.width, jnp.bfloat16, jnp.float32
    section, row, ctx = (lax.axis_index(name) for name in ("section", "dp", "ctx"))
    mate = (1 - section, row, ctx)
    own_rows = pl.ds(pl.multiple_of(ctx * tokens, tokens), tokens)
    first_ffn, ffn_count = plan.of("ffn")[0], len(plan.of("ffn"))
    env = types.SimpleNamespace(
        size=size, section=section, row=row, ctx=ctx, columns=columns, gain_sums=gain_sums,
        cos_q=cos_q, sin_q=sin_q, natural=natural, accum=accum, dmid=mid, do_t=do_t,
        d_attn=d_attn, d_pair=d_pair, x_attn=x_attn, bias=bias, chances=chances,
        grad_scores=grad_scores, kv=kv, q_t=q_t, lse=lse, x=xin,
        kv_send=kv_send, kv_recv=kv_recv, sem_d=sem_d, wq=wq, wk=wk, wv=wv, wo=wo,
    )
    sources = types.SimpleNamespace(
        ffn_x=n2_t, ffn_dy=lambda half, index, inside, cols: d_ffn[
            (index - first_ffn) % 3, half, :, inside : inside + cols.stop - cols.start
        ],
        down_x=df_t, down_dy=inner, attn_x=x_attn, attn_dy=d_attn, pair_dy=d_pair, extra=extra,
    )
    count = len(plan.chunks)
    turns = [step // 8 for step in TAIL_ORDER if step >= 0 and step % 8 == 0]
    reduction = Reduction(
        plan, lambda *place: shard_products(plan, *place, sources), out, refs, turns
    )

    def block_loads(i):
        cols = pl.ds(i * size.step, size.step)
        pairs = [(wd_in, 0), (wg_in, 1), (wu_in, 2)]
        return [
            pltpu.make_async_copy(weight.at[:, cols], blocks.at[i % 2, n], sem_b.at[i % 2, n])
            for weight, n in pairs
        ] + [pltpu.make_async_copy(d_ffn_in.at[:, :, cols], d_ffn.at[i % 3], sem_b.at[i % 2, 3])]

    later = pl.ds(tokens, tokens)
    names = (
        "df", "inner", "mid", "n2", "wo", "cos", "sin", "q", "kv", "lse", "bias", "attn", "d_attn",
        "d_pair", "x", "wq", "wk", "wv", "gain",
    )
    loads = dict(zip(names, (
        pltpu.make_async_copy(source, target, sem_l.at[number])
        for number, (source, target) in enumerate((
            (df_in, df_t), (inner_in, inner), (mid_in, mid), (n2_in, n2_t), (wo_in, wo),
            (cos_in.at[:, own_rows], cos_q), (sin_in.at[:, own_rows], sin_q),
            (q_in, q_t), (kv_in, kv), (lse_in, lse), (bias_in, bias), (attn_in, x_attn),
            (d_attn_in, d_attn.at[:, later]), (d_pair_in, d_pair.at[:, later]),
            (inputs.at[section], xin), (wq_in, wq), (wk_in, wk), (wv_in, wv), (gain_in, gain_sums),
        ))
    )))

    def ready(*names):
        for name in names:
            if name in loads:
                loads.pop(name).wait()

    for name in ("df", "inner"):
        loads[name].start()
    for load in block_loads(0):
        load.start()
    for name in names[2:]:
        loads[name].start()
    greet(reduction.friends())
    spread_columns(size, gains, columns)
    d_attn[:, :tokens, width:] = jnp.zeros((2, tokens, d_attn.shape[2] - width), low_type)

    back_copy = pltpu.make_async_remote_copy(
        stage, grads.at[section], sem_e.at[0], sem_e.at[1], device_id=mate, device_id_type=MESH
    )
    back_store = pltpu.make_async_copy(stage, grads.at[section], sem_e.at[2])

    def keep(app, value):
        stage[...] = value

        @pl.when(section == app)
        def _():
            back_store.start()

        @pl.when(section != app)
        def _():
            back_copy.start()

    def kept(app):
        @pl.when(section == app)
        def _():
            back_store.wait()

        @pl.when(section != app)
        def _():
            back_copy.wait_send()

    ready("df", "inner")
    grad_low = df_t[:, :tokens]
    keep(1, grad_low.astype(full))
    natural[...] = grad_low.T
    accum[...] = jnp.zeros_like(accum)

    def ffn_step(i):
        for load in block_loads(i):
            load.wait()
        if i + 1 < ffn_count:
            assert i < 2 or reduction.done[first_ffn + i - 2] >= 2
            for load in block_loads(i + 1):
                load.start()
        ffn_back(
            env, d_ffn.at[i % 3, 0], d_ffn.at[i % 3, 1], slice(0, tokens), slice(0, size.step),
            blocks[i % 2, 0], blocks[i % 2, 1], blocks[i % 2, 2],
        )

    taken = {-1: 0, -2: 0, -3: 0, -4: 0}
    for step in TAIL_ORDER:
        if step >= 0:
            if plan.chunks[step // 8][0] == "ffn" and step % 8 < 2:
                ready("n2")
                assert taken[-1] > step // 8 - first_ffn
            assert reduction.done[step // 8] == step % 8
            reduction.advance(step // 8)
            continue
        number, taken[step] = taken[step], taken[step] + 1
        if step == -1:
            ffn_step(number)
        elif step == -2:
            assert taken[-1] == ffn_count
            ready("mid", "wo", "gain")
            middle_back(env, grad_low, mid[...])
        elif step == -3:
            ready("q", "kv", "lse", "bias", "attn")
            lax.fori_loop(
                0, size.kv_heads, lambda g, carry: attend_back(env, app_tokens(size, 0), g), None
            )
        else:
            assert taken[-3] == 1
            ready("cos", "sin", "d_attn", "d_pair", "x", "wq", "wk", "wv")
            grad_in = project_back(env)
            kept(1)
            keep(0, grad_in)
            spread_gains(plan, gain_sums, extra)
    reduction.drain()
    drain_grad_copies(env)
    kept(0)
    back_copy.wait_recv()


def run_tail(size, plan, *operands):
    tokens, width, groups = size.tokens, size.width, size.kv_heads
    low, full, both = jnp.bfloat16, jnp.float32, 2 * size.tokens
    vmem = pl.BlockSpec(memory_space=pltpu.VMEM)
    far = pl.BlockSpec(memory_space=pl.ANY)
    dma = pltpu.SemaphoreType.DMA
    others = max(size.ctx - 1, 1)
    kept = front_shapes(size, plan)
    scratch = kept[:4] + [
        ((2, both, kept[4][0][2]), low),
        ((2, both, kept[5][0][2]), low),
        ((3, 2, both, size.step), low),
        *kept[7:],
        ((width, width), low),
        ((size.kv_width, width), low),
        ((size.kv_width, width), low),
        ((width, width), low),
        ((2, 3, width, size.step), low),
        ((HEAD_DIM // 2, tokens), full),
        ((HEAD_DIM // 2, tokens), full),
        ((2, width, LANES), full),
        ((width, tokens), low),
        ((groups, size.length, LANES), low),
        ((others, groups, tokens, LANES), low),
        ((width, tokens), low),
        ((width, tokens), full),
        ((tokens, width), low),
        ((size.length, size.group * tokens), low),
        ((size.length, size.group * tokens), low),
        ((width, tokens), full),
        ((2, plan.dp, 16, LANES), full),
    ]
    return pl.pallas_call(
        functools.partial(tail_kernel, size, plan),
        out_shape=[
            jax.ShapeDtypeStruct((2, plan.cy, plan.cx, plan.total, LANES), low),
            jax.ShapeDtypeStruct((2, width, tokens), full),
        ],
        in_specs=[far, far, far, vmem] + [far] * (len(operands) - 4),
        out_specs=[far, far],
        scratch_shapes=[pltpu.VMEM(*shape) for shape in scratch] + [
            dma((19,)), dma((2, 4)), dma((2, groups, others)), dma((3,)), *plan.scratch(),
        ],
        compiler_params=pltpu.CompilerParams(
            collective_id=2, has_side_effects=True, vmem_limit_bytes=64 << 20
        ),
        cost_estimate=pl.CostEstimate(
            flops=3 * 10**10, bytes_accessed=40 * 10**6, transcendentals=10**7
        ),
    )(*operands)


def rotary(length):
    half = HEAD_DIM // 2
    frequency = 10000.0 ** (-2.0 * np.arange(half) / HEAD_DIM)
    angles = frequency[:, None] * np.arange(length)[None, :]
    return np.asarray(np.cos(angles), np.float32), np.asarray(np.sin(angles), np.float32)


def unpack_kernel(plan, sizes, *refs):
    width, hidden, kv_width, through = sizes
    summed, refs = refs[0], refs[1:]
    (query, key_t, value_t, out, gate, up, down_t, *gains), rest = refs[through : through + 9], refs[through + 9 :]
    for source, target in zip(refs[:through], rest):
        target[...] = source[...]
    full, rows, half_width = jnp.float32, width // plan.dp, width // 2

    def tile(half, index, first, count):
        parts = [
            summed[half, p // plan.cx, p % plan.cx, pl.ds(plan.offsets[index] + place, size), :]
            for p, place, inside, size in plan.spans(index, first, count)
        ]
        return (parts[0] if len(parts) == 1 else jnp.concatenate(parts, 0)).astype(full)

    def put(target, at, cols, value):
        count = min(LANES, target.shape[1] - cols)
        target[at : at + value.shape[0], cols : cols + count] = value[:, :count]

    for index, (kind, start, tiles, height, piece, mode) in enumerate(plan.chunks):
        for half in range(2):
            for number in range(tiles):
                value = tile(half, index, number * height, height)
                cols = (start + number) * LANES
                if kind == "ffn":
                    put((gate, up)[half], 0, cols, value[:rows])
                elif kind == "down":
                    put(down_t, half * half_width, cols, value[:half_width])
                elif kind == "attn":
                    put((query, out)[half], 0, cols, value[:rows])
                else:
                    spare = plan.width_tiles * LANES - width
                    if number == 0:
                        put((query, out)[half], 0, width + spare - LANES, value[:rows])
                    pair_t = value.T[:, :rows]
                    first = number * LANES - LANES + spare
                    if first < 0:
                        pair_t = pair_t[LANES - spare :]
                        first = 0
                    (key_t, value_t)[half][first : first + pair_t.shape[0], :] = pair_t
            if kind == "mixed":
                lines = tile(half, index, tiles * height, 16)
                for number in range(-(-rows // LANES)):
                    put(gains[half], 0, number * LANES, lines[number : number + 1])


def unpack(plan, sizes, summed, *through):
    width, hidden, kv_width = sizes
    rows, full = width // plan.dp, jnp.float32
    shapes = [
        (rows, width), (kv_width, rows), (kv_width, rows), (rows, width),
        (rows, hidden), (rows, hidden), (width, hidden // plan.dp), (1, rows), (1, rows),
    ]
    vmem = pl.BlockSpec(memory_space=pltpu.VMEM)
    return pl.pallas_call(
        functools.partial(unpack_kernel, plan, (*sizes, len(through))),
        out_shape=[jax.ShapeDtypeStruct(shape, full) for shape in shapes]
        + [jax.ShapeDtypeStruct(value.shape, value.dtype) for value in through],
        in_specs=[vmem] * (1 + len(through)),
        out_specs=[vmem] * (len(shapes) + len(through)),
        compiler_params=pltpu.CompilerParams(vmem_limit_bytes=60 << 20),
    )(summed, *through)


def plain_block(
    plan, inputs, segment_ids, cotangent,
    gain_attn, w_query, w_key, w_value, w_out, gain_ffn, w_gate, w_up, w_down,
):
    micro_count, row_count, tok_local, model_width = inputs.shape
    kv_width = w_key.shape[1]
    group_size = HEADS // KV_HEADS
    section_index = lax.axis_index("section")
    on_first = section_index == 0
    ctx_index = lax.axis_index("ctx")
    first_token = ctx_index * tok_local
    query_pos = first_token + jnp.arange(tok_local, dtype=jnp.int32)
    halfway = HEAD_DIM // 2
    frequency = 10000.0 ** (-2.0 * jnp.arange(halfway, dtype=jnp.float32) / HEAD_DIM)
    angles = query_pos.astype(jnp.float32)[:, None] * frequency[None, :]
    cos_table = jnp.cos(angles)
    sine_table = jnp.sin(angles)
    w_pair = jnp.concatenate([w_key, w_value], 1)
    head_shape = (row_count, tok_local, KV_HEADS, group_size, HEAD_DIM)
    state_shape = (row_count, KV_HEADS, group_size, tok_local)

    def front(hidden, segments):
        query_seg = lax.dynamic_slice_in_dim(segments, first_token, tok_local, 1)
        normed, inverse = rms_forward(hidden, gain_attn)
        normed_low = normed.astype(jnp.bfloat16)
        query_pre = jnp.einsum(
            "rcd,de->rce", normed_low, w_query, preferred_element_type=jnp.float32
        )
        pair_pre = jnp.einsum("rcd,de->rce", normed_low, w_pair, preferred_element_type=jnp.float32)
        queries = rotate(
            query_pre.reshape(row_count, tok_local, HEADS, HEAD_DIM), cos_table, sine_table
        )
        queries = queries.astype(jnp.bfloat16).reshape(head_shape)
        key_rot = rotate(
            pair_pre[..., :kv_width].reshape(row_count, tok_local, KV_HEADS, HEAD_DIM),
            cos_table,
            sine_table,
        )
        packed = jnp.concatenate(
            [key_rot.reshape(row_count, tok_local, kv_width), pair_pre[..., kv_width:]], -1
        )
        return (query_seg, inverse, normed_low, queries, packed.astype(jnp.bfloat16))

    def attend_forward(queries, arrived, segments, query_seg):
        start_state = (
            jnp.full(state_shape, mask_floor, jnp.float32),
            jnp.zeros(state_shape, jnp.float32),
            jnp.zeros(state_shape + (HEAD_DIM,), jnp.float32),
        )
        piece_rows = arrived.shape[1]
        block_rows = math.gcd(piece_rows, 512)

        def fold_inner_step(step_index, loop_state):
            run_max, run_sum, run_acc = loop_state
            offset = step_index * block_rows
            key_block = lax.dynamic_slice_in_dim(arrived, step_index * block_rows, block_rows, 1)
            key_part = key_block[..., :kv_width].reshape(row_count, block_rows, KV_HEADS, HEAD_DIM)
            value_part = key_block[..., kv_width:].reshape(
                row_count, block_rows, KV_HEADS, HEAD_DIM
            )
            key_seg = lax.dynamic_slice_in_dim(segments, offset, block_rows, 1)
            scores, allowed = block_scores(queries, key_part, query_seg, key_seg, query_pos, offset)
            masked = jnp.where(allowed, scores, mask_floor)
            new_max = jnp.maximum(run_max, jnp.max(masked, -1))
            weights = jnp.where(allowed, jnp.exp(masked - new_max[..., None]), 0.0)
            rescale = jnp.exp(run_max - new_max)
            run_sum = run_sum * rescale + jnp.sum(weights, -1)
            run_acc = run_acc * rescale[..., None] + jnp.einsum(
                "rkgcn,rnkd->rkgcd",
                weights.astype(jnp.bfloat16),
                value_part,
                preferred_element_type=jnp.float32,
            )
            return (new_max, run_sum, run_acc)

        run_max, run_sum, run_acc = lax.fori_loop(
            0, piece_rows // block_rows, fold_inner_step, start_state
        )
        return (run_acc / run_sum[..., None], run_max + jnp.log(run_sum))

    def rear(hidden, attended):
        attn_low = (
            attended.transpose(0, 3, 1, 2, 4)
            .reshape(row_count, tok_local, HEADS * HEAD_DIM)
            .astype(jnp.bfloat16)
        )
        middle = hidden + jnp.einsum(
            "rce,ed->rcd", attn_low, w_out, preferred_element_type=jnp.float32
        )
        normed_ffn, inverse_ffn = rms_forward(middle, gain_ffn)
        ffn_low = normed_ffn.astype(jnp.bfloat16)
        gate_pre = jnp.einsum("rcd,df->rcf", ffn_low, w_gate, preferred_element_type=jnp.float32)
        upward = jnp.einsum("rcd,df->rcf", ffn_low, w_up, preferred_element_type=jnp.float32)
        inner_act = (jax.nn.silu(gate_pre) * upward).astype(jnp.bfloat16)
        output = middle + jnp.einsum(
            "rcf,fd->rcd", inner_act, w_down, preferred_element_type=jnp.float32
        )
        return (output, (attn_low, middle, inverse_ffn, ffn_low, gate_pre, upward, inner_act))


    assert micro_count == lax.axis_size("section")

    def mine(stacked):
        return lax.dynamic_index_in_dim(stacked, section_index, 0, keepdims=False)

    segments = mine(segment_ids)

    def forward(hidden):
        query_seg, inverse, normed_low, queries, packed = front(hidden, segments)
        arrived = lax.all_gather(packed, "ctx", axis=1, tiled=True)
        attended, log_sum = attend_forward(queries, arrived, segments, query_seg)
        output, saved = rear(hidden, attended)
        return output.astype(jnp.bfloat16), (
            hidden, query_seg, inverse, normed_low, queries, arrived, attended, log_sum, saved
        )

    def backward(grad_out, kept):
        (
            hidden,
            backward_query_seg,
            backward_inverse,
            backward_normed_low,
            backward_queries,
            piece_arrived,
            backward_attended,
            log_sum,
            saved,
        ) = kept
        (
            backward_attn_low,
            backward_middle,
            backward_inverse_ffn,
            backward_ffn_low,
            backward_gate_pre,
            backward_upward,
            backward_inner_act,
        ) = saved
        grad_low = grad_out.astype(jnp.bfloat16)
        grad_inner = jnp.einsum("rcd,fd->rcf", grad_low, w_down, preferred_element_type=jnp.float32)
        sigmoid = jax.nn.sigmoid(backward_gate_pre)
        grad_gate = (
            grad_inner * backward_upward * sigmoid * (1.0 + backward_gate_pre * (1.0 - sigmoid))
        ).astype(jnp.bfloat16)
        grad_up = (grad_inner * backward_gate_pre * sigmoid).astype(jnp.bfloat16)
        grad_norm_ffn = jnp.einsum(
            "rcf,df->rcd", grad_gate, w_gate, preferred_element_type=jnp.float32
        ) + jnp.einsum("rcf,df->rcd", grad_up, w_up, preferred_element_type=jnp.float32)
        grad_mid_norm, backward_sum_gain_ffn = rms_backward(
            backward_middle, gain_ffn, backward_inverse_ffn, grad_norm_ffn
        )
        grad_middle = grad_out + grad_mid_norm
        grad_branch = grad_middle.astype(jnp.bfloat16)
        grad_attn = jnp.einsum(
            "rcd,ed->rce", grad_branch, w_out, preferred_element_type=jnp.float32
        ).astype(jnp.bfloat16)
        grad_heads = grad_attn.reshape(head_shape).transpose(0, 2, 3, 1, 4)
        row_delta = jnp.sum(grad_heads.astype(jnp.float32) * backward_attended, -1)
        query_start = jnp.zeros(state_shape + (HEAD_DIM,), jnp.float32)
        fold_grad_query = query_start
        grad_query = fold_grad_query
        piece_piece_rows = piece_arrived.shape[1]
        piece_block_rows = math.gcd(piece_piece_rows, 512)

        def piece_inner_step(step_index, loop_state):
            grad_query, local_pair = loop_state
            inside = step_index * piece_block_rows
            key_block = lax.dynamic_slice_in_dim(piece_arrived, inside, piece_block_rows, 1)
            key_part = key_block[..., :kv_width].reshape(
                row_count, piece_block_rows, KV_HEADS, HEAD_DIM
            )
            value_part = key_block[..., kv_width:].reshape(
                row_count, piece_block_rows, KV_HEADS, HEAD_DIM
            )
            key_seg = lax.dynamic_slice_in_dim(segments, inside, piece_block_rows, 1)
            scores, allowed = block_scores(
                backward_queries, key_part, backward_query_seg, key_seg, query_pos, inside
            )
            chances = jnp.where(
                allowed, jnp.exp(jnp.where(allowed, scores, mask_floor) - log_sum[..., None]), 0.0
            )
            grad_chance = jnp.einsum(
                "rkgcd,rnkd->rkgcn", grad_heads, value_part, preferred_element_type=jnp.float32
            )
            grad_scores = (chances * (grad_chance - row_delta[..., None])).astype(jnp.bfloat16)
            grad_query = grad_query + score_scale * jnp.einsum(
                "rkgcn,rnkd->rkgcd", grad_scores, key_part, preferred_element_type=jnp.float32
            )
            grad_key = score_scale * jnp.einsum(
                "rkgcn,rckgd->rnkd",
                grad_scores,
                backward_queries,
                preferred_element_type=jnp.float32,
            )
            grad_value = jnp.einsum(
                "rkgcn,rkgcd->rnkd",
                chances.astype(jnp.bfloat16),
                grad_heads,
                preferred_element_type=jnp.float32,
            )
            update = jnp.concatenate(
                [
                    grad_key.reshape(row_count, piece_block_rows, kv_width),
                    grad_value.reshape(row_count, piece_block_rows, kv_width),
                ],
                -1,
            )
            current = lax.dynamic_slice_in_dim(local_pair, inside, piece_block_rows, 1)
            local_pair = lax.dynamic_update_slice_in_dim(local_pair, current + update, inside, 1)
            return (grad_query, local_pair)

        local_start = jnp.zeros((row_count, piece_piece_rows, 2 * kv_width), jnp.float32)
        fold_grad_query, fold_local_pair = lax.fori_loop(
            0, piece_piece_rows // piece_block_rows, piece_inner_step, (grad_query, local_start)
        )
        grad_pair = fold_local_pair
        grad_query, grad_pair = (fold_grad_query, grad_pair)
        pair_share = lax.psum_scatter(
            grad_pair.astype(jnp.bfloat16), "ctx", scatter_dimension=1, tiled=True
        ).astype(jnp.float32)
        query_tok = grad_query.transpose(0, 3, 1, 2, 4).reshape(
            row_count, tok_local, HEADS, HEAD_DIM
        )
        query_back = rotate(query_tok, cos_table, -sine_table).reshape(
            row_count, tok_local, HEADS * HEAD_DIM
        )
        query_back = query_back.astype(jnp.bfloat16)
        key_back = rotate(
            pair_share[..., :kv_width].reshape(row_count, tok_local, KV_HEADS, HEAD_DIM),
            cos_table,
            -sine_table,
        )
        pair_low = jnp.concatenate(
            [key_back.reshape(row_count, tok_local, kv_width), pair_share[..., kv_width:]], -1
        )
        pair_low = pair_low.astype(jnp.bfloat16)
        grad_normed = jnp.einsum(
            "rce,de->rcd", query_back, w_query, preferred_element_type=jnp.float32
        ) + jnp.einsum("rce,de->rcd", pair_low, w_pair, preferred_element_type=jnp.float32)
        grad_front, backward_sum_gain_attn = rms_backward(
            hidden, gain_attn, backward_inverse, grad_normed
        )
        factors = (
            backward_normed_low, backward_attn_low, backward_ffn_low, backward_inner_act,
            query_back, pair_low, grad_branch, grad_gate, grad_up, grad_low,
        )
        tick_grads = (backward_sum_gain_attn, backward_sum_gain_ffn, factors)
        return grad_middle + grad_front, tick_grads

    first_low, first_kept = forward(mine(inputs).astype(jnp.float32))
    second_low, second_kept = forward(first_low.astype(jnp.float32))
    grad_mid, second_grads = backward(mine(cotangent).astype(jnp.float32), second_kept)
    grad_mid_low = grad_mid.astype(jnp.bfloat16)
    grad_in, first_grads = backward(grad_mid_low.astype(jnp.float32), first_kept)
    dp = plan.dp

    def stacked(one, other):
        return jnp.concatenate([one, other], 1).reshape(-1, one.shape[-1])

    normed, attn, ffn, inner, d_query, d_pair, d_branch, d_gate, d_up, d_out = (
        stacked(one, other) for one, other in zip(first_grads[2], second_grads[2])
    )
    tokens = normed.shape[0]

    def sides(values, rows):
        cut = values.reshape(tokens, dp, -1)
        cut = jnp.pad(cut, ((0, 0), (0, 0), (0, rows - cut.shape[2])))
        return cut.transpose(1, 2, 0).reshape(dp * rows, tokens)

    inner = inner.reshape(tokens, dp, -1)
    inner = jnp.pad(
        inner, ((0, 0), (0, 0), (0, plan.down_tiles * LANES - inner.shape[2]))
    ).reshape(tokens, -1)
    spare = plan.width_tiles * LANES - model_width
    gain_sums = jnp.stack([one + other for one, other in zip(first_grads[:2], second_grads[:2])])
    gain_sums = jnp.pad(gain_sums, ((0, 6), (0, plan.width_tiles * LANES - model_width)))
    factors = (
        sides(ffn, plan.rows),
        jnp.stack([d_gate, d_up]),
        d_out.T,
        inner,
        jnp.stack([sides(normed, plan.rows), sides(attn, plan.rows)]),
        jnp.pad(jnp.stack([d_query, d_branch]), ((0, 0), (0, 0), (0, spare))),
        jnp.pad(
            jnp.stack([d_pair[:, :kv_width], d_pair[:, kv_width:]]),
            ((0, 0), (0, 0), (LANES - spare, 0)),
        ),
    )
    acts = (first_low, second_low)
    return acts, (grad_in, grad_mid_low), gain_sums, factors


def fused_block(
    size, plan, inputs, segment_ids, cotangent,
    gain_attn, w_query, w_key, w_value, w_out, gain_ffn, w_gate, w_up, w_down,
):
    cos_in, sin_in = rotary(size.length)
    gains = jnp.stack([gain_attn, gain_ffn]).astype(jnp.float32)
    gains = jnp.pad(gains, ((0, 0), (0, plan.width_tiles * LANES - size.width)))
    hidden = inputs[:, 0].swapaxes(1, 2)
    weights = (w_query, w_key.T, w_value.T, w_out, w_gate, w_up, w_down.T)
    acts, *kept = run_front(
        size, plan, hidden, cotangent[:, 0].swapaxes(1, 2), segment_ids, cos_in, sin_in, gains, *weights
    )
    summed, grads = run_tail(size, plan, hidden, cos_in, sin_in, gains, *kept, *weights)
    return acts, grads, summed


def body(
    inputs,
    segment_ids,
    cotangent,
    gain_attn,
    w_query,
    w_key,
    w_value,
    w_out,
    gain_ffn,
    w_gate,
    w_up,
    w_down,
):
    micro_count, row_count, tok_local, model_width = inputs.shape
    kv_width, hidden = w_key.shape[1], w_gate.shape[1]
    assert micro_count == lax.axis_size("section")
    on_first = lax.axis_index("section") == 0
    plan = Plan(lax.axis_size("dp"), lax.axis_size("ctx"), model_width, hidden, kv_width)
    dp = plan.dp
    size = Block(tok_local, segment_ids.shape[2], model_width, hidden, kv_width, plan.ctx)
    fits = (
        row_count == 1
        and size.length <= 1024
        and tok_local % LANES == 0
        and plan.rows * dp == model_width
        and plan.down_tiles * LANES * dp == hidden
        and len(plan.chunks) == 11
    )
    params = (gain_attn, w_query, w_key, w_value, w_out, gain_ffn, w_gate, w_up, w_down)
    if fits:
        acts, grads, summed = fused_block(size, plan, inputs, segment_ids, cotangent, *params)
    else:
        acts, grads, gain_sums, factors = plain_block(
            plan, inputs, segment_ids, cotangent, *params
        )
        summed = reduce_grads(plan, *factors, gain_sums)
    sizes = (model_width, hidden, kv_width)

    def exchange(for_first, for_last):
        kept = jnp.where(on_first, for_first, for_last)
        sent = jnp.where(on_first, for_last, for_first)
        got = lax.ppermute(sent, "section", [(0, 1), (1, 0)])
        return jnp.where(
            on_first, jnp.stack([kept, got]), jnp.stack([got, kept])
        )

    def turned(values):
        return values[None, :, None].swapaxes(3, 4)

    if fits:
        *parts, acts, grads = unpack(plan, sizes, summed, acts, grads)
        activations, input_grads = turned(acts), turned(grads)
    else:
        parts = unpack(plan, sizes, summed)
        activations = exchange(*acts)[None]
        input_grads = exchange(grads[0].astype(jnp.bfloat16), grads[1]).astype(jnp.float32)[None]
    query, key_t, value_t, out, gate, up, down_t, gain_one, gain_two = parts
    return (
        activations,
        input_grads,
        gain_one.reshape(-1),
        query,
        key_t.T,
        value_t.T,
        out,
        gain_two.reshape(-1),
        gate,
        up,
        down_t.T,
    )


def solution(mesh):
    placed = (
        P(None, "dp", "ctx", None),
        P(None, "dp", None),
        P(None, "dp", "ctx", None),
        P(),
        P(),
        P(),
        P(),
        P(),
        P(),
        P(),
        P(),
        P(),
    )
    return jax.shard_map(
        body,
        mesh=mesh,
        in_specs=placed,
        out_specs=(
            P("section", None, "dp", "ctx", None),
            P("section", None, "dp", "ctx", None),
            P("dp"),
            P("dp", None),
            P("dp", None),
            P("dp", None),
            P("dp", None),
            P("dp"),
            P("dp", None),
            P("dp", None),
            P("dp", None),
        ),
        check_vma=False,
    )
```

```python
import functools
import math
import types

import jax
import jax.numpy as jnp
import numpy as np
from jax import lax
from jax.experimental import pallas as pl
from jax.experimental.pallas import tpu as pltpu
from jax.sharding import PartitionSpec as P

HEADS = 15
KV_HEADS = 5
HEAD_DIM = 64
LANES = 128
Z_CHUNKS = 3
Z_LAG = 2
OWN_SLOTS = 8
PARTNER_SLOTS = 3
MESH = pl.DeviceIdType.MESH


epsilon = 1e-05
score_scale = 0.125
score_unit = score_scale / math.log(2.0)
mask_floor = -1e30


def rms_forward(values, gain_vec):
    inverse = lax.rsqrt(jnp.mean(values * values, -1, keepdims=True) + epsilon)
    return (values * inverse * gain_vec, inverse)


def rms_backward(values, gain_vec, inverse, grad_normed):
    weighted = grad_normed * gain_vec
    grad_gain = jnp.sum(grad_normed * values * inverse, axis=(0, 1))
    cubed = inverse * inverse * inverse
    grad_values = inverse * weighted - values * cubed * jnp.mean(
        weighted * values, -1, keepdims=True
    )
    return (grad_values, grad_gain)


def rotate(values, cos_table, sine_table):
    halfway = values.shape[-1] // 2
    former = values[..., :halfway]
    latter = values[..., halfway:]
    cos_part = cos_table[None, :, None, :]
    sine_part = sine_table[None, :, None, :]
    return jnp.concatenate(
        [former * cos_part - latter * sine_part, latter * cos_part + former * sine_part], -1
    )


def block_scores(queries, key_part, query_seg, key_seg, query_pos, offset):
    block_rows = key_part.shape[1]
    scores = (
        jnp.einsum("rckgd,rnkd->rkgcn", queries, key_part, preferred_element_type=jnp.float32)
        * score_scale
    )
    key_pos = offset + jnp.arange(block_rows, dtype=jnp.int32)
    allowed = (query_seg[:, :, None] == key_seg[:, None, :]) & (
        key_pos[None, None, :] <= query_pos[None, :, None]
    )
    return (scores, allowed[:, None, None, :, :])


def up_to(value, step):
    return -(-value // step) * step


TAIL_ORDER = (
    0, 8, -1, 24, -1, 1, 16, 9, 25, 32, -1, 40, 17, 33, -1, 41, -1, -2, 26, -3,
    48, 2, 49, 56, -4, 3, 42, 4, 57, 64, 34, 58, 10, 72, 43, 27, 18, 65, 19, 11,
    59, 50, 20, 12, 35, 73, 66, 21, 51, 28, 44, 80, 81, 74, 5, 60, 67, 29, 75, 82,
    30, 52, 13, 36, 83, 61, 53, 22, 68, 45, 31, 76, 69, 84, 54, 62, 37, 46, 23, 77,
    6, 85, 70, 38, 63, 14, 78, 86, 39, 55, 71, 47, 15, 7, 79, 87,
)


class Plan:
    def __init__(self, dp, ctx, width, hidden, kv_width):
        self.dp, self.ctx = dp, ctx
        self.cx = 1 << (ctx.bit_length() // 2) if ctx & (ctx - 1) == 0 else ctx
        self.cy = ctx // self.cx
        self.low = max(dp // 2, 1)
        self.shard = width // dp
        self.rows = up_to(width // dp, 16)
        self.down_rows = up_to(width // 2, 16)
        self.down_tiles = up_to(hidden // dp, LANES) // LANES
        self.up_tiles = hidden // LANES
        self.width_tiles = up_to(width, LANES) // LANES
        self.pair_tiles = (width + kv_width) // LANES
        self.step = 4
        chunks = []
        for kind, count, rows, step in (
            ("down", self.down_tiles, self.down_rows, 2),
            ("ffn", self.up_tiles, self.rows, self.step),
            ("attn", self.width_tiles - 1, self.rows, 4),
            ("mixed", self.pair_tiles - self.width_tiles + 1, self.rows, 4),
        ):
            for start in range(0, count, step):
                tiles = min(step, count - start)
                extra = 16 if kind == "mixed" else 0
                piece = up_to(up_to(tiles * rows + extra, ctx) // ctx, 16)
                mode = "z" if len(chunks) < Z_CHUNKS else "xy"
                chunks.append((kind, start, tiles, rows, piece, mode))
        self.chunks = chunks
        self.offsets = [sum(c[4] for c in chunks[:i]) for i in range(len(chunks))]
        self.total = sum(c[4] for c in chunks)
        self.widest = max(c[4] for c in chunks)

    def of(self, kind):
        return [i for i, chunk in enumerate(self.chunks) if chunk[0] == kind]

    def spans(self, index, first, count):
        piece = self.chunks[index][4]
        out, done = [], 0
        while done < count:
            at = first + done
            size = min(count - done, piece - at % piece)
            out.append((at // piece, at % piece, done, size))
            done += size
        return out

    def scratch(self):
        dp, cy, cx, low = self.dp, self.cy, self.cx, self.low
        nx, ny, nz, high = max(cx - 1, 1), max(cy - 1, 1), max(dp - 1, 1), max(dp - low, 1)
        count = len(self.chunks)

        def buffer(*shape):
            return pltpu.VMEM((*shape, LANES), jnp.bfloat16)

        found = [
            buffer(2, dp, cy, cx, self.widest),
            buffer(PARTNER_SLOTS, dp, cy, cx, self.widest),
            buffer(OWN_SLOTS, dp, cy, cx, self.widest),
        ]
        for kind, start, tiles, rows, piece, mode in self.chunks:
            head = up_to(piece // 2, 16)
            rest = max(piece - head, 16)
            if mode == "xy":
                found += [
                    buffer(nz, piece), buffer(nx, low, cy, piece), buffer(ny, high, cx, piece),
                    buffer(nx, high, piece), buffer(ny, low, piece), buffer(piece),
                ]
            else:
                found += [
                    buffer(nz, cy, cx, piece), buffer(nx, cy, head), buffer(ny, cx, rest),
                    buffer(nx, rest), buffer(ny, head), buffer(piece),
                ]
        dma = pltpu.SemaphoreType.DMA
        return found + [
            dma((2, count)), dma((2, count, nx)), dma((2, count, ny)), dma((2, count, nx)),
            dma((2, count, ny)), dma((2, count, nz)), dma((2, count, nx)), dma((2, count, ny)),
            dma((2, count, nx)), dma((2, count, ny)), dma((2, count)), dma((count,)),
            pltpu.SemaphoreType.REGULAR,
        ]


class Reduction:
    def __init__(self, plan, products, out, refs, turns=None):
        self.plan, self.products, self.out = plan, products, out
        count = len(plan.chunks)
        self.turns = list(range(count)) if turns is None else turns
        self.sent, self.partner, self.own_ring = refs[:3]
        self.parts = [refs[3 + 6 * i : 9 + 6 * i] for i in range(count)]
        (
            self.sem_p, self.sem_x1, self.sem_y1, self.sem_x2, self.sem_y2, self.sem_z,
            self.sem_gx, self.sem_gy, self.sem_hx, self.sem_hy, self.sem_m, self.sem_o, self.credit,
        ) = refs[3 + 6 * count :]
        self.section, self.row, self.ctx = (
            lax.axis_index(name) for name in ("section", "dp", "ctx")
        )
        self.px, self.py = lax.rem(self.ctx, plan.cx), lax.div(self.ctx, plan.cx)
        self.mate = (1 - self.section, self.row, self.ctx)
        self.done = [0] * count

    def friends(self):
        plan = self.plan
        found = [self.mate]
        found += [(self.section, lax.rem(self.row + k, plan.dp), self.ctx) for k in range(1, plan.dp)]
        return found + [
            (self.section, self.row, lax.rem(self.ctx + k, plan.ctx)) for k in range(1, plan.ctx)
        ]

    def remote(self, source, target, sems, place, device):
        return pltpu.make_async_remote_copy(
            source, target, sems.at[(0, *place)], sems.at[(1, *place)],
            device_id=device, device_id_type=MESH,
        )

    def x_peers(self):
        for k in range(1, self.plan.cx):
            other = lax.rem(self.px + k, self.plan.cx)
            yield k - 1, other, (self.section, self.row, self.py * self.plan.cx + other)

    def y_peers(self):
        for k in range(1, self.plan.cy):
            other = lax.rem(self.py + k, self.plan.cy)
            yield k - 1, other, (self.section, self.row, other * self.plan.cx + self.px)

    def z_peers(self):
        for k in range(1, self.plan.dp):
            other = lax.rem(self.row + k, self.plan.dp)
            yield k - 1, other, (self.section, other, self.ctx)

    def turn(self, index):
        return self.turns.index(index)

    def own(self, index):
        return self.own_ring.at[self.turn(index) % OWN_SLOTS]

    def at(self, index):
        return pl.ds(self.plan.offsets[index], self.plan.chunks[index][4])

    def head(self, index):
        piece = self.plan.chunks[index][4]
        return up_to(piece // 2, 16)

    def partner_copy(self, index):
        rows = pl.ds(0, self.plan.chunks[index][4])
        return self.remote(
            self.sent.at[self.turn(index) % 2, :, :, :, rows],
            self.partner.at[self.turn(index) % PARTNER_SLOTS, :, :, :, rows],
            self.sem_p, (index,), self.mate,
        )

    def make_partner(self, index):
        turn, cx = self.turn(index), self.plan.cx
        if turn >= 2:
            self.partner_copy(self.turns[turn - 2]).wait_send()
        if turn >= PARTNER_SLOTS:
            pl.semaphore_wait(self.credit, 1)

        def finish(j, first, value):
            for p, place, inside, size in self.plan.spans(index, first, value.shape[0]):
                self.sent[turn % 2, j, p // cx, p % cx, place : place + size, :] = value[
                    inside : inside + size
                ].astype(jnp.bfloat16)

        self.products(index, 1 - self.section, finish)
        self.partner_copy(index).start()

    def make_own(self, index):
        turn = self.turn(index)
        assert turn < OWN_SLOTS or self.done[self.turns[turn - OWN_SLOTS]] > 4
        self.partner_copy(index).wait_recv()
        cx, slot, own = self.plan.cx, turn % PARTNER_SLOTS, self.own(index)

        def finish(j, first, value):
            for p, place, inside, size in self.plan.spans(index, first, value.shape[0]):
                rows = slice(place, place + size)
                other = self.partner[slot, j, p // cx, p % cx, rows, :].astype(jnp.float32)
                own[j, p // cx, p % cx, rows, :] = (
                    value[inside : inside + size] + other
                ).astype(jnp.bfloat16)

        self.products(index, self.section, finish)
        if turn + PARTNER_SLOTS < len(self.plan.chunks):
            pl.semaphore_signal(self.credit, 1, device_id=self.mate, device_id_type=MESH)
        self.start(self.z_copies(index) if self.is_z(index) else self.first_copies(index))

    def is_z(self, index):
        return self.plan.chunks[index][5] == "z"

    def start(self, copies):
        for copy in copies:
            copy.start()

    def wait(self, copies):
        for copy in copies:
            copy.wait()

    def z_copies(self, index):
        own, into = self.own(index), self.parts[index][0]
        piece = pl.ds(0, self.plan.chunks[index][4])
        found = []
        for slot, other, device in self.z_peers():
            if self.is_z(index):
                source = own.at[other, :, :, piece]
            else:
                source = own.at[other, self.py, self.px, piece]
            found.append(self.remote(source, into.at[slot], self.sem_z, (index, slot), device))
        return found

    def halves(self, index):
        plan, piece = self.plan, self.plan.chunks[index][4]
        if self.is_z(index):
            head = self.head(index)
            return (pl.ds(self.row, 1), pl.ds(0, head)), (pl.ds(self.row, 1), pl.ds(head, piece - head))
        rows = pl.ds(0, piece)
        return (pl.ds(0, plan.low), rows), (pl.ds(plan.low, plan.dp - plan.low), rows)

    def has_rest(self, index):
        if self.is_z(index):
            return self.plan.chunks[index][4] > self.head(index)
        return self.plan.dp > self.plan.low

    def first_copies(self, index):
        own = self.own(index)
        (j_x, rows_x), (j_y, rows_y) = self.halves(index)
        _, rx1, ry1, _, _, _ = self.parts[index]
        if self.is_z(index):
            j_x = j_y = self.row
        found = [
            self.remote(own.at[j_x, :, other, rows_x], rx1.at[slot], self.sem_x1, (index, slot), device)
            for slot, other, device in self.x_peers()
        ]
        if self.has_rest(index):
            found += [
                self.remote(
                    own.at[j_y, other, :, rows_y], ry1.at[slot], self.sem_y1, (index, slot), device
                )
                for slot, other, device in self.y_peers()
            ]
        return found

    def second_copies(self, index):
        own = self.own(index)
        (j_x, rows_x), (j_y, rows_y) = self.halves(index)
        _, _, _, rx2, ry2, _ = self.parts[index]
        if self.is_z(index):
            j_x = j_y = self.row
        found = [
            self.remote(
                own.at[j_x, other, self.px, rows_x], ry2.at[slot], self.sem_y2, (index, slot), device
            )
            for slot, other, device in self.y_peers()
        ]
        if self.has_rest(index):
            found += [
                self.remote(
                    own.at[j_y, self.py, other, rows_y], rx2.at[slot], self.sem_x2, (index, slot), device
                )
                for slot, other, device in self.x_peers()
            ]
        return found

    def add_all_z(self, index):
        plan, own, into = self.plan, self.own(index), self.parts[index][0]
        piece = slice(0, plan.chunks[index][4])
        self.wait(self.z_copies(index))
        for y in range(plan.cy):
            for x in range(plan.cx):
                total = own[self.row, y, x, piece, :].astype(jnp.float32)
                for k in range(plan.dp - 1):
                    total = total + into[k, y, x].astype(jnp.float32)
                own[self.row, y, x, piece, :] = total.astype(jnp.bfloat16)
        self.start(self.first_copies(index))

    def add_first(self, index):
        plan, own = self.plan, self.own(index)
        _, rx1, ry1, _, _, _ = self.parts[index]
        piece, is_z = plan.chunks[index][4], self.is_z(index)
        head = self.head(index)
        self.wait(self.first_copies(index))
        places = [(self.row, 0, 0)] if is_z else [(j, j, j - plan.low) for j in range(plan.dp)]
        for j, at_x, at_y in places:
            if is_z or at_x < plan.low:
                rows = slice(0, head) if is_z else slice(0, piece)
                for y in range(plan.cy):
                    total = own[j, y, self.px, rows, :].astype(jnp.float32)
                    for k in range(plan.cx - 1):
                        part = rx1[k, y] if is_z else rx1[k, at_x, y]
                        total = total + part.astype(jnp.float32)
                    own[j, y, self.px, rows, :] = total.astype(jnp.bfloat16)
            if (is_z and piece > head) or (not is_z and at_y >= 0):
                rows = slice(head, piece) if is_z else slice(0, piece)
                for x in range(plan.cx):
                    total = own[j, self.py, x, rows, :].astype(jnp.float32)
                    for k in range(plan.cy - 1):
                        part = ry1[k, x] if is_z else ry1[k, at_y, x]
                        total = total + part.astype(jnp.float32)
                    own[j, self.py, x, rows, :] = total.astype(jnp.bfloat16)
        self.start(self.second_copies(index))

    def add_second(self, index):
        plan, own = self.plan, self.own(index)
        _, _, _, rx2, ry2, _ = self.parts[index]
        piece = slice(0, plan.chunks[index][4])
        self.wait(self.second_copies(index))
        for j in range(plan.dp):
            total = own[j, self.py, self.px, piece, :].astype(jnp.float32)
            if j < plan.low:
                for k in range(plan.cy - 1):
                    total = total + ry2[k, j].astype(jnp.float32)
            else:
                for k in range(plan.cx - 1):
                    total = total + rx2[k, j - plan.low].astype(jnp.float32)
            own[j, self.py, self.px, piece, :] = total.astype(jnp.bfloat16)
        self.start(self.z_copies(index))

    def add_last(self, index):
        plan, own = self.plan, self.own(index)
        rz, _, _, rx2, ry2, final = self.parts[index]
        piece, head = plan.chunks[index][4], self.head(index)
        if self.is_z(index):
            self.wait(self.second_copies(index))
            total = own[self.row, self.py, self.px, 0:head, :].astype(jnp.float32)
            for k in range(plan.cy - 1):
                total = total + ry2[k].astype(jnp.float32)
            final[0:head, :] = total.astype(jnp.bfloat16)
            if piece > head:
                total = own[self.row, self.py, self.px, head:piece, :].astype(jnp.float32)
                for k in range(plan.cx - 1):
                    total = total + rx2[k].astype(jnp.float32)
                final[head:piece, :] = total.astype(jnp.bfloat16)
        else:
            self.wait(self.z_copies(index))
            total = own[self.row, self.py, self.px, 0:piece, :].astype(jnp.float32)
            for k in range(plan.dp - 1):
                total = total + rz[k].astype(jnp.float32)
            final[...] = total.astype(jnp.bfloat16)
        self.place_copy(index).start()
        self.start(self.gather_one(index))

    def place_copy(self, index):
        target = self.out.at[self.section, self.py, self.px, self.at(index)]
        return pltpu.make_async_copy(self.parts[index][5], target, self.sem_o.at[index])

    def gather_parts(self, index):
        offset, piece, head = self.plan.offsets[index], self.plan.chunks[index][4], self.head(index)
        return pl.ds(offset, head), pl.ds(offset + head, piece - head), piece > head

    def gather_one(self, index):
        final, out = self.parts[index][5], self.out
        rows_x, rows_y, rest = self.gather_parts(index)
        head, piece = self.head(index), self.plan.chunks[index][4]
        found = [
            self.remote(
                final.at[pl.ds(0, head)], out.at[self.section, self.py, self.px, rows_x],
                self.sem_gx, (index, slot), device,
            )
            for slot, other, device in self.x_peers()
        ]
        if rest:
            found += [
                self.remote(
                    final.at[pl.ds(head, piece - head)], out.at[self.section, self.py, self.px, rows_y],
                    self.sem_gy, (index, slot), device,
                )
                for slot, other, device in self.y_peers()
            ]
        return found

    def gather_two(self, index):
        out = self.out
        rows_x, rows_y, rest = self.gather_parts(index)
        found = []
        for slot, other, device in self.y_peers():
            region = out.at[self.section, self.py, :, rows_x]
            found.append(self.remote(region, region, self.sem_hy, (index, slot), device))
        if rest:
            for slot, other, device in self.x_peers():
                region = out.at[self.section, :, self.px, rows_y]
                found.append(self.remote(region, region, self.sem_hx, (index, slot), device))
        return found

    def gather_on(self, index):
        self.place_copy(index).wait()
        self.wait(self.gather_one(index))
        self.start(self.gather_two(index))

    def mate_copy(self, index):
        region = self.out.at[self.section, :, :, self.at(index)]
        return self.remote(region, region, self.sem_m, (index,), self.mate)

    def pass_on(self, index):
        self.wait(self.gather_two(index))
        self.mate_copy(index).start()

    def finish(self, index):
        self.mate_copy(index).wait()

    def stages(self, index):
        middle = (self.add_all_z, self.add_first) if self.is_z(index) else (self.add_first, self.add_second)
        return (
            self.make_partner, self.make_own, *middle, self.add_last, self.gather_on, self.pass_on, self.finish
        )

    def advance(self, index, upto=None):
        stages = self.stages(index)
        while self.done[index] < len(stages):
            if upto is not None and self.done[index] >= upto:
                return
            stages[self.done[index]](index)
            self.done[index] += 1
            if upto is None:
                return

    def drain(self):
        todo = []
        for index in range(len(self.done)):
            for stage in range(self.done[index], len(self.stages(index))):
                late = Z_LAG if self.is_z(index) and stage >= 2 else 0
                todo.append((index + stage + late, stage, index))
        for step, stage, index in sorted(todo):
            self.advance(index)
        for index in self.turns[-2:]:
            self.partner_copy(index).wait_send()


def greet(friends):
    barrier = pltpu.get_barrier_semaphore()
    for friend in friends:
        pl.semaphore_signal(barrier, 1, device_id=friend, device_id_type=MESH)
    pl.semaphore_wait(barrier, len(friends))


def shard_products(plan, index, half, finish, sources):
    kind, start, tiles, rows, piece, mode = plan.chunks[index]
    cols = slice(start * LANES, (start + tiles) * LANES)

    def shard(j, carry):
        own = pl.ds(pl.multiple_of(j * plan.rows, 16), plan.rows)
        if kind == "ffn":
            value = dot(sources.ffn_x[own, :], sources.ffn_dy(half, index, 0, cols))
        elif kind == "down":
            first = pl.multiple_of(j * (plan.down_tiles * LANES) + start * LANES, LANES)
            rows_of = pl.ds(pl.multiple_of(half * plan.down_rows, 16), plan.down_rows)
            value = dot(sources.down_x[rows_of, :], sources.down_dy[:, pl.ds(first, tiles * LANES)])
        elif kind == "attn":
            value = dot(sources.attn_x[half, own, :], sources.attn_dy[half, :, cols])
        else:
            value = dot(sources.attn_x[0, own, :], sources.pair_dy[half])
            last = plan.width_tiles - 1
            mixed = dot(sources.attn_x[half, own, :], sources.attn_dy[half, :, last * LANES :])
            value = jnp.concatenate([value[:, :LANES] + mixed, value[:, LANES:]], 1)
        for tile in range(tiles):
            finish(j, tile * rows, value[:, tile * LANES : (tile + 1) * LANES])
        if kind == "mixed":
            finish(j, tiles * rows, sources.extra[half, j])
        return carry

    lax.fori_loop(0, plan.dp, shard, 0)


def spread_gains(plan, gain_sums, extra):
    for half in range(2):
        for j in range(plan.dp):
            for number in range(-(-plan.shard // LANES)):
                start = j * plan.shard + number * LANES
                extra[half, j, number : number + 1, :] = gain_sums[
                    half : half + 1, start : start + LANES
                ]


def reduce_kernel(
    plan, ffn_x, ffn_dy, down_x, down_dy, attn_x, attn_dy, pair_dy, gain_sums, out, extra, *refs
):
    sources = types.SimpleNamespace(
        ffn_x=ffn_x, ffn_dy=lambda half, index, inside, cols: ffn_dy[half, :, cols],
        down_x=down_x, down_dy=down_dy,
        attn_x=attn_x, attn_dy=attn_dy, pair_dy=pair_dy, extra=extra,
    )
    reduction = Reduction(
        plan, lambda *place: shard_products(plan, *place, sources), out, refs
    )
    greet(reduction.friends())
    spread_gains(plan, gain_sums, extra)
    reduction.drain()


def reduce_grads(plan, *operands):
    return pl.pallas_call(
        functools.partial(reduce_kernel, plan),
        out_shape=jax.ShapeDtypeStruct((2, plan.cy, plan.cx, plan.total, LANES), jnp.bfloat16),
        in_specs=[pl.BlockSpec(memory_space=pltpu.VMEM)] * len(operands),
        out_specs=pl.BlockSpec(memory_space=pl.ANY),
        scratch_shapes=[pltpu.VMEM((2, plan.dp, 16, LANES), jnp.float32), *plan.scratch()],
        compiler_params=pltpu.CompilerParams(
            collective_id=0, has_side_effects=True, vmem_limit_bytes=64 << 20
        ),
        cost_estimate=pl.CostEstimate(flops=10**10, bytes_accessed=20 * 10**6, transcendentals=0),
    )(*operands)


class Block:
    def __init__(self, tokens, length, width, hidden, kv_width, ctx):
        self.tokens, self.length, self.width, self.hidden = tokens, length, width, hidden
        self.kv_width, self.ctx = kv_width, ctx
        self.kv_heads = kv_width // HEAD_DIM
        self.group = width // kv_width
        self.step = 512


def dot(one, other, over=(1, 0)):
    return lax.dot_general(
        one, other, (((over[0],), (over[1],)), ((), ())), preferred_element_type=jnp.float32
    )


def fold_rows(values, combine):
    return combine(values.reshape(values.shape[0] // 8, 8, values.shape[1]), 0)


def norm(values):
    return lax.rsqrt(jnp.mean(values * values, 0, keepdims=True) + epsilon)


def app_tokens(size, app):
    return slice(app * size.tokens, (app + 1) * size.tokens)


def head_rows(size, g, h):
    return pl.ds(pl.multiple_of((g * size.group + h) * HEAD_DIM, HEAD_DIM), HEAD_DIM)


def wide_gain(env, which):
    return jnp.concatenate([env.columns[which]] * (env.size.tokens // LANES), 1)


def spread_columns(size, gains, columns):
    for which in range(2):
        for start in range(0, size.width, LANES):
            rows = min(LANES, size.width - start)
            tile = jnp.broadcast_to(gains[which : which + 1, start : start + LANES], (LANES, LANES))
            columns[which, start : start + rows, :] = tile.T[:rows]


def norm_back(env, values, which, grad_normed):
    size = env.size
    inverse = norm(values)
    product = grad_normed * values * inverse
    folded = product[:, :LANES]
    for start in range(LANES, size.tokens, LANES):
        folded = folded + product[:, start : start + LANES]
    for start in range(0, size.width, LANES):
        stop = min(start + LANES, size.width)
        part = folded[start:stop]
        if stop - start < LANES:
            part = jnp.concatenate([part, jnp.zeros((LANES - stop + start, LANES), jnp.float32)], 0)
        env.gain_sums[which : which + 1, start : start + LANES] += jnp.sum(part.T, 0, keepdims=True)
    weighted = grad_normed * wide_gain(env, which)
    cubed = inverse * inverse * inverse
    return inverse * weighted - values * (cubed * jnp.mean(weighted * values, 0, keepdims=True))


def rope(env, values, sign):
    half = HEAD_DIM // 2
    cos, sine = env.cos_q[...], env.sin_q[...] * sign
    out = []
    for start in range(0, values.shape[0], HEAD_DIM):
        former = values[start : start + half]
        latter = values[start + half : start + HEAD_DIM]
        out += [former * cos - latter * sine, latter * cos + former * sine]
    return jnp.concatenate(out, 0)


def ffn_back(env, gate_ref, up_ref, rows, cols, wd, wg, wu):
    gate = gate_ref[rows, cols].astype(jnp.float32)
    upward = up_ref[rows, cols].astype(jnp.float32)
    sigmoid = 1.0 / (1.0 + jnp.exp(-gate))
    scaled = dot(env.natural[...], wd) * sigmoid
    grad_gate = (scaled * upward * (1.0 + gate * (1.0 - sigmoid))).astype(jnp.bfloat16)
    grad_up = (scaled * gate).astype(jnp.bfloat16)
    gate_ref[rows, cols] = grad_gate
    up_ref[rows, cols] = grad_up
    env.accum[...] += dot(wg, grad_gate, (1, 1)) + dot(wu, grad_up, (1, 1))


def middle_back(env, grad_low, mid):
    grad_middle = grad_low.astype(jnp.float32) + norm_back(env, mid, 1, env.accum[...])
    env.dmid[...] = grad_middle
    branch = grad_middle.astype(jnp.bfloat16)
    env.d_attn[1, : env.size.tokens, : env.size.width] = branch.T
    env.do_t[...] = dot(env.wo[...], branch).astype(jnp.bfloat16)


def grad_copy(env, g, k):
    owner = jnp.maximum(env.ctx - k, 0)
    rows = pl.ds(pl.multiple_of(owner * env.size.tokens, env.size.tokens), env.size.tokens)
    return pltpu.make_async_remote_copy(
        env.kv_send.at[g, rows], env.kv_recv.at[k - 1, g],
        env.sem_d.at[0, g, k - 1], env.sem_d.at[1, g, k - 1],
        device_id=(env.section, env.row, owner), device_id_type=MESH,
    )


def attend_back(env, at, g):
    size, low_type = env.size, jnp.bfloat16
    k_t = env.kv[g].T[:HEAD_DIM]
    sides = []
    for h in range(size.group):
        rows, cols = head_rows(size, g, h), slice(h * size.tokens, (h + 1) * size.tokens)
        query, grad_head = env.q_t[rows, :], env.do_t[rows, :]
        empty = jnp.zeros_like(query)
        query = jnp.concatenate([query, empty], 0)
        grad_pad = jnp.concatenate([empty, grad_head], 0)
        delta = jnp.sum(
            grad_head.astype(jnp.float32) * env.x_attn[1, rows, at].astype(jnp.float32),
            0, keepdims=True,
        )
        log_sum = env.lse[g, h : h + 1, :]
        for start in range(0, size.length, 256):
            keys_at = slice(start, start + 256)
            part = dot(env.kv[g, keys_at, :], query) * score_unit + env.bias[keys_at, :]
            chance = jnp.exp2(part - log_sum)
            env.chances[keys_at, cols] = chance.astype(low_type)
            change = dot(env.kv[g, keys_at, :], grad_pad) - delta
            env.grad_scores[keys_at, cols] = (chance * change).astype(low_type)
        sides.append(((query.astype(jnp.float32) * score_scale).astype(low_type), grad_pad))
        env.accum[rows, :] = dot(k_t, env.grad_scores[:, cols]) * score_scale
    small, grad_pad = (jnp.concatenate(side, 1) for side in zip(*sides))
    env.kv_send[g] = (
        dot(env.grad_scores[...], small, (1, 1)) + dot(env.chances[...], grad_pad, (1, 1))
    ).astype(low_type)
    for k in range(1, size.ctx):
        @pl.when(env.ctx - k >= 0)
        def _():
            grad_copy(env, g, k).start()


def project_back(env):
    size, low_type = env.size, jnp.bfloat16
    tokens, width = size.tokens, size.width
    for start in range(0, width, 2 * LANES):
        stop = min(start + 2 * LANES, width)
        tile = rope(env, env.accum[start:stop, :], -1.0).astype(low_type)
        env.natural[:, start:stop] = tile.T
        env.do_t[start:stop, :] = tile
    env.d_attn[0, :tokens, :width] = env.natural[...]
    own_rows = pl.ds(pl.multiple_of(env.ctx * tokens, tokens), tokens)
    pairs = [[], []]
    for g in range(size.kv_heads):
        tile = env.kv_send[g, own_rows, :].astype(jnp.float32)
        for k in range(1, size.ctx):
            @pl.when(env.ctx + k < size.ctx)
            def _():
                grad_copy(env, g, k).wait_recv()
            tile = tile + jnp.where(
                env.ctx + k < size.ctx, env.kv_recv[k - 1, g].astype(jnp.float32), 0.0
            )
        tile = tile.T
        pairs[0].append(rope(env, tile[:HEAD_DIM], -1.0).astype(low_type))
        pairs[1].append(tile[HEAD_DIM:].astype(low_type))
    spare = env.d_pair.shape[2] - size.kv_width
    for half in range(2):
        pairs[half] = jnp.concatenate(pairs[half], 0)
        env.d_pair[half, :tokens, :] = jnp.concatenate(
            [jnp.zeros((spare, tokens), low_type), pairs[half]], 0
        ).T
    grad_normed = (
        dot(env.wq[...], env.do_t[...])
        + dot(env.wk[...], pairs[0], (0, 0))
        + dot(env.wv[...], pairs[1], (0, 0))
    )
    return env.dmid[...] + norm_back(env, env.x[...].astype(jnp.float32), 0, grad_normed)


def drain_grad_copies(env):
    def one(g, carry):
        for k in range(1, env.size.ctx):
            @pl.when(env.ctx - k >= 0)
            def _():
                grad_copy(env, g, k).wait_send()
        return carry

    lax.fori_loop(0, env.size.kv_heads, one, 0)


def front_kernel(
    size, inputs, cotangent, segments, cos_in, sin_in, gains,
    wq_in, wk_in, wv_in, wo_in, wg_in, wu_in, wd_in,
    acts, n2_out, df_out, inner_out, attn_out, d_attn_out, d_pair_out, d_ffn_out,
    mid_out, q_out, kv_out, lse_out, bias_out, gain_out,
    wq, wk, wv, wo, wg, wu, wd, n2_t, df_t, inner, x_attn, d_attn, d_pair, d_ffn, gain_sums,
    cos_q, sin_q, columns, xin, cot, mid, q_t,
    kv, kv_send, kv_recv, lse, do_t, bias, accum, dmid, natural, scores, chances, grad_scores,
    sem_w, sem_k, sem_d, sem_e, sem_o,
):
    tokens, ctx_count, groups, group = size.tokens, size.ctx, size.kv_heads, size.group
    width, low_type, full = size.width, jnp.bfloat16, jnp.float32
    section, row, ctx = (lax.axis_index(name) for name in ("section", "dp", "ctx"))
    mate = (1 - section, row, ctx)
    own_rows = pl.ds(pl.multiple_of(ctx * tokens, tokens), tokens)
    env = types.SimpleNamespace(
        size=size, section=section, row=row, ctx=ctx, columns=columns, gain_sums=gain_sums,
        cos_q=cos_q, sin_q=sin_q, natural=natural, accum=accum, dmid=dmid, do_t=do_t,
        d_attn=d_attn, d_pair=d_pair, x_attn=x_attn, bias=bias, chances=chances,
        grad_scores=grad_scores, kv=kv.at[1], q_t=q_t.at[1], lse=lse.at[1], x=xin.at[1],
        kv_send=kv_send, kv_recv=kv_recv, sem_d=sem_d, wq=wq, wk=wk, wv=wv, wo=wo,
    )
    loads = [
        pltpu.make_async_copy(source, target, sem_w.at[number])
        for number, (source, target) in enumerate((
            (inputs.at[section], xin.at[0]), (cos_in.at[:, own_rows], cos_q),
            (sin_in.at[:, own_rows], sin_q), (wk_in, wk), (wv_in, wv), (wq_in, wq), (wo_in, wo),
            (wg_in, wg), (wu_in, wu), (wd_in, wd), (cotangent.at[section], cot),
        ))
    ]
    for load in loads:
        load.start()
    stores = []

    def store(source, target):
        copy = pltpu.make_async_copy(source, target, sem_o.at[len(stores)])
        copy.start()
        stores.append(copy)

    barrier = pltpu.get_barrier_semaphore()
    friends = [mate] + [(section, row, lax.rem(ctx + k, ctx_count)) for k in range(1, ctx_count)]
    for friend in friends:
        pl.semaphore_signal(barrier, 1, device_id=friend, device_id_type=MESH)
    spread_columns(size, gains, columns)
    query_seg = segments[section, :, own_rows].astype(full)
    query_pos = lax.broadcasted_iota(jnp.int32, (1, tokens), 1) + ctx * tokens
    for start in range(0, size.length, LANES):
        key_seg = jnp.broadcast_to(
            segments[section, :, start : start + LANES].astype(full), (LANES, LANES)
        ).T
        key_pos = lax.broadcasted_iota(jnp.int32, (LANES, tokens), 0) + start
        key_seg = jnp.concatenate([key_seg] * (tokens // LANES), 1)
        allowed = (key_seg == query_seg) & (key_pos <= query_pos)
        bias[start : start + LANES, :] = jnp.where(allowed, 0.0, mask_floor)
    store(bias, bias_out)
    for k in range(1, ctx_count):
        @pl.when(ctx + k < ctx_count)
        def _():
            rows = pl.ds(pl.multiple_of((ctx + k) * tokens, tokens), tokens)
            for app in range(2):
                kv[app, :, rows, :] = jnp.zeros((groups, tokens, LANES), low_type)
    pl.semaphore_wait(barrier, len(friends))

    def kv_copy(app, g, k):
        return pltpu.make_async_remote_copy(
            kv.at[app, g, own_rows], kv.at[app, g, own_rows],
            sem_k.at[0, app, g, k - 1], sem_k.at[1, app, g, k - 1],
            device_id=(section, row, jnp.minimum(ctx + k, ctx_count - 1)), device_id_type=MESH,
        )

    def act_copy(app):
        return pltpu.make_async_remote_copy(
            xin.at[app + 1], acts.at[section], sem_e.at[0], sem_e.at[1],
            device_id=mate, device_id_type=MESH,
        )

    def act_store(app):
        return pltpu.make_async_copy(xin.at[app + 1], acts.at[section], sem_e.at[2])

    early = [
        pltpu.make_async_copy(source, target, sem_o.at[number])
        for number, (source, target) in enumerate((
            (q_t.at[0], q_out), (kv.at[0], kv_out), (lse.at[0], lse_out), (mid.at[0], mid_out)
        ))
    ]
    stores += early

    def forward(app, carry):
        at = pl.ds(pl.multiple_of(app * tokens, tokens), tokens)
        x = xin[app].astype(full)
        normed = (x * norm(x) * wide_gain(env, 0)).astype(low_type)
        x_attn[0, :, at] = normed

        @pl.when(app == 0)
        def _():
            for load in loads[1:6]:
                load.wait()

        keys = rope(env, dot(wk[...], normed), 1.0).astype(low_type)
        values = dot(wv[...], normed).astype(low_type)
        for g in range(groups):
            piece = slice(g * HEAD_DIM, (g + 1) * HEAD_DIM)
            kv[app, g, own_rows, :] = jnp.concatenate([keys[piece], values[piece]], 0).T
            for k in range(1, ctx_count):
                @pl.when(ctx + k < ctx_count)
                def _():
                    kv_copy(app, g, k).start()
        for start in range(0, width, 2 * LANES):
            stop = min(start + 2 * LANES, width)
            tile = dot(wq[:, start:stop], normed, (0, 0))
            q_t[app, start:stop, :] = rope(env, tile, 1.0).astype(low_type)

        def heads(g, carry):
            for k in range(1, ctx_count):
                @pl.when(ctx - k >= 0)
                def _():
                    kv_copy(app, g, k).wait_recv()
            v_t = kv[app, g].T[HEAD_DIM:]
            most, query = [None] * group, None
            for h in range(group + 1):
                if h < group:
                    query = q_t[app, head_rows(size, g, h), :]
                    query = jnp.concatenate([query, jnp.zeros_like(query)], 0)
                if h > 0:
                    largest = jnp.max(most[h - 1], 0, keepdims=True)
                    total = jnp.zeros((8, tokens), full)
                for start in range(0, size.length, LANES):
                    keys_at = slice(start, start + LANES)
                    if h < group:
                        part = dot(kv[app, g, keys_at, :], query) * score_unit + bias[keys_at, :]
                        scores[h, keys_at, :] = part
                        part = fold_rows(part, jnp.max)
                        most[h] = part if most[h] is None else jnp.maximum(most[h], part)
                    if h > 0:
                        for inside in range(start, start + LANES, 64):
                            at_once = slice(inside, inside + 64)
                            weights = jnp.exp2(scores[h - 1, at_once, :] - largest)
                            total = total + fold_rows(weights, jnp.sum)
                            chances[at_once, (h - 1) * tokens : h * tokens] = weights.astype(low_type)
                if h > 0:
                    total = jnp.sum(total, 0, keepdims=True)
                    out = dot(v_t, chances[:, (h - 1) * tokens : h * tokens]) / total
                    lse[app, g, h - 1 : h, :] = largest + jnp.log(total) * (1.0 / math.log(2.0))
                    x_attn[1, head_rows(size, g, h - 1), at] = out.astype(low_type)
            return carry

        lax.fori_loop(0, groups, heads, 0)

        @pl.when(app == 0)
        def _():
            for copy in early[:3]:
                copy.start()
            loads[6].wait()

        middle = xin[app].astype(full) + dot(wo[...], x_attn[1, :, at], (0, 0))
        mid[app] = middle
        ffn = (middle * norm(middle) * wide_gain(env, 1)).astype(low_type)
        n2_t[:, at] = ffn
        natural[...] = ffn.T

        @pl.when(app == 0)
        def _():
            early[3].start()
            for load in loads[7:10]:
                load.wait()

        accum[...] = middle

        def chunk(i, carry):
            cols = pl.ds(pl.multiple_of(i * size.step, size.step), size.step)
            gate = dot(natural[...], wg[:, cols])
            upward = dot(natural[...], wu[:, cols])
            hidden = (gate / (1.0 + jnp.exp(-gate)) * upward).astype(low_type)
            d_ffn[0, at, cols] = gate.astype(low_type)
            d_ffn[1, at, cols] = upward.astype(low_type)
            inner[at, cols] = hidden
            accum[...] += dot(wd[:, cols], hidden, (1, 1))
            return carry

        lax.fori_loop(0, size.hidden // size.step, chunk, 0)
        xin[app + 1] = accum[...].astype(low_type)

        @pl.when(section == app)
        def _():
            act_store(app).start()

        @pl.when(section != app)
        def _():
            act_copy(app).start()

        return carry

    gain_sums[...] = jnp.zeros_like(gain_sums)
    d_attn[:, :, width:] = jnp.zeros((2, tokens, d_attn.shape[2] - width), low_type)
    loads[0].wait()
    lax.fori_loop(0, 2, forward, 0)
    for source, target in ((x_attn, attn_out), (n2_t, n2_out), (inner, inner_out)):
        store(source, target)
    loads[10].wait()
    grad_low = cot[...]
    at = app_tokens(size, 1)
    df_t[:, at] = grad_low
    natural[...] = grad_low.T
    accum[...] = jnp.zeros_like(accum)

    def chunk(i, carry):
        cols = pl.ds(pl.multiple_of(i * size.step, size.step), size.step)
        ffn_back(env, d_ffn.at[0], d_ffn.at[1], at, cols, wd[:, cols], wg[:, cols], wu[:, cols])
        return carry

    lax.fori_loop(0, size.hidden // size.step, chunk, 0)
    store(d_ffn, d_ffn_out)
    middle_back(env, grad_low, mid[1])
    lax.fori_loop(0, groups, lambda g, carry: attend_back(env, at, g), None)
    df_t[:, app_tokens(size, 0)] = project_back(env).astype(low_type)
    for source, target in (
        (df_t, df_out), (d_attn, d_attn_out), (d_pair, d_pair_out), (gain_sums, gain_out)
    ):
        store(source, target)

    def drain(g, carry):
        for app in range(2):
            for k in range(1, ctx_count):
                @pl.when(ctx + k < ctx_count)
                def _():
                    kv_copy(app, g, k).wait_send()
        return carry

    lax.fori_loop(0, groups, drain, 0)
    drain_grad_copies(env)
    act_copy(0).wait()
    act_store(0).wait()
    for copy in stores:
        copy.wait()


def front_shapes(size, plan):
    tokens, width, hidden, groups = size.tokens, size.width, size.hidden, size.kv_heads
    low, full, both = jnp.bfloat16, jnp.float32, 2 * size.tokens
    return [
        ((width, both), low),
        ((width, both), low),
        ((both, hidden), low),
        ((2, width, both), low),
        ((2, tokens, plan.width_tiles * LANES), low),
        ((2, tokens, (plan.pair_tiles - plan.width_tiles + 1) * LANES), low),
        ((2, both, hidden), low),
        ((width, tokens), full),
        ((width, tokens), low),
        ((groups, size.length, LANES), low),
        ((groups, 8, tokens), full),
        ((size.length, tokens), full),
        ((8, plan.width_tiles * LANES), full),
    ]


def run_front(size, plan, *operands):
    tokens, width, hidden, groups = size.tokens, size.width, size.hidden, size.kv_heads
    low, full = jnp.bfloat16, jnp.float32
    vmem = pl.BlockSpec(memory_space=pltpu.VMEM)
    far = pl.BlockSpec(memory_space=pl.ANY)
    dma = pltpu.SemaphoreType.DMA
    others = max(size.ctx - 1, 1)
    kept = front_shapes(size, plan)
    shapes = [((2, width, tokens), low)] + kept
    scratch = [
        ((width, width), low),
        ((size.kv_width, width), low),
        ((size.kv_width, width), low),
        ((width, width), low),
        ((width, hidden), low),
        ((width, hidden), low),
        ((width, hidden), low),
        *kept[:7],
        kept[12],
        ((HEAD_DIM // 2, tokens), full),
        ((HEAD_DIM // 2, tokens), full),
        ((2, width, LANES), full),
        ((3, width, tokens), low),
        ((width, tokens), low),
        ((2, width, tokens), full),
        ((2, width, tokens), low),
        ((2, groups, size.length, LANES), low),
        ((groups, size.length, LANES), low),
        ((others, groups, tokens, LANES), low),
        ((2, groups, 8, tokens), full),
        ((width, tokens), low),
        ((size.length, tokens), full),
        ((width, tokens), full),
        ((width, tokens), full),
        ((tokens, width), low),
        ((size.group, size.length, tokens), full),
        ((size.length, size.group * tokens), low),
        ((size.length, size.group * tokens), low),
    ]
    return pl.pallas_call(
        functools.partial(front_kernel, size),
        out_shape=[jax.ShapeDtypeStruct(*shape) for shape in shapes],
        in_specs=[far, far, vmem, far, far, vmem] + [far] * 7,
        out_specs=[far] * len(shapes),
        scratch_shapes=[pltpu.VMEM(*shape) for shape in scratch] + [
            dma((11,)), dma((2, 2, groups, others)), dma((2, groups, others)), dma((3,)),
            dma((len(kept),)),
        ],
        compiler_params=pltpu.CompilerParams(
            collective_id=1, has_side_effects=True, vmem_limit_bytes=64 << 20
        ),
        cost_estimate=pl.CostEstimate(
            flops=3 * 10**10, bytes_accessed=40 * 10**6, transcendentals=3 * 10**7
        ),
    )(*operands)


def tail_kernel(
    size, plan, inputs, cos_in, sin_in, gains, n2_in, df_in, inner_in, attn_in, d_attn_in, d_pair_in,
    d_ffn_in, mid_in, q_in, kv_in, lse_in, bias_in, gain_in,
    wq_in, wk_in, wv_in, wo_in, wg_in, wu_in, wd_in,
    out, grads,
    n2_t, df_t, inner, x_attn, d_attn, d_pair, d_ffn, mid, q_t, kv, lse, bias, gain_sums,
    wq, wk, wv, wo, blocks, cos_q, sin_q, columns, xin, kv_send, kv_recv, do_t, accum, natural,
    chances, grad_scores, stage, extra, sem_l, sem_b, sem_d, sem_e, *refs,
):
    tokens, width, low_type, full = size.tokens, size.width, jnp.bfloat16, jnp.float32
    section, row, ctx = (lax.axis_index(name) for name in ("section", "dp", "ctx"))
    mate = (1 - section, row, ctx)
    own_rows = pl.ds(pl.multiple_of(ctx * tokens, tokens), tokens)
    first_ffn, ffn_count = plan.of("ffn")[0], len(plan.of("ffn"))
    env = types.SimpleNamespace(
        size=size, section=section, row=row, ctx=ctx, columns=columns, gain_sums=gain_sums,
        cos_q=cos_q, sin_q=sin_q, natural=natural, accum=accum, dmid=mid, do_t=do_t,
        d_attn=d_attn, d_pair=d_pair, x_attn=x_attn, bias=bias, chances=chances,
        grad_scores=grad_scores, kv=kv, q_t=q_t, lse=lse, x=xin,
        kv_send=kv_send, kv_recv=kv_recv, sem_d=sem_d, wq=wq, wk=wk, wv=wv, wo=wo,
    )
    sources = types.SimpleNamespace(
        ffn_x=n2_t, ffn_dy=lambda half, index, inside, cols: d_ffn[
            (index - first_ffn) % 3, half, :, inside : inside + cols.stop - cols.start
        ],
        down_x=df_t, down_dy=inner, attn_x=x_attn, attn_dy=d_attn, pair_dy=d_pair, extra=extra,
    )
    count = len(plan.chunks)
    turns = [step // 8 for step in TAIL_ORDER if step >= 0 and step % 8 == 0]
    reduction = Reduction(
        plan, lambda *place: shard_products(plan, *place, sources), out, refs, turns
    )

    def block_loads(i):
        cols = pl.ds(i * size.step, size.step)
        pairs = [(wd_in, 0), (wg_in, 1), (wu_in, 2)]
        return [
            pltpu.make_async_copy(weight.at[:, cols], blocks.at[i % 2, n], sem_b.at[i % 2, n])
            for weight, n in pairs
        ] + [pltpu.make_async_copy(d_ffn_in.at[:, :, cols], d_ffn.at[i % 3], sem_b.at[i % 2, 3])]

    later = pl.ds(tokens, tokens)
    names = (
        "df", "inner", "mid", "n2", "wo", "cos", "sin", "q", "kv", "lse", "bias", "attn", "d_attn",
        "d_pair", "x", "wq", "wk", "wv", "gain",
    )
    loads = dict(zip(names, (
        pltpu.make_async_copy(source, target, sem_l.at[number])
        for number, (source, target) in enumerate((
            (df_in, df_t), (inner_in, inner), (mid_in, mid), (n2_in, n2_t), (wo_in, wo),
            (cos_in.at[:, own_rows], cos_q), (sin_in.at[:, own_rows], sin_q),
            (q_in, q_t), (kv_in, kv), (lse_in, lse), (bias_in, bias), (attn_in, x_attn),
            (d_attn_in, d_attn.at[:, later]), (d_pair_in, d_pair.at[:, later]),
            (inputs.at[section], xin), (wq_in, wq), (wk_in, wk), (wv_in, wv), (gain_in, gain_sums),
        ))
    )))

    def ready(*names):
        for name in names:
            if name in loads:
                loads.pop(name).wait()

    for name in ("df", "inner"):
        loads[name].start()
    for load in block_loads(0):
        load.start()
    for name in names[2:]:
        loads[name].start()
    greet(reduction.friends())
    spread_columns(size, gains, columns)
    d_attn[:, :tokens, width:] = jnp.zeros((2, tokens, d_attn.shape[2] - width), low_type)

    back_copy = pltpu.make_async_remote_copy(
        stage, grads.at[section], sem_e.at[0], sem_e.at[1], device_id=mate, device_id_type=MESH
    )
    back_store = pltpu.make_async_copy(stage, grads.at[section], sem_e.at[2])

    def keep(app, value):
        stage[...] = value

        @pl.when(section == app)
        def _():
            back_store.start()

        @pl.when(section != app)
        def _():
            back_copy.start()

    def kept(app):
        @pl.when(section == app)
        def _():
            back_store.wait()

        @pl.when(section != app)
        def _():
            back_copy.wait_send()

    ready("df", "inner")
    grad_low = df_t[:, :tokens]
    keep(1, grad_low.astype(full))
    natural[...] = grad_low.T
    accum[...] = jnp.zeros_like(accum)

    def ffn_step(i):
        for load in block_loads(i):
            load.wait()
        if i + 1 < ffn_count:
            assert i < 2 or reduction.done[first_ffn + i - 2] >= 2
            for load in block_loads(i + 1):
                load.start()
        ffn_back(
            env, d_ffn.at[i % 3, 0], d_ffn.at[i % 3, 1], slice(0, tokens), slice(0, size.step),
            blocks[i % 2, 0], blocks[i % 2, 1], blocks[i % 2, 2],
        )

    taken = {-1: 0, -2: 0, -3: 0, -4: 0}
    for step in TAIL_ORDER:
        if step >= 0:
            if plan.chunks[step // 8][0] == "ffn" and step % 8 < 2:
                ready("n2")
                assert taken[-1] > step // 8 - first_ffn
            assert reduction.done[step // 8] == step % 8
            reduction.advance(step // 8)
            continue
        number, taken[step] = taken[step], taken[step] + 1
        if step == -1:
            ffn_step(number)
        elif step == -2:
            assert taken[-1] == ffn_count
            ready("mid", "wo", "gain")
            middle_back(env, grad_low, mid[...])
        elif step == -3:
            ready("q", "kv", "lse", "bias", "attn")
            lax.fori_loop(
                0, size.kv_heads, lambda g, carry: attend_back(env, app_tokens(size, 0), g), None
            )
        else:
            assert taken[-3] == 1
            ready("cos", "sin", "d_attn", "d_pair", "x", "wq", "wk", "wv")
            grad_in = project_back(env)
            kept(1)
            keep(0, grad_in)
            spread_gains(plan, gain_sums, extra)
    reduction.drain()
    drain_grad_copies(env)
    kept(0)
    back_copy.wait_recv()


def run_tail(size, plan, *operands):
    tokens, width, groups = size.tokens, size.width, size.kv_heads
    low, full, both = jnp.bfloat16, jnp.float32, 2 * size.tokens
    vmem = pl.BlockSpec(memory_space=pltpu.VMEM)
    far = pl.BlockSpec(memory_space=pl.ANY)
    dma = pltpu.SemaphoreType.DMA
    others = max(size.ctx - 1, 1)
    kept = front_shapes(size, plan)
    scratch = kept[:4] + [
        ((2, both, kept[4][0][2]), low),
        ((2, both, kept[5][0][2]), low),
        ((3, 2, both, size.step), low),
        *kept[7:],
        ((width, width), low),
        ((size.kv_width, width), low),
        ((size.kv_width, width), low),
        ((width, width), low),
        ((2, 3, width, size.step), low),
        ((HEAD_DIM // 2, tokens), full),
        ((HEAD_DIM // 2, tokens), full),
        ((2, width, LANES), full),
        ((width, tokens), low),
        ((groups, size.length, LANES), low),
        ((others, groups, tokens, LANES), low),
        ((width, tokens), low),
        ((width, tokens), full),
        ((tokens, width), low),
        ((size.length, size.group * tokens), low),
        ((size.length, size.group * tokens), low),
        ((width, tokens), full),
        ((2, plan.dp, 16, LANES), full),
    ]
    return pl.pallas_call(
        functools.partial(tail_kernel, size, plan),
        out_shape=[
            jax.ShapeDtypeStruct((2, plan.cy, plan.cx, plan.total, LANES), low),
            jax.ShapeDtypeStruct((2, width, tokens), full),
        ],
        in_specs=[far, far, far, vmem] + [far] * (len(operands) - 4),
        out_specs=[far, far],
        scratch_shapes=[pltpu.VMEM(*shape) for shape in scratch] + [
            dma((19,)), dma((2, 4)), dma((2, groups, others)), dma((3,)), *plan.scratch(),
        ],
        compiler_params=pltpu.CompilerParams(
            collective_id=2, has_side_effects=True, vmem_limit_bytes=64 << 20
        ),
        cost_estimate=pl.CostEstimate(
            flops=3 * 10**10, bytes_accessed=40 * 10**6, transcendentals=10**7
        ),
    )(*operands)


def rotary(length):
    half = HEAD_DIM // 2
    frequency = 10000.0 ** (-2.0 * np.arange(half) / HEAD_DIM)
    angles = frequency[:, None] * np.arange(length)[None, :]
    return np.asarray(np.cos(angles), np.float32), np.asarray(np.sin(angles), np.float32)


def unpack_kernel(plan, sizes, *refs):
    width, hidden, kv_width, through = sizes
    summed, refs = refs[0], refs[1:]
    (query, key_t, value_t, out, gate, up, down_t, *gains), rest = refs[through : through + 9], refs[through + 9 :]
    for source, target in zip(refs[:through], rest):
        target[...] = source[...]
    full, rows, half_width = jnp.float32, width // plan.dp, width // 2

    def tile(half, index, first, count):
        parts = [
            summed[half, p // plan.cx, p % plan.cx, pl.ds(plan.offsets[index] + place, size), :]
            for p, place, inside, size in plan.spans(index, first, count)
        ]
        return (parts[0] if len(parts) == 1 else jnp.concatenate(parts, 0)).astype(full)

    def put(target, at, cols, value):
        count = min(LANES, target.shape[1] - cols)
        target[at : at + value.shape[0], cols : cols + count] = value[:, :count]

    for index, (kind, start, tiles, height, piece, mode) in enumerate(plan.chunks):
        for half in range(2):
            for number in range(tiles):
                value = tile(half, index, number * height, height)
                cols = (start + number) * LANES
                if kind == "ffn":
                    put((gate, up)[half], 0, cols, value[:rows])
                elif kind == "down":
                    put(down_t, half * half_width, cols, value[:half_width])
                elif kind == "attn":
                    put((query, out)[half], 0, cols, value[:rows])
                else:
                    spare = plan.width_tiles * LANES - width
                    if number == 0:
                        put((query, out)[half], 0, width + spare - LANES, value[:rows])
                    pair_t = value.T[:, :rows]
                    first = number * LANES - LANES + spare
                    if first < 0:
                        pair_t = pair_t[LANES - spare :]
                        first = 0
                    (key_t, value_t)[half][first : first + pair_t.shape[0], :] = pair_t
            if kind == "mixed":
                lines = tile(half, index, tiles * height, 16)
                for number in range(-(-rows // LANES)):
                    put(gains[half], 0, number * LANES, lines[number : number + 1])


def unpack(plan, sizes, summed, *through):
    width, hidden, kv_width = sizes
    rows, full = width // plan.dp, jnp.float32
    shapes = [
        (rows, width), (kv_width, rows), (kv_width, rows), (rows, width),
        (rows, hidden), (rows, hidden), (width, hidden // plan.dp), (1, rows), (1, rows),
    ]
    vmem = pl.BlockSpec(memory_space=pltpu.VMEM)
    return pl.pallas_call(
        functools.partial(unpack_kernel, plan, (*sizes, len(through))),
        out_shape=[jax.ShapeDtypeStruct(shape, full) for shape in shapes]
        + [jax.ShapeDtypeStruct(value.shape, value.dtype) for value in through],
        in_specs=[vmem] * (1 + len(through)),
        out_specs=[vmem] * (len(shapes) + len(through)),
        compiler_params=pltpu.CompilerParams(vmem_limit_bytes=60 << 20),
    )(summed, *through)


def plain_block(
    plan, inputs, segment_ids, cotangent,
    gain_attn, w_query, w_key, w_value, w_out, gain_ffn, w_gate, w_up, w_down,
):
    micro_count, row_count, tok_local, model_width = inputs.shape
    kv_width = w_key.shape[1]
    group_size = HEADS // KV_HEADS
    section_index = lax.axis_index("section")
    on_first = section_index == 0
    ctx_index = lax.axis_index("ctx")
    first_token = ctx_index * tok_local
    query_pos = first_token + jnp.arange(tok_local, dtype=jnp.int32)
    halfway = HEAD_DIM // 2
    frequency = 10000.0 ** (-2.0 * jnp.arange(halfway, dtype=jnp.float32) / HEAD_DIM)
    angles = query_pos.astype(jnp.float32)[:, None] * frequency[None, :]
    cos_table = jnp.cos(angles)
    sine_table = jnp.sin(angles)
    w_pair = jnp.concatenate([w_key, w_value], 1)
    head_shape = (row_count, tok_local, KV_HEADS, group_size, HEAD_DIM)
    state_shape = (row_count, KV_HEADS, group_size, tok_local)

    def front(hidden, segments):
        query_seg = lax.dynamic_slice_in_dim(segments, first_token, tok_local, 1)
        normed, inverse = rms_forward(hidden, gain_attn)
        normed_low = normed.astype(jnp.bfloat16)
        query_pre = jnp.einsum(
            "rcd,de->rce", normed_low, w_query, preferred_element_type=jnp.float32
        )
        pair_pre = jnp.einsum("rcd,de->rce", normed_low, w_pair, preferred_element_type=jnp.float32)
        queries = rotate(
            query_pre.reshape(row_count, tok_local, HEADS, HEAD_DIM), cos_table, sine_table
        )
        queries = queries.astype(jnp.bfloat16).reshape(head_shape)
        key_rot = rotate(
            pair_pre[..., :kv_width].reshape(row_count, tok_local, KV_HEADS, HEAD_DIM),
            cos_table,
            sine_table,
        )
        packed = jnp.concatenate(
            [key_rot.reshape(row_count, tok_local, kv_width), pair_pre[..., kv_width:]], -1
        )
        return (query_seg, inverse, normed_low, queries, packed.astype(jnp.bfloat16))

    def attend_forward(queries, arrived, segments, query_seg):
        start_state = (
            jnp.full(state_shape, mask_floor, jnp.float32),
            jnp.zeros(state_shape, jnp.float32),
            jnp.zeros(state_shape + (HEAD_DIM,), jnp.float32),
        )
        piece_rows = arrived.shape[1]
        block_rows = math.gcd(piece_rows, 512)

        def fold_inner_step(step_index, loop_state):
            run_max, run_sum, run_acc = loop_state
            offset = step_index * block_rows
            key_block = lax.dynamic_slice_in_dim(arrived, step_index * block_rows, block_rows, 1)
            key_part = key_block[..., :kv_width].reshape(row_count, block_rows, KV_HEADS, HEAD_DIM)
            value_part = key_block[..., kv_width:].reshape(
                row_count, block_rows, KV_HEADS, HEAD_DIM
            )
            key_seg = lax.dynamic_slice_in_dim(segments, offset, block_rows, 1)
            scores, allowed = block_scores(queries, key_part, query_seg, key_seg, query_pos, offset)
            masked = jnp.where(allowed, scores, mask_floor)
            new_max = jnp.maximum(run_max, jnp.max(masked, -1))
            weights = jnp.where(allowed, jnp.exp(masked - new_max[..., None]), 0.0)
            rescale = jnp.exp(run_max - new_max)
            run_sum = run_sum * rescale + jnp.sum(weights, -1)
            run_acc = run_acc * rescale[..., None] + jnp.einsum(
                "rkgcn,rnkd->rkgcd",
                weights.astype(jnp.bfloat16),
                value_part,
                preferred_element_type=jnp.float32,
            )
            return (new_max, run_sum, run_acc)

        run_max, run_sum, run_acc = lax.fori_loop(
            0, piece_rows // block_rows, fold_inner_step, start_state
        )
        return (run_acc / run_sum[..., None], run_max + jnp.log(run_sum))

    def rear(hidden, attended):
        attn_low = (
            attended.transpose(0, 3, 1, 2, 4)
            .reshape(row_count, tok_local, HEADS * HEAD_DIM)
            .astype(jnp.bfloat16)
        )
        middle = hidden + jnp.einsum(
            "rce,ed->rcd", attn_low, w_out, preferred_element_type=jnp.float32
        )
        normed_ffn, inverse_ffn = rms_forward(middle, gain_ffn)
        ffn_low = normed_ffn.astype(jnp.bfloat16)
        gate_pre = jnp.einsum("rcd,df->rcf", ffn_low, w_gate, preferred_element_type=jnp.float32)
        upward = jnp.einsum("rcd,df->rcf", ffn_low, w_up, preferred_element_type=jnp.float32)
        inner_act = (jax.nn.silu(gate_pre) * upward).astype(jnp.bfloat16)
        output = middle + jnp.einsum(
            "rcf,fd->rcd", inner_act, w_down, preferred_element_type=jnp.float32
        )
        return (output, (attn_low, middle, inverse_ffn, ffn_low, gate_pre, upward, inner_act))


    assert micro_count == lax.axis_size("section")

    def mine(stacked):
        return lax.dynamic_index_in_dim(stacked, section_index, 0, keepdims=False)

    segments = mine(segment_ids)

    def forward(hidden):
        query_seg, inverse, normed_low, queries, packed = front(hidden, segments)
        arrived = lax.all_gather(packed, "ctx", axis=1, tiled=True)
        attended, log_sum = attend_forward(queries, arrived, segments, query_seg)
        output, saved = rear(hidden, attended)
        return output.astype(jnp.bfloat16), (
            hidden, query_seg, inverse, normed_low, queries, arrived, attended, log_sum, saved
        )

    def backward(grad_out, kept):
        (
            hidden,
            backward_query_seg,
            backward_inverse,
            backward_normed_low,
            backward_queries,
            piece_arrived,
            backward_attended,
            log_sum,
            saved,
        ) = kept
        (
            backward_attn_low,
            backward_middle,
            backward_inverse_ffn,
            backward_ffn_low,
            backward_gate_pre,
            backward_upward,
            backward_inner_act,
        ) = saved
        grad_low = grad_out.astype(jnp.bfloat16)
        grad_inner = jnp.einsum("rcd,fd->rcf", grad_low, w_down, preferred_element_type=jnp.float32)
        sigmoid = jax.nn.sigmoid(backward_gate_pre)
        grad_gate = (
            grad_inner * backward_upward * sigmoid * (1.0 + backward_gate_pre * (1.0 - sigmoid))
        ).astype(jnp.bfloat16)
        grad_up = (grad_inner * backward_gate_pre * sigmoid).astype(jnp.bfloat16)
        grad_norm_ffn = jnp.einsum(
            "rcf,df->rcd", grad_gate, w_gate, preferred_element_type=jnp.float32
        ) + jnp.einsum("rcf,df->rcd", grad_up, w_up, preferred_element_type=jnp.float32)
        grad_mid_norm, backward_sum_gain_ffn = rms_backward(
            backward_middle, gain_ffn, backward_inverse_ffn, grad_norm_ffn
        )
        grad_middle = grad_out + grad_mid_norm
        grad_branch = grad_middle.astype(jnp.bfloat16)
        grad_attn = jnp.einsum(
            "rcd,ed->rce", grad_branch, w_out, preferred_element_type=jnp.float32
        ).astype(jnp.bfloat16)
        grad_heads = grad_attn.reshape(head_shape).transpose(0, 2, 3, 1, 4)
        row_delta = jnp.sum(grad_heads.astype(jnp.float32) * backward_attended, -1)
        query_start = jnp.zeros(state_shape + (HEAD_DIM,), jnp.float32)
        fold_grad_query = query_start
        grad_query = fold_grad_query
        piece_piece_rows = piece_arrived.shape[1]
        piece_block_rows = math.gcd(piece_piece_rows, 512)

        def piece_inner_step(step_index, loop_state):
            grad_query, local_pair = loop_state
            inside = step_index * piece_block_rows
            key_block = lax.dynamic_slice_in_dim(piece_arrived, inside, piece_block_rows, 1)
            key_part = key_block[..., :kv_width].reshape(
                row_count, piece_block_rows, KV_HEADS, HEAD_DIM
            )
            value_part = key_block[..., kv_width:].reshape(
                row_count, piece_block_rows, KV_HEADS, HEAD_DIM
            )
            key_seg = lax.dynamic_slice_in_dim(segments, inside, piece_block_rows, 1)
            scores, allowed = block_scores(
                backward_queries, key_part, backward_query_seg, key_seg, query_pos, inside
            )
            chances = jnp.where(
                allowed, jnp.exp(jnp.where(allowed, scores, mask_floor) - log_sum[..., None]), 0.0
            )
            grad_chance = jnp.einsum(
                "rkgcd,rnkd->rkgcn", grad_heads, value_part, preferred_element_type=jnp.float32
            )
            grad_scores = (chances * (grad_chance - row_delta[..., None])).astype(jnp.bfloat16)
            grad_query = grad_query + score_scale * jnp.einsum(
                "rkgcn,rnkd->rkgcd", grad_scores, key_part, preferred_element_type=jnp.float32
            )
            grad_key = score_scale * jnp.einsum(
                "rkgcn,rckgd->rnkd",
                grad_scores,
                backward_queries,
                preferred_element_type=jnp.float32,
            )
            grad_value = jnp.einsum(
                "rkgcn,rkgcd->rnkd",
                chances.astype(jnp.bfloat16),
                grad_heads,
                preferred_element_type=jnp.float32,
            )
            update = jnp.concatenate(
                [
                    grad_key.reshape(row_count, piece_block_rows, kv_width),
                    grad_value.reshape(row_count, piece_block_rows, kv_width),
                ],
                -1,
            )
            current = lax.dynamic_slice_in_dim(local_pair, inside, piece_block_rows, 1)
            local_pair = lax.dynamic_update_slice_in_dim(local_pair, current + update, inside, 1)
            return (grad_query, local_pair)

        local_start = jnp.zeros((row_count, piece_piece_rows, 2 * kv_width), jnp.float32)
        fold_grad_query, fold_local_pair = lax.fori_loop(
            0, piece_piece_rows // piece_block_rows, piece_inner_step, (grad_query, local_start)
        )
        grad_pair = fold_local_pair
        grad_query, grad_pair = (fold_grad_query, grad_pair)
        pair_share = lax.psum_scatter(
            grad_pair.astype(jnp.bfloat16), "ctx", scatter_dimension=1, tiled=True
        ).astype(jnp.float32)
        query_tok = grad_query.transpose(0, 3, 1, 2, 4).reshape(
            row_count, tok_local, HEADS, HEAD_DIM
        )
        query_back = rotate(query_tok, cos_table, -sine_table).reshape(
            row_count, tok_local, HEADS * HEAD_DIM
        )
        query_back = query_back.astype(jnp.bfloat16)
        key_back = rotate(
            pair_share[..., :kv_width].reshape(row_count, tok_local, KV_HEADS, HEAD_DIM),
            cos_table,
            -sine_table,
        )
        pair_low = jnp.concatenate(
            [key_back.reshape(row_count, tok_local, kv_width), pair_share[..., kv_width:]], -1
        )
        pair_low = pair_low.astype(jnp.bfloat16)
        grad_normed = jnp.einsum(
            "rce,de->rcd", query_back, w_query, preferred_element_type=jnp.float32
        ) + jnp.einsum("rce,de->rcd", pair_low, w_pair, preferred_element_type=jnp.float32)
        grad_front, backward_sum_gain_attn = rms_backward(
            hidden, gain_attn, backward_inverse, grad_normed
        )
        factors = (
            backward_normed_low, backward_attn_low, backward_ffn_low, backward_inner_act,
            query_back, pair_low, grad_branch, grad_gate, grad_up, grad_low,
        )
        tick_grads = (backward_sum_gain_attn, backward_sum_gain_ffn, factors)
        return grad_middle + grad_front, tick_grads

    first_low, first_kept = forward(mine(inputs).astype(jnp.float32))
    second_low, second_kept = forward(first_low.astype(jnp.float32))
    grad_mid, second_grads = backward(mine(cotangent).astype(jnp.float32), second_kept)
    grad_mid_low = grad_mid.astype(jnp.bfloat16)
    grad_in, first_grads = backward(grad_mid_low.astype(jnp.float32), first_kept)
    dp = plan.dp

    def stacked(one, other):
        return jnp.concatenate([one, other], 1).reshape(-1, one.shape[-1])

    normed, attn, ffn, inner, d_query, d_pair, d_branch, d_gate, d_up, d_out = (
        stacked(one, other) for one, other in zip(first_grads[2], second_grads[2])
    )
    tokens = normed.shape[0]

    def sides(values, rows):
        cut = values.reshape(tokens, dp, -1)
        cut = jnp.pad(cut, ((0, 0), (0, 0), (0, rows - cut.shape[2])))
        return cut.transpose(1, 2, 0).reshape(dp * rows, tokens)

    inner = inner.reshape(tokens, dp, -1)
    inner = jnp.pad(
        inner, ((0, 0), (0, 0), (0, plan.down_tiles * LANES - inner.shape[2]))
    ).reshape(tokens, -1)
    spare = plan.width_tiles * LANES - model_width
    gain_sums = jnp.stack([one + other for one, other in zip(first_grads[:2], second_grads[:2])])
    gain_sums = jnp.pad(gain_sums, ((0, 6), (0, plan.width_tiles * LANES - model_width)))
    factors = (
        sides(ffn, plan.rows),
        jnp.stack([d_gate, d_up]),
        d_out.T,
        inner,
        jnp.stack([sides(normed, plan.rows), sides(attn, plan.rows)]),
        jnp.pad(jnp.stack([d_query, d_branch]), ((0, 0), (0, 0), (0, spare))),
        jnp.pad(
            jnp.stack([d_pair[:, :kv_width], d_pair[:, kv_width:]]),
            ((0, 0), (0, 0), (LANES - spare, 0)),
        ),
    )
    acts = (first_low, second_low)
    return acts, (grad_in, grad_mid_low), gain_sums, factors


def fused_block(
    size, plan, inputs, segment_ids, cotangent,
    gain_attn, w_query, w_key, w_value, w_out, gain_ffn, w_gate, w_up, w_down,
):
    cos_in, sin_in = rotary(size.length)
    gains = jnp.stack([gain_attn, gain_ffn]).astype(jnp.float32)
    gains = jnp.pad(gains, ((0, 0), (0, plan.width_tiles * LANES - size.width)))
    hidden = inputs[:, 0].swapaxes(1, 2)
    weights = (w_query, w_key.T, w_value.T, w_out, w_gate, w_up, w_down.T)
    acts, *kept = run_front(
        size, plan, hidden, cotangent[:, 0].swapaxes(1, 2), segment_ids, cos_in, sin_in, gains, *weights
    )
    summed, grads = run_tail(size, plan, hidden, cos_in, sin_in, gains, *kept, *weights)
    return acts, grads, summed


def body(
    inputs,
    segment_ids,
    cotangent,
    gain_attn,
    w_query,
    w_key,
    w_value,
    w_out,
    gain_ffn,
    w_gate,
    w_up,
    w_down,
):
    micro_count, row_count, tok_local, model_width = inputs.shape
    kv_width, hidden = w_key.shape[1], w_gate.shape[1]
    assert micro_count == lax.axis_size("section")
    on_first = lax.axis_index("section") == 0
    plan = Plan(lax.axis_size("dp"), lax.axis_size("ctx"), model_width, hidden, kv_width)
    dp = plan.dp
    size = Block(tok_local, segment_ids.shape[2], model_width, hidden, kv_width, plan.ctx)
    fits = (
        row_count == 1
        and size.length <= 1024
        and tok_local % LANES == 0
        and plan.rows * dp == model_width
        and plan.down_tiles * LANES * dp == hidden
        and len(plan.chunks) == 11
    )
    params = (gain_attn, w_query, w_key, w_value, w_out, gain_ffn, w_gate, w_up, w_down)
    if fits:
        acts, grads, summed = fused_block(size, plan, inputs, segment_ids, cotangent, *params)
    else:
        acts, grads, gain_sums, factors = plain_block(
            plan, inputs, segment_ids, cotangent, *params
        )
        summed = reduce_grads(plan, *factors, gain_sums)
    sizes = (model_width, hidden, kv_width)

    def exchange(for_first, for_last):
        kept = jnp.where(on_first, for_first, for_last)
        sent = jnp.where(on_first, for_last, for_first)
        got = lax.ppermute(sent, "section", [(0, 1), (1, 0)])
        return jnp.where(
            on_first, jnp.stack([kept, got]), jnp.stack([got, kept])
        )

    def turned(values):
        return values[None, :, None].swapaxes(3, 4)

    if fits:
        *parts, acts, grads = unpack(plan, sizes, summed, acts, grads)
        activations, input_grads = turned(acts), turned(grads)
    else:
        parts = unpack(plan, sizes, summed)
        activations = exchange(*acts)[None]
        input_grads = exchange(grads[0].astype(jnp.bfloat16), grads[1]).astype(jnp.float32)[None]
    query, key_t, value_t, out, gate, up, down_t, gain_one, gain_two = parts
    return (
        activations,
        input_grads,
        gain_one.reshape(-1),
        query,
        key_t.T,
        value_t.T,
        out,
        gain_two.reshape(-1),
        gate,
        up,
        down_t.T,
    )


def solution(mesh):
    placed = (
        P(None, "dp", "ctx", None),
        P(None, "dp", None),
        P(None, "dp", "ctx", None),
        P(),
        P(),
        P(),
        P(),
        P(),
        P(),
        P(),
        P(),
        P(),
    )
    return jax.shard_map(
        body,
        mesh=mesh,
        in_specs=placed,
        out_specs=(
            P("section", None, "dp", "ctx", None),
            P("section", None, "dp", "ctx", None),
            P("dp"),
            P("dp", None),
            P("dp", None),
            P("dp", None),
            P("dp", None),
            P("dp"),
            P("dp", None),
            P("dp", None),
            P("dp", None),
        ),
        check_vma=False,
    )
```

```python
import functools
import math
import types

import jax
import jax.numpy as jnp
import numpy as np
from jax import lax
from jax.experimental import pallas as pl
from jax.experimental.pallas import tpu as pltpu
from jax.sharding import PartitionSpec as P

HEADS = 15
KV_HEADS = 5
HEAD_DIM = 64
LANES = 128
Z_CHUNKS = 3
Z_LAG = 2
OWN_SLOTS = 8
PARTNER_SLOTS = 3
MESH = pl.DeviceIdType.MESH


epsilon = 1e-05
score_scale = 0.125
score_unit = score_scale / math.log(2.0)
mask_floor = -1e30


def rms_forward(values, gain_vec):
    inverse = lax.rsqrt(jnp.mean(values * values, -1, keepdims=True) + epsilon)
    return (values * inverse * gain_vec, inverse)


def rms_backward(values, gain_vec, inverse, grad_normed):
    weighted = grad_normed * gain_vec
    grad_gain = jnp.sum(grad_normed * values * inverse, axis=(0, 1))
    cubed = inverse * inverse * inverse
    grad_values = inverse * weighted - values * cubed * jnp.mean(
        weighted * values, -1, keepdims=True
    )
    return (grad_values, grad_gain)


def rotate(values, cos_table, sine_table):
    halfway = values.shape[-1] // 2
    former = values[..., :halfway]
    latter = values[..., halfway:]
    cos_part = cos_table[None, :, None, :]
    sine_part = sine_table[None, :, None, :]
    return jnp.concatenate(
        [former * cos_part - latter * sine_part, latter * cos_part + former * sine_part], -1
    )


def block_scores(queries, key_part, query_seg, key_seg, query_pos, offset):
    block_rows = key_part.shape[1]
    scores = (
        jnp.einsum("rckgd,rnkd->rkgcn", queries, key_part, preferred_element_type=jnp.float32)
        * score_scale
    )
    key_pos = offset + jnp.arange(block_rows, dtype=jnp.int32)
    allowed = (query_seg[:, :, None] == key_seg[:, None, :]) & (
        key_pos[None, None, :] <= query_pos[None, :, None]
    )
    return (scores, allowed[:, None, None, :, :])


def up_to(value, step):
    return -(-value // step) * step


TAIL_ORDER = (
    0, 8, -1, 24, -1, 1, 16, 9, 25, 32, -1, 40, 17, 33, -1, 41, -1, -2, 26, -3,
    48, 2, 49, 56, -4, 3, 42, 4, 57, 64, 34, 58, 10, 72, 43, 27, 18, 65, 19, 11,
    59, 50, 20, 12, 35, 73, 66, 21, 51, 28, 44, 80, 81, 74, 5, 60, 67, 29, 75, 82,
    30, 52, 13, 36, 83, 61, 53, 22, 68, 45, 31, 76, 69, 84, 54, 62, 37, 46, 23, 77,
    6, 85, 70, 38, 63, 14, 78, 86, 39, 55, 71, 47, 15, 7, 79, 87,
)


class Plan:
    def __init__(self, dp, ctx, width, hidden, kv_width):
        self.dp, self.ctx = dp, ctx
        self.cx = 1 << (ctx.bit_length() // 2) if ctx & (ctx - 1) == 0 else ctx
        self.cy = ctx // self.cx
        self.low = max(dp // 2, 1)
        self.shard = width // dp
        self.rows = up_to(width // dp, 16)
        self.down_rows = up_to(width // 2, 16)
        self.down_tiles = up_to(hidden // dp, LANES) // LANES
        self.up_tiles = hidden // LANES
        self.width_tiles = up_to(width, LANES) // LANES
        self.pair_tiles = (width + kv_width) // LANES
        self.step = 4
        chunks = []
        for kind, count, rows, step in (
            ("down", self.down_tiles, self.down_rows, 2),
            ("ffn", self.up_tiles, self.rows, self.step),
            ("attn", self.width_tiles - 1, self.rows, 4),
            ("mixed", self.pair_tiles - self.width_tiles + 1, self.rows, 4),
        ):
            for start in range(0, count, step):
                tiles = min(step, count - start)
                extra = 16 if kind == "mixed" else 0
                piece = up_to(up_to(tiles * rows + extra, ctx) // ctx, 16)
                mode = "z" if len(chunks) < Z_CHUNKS else "xy"
                chunks.append((kind, start, tiles, rows, piece, mode))
        self.chunks = chunks
        self.offsets = [sum(c[4] for c in chunks[:i]) for i in range(len(chunks))]
        self.total = sum(c[4] for c in chunks)
        self.widest = max(c[4] for c in chunks)

    def of(self, kind):
        return [i for i, chunk in enumerate(self.chunks) if chunk[0] == kind]

    def spans(self, index, first, count):
        piece = self.chunks[index][4]
        out, done = [], 0
        while done < count:
            at = first + done
            size = min(count - done, piece - at % piece)
            out.append((at // piece, at % piece, done, size))
            done += size
        return out

    def scratch(self):
        dp, cy, cx, low = self.dp, self.cy, self.cx, self.low
        nx, ny, nz, high = max(cx - 1, 1), max(cy - 1, 1), max(dp - 1, 1), max(dp - low, 1)
        count = len(self.chunks)

        def buffer(*shape):
            return pltpu.VMEM((*shape, LANES), jnp.bfloat16)

        found = [
            buffer(2, dp, cy, cx, self.widest),
            buffer(PARTNER_SLOTS, dp, cy, cx, self.widest),
            buffer(OWN_SLOTS, dp, cy, cx, self.widest),
        ]
        for kind, start, tiles, rows, piece, mode in self.chunks:
            head = up_to(piece // 2, 16)
            rest = max(piece - head, 16)
            if mode == "xy":
                found += [
                    buffer(nz, piece), buffer(nx, low, cy, piece), buffer(ny, high, cx, piece),
                    buffer(nx, high, piece), buffer(ny, low, piece), buffer(piece),
                ]
            else:
                found += [
                    buffer(nz, cy, cx, piece), buffer(nx, cy, head), buffer(ny, cx, rest),
                    buffer(nx, rest), buffer(ny, head), buffer(piece),
                ]
        dma = pltpu.SemaphoreType.DMA
        return found + [
            dma((2, count)), dma((2, count, nx)), dma((2, count, ny)), dma((2, count, nx)),
            dma((2, count, ny)), dma((2, count, nz)), dma((2, count, nx)), dma((2, count, ny)),
            dma((2, count, nx)), dma((2, count, ny)), dma((2, count)), dma((count,)),
            pltpu.SemaphoreType.REGULAR,
        ]


class Reduction:
    def __init__(self, plan, products, out, refs, turns=None):
        self.plan, self.products, self.out = plan, products, out
        count = len(plan.chunks)
        self.turns = list(range(count)) if turns is None else turns
        self.sent, self.partner, self.own_ring = refs[:3]
        self.parts = [refs[3 + 6 * i : 9 + 6 * i] for i in range(count)]
        (
            self.sem_p, self.sem_x1, self.sem_y1, self.sem_x2, self.sem_y2, self.sem_z,
            self.sem_gx, self.sem_gy, self.sem_hx, self.sem_hy, self.sem_m, self.sem_o, self.credit,
        ) = refs[3 + 6 * count :]
        self.section, self.row, self.ctx = (
            lax.axis_index(name) for name in ("section", "dp", "ctx")
        )
        self.px, self.py = lax.rem(self.ctx, plan.cx), lax.div(self.ctx, plan.cx)
        self.mate = (1 - self.section, self.row, self.ctx)
        self.done = [0] * count

    def friends(self):
        plan = self.plan
        found = [self.mate]
        found += [(self.section, lax.rem(self.row + k, plan.dp), self.ctx) for k in range(1, plan.dp)]
        return found + [
            (self.section, self.row, lax.rem(self.ctx + k, plan.ctx)) for k in range(1, plan.ctx)
        ]

    def remote(self, source, target, sems, place, device):
        return pltpu.make_async_remote_copy(
            source, target, sems.at[(0, *place)], sems.at[(1, *place)],
            device_id=device, device_id_type=MESH,
        )

    def x_peers(self):
        for k in range(1, self.plan.cx):
            other = lax.rem(self.px + k, self.plan.cx)
            yield k - 1, other, (self.section, self.row, self.py * self.plan.cx + other)

    def y_peers(self):
        for k in range(1, self.plan.cy):
            other = lax.rem(self.py + k, self.plan.cy)
            yield k - 1, other, (self.section, self.row, other * self.plan.cx + self.px)

    def z_peers(self):
        for k in range(1, self.plan.dp):
            other = lax.rem(self.row + k, self.plan.dp)
            yield k - 1, other, (self.section, other, self.ctx)

    def turn(self, index):
        return self.turns.index(index)

    def own(self, index):
        return self.own_ring.at[self.turn(index) % OWN_SLOTS]

    def at(self, index):
        return pl.ds(self.plan.offsets[index], self.plan.chunks[index][4])

    def head(self, index):
        piece = self.plan.chunks[index][4]
        return up_to(piece // 2, 16)

    def partner_copy(self, index):
        rows = pl.ds(0, self.plan.chunks[index][4])
        return self.remote(
            self.sent.at[self.turn(index) % 2, :, :, :, rows],
            self.partner.at[self.turn(index) % PARTNER_SLOTS, :, :, :, rows],
            self.sem_p, (index,), self.mate,
        )

    def make_partner(self, index):
        turn, cx = self.turn(index), self.plan.cx
        if turn >= 2:
            self.partner_copy(self.turns[turn - 2]).wait_send()
        if turn >= PARTNER_SLOTS:
            pl.semaphore_wait(self.credit, 1)

        def finish(j, first, value):
            for p, place, inside, size in self.plan.spans(index, first, value.shape[0]):
                self.sent[turn % 2, j, p // cx, p % cx, place : place + size, :] = value[
                    inside : inside + size
                ].astype(jnp.bfloat16)

        self.products(index, 1 - self.section, finish)
        self.partner_copy(index).start()

    def make_own(self, index):
        turn = self.turn(index)
        assert turn < OWN_SLOTS or self.done[self.turns[turn - OWN_SLOTS]] > 4
        self.partner_copy(index).wait_recv()
        cx, slot, own = self.plan.cx, turn % PARTNER_SLOTS, self.own(index)

        def finish(j, first, value):
            for p, place, inside, size in self.plan.spans(index, first, value.shape[0]):
                rows = slice(place, place + size)
                other = self.partner[slot, j, p // cx, p % cx, rows, :].astype(jnp.float32)
                own[j, p // cx, p % cx, rows, :] = (
                    value[inside : inside + size] + other
                ).astype(jnp.bfloat16)

        self.products(index, self.section, finish)
        if turn + PARTNER_SLOTS < len(self.plan.chunks):
            pl.semaphore_signal(self.credit, 1, device_id=self.mate, device_id_type=MESH)
        self.start(self.z_copies(index) if self.is_z(index) else self.first_copies(index))

    def is_z(self, index):
        return self.plan.chunks[index][5] == "z"

    def start(self, copies):
        for copy in copies:
            copy.start()

    def wait(self, copies):
        for copy in copies:
            copy.wait()

    def z_copies(self, index):
        own, into = self.own(index), self.parts[index][0]
        piece = pl.ds(0, self.plan.chunks[index][4])
        found = []
        for slot, other, device in self.z_peers():
            if self.is_z(index):
                source = own.at[other, :, :, piece]
            else:
                source = own.at[other, self.py, self.px, piece]
            found.append(self.remote(source, into.at[slot], self.sem_z, (index, slot), device))
        return found

    def halves(self, index):
        plan, piece = self.plan, self.plan.chunks[index][4]
        if self.is_z(index):
            head = self.head(index)
            return (pl.ds(self.row, 1), pl.ds(0, head)), (pl.ds(self.row, 1), pl.ds(head, piece - head))
        rows = pl.ds(0, piece)
        return (pl.ds(0, plan.low), rows), (pl.ds(plan.low, plan.dp - plan.low), rows)

    def has_rest(self, index):
        if self.is_z(index):
            return self.plan.chunks[index][4] > self.head(index)
        return self.plan.dp > self.plan.low

    def first_copies(self, index):
        own = self.own(index)
        (j_x, rows_x), (j_y, rows_y) = self.halves(index)
        _, rx1, ry1, _, _, _ = self.parts[index]
        if self.is_z(index):
            j_x = j_y = self.row
        found = [
            self.remote(own.at[j_x, :, other, rows_x], rx1.at[slot], self.sem_x1, (index, slot), device)
            for slot, other, device in self.x_peers()
        ]
        if self.has_rest(index):
            found += [
                self.remote(
                    own.at[j_y, other, :, rows_y], ry1.at[slot], self.sem_y1, (index, slot), device
                )
                for slot, other, device in self.y_peers()
            ]
        return found

    def second_copies(self, index):
        own = self.own(index)
        (j_x, rows_x), (j_y, rows_y) = self.halves(index)
        _, _, _, rx2, ry2, _ = self.parts[index]
        if self.is_z(index):
            j_x = j_y = self.row
        found = [
            self.remote(
                own.at[j_x, other, self.px, rows_x], ry2.at[slot], self.sem_y2, (index, slot), device
            )
            for slot, other, device in self.y_peers()
        ]
        if self.has_rest(index):
            found += [
                self.remote(
                    own.at[j_y, self.py, other, rows_y], rx2.at[slot], self.sem_x2, (index, slot), device
                )
                for slot, other, device in self.x_peers()
            ]
        return found

    def add_all_z(self, index):
        plan, own, into = self.plan, self.own(index), self.parts[index][0]
        piece = slice(0, plan.chunks[index][4])
        self.wait(self.z_copies(index))
        for y in range(plan.cy):
            for x in range(plan.cx):
                total = own[self.row, y, x, piece, :].astype(jnp.float32)
                for k in range(plan.dp - 1):
                    total = total + into[k, y, x].astype(jnp.float32)
                own[self.row, y, x, piece, :] = total.astype(jnp.bfloat16)
        self.start(self.first_copies(index))

    def add_first(self, index):
        plan, own = self.plan, self.own(index)
        _, rx1, ry1, _, _, _ = self.parts[index]
        piece, is_z = plan.chunks[index][4], self.is_z(index)
        head = self.head(index)
        self.wait(self.first_copies(index))
        places = [(self.row, 0, 0)] if is_z else [(j, j, j - plan.low) for j in range(plan.dp)]
        for j, at_x, at_y in places:
            if is_z or at_x < plan.low:
                rows = slice(0, head) if is_z else slice(0, piece)
                for y in range(plan.cy):
                    total = own[j, y, self.px, rows, :].astype(jnp.float32)
                    for k in range(plan.cx - 1):
                        part = rx1[k, y] if is_z else rx1[k, at_x, y]
                        total = total + part.astype(jnp.float32)
                    own[j, y, self.px, rows, :] = total.astype(jnp.bfloat16)
            if (is_z and piece > head) or (not is_z and at_y >= 0):
                rows = slice(head, piece) if is_z else slice(0, piece)
                for x in range(plan.cx):
                    total = own[j, self.py, x, rows, :].astype(jnp.float32)
                    for k in range(plan.cy - 1):
                        part = ry1[k, x] if is_z else ry1[k, at_y, x]
                        total = total + part.astype(jnp.float32)
                    own[j, self.py, x, rows, :] = total.astype(jnp.bfloat16)
        self.start(self.second_copies(index))

    def add_second(self, index):
        plan, own = self.plan, self.own(index)
        _, _, _, rx2, ry2, _ = self.parts[index]
        piece = slice(0, plan.chunks[index][4])
        self.wait(self.second_copies(index))
        for j in range(plan.dp):
            total = own[j, self.py, self.px, piece, :].astype(jnp.float32)
            if j < plan.low:
                for k in range(plan.cy - 1):
                    total = total + ry2[k, j].astype(jnp.float32)
            else:
                for k in range(plan.cx - 1):
                    total = total + rx2[k, j - plan.low].astype(jnp.float32)
            own[j, self.py, self.px, piece, :] = total.astype(jnp.bfloat16)
        self.start(self.z_copies(index))

    def add_last(self, index):
        plan, own = self.plan, self.own(index)
        rz, _, _, rx2, ry2, final = self.parts[index]
        piece, head = plan.chunks[index][4], self.head(index)
        if self.is_z(index):
            self.wait(self.second_copies(index))
            total = own[self.row, self.py, self.px, 0:head, :].astype(jnp.float32)
            for k in range(plan.cy - 1):
                total = total + ry2[k].astype(jnp.float32)
            final[0:head, :] = total.astype(jnp.bfloat16)
            if piece > head:
                total = own[self.row, self.py, self.px, head:piece, :].astype(jnp.float32)
                for k in range(plan.cx - 1):
                    total = total + rx2[k].astype(jnp.float32)
                final[head:piece, :] = total.astype(jnp.bfloat16)
        else:
            self.wait(self.z_copies(index))
            total = own[self.row, self.py, self.px, 0:piece, :].astype(jnp.float32)
            for k in range(plan.dp - 1):
                total = total + rz[k].astype(jnp.float32)
            final[...] = total.astype(jnp.bfloat16)
        self.place_copy(index).start()
        self.start(self.gather_one(index))

    def place_copy(self, index):
        target = self.out.at[self.section, self.py, self.px, self.at(index)]
        return pltpu.make_async_copy(self.parts[index][5], target, self.sem_o.at[index])

    def gather_parts(self, index):
        offset, piece, head = self.plan.offsets[index], self.plan.chunks[index][4], self.head(index)
        return pl.ds(offset, head), pl.ds(offset + head, piece - head), piece > head

    def gather_one(self, index):
        final, out = self.parts[index][5], self.out
        rows_x, rows_y, rest = self.gather_parts(index)
        head, piece = self.head(index), self.plan.chunks[index][4]
        found = [
            self.remote(
                final.at[pl.ds(0, head)], out.at[self.section, self.py, self.px, rows_x],
                self.sem_gx, (index, slot), device,
            )
            for slot, other, device in self.x_peers()
        ]
        if rest:
            found += [
                self.remote(
                    final.at[pl.ds(head, piece - head)], out.at[self.section, self.py, self.px, rows_y],
                    self.sem_gy, (index, slot), device,
                )
                for slot, other, device in self.y_peers()
            ]
        return found

    def gather_two(self, index):
        out = self.out
        rows_x, rows_y, rest = self.gather_parts(index)
        found = []
        for slot, other, device in self.y_peers():
            region = out.at[self.section, self.py, :, rows_x]
            found.append(self.remote(region, region, self.sem_hy, (index, slot), device))
        if rest:
            for slot, other, device in self.x_peers():
                region = out.at[self.section, :, self.px, rows_y]
                found.append(self.remote(region, region, self.sem_hx, (index, slot), device))
        return found

    def gather_on(self, index):
        self.place_copy(index).wait()
        self.wait(self.gather_one(index))
        self.start(self.gather_two(index))

    def mate_copy(self, index):
        region = self.out.at[self.section, :, :, self.at(index)]
        return self.remote(region, region, self.sem_m, (index,), self.mate)

    def pass_on(self, index):
        self.wait(self.gather_two(index))
        self.mate_copy(index).start()

    def finish(self, index):
        self.mate_copy(index).wait()

    def stages(self, index):
        middle = (self.add_all_z, self.add_first) if self.is_z(index) else (self.add_first, self.add_second)
        return (
            self.make_partner, self.make_own, *middle, self.add_last, self.gather_on, self.pass_on, self.finish
        )

    def advance(self, index, upto=None):
        stages = self.stages(index)
        while self.done[index] < len(stages):
            if upto is not None and self.done[index] >= upto:
                return
            stages[self.done[index]](index)
            self.done[index] += 1
            if upto is None:
                return

    def drain(self):
        todo = []
        for index in range(len(self.done)):
            for stage in range(self.done[index], len(self.stages(index))):
                late = Z_LAG if self.is_z(index) and stage >= 2 else 0
                todo.append((index + stage + late, stage, index))
        for step, stage, index in sorted(todo):
            self.advance(index)
        for index in self.turns[-2:]:
            self.partner_copy(index).wait_send()


def greet(friends):
    barrier = pltpu.get_barrier_semaphore()
    for friend in friends:
        pl.semaphore_signal(barrier, 1, device_id=friend, device_id_type=MESH)
    pl.semaphore_wait(barrier, len(friends))


def shard_products(plan, index, half, finish, sources):
    kind, start, tiles, rows, piece, mode = plan.chunks[index]
    cols = slice(start * LANES, (start + tiles) * LANES)

    def shard(j, carry):
        own = pl.ds(pl.multiple_of(j * plan.rows, 16), plan.rows)
        if kind == "ffn":
            value = dot(sources.ffn_x[own, :], sources.ffn_dy(half, index, 0, cols))
        elif kind == "down":
            first = pl.multiple_of(j * (plan.down_tiles * LANES) + start * LANES, LANES)
            rows_of = pl.ds(pl.multiple_of(half * plan.down_rows, 16), plan.down_rows)
            value = dot(sources.down_x[rows_of, :], sources.down_dy[:, pl.ds(first, tiles * LANES)])
        elif kind == "attn":
            value = dot(sources.attn_x[half, own, :], sources.attn_dy[half, :, cols])
        else:
            value = dot(sources.attn_x[0, own, :], sources.pair_dy[half])
            last = plan.width_tiles - 1
            mixed = dot(sources.attn_x[half, own, :], sources.attn_dy[half, :, last * LANES :])
            value = jnp.concatenate([value[:, :LANES] + mixed, value[:, LANES:]], 1)
        for tile in range(tiles):
            finish(j, tile * rows, value[:, tile * LANES : (tile + 1) * LANES])
        if kind == "mixed":
            finish(j, tiles * rows, sources.extra[half, j])
        return carry

    lax.fori_loop(0, plan.dp, shard, 0)


def spread_gains(plan, gain_sums, extra):
    for half in range(2):
        for j in range(plan.dp):
            for number in range(-(-plan.shard // LANES)):
                start = j * plan.shard + number * LANES
                extra[half, j, number : number + 1, :] = gain_sums[
                    half : half + 1, start : start + LANES
                ]


def reduce_kernel(
    plan, ffn_x, ffn_dy, down_x, down_dy, attn_x, attn_dy, pair_dy, gain_sums, out, extra, *refs
):
    sources = types.SimpleNamespace(
        ffn_x=ffn_x, ffn_dy=lambda half, index, inside, cols: ffn_dy[half, :, cols],
        down_x=down_x, down_dy=down_dy,
        attn_x=attn_x, attn_dy=attn_dy, pair_dy=pair_dy, extra=extra,
    )
    reduction = Reduction(
        plan, lambda *place: shard_products(plan, *place, sources), out, refs
    )
    greet(reduction.friends())
    spread_gains(plan, gain_sums, extra)
    reduction.drain()


def reduce_grads(plan, *operands):
    return pl.pallas_call(
        functools.partial(reduce_kernel, plan),
        out_shape=jax.ShapeDtypeStruct((2, plan.cy, plan.cx, plan.total, LANES), jnp.bfloat16),
        in_specs=[pl.BlockSpec(memory_space=pltpu.VMEM)] * len(operands),
        out_specs=pl.BlockSpec(memory_space=pl.ANY),
        scratch_shapes=[pltpu.VMEM((2, plan.dp, 16, LANES), jnp.float32), *plan.scratch()],
        compiler_params=pltpu.CompilerParams(
            collective_id=0, has_side_effects=True, vmem_limit_bytes=64 << 20
        ),
        cost_estimate=pl.CostEstimate(flops=10**10, bytes_accessed=20 * 10**6, transcendentals=0),
    )(*operands)


class Block:
    def __init__(self, tokens, length, width, hidden, kv_width, ctx):
        self.tokens, self.length, self.width, self.hidden = tokens, length, width, hidden
        self.kv_width, self.ctx = kv_width, ctx
        self.kv_heads = kv_width // HEAD_DIM
        self.group = width // kv_width
        self.step = 512


def dot(one, other, over=(1, 0)):
    return lax.dot_general(
        one, other, (((over[0],), (over[1],)), ((), ())), preferred_element_type=jnp.float32
    )


def fold_rows(values, combine):
    return combine(values.reshape(values.shape[0] // 8, 8, values.shape[1]), 0)


def norm(values):
    return lax.rsqrt(jnp.mean(values * values, 0, keepdims=True) + epsilon)


def app_tokens(size, app):
    return slice(app * size.tokens, (app + 1) * size.tokens)


def head_rows(size, g, h):
    return pl.ds(pl.multiple_of((g * size.group + h) * HEAD_DIM, HEAD_DIM), HEAD_DIM)


def wide_gain(env, which):
    return jnp.concatenate([env.columns[which]] * (env.size.tokens // LANES), 1)


def spread_columns(size, gains, columns):
    for which, gain in enumerate(gains):
        for start in range(0, size.width, LANES):
            stop = min(start + LANES, size.width)
            part = gain[start:stop].astype(jnp.float32)[None]
            if stop - start < LANES:
                part = jnp.concatenate([part, jnp.zeros((1, LANES - stop + start), jnp.float32)], 1)
            tile = jnp.broadcast_to(part, (LANES, LANES))
            columns[which, start:stop, :] = tile.T[: stop - start]


def norm_back(env, values, which, grad_normed):
    size = env.size
    inverse = norm(values)
    product = grad_normed * values * inverse
    folded = product[:, :LANES]
    for start in range(LANES, size.tokens, LANES):
        folded = folded + product[:, start : start + LANES]
    for start in range(0, size.width, LANES):
        stop = min(start + LANES, size.width)
        part = folded[start:stop]
        if stop - start < LANES:
            part = jnp.concatenate([part, jnp.zeros((LANES - stop + start, LANES), jnp.float32)], 0)
        env.gain_sums[which : which + 1, start : start + LANES] += jnp.sum(part.T, 0, keepdims=True)
    weighted = grad_normed * wide_gain(env, which)
    cubed = inverse * inverse * inverse
    return inverse * weighted - values * (cubed * jnp.mean(weighted * values, 0, keepdims=True))


def rope(env, values, sign):
    half = HEAD_DIM // 2
    cos, sine = env.cos_q[...], env.sin_q[...] * sign
    out = []
    for start in range(0, values.shape[0], HEAD_DIM):
        former = values[start : start + half]
        latter = values[start + half : start + HEAD_DIM]
        out += [former * cos - latter * sine, latter * cos + former * sine]
    return jnp.concatenate(out, 0)


def ffn_back(env, gate_ref, up_ref, rows, cols, wd, wg, wu):
    gate = gate_ref[rows, cols].astype(jnp.float32)
    upward = up_ref[rows, cols].astype(jnp.float32)
    sigmoid = 1.0 / (1.0 + jnp.exp(-gate))
    scaled = dot(env.natural[...], wd) * sigmoid
    grad_gate = (scaled * upward * (1.0 + gate * (1.0 - sigmoid))).astype(jnp.bfloat16)
    grad_up = (scaled * gate).astype(jnp.bfloat16)
    gate_ref[rows, cols] = grad_gate
    up_ref[rows, cols] = grad_up
    env.accum[...] += dot(wg, grad_gate, (1, 1)) + dot(wu, grad_up, (1, 1))


def middle_back(env, grad_low, mid):
    grad_middle = grad_low.astype(jnp.float32) + norm_back(env, mid, 1, env.accum[...])
    env.dmid[...] = grad_middle
    branch = grad_middle.astype(jnp.bfloat16)
    env.d_attn[1, : env.size.tokens, : env.size.width] = branch.T
    env.do_t[...] = dot(env.wo[...], branch).astype(jnp.bfloat16)


def grad_copy(env, g, k):
    owner = jnp.maximum(env.ctx - k, 0)
    rows = pl.ds(pl.multiple_of(owner * env.size.tokens, env.size.tokens), env.size.tokens)
    return pltpu.make_async_remote_copy(
        env.kv_send.at[g, rows], env.kv_recv.at[k - 1, g],
        env.sem_d.at[0, g, k - 1], env.sem_d.at[1, g, k - 1],
        device_id=(env.section, env.row, owner), device_id_type=MESH,
    )


def attend_back(env, at, g):
    size, low_type = env.size, jnp.bfloat16
    k_t = env.kv[g].T[:HEAD_DIM]
    sides = []
    for h in range(size.group):
        rows, cols = head_rows(size, g, h), slice(h * size.tokens, (h + 1) * size.tokens)
        query, grad_head = env.q_t[rows, :], env.do_t[rows, :]
        empty = jnp.zeros_like(query)
        query = jnp.concatenate([query, empty], 0)
        grad_pad = jnp.concatenate([empty, grad_head], 0)
        delta = jnp.sum(
            grad_head.astype(jnp.float32) * env.x_attn[1, rows, at].astype(jnp.float32),
            0, keepdims=True,
        )
        log_sum = env.lse[g, h : h + 1, :]
        for start in range(0, size.length, 256):
            keys_at = slice(start, start + 256)
            part = dot(env.kv[g, keys_at, :], query) * score_unit + env.bias[keys_at, :]
            chance = jnp.exp2(part - log_sum)
            env.chances[keys_at, cols] = chance.astype(low_type)
            change = dot(env.kv[g, keys_at, :], grad_pad) - delta
            env.grad_scores[keys_at, cols] = (chance * change).astype(low_type)
        sides.append(((query.astype(jnp.float32) * score_scale).astype(low_type), grad_pad))
        env.accum[rows, :] = dot(k_t, env.grad_scores[:, cols]) * score_scale
    small, grad_pad = (jnp.concatenate(side, 1) for side in zip(*sides))
    env.kv_send[g] = (
        dot(env.grad_scores[...], small, (1, 1)) + dot(env.chances[...], grad_pad, (1, 1))
    ).astype(low_type)
    for k in range(1, size.ctx):
        @pl.when(env.ctx - k >= 0)
        def _():
            grad_copy(env, g, k).start()


def project_back(env):
    size, low_type = env.size, jnp.bfloat16
    tokens, width = size.tokens, size.width
    for start in range(0, width, 2 * LANES):
        stop = min(start + 2 * LANES, width)
        tile = rope(env, env.accum[start:stop, :], -1.0).astype(low_type)
        env.natural[:, start:stop] = tile.T
        env.do_t[start:stop, :] = tile
    env.d_attn[0, :tokens, :width] = env.natural[...]
    own_rows = pl.ds(pl.multiple_of(env.ctx * tokens, tokens), tokens)
    pairs = [[], []]
    for g in range(size.kv_heads):
        tile = env.kv_send[g, own_rows, :].astype(jnp.float32)
        for k in range(1, size.ctx):
            @pl.when(env.ctx + k < size.ctx)
            def _():
                grad_copy(env, g, k).wait_recv()
            tile = tile + jnp.where(
                env.ctx + k < size.ctx, env.kv_recv[k - 1, g].astype(jnp.float32), 0.0
            )
        tile = tile.T
        pairs[0].append(rope(env, tile[:HEAD_DIM], -1.0).astype(low_type))
        pairs[1].append(tile[HEAD_DIM:].astype(low_type))
    spare = env.d_pair.shape[2] - size.kv_width
    for half in range(2):
        pairs[half] = jnp.concatenate(pairs[half], 0)
        env.d_pair[half, :tokens, :] = jnp.concatenate(
            [jnp.zeros((spare, tokens), low_type), pairs[half]], 0
        ).T
    grad_normed = (
        dot(env.wq[...], env.do_t[...])
        + dot(env.wk[...], pairs[0], (0, 0))
        + dot(env.wv[...], pairs[1], (0, 0))
    )
    return env.dmid[...] + norm_back(env, env.x[...].astype(jnp.float32), 0, grad_normed)


def drain_grad_copies(env):
    def one(g, carry):
        for k in range(1, env.size.ctx):
            @pl.when(env.ctx - k >= 0)
            def _():
                grad_copy(env, g, k).wait_send()
        return carry

    lax.fori_loop(0, env.size.kv_heads, one, 0)


def front_kernel(
    size, inputs, cotangent, segments, cos_in, sin_in, gain_attn, gain_ffn,
    wq_in, wk_in, wv_in, wo_in, wg_in, wu_in, wd_in,
    acts, n2_out, df_out, inner_out, attn_out, d_attn_out, d_pair_out, d_ffn_out,
    mid_out, q_out, kv_out, lse_out, bias_out, gain_out,
    wq, wk, wv, wo, wg, wu, wd, n2_t, df_t, inner, x_attn, d_attn, d_pair, d_ffn, gain_sums,
    cos_q, sin_q, columns, xin, cot, mid, q_t,
    kv, kv_send, kv_recv, lse, do_t, bias, accum, dmid, natural, scores, chances, grad_scores,
    sem_w, sem_k, sem_d, sem_e, sem_o,
):
    tokens, ctx_count, groups, group = size.tokens, size.ctx, size.kv_heads, size.group
    width, low_type, full = size.width, jnp.bfloat16, jnp.float32
    section, row, ctx = (lax.axis_index(name) for name in ("section", "dp", "ctx"))
    mate = (1 - section, row, ctx)
    own_rows = pl.ds(pl.multiple_of(ctx * tokens, tokens), tokens)
    env = types.SimpleNamespace(
        size=size, section=section, row=row, ctx=ctx, columns=columns, gain_sums=gain_sums,
        cos_q=cos_q, sin_q=sin_q, natural=natural, accum=accum, dmid=dmid, do_t=do_t,
        d_attn=d_attn, d_pair=d_pair, x_attn=x_attn, bias=bias, chances=chances,
        grad_scores=grad_scores, kv=kv.at[1], q_t=q_t.at[1], lse=lse.at[1], x=xin.at[1],
        kv_send=kv_send, kv_recv=kv_recv, sem_d=sem_d, wq=wq, wk=wk, wv=wv, wo=wo,
    )
    loads = [
        pltpu.make_async_copy(source, target, sem_w.at[number])
        for number, (source, target) in enumerate((
            (inputs.at[section], xin.at[0]), (cos_in.at[:, own_rows], cos_q),
            (sin_in.at[:, own_rows], sin_q), (wk_in, wk), (wv_in, wv), (wq_in, wq), (wo_in, wo),
            (wg_in, wg), (wu_in, wu), (wd_in, wd), (cotangent.at[section], cot),
        ))
    ]
    for load in loads:
        load.start()
    stores = []

    def store(source, target):
        copy = pltpu.make_async_copy(source, target, sem_o.at[len(stores)])
        copy.start()
        stores.append(copy)

    barrier = pltpu.get_barrier_semaphore()
    friends = [mate] + [(section, row, lax.rem(ctx + k, ctx_count)) for k in range(1, ctx_count)]
    for friend in friends:
        pl.semaphore_signal(barrier, 1, device_id=friend, device_id_type=MESH)
    spread_columns(size, (gain_attn, gain_ffn), columns)
    query_seg = segments[section, :, own_rows].astype(full)
    query_pos = lax.broadcasted_iota(jnp.int32, (1, tokens), 1) + ctx * tokens
    for start in range(0, size.length, LANES):
        key_seg = jnp.broadcast_to(
            segments[section, :, start : start + LANES].astype(full), (LANES, LANES)
        ).T
        key_pos = lax.broadcasted_iota(jnp.int32, (LANES, tokens), 0) + start
        key_seg = jnp.concatenate([key_seg] * (tokens // LANES), 1)
        allowed = (key_seg == query_seg) & (key_pos <= query_pos)
        bias[start : start + LANES, :] = jnp.where(allowed, 0.0, mask_floor)
    store(bias, bias_out)
    for k in range(1, ctx_count):
        @pl.when(ctx + k < ctx_count)
        def _():
            rows = pl.ds(pl.multiple_of((ctx + k) * tokens, tokens), tokens)
            for app in range(2):
                kv[app, :, rows, :] = jnp.zeros((groups, tokens, LANES), low_type)
    pl.semaphore_wait(barrier, len(friends))

    def kv_copy(app, g, k):
        return pltpu.make_async_remote_copy(
            kv.at[app, g, own_rows], kv.at[app, g, own_rows],
            sem_k.at[0, app, g, k - 1], sem_k.at[1, app, g, k - 1],
            device_id=(section, row, jnp.minimum(ctx + k, ctx_count - 1)), device_id_type=MESH,
        )

    def act_copy(app):
        return pltpu.make_async_remote_copy(
            xin.at[app + 1], acts.at[section], sem_e.at[0], sem_e.at[1],
            device_id=mate, device_id_type=MESH,
        )

    def act_store(app):
        return pltpu.make_async_copy(xin.at[app + 1], acts.at[section], sem_e.at[2])

    early = [
        pltpu.make_async_copy(source, target, sem_o.at[number])
        for number, (source, target) in enumerate((
            (q_t.at[0], q_out), (kv.at[0], kv_out), (lse.at[0], lse_out), (mid.at[0], mid_out)
        ))
    ]
    stores += early

    def forward(app, carry):
        at = pl.ds(pl.multiple_of(app * tokens, tokens), tokens)
        x = xin[app].astype(full)
        normed = (x * norm(x) * wide_gain(env, 0)).astype(low_type)
        x_attn[0, :, at] = normed

        @pl.when(app == 0)
        def _():
            for load in loads[1:6]:
                load.wait()

        keys = rope(env, dot(wk[...], normed), 1.0).astype(low_type)
        values = dot(wv[...], normed).astype(low_type)
        for g in range(groups):
            piece = slice(g * HEAD_DIM, (g + 1) * HEAD_DIM)
            kv[app, g, own_rows, :] = jnp.concatenate([keys[piece], values[piece]], 0).T
            for k in range(1, ctx_count):
                @pl.when(ctx + k < ctx_count)
                def _():
                    kv_copy(app, g, k).start()
        for start in range(0, width, 2 * LANES):
            stop = min(start + 2 * LANES, width)
            tile = dot(wq[:, start:stop], normed, (0, 0))
            q_t[app, start:stop, :] = rope(env, tile, 1.0).astype(low_type)

        def heads(g, carry):
            for k in range(1, ctx_count):
                @pl.when(ctx - k >= 0)
                def _():
                    kv_copy(app, g, k).wait_recv()
            v_t = kv[app, g].T[HEAD_DIM:]
            most, query = [None] * group, None
            for h in range(group + 1):
                if h < group:
                    query = q_t[app, head_rows(size, g, h), :]
                    query = jnp.concatenate([query, jnp.zeros_like(query)], 0)
                if h > 0:
                    largest = jnp.max(most[h - 1], 0, keepdims=True)
                    total = jnp.zeros((8, tokens), full)
                for start in range(0, size.length, LANES):
                    keys_at = slice(start, start + LANES)
                    if h < group:
                        part = dot(kv[app, g, keys_at, :], query) * score_unit + bias[keys_at, :]
                        scores[h, keys_at, :] = part
                        part = fold_rows(part, jnp.max)
                        most[h] = part if most[h] is None else jnp.maximum(most[h], part)
                    if h > 0:
                        for inside in range(start, start + LANES, 64):
                            at_once = slice(inside, inside + 64)
                            weights = jnp.exp2(scores[h - 1, at_once, :] - largest)
                            total = total + fold_rows(weights, jnp.sum)
                            chances[at_once, (h - 1) * tokens : h * tokens] = weights.astype(low_type)
                if h > 0:
                    total = jnp.sum(total, 0, keepdims=True)
                    out = dot(v_t, chances[:, (h - 1) * tokens : h * tokens]) / total
                    lse[app, g, h - 1 : h, :] = largest + jnp.log(total) * (1.0 / math.log(2.0))
                    x_attn[1, head_rows(size, g, h - 1), at] = out.astype(low_type)
            return carry

        lax.fori_loop(0, groups, heads, 0)

        @pl.when(app == 0)
        def _():
            for copy in early[:3]:
                copy.start()
            loads[6].wait()

        middle = xin[app].astype(full) + dot(wo[...], x_attn[1, :, at], (0, 0))
        mid[app] = middle
        ffn = (middle * norm(middle) * wide_gain(env, 1)).astype(low_type)
        n2_t[:, at] = ffn
        natural[...] = ffn.T

        @pl.when(app == 0)
        def _():
            early[3].start()
            for load in loads[7:10]:
                load.wait()

        accum[...] = middle

        def chunk(i, carry):
            cols = pl.ds(pl.multiple_of(i * size.step, size.step), size.step)
            gate = dot(natural[...], wg[:, cols])
            upward = dot(natural[...], wu[:, cols])
            hidden = (gate / (1.0 + jnp.exp(-gate)) * upward).astype(low_type)
            d_ffn[0, at, cols] = gate.astype(low_type)
            d_ffn[1, at, cols] = upward.astype(low_type)
            inner[at, cols] = hidden
            accum[...] += dot(wd[:, cols], hidden, (1, 1))
            return carry

        lax.fori_loop(0, size.hidden // size.step, chunk, 0)
        xin[app + 1] = accum[...].astype(low_type)

        @pl.when(section == app)
        def _():
            act_store(app).start()

        @pl.when(section != app)
        def _():
            act_copy(app).start()

        return carry

    gain_sums[...] = jnp.zeros_like(gain_sums)
    d_attn[:, :, width:] = jnp.zeros((2, tokens, d_attn.shape[2] - width), low_type)
    loads[0].wait()
    lax.fori_loop(0, 2, forward, 0)
    for source, target in ((x_attn, attn_out), (n2_t, n2_out), (inner, inner_out)):
        store(source, target)
    loads[10].wait()
    grad_low = cot[...]
    at = app_tokens(size, 1)
    df_t[:, at] = grad_low
    natural[...] = grad_low.T
    accum[...] = jnp.zeros_like(accum)

    def chunk(i, carry):
        cols = pl.ds(pl.multiple_of(i * size.step, size.step), size.step)
        ffn_back(env, d_ffn.at[0], d_ffn.at[1], at, cols, wd[:, cols], wg[:, cols], wu[:, cols])
        return carry

    lax.fori_loop(0, size.hidden // size.step, chunk, 0)
    store(d_ffn, d_ffn_out)
    middle_back(env, grad_low, mid[1])
    lax.fori_loop(0, groups, lambda g, carry: attend_back(env, at, g), None)
    df_t[:, app_tokens(size, 0)] = project_back(env).astype(low_type)
    for source, target in (
        (df_t, df_out), (d_attn, d_attn_out), (d_pair, d_pair_out), (gain_sums, gain_out)
    ):
        store(source, target)

    def drain(g, carry):
        for app in range(2):
            for k in range(1, ctx_count):
                @pl.when(ctx + k < ctx_count)
                def _():
                    kv_copy(app, g, k).wait_send()
        return carry

    lax.fori_loop(0, groups, drain, 0)
    drain_grad_copies(env)
    act_copy(0).wait()
    act_store(0).wait()
    for copy in stores:
        copy.wait()


def front_shapes(size, plan):
    tokens, width, hidden, groups = size.tokens, size.width, size.hidden, size.kv_heads
    low, full, both = jnp.bfloat16, jnp.float32, 2 * size.tokens
    return [
        ((width, both), low),
        ((width, both), low),
        ((both, hidden), low),
        ((2, width, both), low),
        ((2, tokens, plan.width_tiles * LANES), low),
        ((2, tokens, (plan.pair_tiles - plan.width_tiles + 1) * LANES), low),
        ((2, both, hidden), low),
        ((width, tokens), full),
        ((width, tokens), low),
        ((groups, size.length, LANES), low),
        ((groups, 8, tokens), full),
        ((size.length, tokens), full),
        ((8, plan.width_tiles * LANES), full),
    ]


def run_front(size, plan, *operands):
    tokens, width, hidden, groups = size.tokens, size.width, size.hidden, size.kv_heads
    low, full = jnp.bfloat16, jnp.float32
    vmem = pl.BlockSpec(memory_space=pltpu.VMEM)
    far = pl.BlockSpec(memory_space=pl.ANY)
    dma = pltpu.SemaphoreType.DMA
    others = max(size.ctx - 1, 1)
    kept = front_shapes(size, plan)
    shapes = [((2, width, tokens), low)] + kept
    scratch = [
        ((width, width), low),
        ((size.kv_width, width), low),
        ((size.kv_width, width), low),
        ((width, width), low),
        ((width, hidden), low),
        ((width, hidden), low),
        ((width, hidden), low),
        *kept[:7],
        kept[12],
        ((HEAD_DIM // 2, tokens), full),
        ((HEAD_DIM // 2, tokens), full),
        ((2, width, LANES), full),
        ((3, width, tokens), low),
        ((width, tokens), low),
        ((2, width, tokens), full),
        ((2, width, tokens), low),
        ((2, groups, size.length, LANES), low),
        ((groups, size.length, LANES), low),
        ((others, groups, tokens, LANES), low),
        ((2, groups, 8, tokens), full),
        ((width, tokens), low),
        ((size.length, tokens), full),
        ((width, tokens), full),
        ((width, tokens), full),
        ((tokens, width), low),
        ((size.group, size.length, tokens), full),
        ((size.length, size.group * tokens), low),
        ((size.length, size.group * tokens), low),
    ]
    return pl.pallas_call(
        functools.partial(front_kernel, size),
        out_shape=[jax.ShapeDtypeStruct(*shape) for shape in shapes],
        in_specs=[far, far, vmem, far, far, vmem, vmem] + [far] * 7,
        out_specs=[far] * len(shapes),
        scratch_shapes=[pltpu.VMEM(*shape) for shape in scratch] + [
            dma((11,)), dma((2, 2, groups, others)), dma((2, groups, others)), dma((3,)),
            dma((len(kept),)),
        ],
        compiler_params=pltpu.CompilerParams(
            collective_id=1, has_side_effects=True, vmem_limit_bytes=64 << 20
        ),
        cost_estimate=pl.CostEstimate(
            flops=3 * 10**10, bytes_accessed=40 * 10**6, transcendentals=3 * 10**7
        ),
    )(*operands)


def tail_kernel(
    size, plan, inputs, cos_in, sin_in, gain_attn, gain_ffn, n2_in, df_in, inner_in, attn_in, d_attn_in, d_pair_in,
    d_ffn_in, mid_in, q_in, kv_in, lse_in, bias_in, gain_in,
    wq_in, wk_in, wv_in, wo_in, wg_in, wu_in, wd_in,
    out, grads,
    n2_t, df_t, inner, x_attn, d_attn, d_pair, d_ffn, mid, q_t, kv, lse, bias, gain_sums,
    wq, wk, wv, wo, blocks, cos_q, sin_q, columns, xin, kv_send, kv_recv, do_t, accum, natural,
    chances, grad_scores, stage, extra, sem_l, sem_b, sem_d, sem_e, *refs,
):
    tokens, width, low_type, full = size.tokens, size.width, jnp.bfloat16, jnp.float32
    section, row, ctx = (lax.axis_index(name) for name in ("section", "dp", "ctx"))
    mate = (1 - section, row, ctx)
    own_rows = pl.ds(pl.multiple_of(ctx * tokens, tokens), tokens)
    first_ffn, ffn_count = plan.of("ffn")[0], len(plan.of("ffn"))
    env = types.SimpleNamespace(
        size=size, section=section, row=row, ctx=ctx, columns=columns, gain_sums=gain_sums,
        cos_q=cos_q, sin_q=sin_q, natural=natural, accum=accum, dmid=mid, do_t=do_t,
        d_attn=d_attn, d_pair=d_pair, x_attn=x_attn, bias=bias, chances=chances,
        grad_scores=grad_scores, kv=kv, q_t=q_t, lse=lse, x=xin,
        kv_send=kv_send, kv_recv=kv_recv, sem_d=sem_d, wq=wq, wk=wk, wv=wv, wo=wo,
    )
    sources = types.SimpleNamespace(
        ffn_x=n2_t, ffn_dy=lambda half, index, inside, cols: d_ffn[
            (index - first_ffn) % 3, half, :, inside : inside + cols.stop - cols.start
        ],
        down_x=df_t, down_dy=inner, attn_x=x_attn, attn_dy=d_attn, pair_dy=d_pair, extra=extra,
    )
    count = len(plan.chunks)
    turns = [step // 8 for step in TAIL_ORDER if step >= 0 and step % 8 == 0]
    reduction = Reduction(
        plan, lambda *place: shard_products(plan, *place, sources), out, refs, turns
    )

    def block_loads(i):
        cols = pl.ds(i * size.step, size.step)
        pairs = [(wd_in, 0), (wg_in, 1), (wu_in, 2)]
        return [
            pltpu.make_async_copy(weight.at[:, cols], blocks.at[i % 2, n], sem_b.at[i % 2, n])
            for weight, n in pairs
        ] + [pltpu.make_async_copy(d_ffn_in.at[:, :, cols], d_ffn.at[i % 3], sem_b.at[i % 2, 3])]

    later = pl.ds(tokens, tokens)
    names = (
        "df", "inner", "mid", "n2", "wo", "cos", "sin", "q", "kv", "lse", "bias", "attn", "d_attn",
        "d_pair", "x", "wq", "wk", "wv", "gain",
    )
    loads = dict(zip(names, (
        pltpu.make_async_copy(source, target, sem_l.at[number])
        for number, (source, target) in enumerate((
            (df_in, df_t), (inner_in, inner), (mid_in, mid), (n2_in, n2_t), (wo_in, wo),
            (cos_in.at[:, own_rows], cos_q), (sin_in.at[:, own_rows], sin_q),
            (q_in, q_t), (kv_in, kv), (lse_in, lse), (bias_in, bias), (attn_in, x_attn),
            (d_attn_in, d_attn.at[:, later]), (d_pair_in, d_pair.at[:, later]),
            (inputs.at[section], xin), (wq_in, wq), (wk_in, wk), (wv_in, wv), (gain_in, gain_sums),
        ))
    )))

    def ready(*names):
        for name in names:
            if name in loads:
                loads.pop(name).wait()

    for name in ("df", "inner"):
        loads[name].start()
    for load in block_loads(0):
        load.start()
    for name in names[2:]:
        loads[name].start()
    greet(reduction.friends())
    spread_columns(size, (gain_attn, gain_ffn), columns)
    d_attn[:, :tokens, width:] = jnp.zeros((2, tokens, d_attn.shape[2] - width), low_type)

    back_copy = pltpu.make_async_remote_copy(
        stage, grads.at[section], sem_e.at[0], sem_e.at[1], device_id=mate, device_id_type=MESH
    )
    back_store = pltpu.make_async_copy(stage, grads.at[section], sem_e.at[2])

    def keep(app, value):
        stage[...] = value

        @pl.when(section == app)
        def _():
            back_store.start()

        @pl.when(section != app)
        def _():
            back_copy.start()

    def kept(app):
        @pl.when(section == app)
        def _():
            back_store.wait()

        @pl.when(section != app)
        def _():
            back_copy.wait_send()

    ready("df", "inner")
    grad_low = df_t[:, :tokens]
    keep(1, grad_low.astype(full))
    natural[...] = grad_low.T
    accum[...] = jnp.zeros_like(accum)

    def ffn_step(i):
        for load in block_loads(i):
            load.wait()
        if i + 1 < ffn_count:
            assert i < 2 or reduction.done[first_ffn + i - 2] >= 2
            for load in block_loads(i + 1):
                load.start()
        ffn_back(
            env, d_ffn.at[i % 3, 0], d_ffn.at[i % 3, 1], slice(0, tokens), slice(0, size.step),
            blocks[i % 2, 0], blocks[i % 2, 1], blocks[i % 2, 2],
        )

    taken = {-1: 0, -2: 0, -3: 0, -4: 0}
    for step in TAIL_ORDER:
        if step >= 0:
            if plan.chunks[step // 8][0] == "ffn" and step % 8 < 2:
                ready("n2")
                assert taken[-1] > step // 8 - first_ffn
            assert reduction.done[step // 8] == step % 8
            reduction.advance(step // 8)
            continue
        number, taken[step] = taken[step], taken[step] + 1
        if step == -1:
            ffn_step(number)
        elif step == -2:
            assert taken[-1] == ffn_count
            ready("mid", "wo", "gain")
            middle_back(env, grad_low, mid[...])
        elif step == -3:
            ready("q", "kv", "lse", "bias", "attn")
            lax.fori_loop(
                0, size.kv_heads, lambda g, carry: attend_back(env, app_tokens(size, 0), g), None
            )
        else:
            assert taken[-3] == 1
            ready("cos", "sin", "d_attn", "d_pair", "x", "wq", "wk", "wv")
            grad_in = project_back(env)
            kept(1)
            keep(0, grad_in)
            spread_gains(plan, gain_sums, extra)
    reduction.drain()
    drain_grad_copies(env)
    kept(0)
    back_copy.wait_recv()


def run_tail(size, plan, *operands):
    tokens, width, groups = size.tokens, size.width, size.kv_heads
    low, full, both = jnp.bfloat16, jnp.float32, 2 * size.tokens
    vmem = pl.BlockSpec(memory_space=pltpu.VMEM)
    far = pl.BlockSpec(memory_space=pl.ANY)
    dma = pltpu.SemaphoreType.DMA
    others = max(size.ctx - 1, 1)
    kept = front_shapes(size, plan)
    scratch = kept[:4] + [
        ((2, both, kept[4][0][2]), low),
        ((2, both, kept[5][0][2]), low),
        ((3, 2, both, size.step), low),
        *kept[7:],
        ((width, width), low),
        ((size.kv_width, width), low),
        ((size.kv_width, width), low),
        ((width, width), low),
        ((2, 3, width, size.step), low),
        ((HEAD_DIM // 2, tokens), full),
        ((HEAD_DIM // 2, tokens), full),
        ((2, width, LANES), full),
        ((width, tokens), low),
        ((groups, size.length, LANES), low),
        ((others, groups, tokens, LANES), low),
        ((width, tokens), low),
        ((width, tokens), full),
        ((tokens, width), low),
        ((size.length, size.group * tokens), low),
        ((size.length, size.group * tokens), low),
        ((width, tokens), full),
        ((2, plan.dp, 16, LANES), full),
    ]
    return pl.pallas_call(
        functools.partial(tail_kernel, size, plan),
        out_shape=[
            jax.ShapeDtypeStruct((2, plan.cy, plan.cx, plan.total, LANES), low),
            jax.ShapeDtypeStruct((2, width, tokens), full),
        ],
        in_specs=[far, far, far, vmem, vmem] + [far] * (len(operands) - 5),
        out_specs=[far, far],
        scratch_shapes=[pltpu.VMEM(*shape) for shape in scratch] + [
            dma((19,)), dma((2, 4)), dma((2, groups, others)), dma((3,)), *plan.scratch(),
        ],
        compiler_params=pltpu.CompilerParams(
            collective_id=2, has_side_effects=True, vmem_limit_bytes=64 << 20
        ),
        cost_estimate=pl.CostEstimate(
            flops=3 * 10**10, bytes_accessed=40 * 10**6, transcendentals=10**7
        ),
    )(*operands)


def rotary(length):
    half = HEAD_DIM // 2
    frequency = 10000.0 ** (-2.0 * np.arange(half) / HEAD_DIM)
    angles = frequency[:, None] * np.arange(length)[None, :]
    return np.asarray(np.cos(angles), np.float32), np.asarray(np.sin(angles), np.float32)


def unpack_kernel(plan, sizes, *refs):
    width, hidden, kv_width, through = sizes
    summed, refs = refs[0], refs[1:]
    (query, key_t, value_t, out, gate, up, down_t, *gains), rest = refs[through : through + 9], refs[through + 9 :]
    for source, target in zip(refs[:through], rest):
        target[...] = source[...]
    full, rows, half_width = jnp.float32, width // plan.dp, width // 2

    def tile(half, index, first, count):
        parts = [
            summed[half, p // plan.cx, p % plan.cx, pl.ds(plan.offsets[index] + place, size), :]
            for p, place, inside, size in plan.spans(index, first, count)
        ]
        return (parts[0] if len(parts) == 1 else jnp.concatenate(parts, 0)).astype(full)

    def put(target, at, cols, value):
        count = min(LANES, target.shape[1] - cols)
        target[at : at + value.shape[0], cols : cols + count] = value[:, :count]

    for index, (kind, start, tiles, height, piece, mode) in enumerate(plan.chunks):
        for half in range(2):
            for number in range(tiles):
                value = tile(half, index, number * height, height)
                cols = (start + number) * LANES
                if kind == "ffn":
                    put((gate, up)[half], 0, cols, value[:rows])
                elif kind == "down":
                    put(down_t, half * half_width, cols, value[:half_width])
                elif kind == "attn":
                    put((query, out)[half], 0, cols, value[:rows])
                else:
                    spare = plan.width_tiles * LANES - width
                    if number == 0:
                        put((query, out)[half], 0, width + spare - LANES, value[:rows])
                    pair_t = value.T[:, :rows]
                    first = number * LANES - LANES + spare
                    if first < 0:
                        pair_t = pair_t[LANES - spare :]
                        first = 0
                    (key_t, value_t)[half][first : first + pair_t.shape[0], :] = pair_t
            if kind == "mixed":
                lines = tile(half, index, tiles * height, 16)
                for number in range(-(-rows // LANES)):
                    put(gains[half], 0, number * LANES, lines[number : number + 1])


def unpack(plan, sizes, summed, *through):
    width, hidden, kv_width = sizes
    rows, full = width // plan.dp, jnp.float32
    shapes = [
        (rows, width), (kv_width, rows), (kv_width, rows), (rows, width),
        (rows, hidden), (rows, hidden), (width, hidden // plan.dp), (1, rows), (1, rows),
    ]
    vmem = pl.BlockSpec(memory_space=pltpu.VMEM)
    return pl.pallas_call(
        functools.partial(unpack_kernel, plan, (*sizes, len(through))),
        out_shape=[jax.ShapeDtypeStruct(shape, full) for shape in shapes]
        + [jax.ShapeDtypeStruct(value.shape, value.dtype) for value in through],
        in_specs=[vmem] * (1 + len(through)),
        out_specs=[vmem] * (len(shapes) + len(through)),
        compiler_params=pltpu.CompilerParams(vmem_limit_bytes=60 << 20),
    )(summed, *through)


def plain_block(
    plan, inputs, segment_ids, cotangent,
    gain_attn, w_query, w_key, w_value, w_out, gain_ffn, w_gate, w_up, w_down,
):
    micro_count, row_count, tok_local, model_width = inputs.shape
    kv_width = w_key.shape[1]
    group_size = HEADS // KV_HEADS
    section_index = lax.axis_index("section")
    on_first = section_index == 0
    ctx_index = lax.axis_index("ctx")
    first_token = ctx_index * tok_local
    query_pos = first_token + jnp.arange(tok_local, dtype=jnp.int32)
    halfway = HEAD_DIM // 2
    frequency = 10000.0 ** (-2.0 * jnp.arange(halfway, dtype=jnp.float32) / HEAD_DIM)
    angles = query_pos.astype(jnp.float32)[:, None] * frequency[None, :]
    cos_table = jnp.cos(angles)
    sine_table = jnp.sin(angles)
    w_pair = jnp.concatenate([w_key, w_value], 1)
    head_shape = (row_count, tok_local, KV_HEADS, group_size, HEAD_DIM)
    state_shape = (row_count, KV_HEADS, group_size, tok_local)

    def front(hidden, segments):
        query_seg = lax.dynamic_slice_in_dim(segments, first_token, tok_local, 1)
        normed, inverse = rms_forward(hidden, gain_attn)
        normed_low = normed.astype(jnp.bfloat16)
        query_pre = jnp.einsum(
            "rcd,de->rce", normed_low, w_query, preferred_element_type=jnp.float32
        )
        pair_pre = jnp.einsum("rcd,de->rce", normed_low, w_pair, preferred_element_type=jnp.float32)
        queries = rotate(
            query_pre.reshape(row_count, tok_local, HEADS, HEAD_DIM), cos_table, sine_table
        )
        queries = queries.astype(jnp.bfloat16).reshape(head_shape)
        key_rot = rotate(
            pair_pre[..., :kv_width].reshape(row_count, tok_local, KV_HEADS, HEAD_DIM),
            cos_table,
            sine_table,
        )
        packed = jnp.concatenate(
            [key_rot.reshape(row_count, tok_local, kv_width), pair_pre[..., kv_width:]], -1
        )
        return (query_seg, inverse, normed_low, queries, packed.astype(jnp.bfloat16))

    def attend_forward(queries, arrived, segments, query_seg):
        start_state = (
            jnp.full(state_shape, mask_floor, jnp.float32),
            jnp.zeros(state_shape, jnp.float32),
            jnp.zeros(state_shape + (HEAD_DIM,), jnp.float32),
        )
        piece_rows = arrived.shape[1]
        block_rows = math.gcd(piece_rows, 512)

        def fold_inner_step(step_index, loop_state):
            run_max, run_sum, run_acc = loop_state
            offset = step_index * block_rows
            key_block = lax.dynamic_slice_in_dim(arrived, step_index * block_rows, block_rows, 1)
            key_part = key_block[..., :kv_width].reshape(row_count, block_rows, KV_HEADS, HEAD_DIM)
            value_part = key_block[..., kv_width:].reshape(
                row_count, block_rows, KV_HEADS, HEAD_DIM
            )
            key_seg = lax.dynamic_slice_in_dim(segments, offset, block_rows, 1)
            scores, allowed = block_scores(queries, key_part, query_seg, key_seg, query_pos, offset)
            masked = jnp.where(allowed, scores, mask_floor)
            new_max = jnp.maximum(run_max, jnp.max(masked, -1))
            weights = jnp.where(allowed, jnp.exp(masked - new_max[..., None]), 0.0)
            rescale = jnp.exp(run_max - new_max)
            run_sum = run_sum * rescale + jnp.sum(weights, -1)
            run_acc = run_acc * rescale[..., None] + jnp.einsum(
                "rkgcn,rnkd->rkgcd",
                weights.astype(jnp.bfloat16),
                value_part,
                preferred_element_type=jnp.float32,
            )
            return (new_max, run_sum, run_acc)

        run_max, run_sum, run_acc = lax.fori_loop(
            0, piece_rows // block_rows, fold_inner_step, start_state
        )
        return (run_acc / run_sum[..., None], run_max + jnp.log(run_sum))

    def rear(hidden, attended):
        attn_low = (
            attended.transpose(0, 3, 1, 2, 4)
            .reshape(row_count, tok_local, HEADS * HEAD_DIM)
            .astype(jnp.bfloat16)
        )
        middle = hidden + jnp.einsum(
            "rce,ed->rcd", attn_low, w_out, preferred_element_type=jnp.float32
        )
        normed_ffn, inverse_ffn = rms_forward(middle, gain_ffn)
        ffn_low = normed_ffn.astype(jnp.bfloat16)
        gate_pre = jnp.einsum("rcd,df->rcf", ffn_low, w_gate, preferred_element_type=jnp.float32)
        upward = jnp.einsum("rcd,df->rcf", ffn_low, w_up, preferred_element_type=jnp.float32)
        inner_act = (jax.nn.silu(gate_pre) * upward).astype(jnp.bfloat16)
        output = middle + jnp.einsum(
            "rcf,fd->rcd", inner_act, w_down, preferred_element_type=jnp.float32
        )
        return (output, (attn_low, middle, inverse_ffn, ffn_low, gate_pre, upward, inner_act))


    assert micro_count == lax.axis_size("section")

    def mine(stacked):
        return lax.dynamic_index_in_dim(stacked, section_index, 0, keepdims=False)

    segments = mine(segment_ids)

    def forward(hidden):
        query_seg, inverse, normed_low, queries, packed = front(hidden, segments)
        arrived = lax.all_gather(packed, "ctx", axis=1, tiled=True)
        attended, log_sum = attend_forward(queries, arrived, segments, query_seg)
        output, saved = rear(hidden, attended)
        return output.astype(jnp.bfloat16), (
            hidden, query_seg, inverse, normed_low, queries, arrived, attended, log_sum, saved
        )

    def backward(grad_out, kept):
        (
            hidden,
            backward_query_seg,
            backward_inverse,
            backward_normed_low,
            backward_queries,
            piece_arrived,
            backward_attended,
            log_sum,
            saved,
        ) = kept
        (
            backward_attn_low,
            backward_middle,
            backward_inverse_ffn,
            backward_ffn_low,
            backward_gate_pre,
            backward_upward,
            backward_inner_act,
        ) = saved
        grad_low = grad_out.astype(jnp.bfloat16)
        grad_inner = jnp.einsum("rcd,fd->rcf", grad_low, w_down, preferred_element_type=jnp.float32)
        sigmoid = jax.nn.sigmoid(backward_gate_pre)
        grad_gate = (
            grad_inner * backward_upward * sigmoid * (1.0 + backward_gate_pre * (1.0 - sigmoid))
        ).astype(jnp.bfloat16)
        grad_up = (grad_inner * backward_gate_pre * sigmoid).astype(jnp.bfloat16)
        grad_norm_ffn = jnp.einsum(
            "rcf,df->rcd", grad_gate, w_gate, preferred_element_type=jnp.float32
        ) + jnp.einsum("rcf,df->rcd", grad_up, w_up, preferred_element_type=jnp.float32)
        grad_mid_norm, backward_sum_gain_ffn = rms_backward(
            backward_middle, gain_ffn, backward_inverse_ffn, grad_norm_ffn
        )
        grad_middle = grad_out + grad_mid_norm
        grad_branch = grad_middle.astype(jnp.bfloat16)
        grad_attn = jnp.einsum(
            "rcd,ed->rce", grad_branch, w_out, preferred_element_type=jnp.float32
        ).astype(jnp.bfloat16)
        grad_heads = grad_attn.reshape(head_shape).transpose(0, 2, 3, 1, 4)
        row_delta = jnp.sum(grad_heads.astype(jnp.float32) * backward_attended, -1)
        query_start = jnp.zeros(state_shape + (HEAD_DIM,), jnp.float32)
        fold_grad_query = query_start
        grad_query = fold_grad_query
        piece_piece_rows = piece_arrived.shape[1]
        piece_block_rows = math.gcd(piece_piece_rows, 512)

        def piece_inner_step(step_index, loop_state):
            grad_query, local_pair = loop_state
            inside = step_index * piece_block_rows
            key_block = lax.dynamic_slice_in_dim(piece_arrived, inside, piece_block_rows, 1)
            key_part = key_block[..., :kv_width].reshape(
                row_count, piece_block_rows, KV_HEADS, HEAD_DIM
            )
            value_part = key_block[..., kv_width:].reshape(
                row_count, piece_block_rows, KV_HEADS, HEAD_DIM
            )
            key_seg = lax.dynamic_slice_in_dim(segments, inside, piece_block_rows, 1)
            scores, allowed = block_scores(
                backward_queries, key_part, backward_query_seg, key_seg, query_pos, inside
            )
            chances = jnp.where(
                allowed, jnp.exp(jnp.where(allowed, scores, mask_floor) - log_sum[..., None]), 0.0
            )
            grad_chance = jnp.einsum(
                "rkgcd,rnkd->rkgcn", grad_heads, value_part, preferred_element_type=jnp.float32
            )
            grad_scores = (chances * (grad_chance - row_delta[..., None])).astype(jnp.bfloat16)
            grad_query = grad_query + score_scale * jnp.einsum(
                "rkgcn,rnkd->rkgcd", grad_scores, key_part, preferred_element_type=jnp.float32
            )
            grad_key = score_scale * jnp.einsum(
                "rkgcn,rckgd->rnkd",
                grad_scores,
                backward_queries,
                preferred_element_type=jnp.float32,
            )
            grad_value = jnp.einsum(
                "rkgcn,rkgcd->rnkd",
                chances.astype(jnp.bfloat16),
                grad_heads,
                preferred_element_type=jnp.float32,
            )
            update = jnp.concatenate(
                [
                    grad_key.reshape(row_count, piece_block_rows, kv_width),
                    grad_value.reshape(row_count, piece_block_rows, kv_width),
                ],
                -1,
            )
            current = lax.dynamic_slice_in_dim(local_pair, inside, piece_block_rows, 1)
            local_pair = lax.dynamic_update_slice_in_dim(local_pair, current + update, inside, 1)
            return (grad_query, local_pair)

        local_start = jnp.zeros((row_count, piece_piece_rows, 2 * kv_width), jnp.float32)
        fold_grad_query, fold_local_pair = lax.fori_loop(
            0, piece_piece_rows // piece_block_rows, piece_inner_step, (grad_query, local_start)
        )
        grad_pair = fold_local_pair
        grad_query, grad_pair = (fold_grad_query, grad_pair)
        pair_share = lax.psum_scatter(
            grad_pair.astype(jnp.bfloat16), "ctx", scatter_dimension=1, tiled=True
        ).astype(jnp.float32)
        query_tok = grad_query.transpose(0, 3, 1, 2, 4).reshape(
            row_count, tok_local, HEADS, HEAD_DIM
        )
        query_back = rotate(query_tok, cos_table, -sine_table).reshape(
            row_count, tok_local, HEADS * HEAD_DIM
        )
        query_back = query_back.astype(jnp.bfloat16)
        key_back = rotate(
            pair_share[..., :kv_width].reshape(row_count, tok_local, KV_HEADS, HEAD_DIM),
            cos_table,
            -sine_table,
        )
        pair_low = jnp.concatenate(
            [key_back.reshape(row_count, tok_local, kv_width), pair_share[..., kv_width:]], -1
        )
        pair_low = pair_low.astype(jnp.bfloat16)
        grad_normed = jnp.einsum(
            "rce,de->rcd", query_back, w_query, preferred_element_type=jnp.float32
        ) + jnp.einsum("rce,de->rcd", pair_low, w_pair, preferred_element_type=jnp.float32)
        grad_front, backward_sum_gain_attn = rms_backward(
            hidden, gain_attn, backward_inverse, grad_normed
        )
        factors = (
            backward_normed_low, backward_attn_low, backward_ffn_low, backward_inner_act,
            query_back, pair_low, grad_branch, grad_gate, grad_up, grad_low,
        )
        tick_grads = (backward_sum_gain_attn, backward_sum_gain_ffn, factors)
        return grad_middle + grad_front, tick_grads

    first_low, first_kept = forward(mine(inputs).astype(jnp.float32))
    second_low, second_kept = forward(first_low.astype(jnp.float32))
    grad_mid, second_grads = backward(mine(cotangent).astype(jnp.float32), second_kept)
    grad_mid_low = grad_mid.astype(jnp.bfloat16)
    grad_in, first_grads = backward(grad_mid_low.astype(jnp.float32), first_kept)
    dp = plan.dp

    def stacked(one, other):
        return jnp.concatenate([one, other], 1).reshape(-1, one.shape[-1])

    normed, attn, ffn, inner, d_query, d_pair, d_branch, d_gate, d_up, d_out = (
        stacked(one, other) for one, other in zip(first_grads[2], second_grads[2])
    )
    tokens = normed.shape[0]

    def sides(values, rows):
        cut = values.reshape(tokens, dp, -1)
        cut = jnp.pad(cut, ((0, 0), (0, 0), (0, rows - cut.shape[2])))
        return cut.transpose(1, 2, 0).reshape(dp * rows, tokens)

    inner = inner.reshape(tokens, dp, -1)
    inner = jnp.pad(
        inner, ((0, 0), (0, 0), (0, plan.down_tiles * LANES - inner.shape[2]))
    ).reshape(tokens, -1)
    spare = plan.width_tiles * LANES - model_width
    gain_sums = jnp.stack([one + other for one, other in zip(first_grads[:2], second_grads[:2])])
    gain_sums = jnp.pad(gain_sums, ((0, 6), (0, plan.width_tiles * LANES - model_width)))
    factors = (
        sides(ffn, plan.rows),
        jnp.stack([d_gate, d_up]),
        d_out.T,
        inner,
        jnp.stack([sides(normed, plan.rows), sides(attn, plan.rows)]),
        jnp.pad(jnp.stack([d_query, d_branch]), ((0, 0), (0, 0), (0, spare))),
        jnp.pad(
            jnp.stack([d_pair[:, :kv_width], d_pair[:, kv_width:]]),
            ((0, 0), (0, 0), (LANES - spare, 0)),
        ),
    )
    acts = (first_low, second_low)
    return acts, (grad_in, grad_mid_low), gain_sums, factors


def fused_block(
    size, plan, inputs, segment_ids, cotangent,
    gain_attn, w_query, w_key, w_value, w_out, gain_ffn, w_gate, w_up, w_down,
):
    cos_in, sin_in = rotary(size.length)
    gains = (gain_attn, gain_ffn)
    hidden = inputs[:, 0].swapaxes(1, 2)
    weights = (w_query, w_key.T, w_value.T, w_out, w_gate, w_up, w_down.T)
    acts, *kept = run_front(
        size, plan, hidden, cotangent[:, 0].swapaxes(1, 2), segment_ids, cos_in, sin_in, *gains, *weights
    )
    summed, grads = run_tail(size, plan, hidden, cos_in, sin_in, *gains, *kept, *weights)
    return acts, grads, summed


def body(
    inputs,
    segment_ids,
    cotangent,
    gain_attn,
    w_query,
    w_key,
    w_value,
    w_out,
    gain_ffn,
    w_gate,
    w_up,
    w_down,
):
    micro_count, row_count, tok_local, model_width = inputs.shape
    kv_width, hidden = w_key.shape[1], w_gate.shape[1]
    assert micro_count == lax.axis_size("section")
    on_first = lax.axis_index("section") == 0
    plan = Plan(lax.axis_size("dp"), lax.axis_size("ctx"), model_width, hidden, kv_width)
    dp = plan.dp
    size = Block(tok_local, segment_ids.shape[2], model_width, hidden, kv_width, plan.ctx)
    fits = (
        row_count == 1
        and size.length <= 1024
        and tok_local % LANES == 0
        and plan.rows * dp == model_width
        and plan.down_tiles * LANES * dp == hidden
        and len(plan.chunks) == 11
    )
    params = (gain_attn, w_query, w_key, w_value, w_out, gain_ffn, w_gate, w_up, w_down)
    if fits:
        acts, grads, summed = fused_block(size, plan, inputs, segment_ids, cotangent, *params)
    else:
        acts, grads, gain_sums, factors = plain_block(
            plan, inputs, segment_ids, cotangent, *params
        )
        summed = reduce_grads(plan, *factors, gain_sums)
    sizes = (model_width, hidden, kv_width)

    def exchange(for_first, for_last):
        kept = jnp.where(on_first, for_first, for_last)
        sent = jnp.where(on_first, for_last, for_first)
        got = lax.ppermute(sent, "section", [(0, 1), (1, 0)])
        return jnp.where(
            on_first, jnp.stack([kept, got]), jnp.stack([got, kept])
        )

    def turned(values):
        return values[None, :, None].swapaxes(3, 4)

    if fits:
        *parts, acts, grads = unpack(plan, sizes, summed, acts, grads)
        activations, input_grads = turned(acts), turned(grads)
    else:
        parts = unpack(plan, sizes, summed)
        activations = exchange(*acts)[None]
        input_grads = exchange(grads[0].astype(jnp.bfloat16), grads[1]).astype(jnp.float32)[None]
    query, key_t, value_t, out, gate, up, down_t, gain_one, gain_two = parts
    return (
        activations,
        input_grads,
        gain_one.reshape(-1),
        query,
        key_t.T,
        value_t.T,
        out,
        gain_two.reshape(-1),
        gate,
        up,
        down_t.T,
    )


def solution(mesh):
    placed = (
        P(None, "dp", "ctx", None),
        P(None, "dp", None),
        P(None, "dp", "ctx", None),
        P(),
        P(),
        P(),
        P(),
        P(),
        P(),
        P(),
        P(),
        P(),
    )
    return jax.shard_map(
        body,
        mesh=mesh,
        in_specs=placed,
        out_specs=(
            P("section", None, "dp", "ctx", None),
            P("section", None, "dp", "ctx", None),
            P("dp"),
            P("dp", None),
            P("dp", None),
            P("dp", None),
            P("dp", None),
            P("dp"),
            P("dp", None),
            P("dp", None),
            P("dp", None),
        ),
        check_vma=False,
    )
```

```python
import functools
import math
import types

import jax
import jax.numpy as jnp
import numpy as np
from jax import lax
from jax.experimental import pallas as pl
from jax.experimental.pallas import tpu as pltpu
from jax.sharding import PartitionSpec as P

HEADS = 15
KV_HEADS = 5
HEAD_DIM = 64
LANES = 128
Z_CHUNKS = 3
Z_LAG = 2
OWN_SLOTS = 8
PARTNER_SLOTS = 3
MESH = pl.DeviceIdType.MESH


epsilon = 1e-05
score_scale = 0.125
score_unit = score_scale / math.log(2.0)
mask_floor = -1e30


def rms_forward(values, gain_vec):
    inverse = lax.rsqrt(jnp.mean(values * values, -1, keepdims=True) + epsilon)
    return (values * inverse * gain_vec, inverse)


def rms_backward(values, gain_vec, inverse, grad_normed):
    weighted = grad_normed * gain_vec
    grad_gain = jnp.sum(grad_normed * values * inverse, axis=(0, 1))
    cubed = inverse * inverse * inverse
    grad_values = inverse * weighted - values * cubed * jnp.mean(
        weighted * values, -1, keepdims=True
    )
    return (grad_values, grad_gain)


def rotate(values, cos_table, sine_table):
    halfway = values.shape[-1] // 2
    former = values[..., :halfway]
    latter = values[..., halfway:]
    cos_part = cos_table[None, :, None, :]
    sine_part = sine_table[None, :, None, :]
    return jnp.concatenate(
        [former * cos_part - latter * sine_part, latter * cos_part + former * sine_part], -1
    )


def block_scores(queries, key_part, query_seg, key_seg, query_pos, offset):
    block_rows = key_part.shape[1]
    scores = (
        jnp.einsum("rckgd,rnkd->rkgcn", queries, key_part, preferred_element_type=jnp.float32)
        * score_scale
    )
    key_pos = offset + jnp.arange(block_rows, dtype=jnp.int32)
    allowed = (query_seg[:, :, None] == key_seg[:, None, :]) & (
        key_pos[None, None, :] <= query_pos[None, :, None]
    )
    return (scores, allowed[:, None, None, :, :])


def up_to(value, step):
    return -(-value // step) * step


TAIL_ORDER = (
    0, 8, -1, 24, -1, 1, 16, 9, 25, 32, -1, 40, 17, 33, -1, 41, -1, -2, 26, -3,
    48, 2, 49, 56, -4, 3, 42, 4, 57, 64, 34, 58, 10, 72, 43, 27, 18, 65, 19, 11,
    59, 50, 20, 12, 35, 73, 66, 21, 51, 28, 44, 80, 81, 74, 5, 60, 67, 29, 75, 82,
    30, 52, 13, 36, 83, 61, 53, 22, 68, 45, 31, 76, 69, 84, 54, 62, 37, 46, 23, 77,
    6, 85, 70, 38, 63, 14, 78, 86, 39, 55, 71, 47, 15, 7, 79, 87,
)


class Plan:
    def __init__(self, dp, ctx, width, hidden, kv_width):
        self.dp, self.ctx = dp, ctx
        self.cx = 1 << (ctx.bit_length() // 2) if ctx & (ctx - 1) == 0 else ctx
        self.cy = ctx // self.cx
        self.low = max(dp // 2, 1)
        self.shard = width // dp
        self.rows = up_to(width // dp, 16)
        self.down_rows = up_to(width // 2, 16)
        self.down_tiles = up_to(hidden // dp, LANES) // LANES
        self.up_tiles = hidden // LANES
        self.width_tiles = up_to(width, LANES) // LANES
        self.pair_tiles = (width + kv_width) // LANES
        self.step = 4
        chunks = []
        for kind, count, rows, step in (
            ("down", self.down_tiles, self.down_rows, 2),
            ("ffn", self.up_tiles, self.rows, self.step),
            ("attn", self.width_tiles - 1, self.rows, 4),
            ("mixed", self.pair_tiles - self.width_tiles + 1, self.rows, 4),
        ):
            for start in range(0, count, step):
                tiles = min(step, count - start)
                extra = 16 if kind == "mixed" else 0
                piece = up_to(up_to(tiles * rows + extra, ctx) // ctx, 16)
                mode = "z" if len(chunks) < Z_CHUNKS else "xy"
                chunks.append((kind, start, tiles, rows, piece, mode))
        self.chunks = chunks
        self.offsets = [sum(c[4] for c in chunks[:i]) for i in range(len(chunks))]
        self.total = sum(c[4] for c in chunks)
        self.widest = max(c[4] for c in chunks)

    def of(self, kind):
        return [i for i, chunk in enumerate(self.chunks) if chunk[0] == kind]

    def spans(self, index, first, count):
        piece = self.chunks[index][4]
        out, done = [], 0
        while done < count:
            at = first + done
            size = min(count - done, piece - at % piece)
            out.append((at // piece, at % piece, done, size))
            done += size
        return out

    def scratch(self):
        dp, cy, cx, low = self.dp, self.cy, self.cx, self.low
        nx, ny, nz, high = max(cx - 1, 1), max(cy - 1, 1), max(dp - 1, 1), max(dp - low, 1)
        count = len(self.chunks)

        def buffer(*shape):
            return pltpu.VMEM((*shape, LANES), jnp.bfloat16)

        found = [
            buffer(2, dp, cy, cx, self.widest),
            buffer(PARTNER_SLOTS, dp, cy, cx, self.widest),
            buffer(OWN_SLOTS, dp, cy, cx, self.widest),
        ]
        for kind, start, tiles, rows, piece, mode in self.chunks:
            head = up_to(piece // 2, 16)
            rest = max(piece - head, 16)
            if mode == "xy":
                found += [
                    buffer(nz, piece), buffer(nx, low, cy, piece), buffer(ny, high, cx, piece),
                    buffer(nx, high, piece), buffer(ny, low, piece), buffer(piece),
                ]
            else:
                found += [
                    buffer(nz, cy, cx, piece), buffer(nx, cy, head), buffer(ny, cx, rest),
                    buffer(nx, rest), buffer(ny, head), buffer(piece),
                ]
        dma = pltpu.SemaphoreType.DMA
        return found + [
            dma((2, count)), dma((2, count, nx)), dma((2, count, ny)), dma((2, count, nx)),
            dma((2, count, ny)), dma((2, count, nz)), dma((2, count, nx)), dma((2, count, ny)),
            dma((2, count, nx)), dma((2, count, ny)), dma((2, count)), dma((count,)),
            pltpu.SemaphoreType.REGULAR,
        ]


class Reduction:
    def __init__(self, plan, products, out, refs, turns=None):
        self.plan, self.products, self.out = plan, products, out
        count = len(plan.chunks)
        self.turns = list(range(count)) if turns is None else turns
        self.sent, self.partner, self.own_ring = refs[:3]
        self.parts = [refs[3 + 6 * i : 9 + 6 * i] for i in range(count)]
        (
            self.sem_p, self.sem_x1, self.sem_y1, self.sem_x2, self.sem_y2, self.sem_z,
            self.sem_gx, self.sem_gy, self.sem_hx, self.sem_hy, self.sem_m, self.sem_o, self.credit,
        ) = refs[3 + 6 * count :]
        self.section, self.row, self.ctx = (
            lax.axis_index(name) for name in ("section", "dp", "ctx")
        )
        self.px, self.py = lax.rem(self.ctx, plan.cx), lax.div(self.ctx, plan.cx)
        self.mate = (1 - self.section, self.row, self.ctx)
        self.done = [0] * count

    def friends(self):
        plan = self.plan
        found = [self.mate]
        found += [(self.section, lax.rem(self.row + k, plan.dp), self.ctx) for k in range(1, plan.dp)]
        return found + [
            (self.section, self.row, lax.rem(self.ctx + k, plan.ctx)) for k in range(1, plan.ctx)
        ]

    def remote(self, source, target, sems, place, device):
        return pltpu.make_async_remote_copy(
            source, target, sems.at[(0, *place)], sems.at[(1, *place)],
            device_id=device, device_id_type=MESH,
        )

    def x_peers(self):
        for k in range(1, self.plan.cx):
            other = lax.rem(self.px + k, self.plan.cx)
            yield k - 1, other, (self.section, self.row, self.py * self.plan.cx + other)

    def y_peers(self):
        for k in range(1, self.plan.cy):
            other = lax.rem(self.py + k, self.plan.cy)
            yield k - 1, other, (self.section, self.row, other * self.plan.cx + self.px)

    def z_peers(self):
        for k in range(1, self.plan.dp):
            other = lax.rem(self.row + k, self.plan.dp)
            yield k - 1, other, (self.section, other, self.ctx)

    def turn(self, index):
        return self.turns.index(index)

    def own(self, index):
        return self.own_ring.at[self.turn(index) % OWN_SLOTS]

    def at(self, index):
        return pl.ds(self.plan.offsets[index], self.plan.chunks[index][4])

    def head(self, index):
        piece = self.plan.chunks[index][4]
        return up_to(piece // 2, 16)

    def partner_copy(self, index):
        rows = pl.ds(0, self.plan.chunks[index][4])
        return self.remote(
            self.sent.at[self.turn(index) % 2, :, :, :, rows],
            self.partner.at[self.turn(index) % PARTNER_SLOTS, :, :, :, rows],
            self.sem_p, (index,), self.mate,
        )

    def make_partner(self, index):
        turn, cx = self.turn(index), self.plan.cx
        if turn >= 2:
            self.partner_copy(self.turns[turn - 2]).wait_send()
        if turn >= PARTNER_SLOTS:
            pl.semaphore_wait(self.credit, 1)

        def finish(j, first, value):
            for p, place, inside, size in self.plan.spans(index, first, value.shape[0]):
                self.sent[turn % 2, j, p // cx, p % cx, place : place + size, :] = value[
                    inside : inside + size
                ].astype(jnp.bfloat16)

        self.products(index, 1 - self.section, finish)
        self.partner_copy(index).start()

    def make_own(self, index):
        turn = self.turn(index)
        assert turn < OWN_SLOTS or self.done[self.turns[turn - OWN_SLOTS]] > 4
        self.partner_copy(index).wait_recv()
        cx, slot, own = self.plan.cx, turn % PARTNER_SLOTS, self.own(index)

        def finish(j, first, value):
            for p, place, inside, size in self.plan.spans(index, first, value.shape[0]):
                rows = slice(place, place + size)
                other = self.partner[slot, j, p // cx, p % cx, rows, :].astype(jnp.float32)
                own[j, p // cx, p % cx, rows, :] = (
                    value[inside : inside + size] + other
                ).astype(jnp.bfloat16)

        self.products(index, self.section, finish)
        if turn + PARTNER_SLOTS < len(self.plan.chunks):
            pl.semaphore_signal(self.credit, 1, device_id=self.mate, device_id_type=MESH)
        self.start(self.z_copies(index) if self.is_z(index) else self.first_copies(index))

    def is_z(self, index):
        return self.plan.chunks[index][5] == "z"

    def start(self, copies):
        for copy in copies:
            copy.start()

    def wait(self, copies):
        for copy in copies:
            copy.wait()

    def z_copies(self, index):
        own, into = self.own(index), self.parts[index][0]
        piece = pl.ds(0, self.plan.chunks[index][4])
        found = []
        for slot, other, device in self.z_peers():
            if self.is_z(index):
                source = own.at[other, :, :, piece]
            else:
                source = own.at[other, self.py, self.px, piece]
            found.append(self.remote(source, into.at[slot], self.sem_z, (index, slot), device))
        return found

    def halves(self, index):
        plan, piece = self.plan, self.plan.chunks[index][4]
        if self.is_z(index):
            head = self.head(index)
            return (pl.ds(self.row, 1), pl.ds(0, head)), (pl.ds(self.row, 1), pl.ds(head, piece - head))
        rows = pl.ds(0, piece)
        return (pl.ds(0, plan.low), rows), (pl.ds(plan.low, plan.dp - plan.low), rows)

    def has_rest(self, index):
        if self.is_z(index):
            return self.plan.chunks[index][4] > self.head(index)
        return self.plan.dp > self.plan.low

    def first_copies(self, index):
        own = self.own(index)
        (j_x, rows_x), (j_y, rows_y) = self.halves(index)
        _, rx1, ry1, _, _, _ = self.parts[index]
        if self.is_z(index):
            j_x = j_y = self.row
        found = [
            self.remote(own.at[j_x, :, other, rows_x], rx1.at[slot], self.sem_x1, (index, slot), device)
            for slot, other, device in self.x_peers()
        ]
        if self.has_rest(index):
            found += [
                self.remote(
                    own.at[j_y, other, :, rows_y], ry1.at[slot], self.sem_y1, (index, slot), device
                )
                for slot, other, device in self.y_peers()
            ]
        return found

    def second_copies(self, index):
        own = self.own(index)
        (j_x, rows_x), (j_y, rows_y) = self.halves(index)
        _, _, _, rx2, ry2, _ = self.parts[index]
        if self.is_z(index):
            j_x = j_y = self.row
        found = [
            self.remote(
                own.at[j_x, other, self.px, rows_x], ry2.at[slot], self.sem_y2, (index, slot), device
            )
            for slot, other, device in self.y_peers()
        ]
        if self.has_rest(index):
            found += [
                self.remote(
                    own.at[j_y, self.py, other, rows_y], rx2.at[slot], self.sem_x2, (index, slot), device
                )
                for slot, other, device in self.x_peers()
            ]
        return found

    def add_all_z(self, index):
        plan, own, into = self.plan, self.own(index), self.parts[index][0]
        piece = slice(0, plan.chunks[index][4])
        self.wait(self.z_copies(index))
        for y in range(plan.cy):
            for x in range(plan.cx):
                total = own[self.row, y, x, piece, :].astype(jnp.float32)
                for k in range(plan.dp - 1):
                    total = total + into[k, y, x].astype(jnp.float32)
                own[self.row, y, x, piece, :] = total.astype(jnp.bfloat16)
        self.start(self.first_copies(index))

    def add_first(self, index):
        plan, own = self.plan, self.own(index)
        _, rx1, ry1, _, _, _ = self.parts[index]
        piece, is_z = plan.chunks[index][4], self.is_z(index)
        head = self.head(index)
        self.wait(self.first_copies(index))
        places = [(self.row, 0, 0)] if is_z else [(j, j, j - plan.low) for j in range(plan.dp)]
        for j, at_x, at_y in places:
            if is_z or at_x < plan.low:
                rows = slice(0, head) if is_z else slice(0, piece)
                for y in range(plan.cy):
                    total = own[j, y, self.px, rows, :].astype(jnp.float32)
                    for k in range(plan.cx - 1):
                        part = rx1[k, y] if is_z else rx1[k, at_x, y]
                        total = total + part.astype(jnp.float32)
                    own[j, y, self.px, rows, :] = total.astype(jnp.bfloat16)
            if (is_z and piece > head) or (not is_z and at_y >= 0):
                rows = slice(head, piece) if is_z else slice(0, piece)
                for x in range(plan.cx):
                    total = own[j, self.py, x, rows, :].astype(jnp.float32)
                    for k in range(plan.cy - 1):
                        part = ry1[k, x] if is_z else ry1[k, at_y, x]
                        total = total + part.astype(jnp.float32)
                    own[j, self.py, x, rows, :] = total.astype(jnp.bfloat16)
        self.start(self.second_copies(index))

    def add_second(self, index):
        plan, own = self.plan, self.own(index)
        _, _, _, rx2, ry2, _ = self.parts[index]
        piece = slice(0, plan.chunks[index][4])
        self.wait(self.second_copies(index))
        for j in range(plan.dp):
            total = own[j, self.py, self.px, piece, :].astype(jnp.float32)
            if j < plan.low:
                for k in range(plan.cy - 1):
                    total = total + ry2[k, j].astype(jnp.float32)
            else:
                for k in range(plan.cx - 1):
                    total = total + rx2[k, j - plan.low].astype(jnp.float32)
            own[j, self.py, self.px, piece, :] = total.astype(jnp.bfloat16)
        self.start(self.z_copies(index))

    def add_last(self, index):
        plan, own = self.plan, self.own(index)
        rz, _, _, rx2, ry2, final = self.parts[index]
        piece, head = plan.chunks[index][4], self.head(index)
        if self.is_z(index):
            self.wait(self.second_copies(index))
            total = own[self.row, self.py, self.px, 0:head, :].astype(jnp.float32)
            for k in range(plan.cy - 1):
                total = total + ry2[k].astype(jnp.float32)
            final[0:head, :] = total.astype(jnp.bfloat16)
            if piece > head:
                total = own[self.row, self.py, self.px, head:piece, :].astype(jnp.float32)
                for k in range(plan.cx - 1):
                    total = total + rx2[k].astype(jnp.float32)
                final[head:piece, :] = total.astype(jnp.bfloat16)
        else:
            self.wait(self.z_copies(index))
            total = own[self.row, self.py, self.px, 0:piece, :].astype(jnp.float32)
            for k in range(plan.dp - 1):
                total = total + rz[k].astype(jnp.float32)
            final[...] = total.astype(jnp.bfloat16)
        self.place_copy(index).start()
        self.start(self.gather_one(index))

    def place_copy(self, index):
        target = self.out.at[self.section, self.py, self.px, self.at(index)]
        return pltpu.make_async_copy(self.parts[index][5], target, self.sem_o.at[index])

    def gather_parts(self, index):
        offset, piece, head = self.plan.offsets[index], self.plan.chunks[index][4], self.head(index)
        return pl.ds(offset, head), pl.ds(offset + head, piece - head), piece > head

    def gather_one(self, index):
        final, out = self.parts[index][5], self.out
        rows_x, rows_y, rest = self.gather_parts(index)
        head, piece = self.head(index), self.plan.chunks[index][4]
        found = [
            self.remote(
                final.at[pl.ds(0, head)], out.at[self.section, self.py, self.px, rows_x],
                self.sem_gx, (index, slot), device,
            )
            for slot, other, device in self.x_peers()
        ]
        if rest:
            found += [
                self.remote(
                    final.at[pl.ds(head, piece - head)], out.at[self.section, self.py, self.px, rows_y],
                    self.sem_gy, (index, slot), device,
                )
                for slot, other, device in self.y_peers()
            ]
        return found

    def gather_two(self, index):
        out = self.out
        rows_x, rows_y, rest = self.gather_parts(index)
        found = []
        for slot, other, device in self.y_peers():
            region = out.at[self.section, self.py, :, rows_x]
            found.append(self.remote(region, region, self.sem_hy, (index, slot), device))
        if rest:
            for slot, other, device in self.x_peers():
                region = out.at[self.section, :, self.px, rows_y]
                found.append(self.remote(region, region, self.sem_hx, (index, slot), device))
        return found

    def gather_on(self, index):
        self.place_copy(index).wait()
        self.wait(self.gather_one(index))
        self.start(self.gather_two(index))

    def mate_copy(self, index):
        region = self.out.at[self.section, :, :, self.at(index)]
        return self.remote(region, region, self.sem_m, (index,), self.mate)

    def pass_on(self, index):
        self.wait(self.gather_two(index))
        self.mate_copy(index).start()

    def finish(self, index):
        self.mate_copy(index).wait()

    def stages(self, index):
        middle = (self.add_all_z, self.add_first) if self.is_z(index) else (self.add_first, self.add_second)
        return (
            self.make_partner, self.make_own, *middle, self.add_last, self.gather_on, self.pass_on, self.finish
        )

    def advance(self, index, upto=None):
        stages = self.stages(index)
        while self.done[index] < len(stages):
            if upto is not None and self.done[index] >= upto:
                return
            stages[self.done[index]](index)
            self.done[index] += 1
            if upto is None:
                return

    def drain(self):
        todo = []
        for index in range(len(self.done)):
            for stage in range(self.done[index], len(self.stages(index))):
                late = Z_LAG if self.is_z(index) and stage >= 2 else 0
                todo.append((index + stage + late, stage, index))
        for step, stage, index in sorted(todo):
            self.advance(index)
        for index in self.turns[-2:]:
            self.partner_copy(index).wait_send()


def greet(friends):
    barrier = pltpu.get_barrier_semaphore()
    for friend in friends:
        pl.semaphore_signal(barrier, 1, device_id=friend, device_id_type=MESH)
    pl.semaphore_wait(barrier, len(friends))


def shard_products(plan, index, half, finish, sources):
    kind, start, tiles, rows, piece, mode = plan.chunks[index]
    cols = slice(start * LANES, (start + tiles) * LANES)

    def shard(j, carry):
        own = pl.ds(pl.multiple_of(j * plan.rows, 16), plan.rows)
        if kind == "ffn":
            value = dot(sources.ffn_x[own, :], sources.ffn_dy(half, index, 0, cols))
        elif kind == "down":
            first = pl.multiple_of(j * (plan.down_tiles * LANES) + start * LANES, LANES)
            rows_of = pl.ds(pl.multiple_of(half * plan.down_rows, 16), plan.down_rows)
            value = dot(sources.down_x[rows_of, :], sources.down_dy[:, pl.ds(first, tiles * LANES)])
        elif kind == "attn":
            value = dot(sources.attn_x[half, own, :], sources.attn_dy[half, :, cols])
        else:
            value = dot(sources.attn_x[0, own, :], sources.pair_dy[half])
            last = plan.width_tiles - 1
            mixed = dot(sources.attn_x[half, own, :], sources.attn_dy[half, :, last * LANES :])
            value = jnp.concatenate([value[:, :LANES] + mixed, value[:, LANES:]], 1)
        for tile in range(tiles):
            finish(j, tile * rows, value[:, tile * LANES : (tile + 1) * LANES])
        if kind == "mixed":
            finish(j, tiles * rows, sources.extra[half, j])
        return carry

    lax.fori_loop(0, plan.dp, shard, 0)


def spread_gains(plan, gain_sums, extra):
    for half in range(2):
        for j in range(plan.dp):
            for number in range(-(-plan.shard // LANES)):
                start = j * plan.shard + number * LANES
                extra[half, j, number : number + 1, :] = gain_sums[
                    half : half + 1, start : start + LANES
                ]


def reduce_kernel(
    plan, ffn_x, ffn_dy, down_x, down_dy, attn_x, attn_dy, pair_dy, gain_sums, out, extra, *refs
):
    sources = types.SimpleNamespace(
        ffn_x=ffn_x, ffn_dy=lambda half, index, inside, cols: ffn_dy[half, :, cols],
        down_x=down_x, down_dy=down_dy,
        attn_x=attn_x, attn_dy=attn_dy, pair_dy=pair_dy, extra=extra,
    )
    reduction = Reduction(
        plan, lambda *place: shard_products(plan, *place, sources), out, refs
    )
    greet(reduction.friends())
    spread_gains(plan, gain_sums, extra)
    reduction.drain()


def reduce_grads(plan, *operands):
    return pl.pallas_call(
        functools.partial(reduce_kernel, plan),
        out_shape=jax.ShapeDtypeStruct((2, plan.cy, plan.cx, plan.total, LANES), jnp.bfloat16),
        in_specs=[pl.BlockSpec(memory_space=pltpu.VMEM)] * len(operands),
        out_specs=pl.BlockSpec(memory_space=pl.ANY),
        scratch_shapes=[pltpu.VMEM((2, plan.dp, 16, LANES), jnp.float32), *plan.scratch()],
        compiler_params=pltpu.CompilerParams(
            collective_id=0, has_side_effects=True, vmem_limit_bytes=64 << 20
        ),
        cost_estimate=pl.CostEstimate(flops=10**10, bytes_accessed=20 * 10**6, transcendentals=0),
    )(*operands)


class Block:
    def __init__(self, tokens, length, width, hidden, kv_width, ctx):
        self.tokens, self.length, self.width, self.hidden = tokens, length, width, hidden
        self.kv_width, self.ctx = kv_width, ctx
        self.kv_heads = kv_width // HEAD_DIM
        self.group = width // kv_width
        self.step, self.front_step = 512, hidden // 2


def dot(one, other, over=(1, 0)):
    return lax.dot_general(
        one, other, (((over[0],), (over[1],)), ((), ())), preferred_element_type=jnp.float32
    )


def fold_rows(values, combine):
    return combine(values.reshape(values.shape[0] // 8, 8, values.shape[1]), 0)


def norm(values):
    return lax.rsqrt(jnp.mean(values * values, 0, keepdims=True) + epsilon)


def app_tokens(size, app):
    return slice(app * size.tokens, (app + 1) * size.tokens)


def head_rows(size, g, h):
    return pl.ds(pl.multiple_of((g * size.group + h) * HEAD_DIM, HEAD_DIM), HEAD_DIM)


def wide_gain(env, which):
    return jnp.concatenate([env.columns[which]] * (env.size.tokens // LANES), 1)


def spread_columns(size, gains, columns):
    for which, gain in enumerate(gains):
        for start in range(0, size.width, LANES):
            stop = min(start + LANES, size.width)
            part = gain[start:stop].astype(jnp.float32)[None]
            if stop - start < LANES:
                part = jnp.concatenate([part, jnp.zeros((1, LANES - stop + start), jnp.float32)], 1)
            tile = jnp.broadcast_to(part, (LANES, LANES))
            columns[which, start:stop, :] = tile.T[: stop - start]


def norm_back(env, values, which, grad_normed):
    size = env.size
    inverse = norm(values)
    product = grad_normed * values * inverse
    folded = product[:, :LANES]
    for start in range(LANES, size.tokens, LANES):
        folded = folded + product[:, start : start + LANES]
    for start in range(0, size.width, LANES):
        stop = min(start + LANES, size.width)
        part = folded[start:stop]
        if stop - start < LANES:
            part = jnp.concatenate([part, jnp.zeros((LANES - stop + start, LANES), jnp.float32)], 0)
        env.gain_sums[which : which + 1, start : start + LANES] += jnp.sum(part.T, 0, keepdims=True)
    weighted = grad_normed * wide_gain(env, which)
    cubed = inverse * inverse * inverse
    return inverse * weighted - values * (cubed * jnp.mean(weighted * values, 0, keepdims=True))


def rope(env, values, sign):
    half = HEAD_DIM // 2
    cos, sine = env.cos_q[...], env.sin_q[...] * sign
    out = []
    for start in range(0, values.shape[0], HEAD_DIM):
        former = values[start : start + half]
        latter = values[start + half : start + HEAD_DIM]
        out += [former * cos - latter * sine, latter * cos + former * sine]
    return jnp.concatenate(out, 0)


def ffn_back(env, gate_ref, up_ref, rows, cols, wd, wg, wu):
    gate = gate_ref[rows, cols].astype(jnp.float32)
    upward = up_ref[rows, cols].astype(jnp.float32)
    sigmoid = 1.0 / (1.0 + jnp.exp(-gate))
    scaled = dot(env.natural[...], wd) * sigmoid
    grad_gate = (scaled * upward * (1.0 + gate * (1.0 - sigmoid))).astype(jnp.bfloat16)
    grad_up = (scaled * gate).astype(jnp.bfloat16)
    gate_ref[rows, cols] = grad_gate
    up_ref[rows, cols] = grad_up
    env.accum[...] += dot(wg, grad_gate, (1, 1)) + dot(wu, grad_up, (1, 1))


def middle_back(env, grad_low, mid):
    grad_middle = grad_low.astype(jnp.float32) + norm_back(env, mid, 1, env.accum[...])
    env.dmid[...] = grad_middle
    branch = grad_middle.astype(jnp.bfloat16)
    env.d_attn[1, : env.size.tokens, : env.size.width] = branch.T
    env.do_t[...] = dot(env.wo[...], branch).astype(jnp.bfloat16)


def grad_copy(env, g, k):
    owner = jnp.maximum(env.ctx - k, 0)
    rows = pl.ds(pl.multiple_of(owner * env.size.tokens, env.size.tokens), env.size.tokens)
    return pltpu.make_async_remote_copy(
        env.kv_send.at[g, rows], env.kv_recv.at[k - 1, g],
        env.sem_d.at[0, g, k - 1], env.sem_d.at[1, g, k - 1],
        device_id=(env.section, env.row, owner), device_id_type=MESH,
    )


def attend_back(env, at, g):
    size, low_type = env.size, jnp.bfloat16
    k_t = env.kv[g].T[:HEAD_DIM]
    sides = []
    for h in range(size.group):
        rows, cols = head_rows(size, g, h), slice(h * size.tokens, (h + 1) * size.tokens)
        query, grad_head = env.q_t[rows, :], env.do_t[rows, :]
        empty = jnp.zeros_like(query)
        query = jnp.concatenate([query, empty], 0)
        grad_pad = jnp.concatenate([empty, grad_head], 0)
        delta = jnp.sum(
            grad_head.astype(jnp.float32) * env.x_attn[1, rows, at].astype(jnp.float32),
            0, keepdims=True,
        )
        log_sum = env.lse[g, h : h + 1, :]
        for start in range(0, size.length, 256):
            keys_at = slice(start, start + 256)
            part = dot(env.kv[g, keys_at, :], query) * score_unit + env.bias[keys_at, :]
            chance = jnp.exp2(part - log_sum)
            env.chances[keys_at, cols] = chance.astype(low_type)
            change = dot(env.kv[g, keys_at, :], grad_pad) - delta
            env.grad_scores[keys_at, cols] = (chance * change).astype(low_type)
        sides.append(((query.astype(jnp.float32) * score_scale).astype(low_type), grad_pad))
        env.accum[rows, :] = dot(k_t, env.grad_scores[:, cols]) * score_scale
    small, grad_pad = (jnp.concatenate(side, 1) for side in zip(*sides))
    env.kv_send[g] = (
        dot(env.grad_scores[...], small, (1, 1)) + dot(env.chances[...], grad_pad, (1, 1))
    ).astype(low_type)
    for k in range(1, size.ctx):
        @pl.when(env.ctx - k >= 0)
        def _():
            grad_copy(env, g, k).start()


def project_back(env):
    size, low_type = env.size, jnp.bfloat16
    tokens, width = size.tokens, size.width
    for start in range(0, width, 2 * LANES):
        stop = min(start + 2 * LANES, width)
        tile = rope(env, env.accum[start:stop, :], -1.0).astype(low_type)
        env.natural[:, start:stop] = tile.T
        env.do_t[start:stop, :] = tile
    env.d_attn[0, :tokens, :width] = env.natural[...]
    own_rows = pl.ds(pl.multiple_of(env.ctx * tokens, tokens), tokens)
    pairs = [[], []]
    for g in range(size.kv_heads):
        tile = env.kv_send[g, own_rows, :].astype(jnp.float32)
        for k in range(1, size.ctx):
            @pl.when(env.ctx + k < size.ctx)
            def _():
                grad_copy(env, g, k).wait_recv()
            tile = tile + jnp.where(
                env.ctx + k < size.ctx, env.kv_recv[k - 1, g].astype(jnp.float32), 0.0
            )
        tile = tile.T
        pairs[0].append(rope(env, tile[:HEAD_DIM], -1.0).astype(low_type))
        pairs[1].append(tile[HEAD_DIM:].astype(low_type))
    spare = env.d_pair.shape[2] - size.kv_width
    for half in range(2):
        pairs[half] = jnp.concatenate(pairs[half], 0)
        env.d_pair[half, :tokens, :] = jnp.concatenate(
            [jnp.zeros((spare, tokens), low_type), pairs[half]], 0
        ).T
    grad_normed = (
        dot(env.wq[...], env.do_t[...])
        + dot(env.wk[...], pairs[0], (0, 0))
        + dot(env.wv[...], pairs[1], (0, 0))
    )
    return env.dmid[...] + norm_back(env, env.x[...].astype(jnp.float32), 0, grad_normed)


def drain_grad_copies(env):
    def one(g, carry):
        for k in range(1, env.size.ctx):
            @pl.when(env.ctx - k >= 0)
            def _():
                grad_copy(env, g, k).wait_send()
        return carry

    lax.fori_loop(0, env.size.kv_heads, one, 0)


def front_kernel(
    size, inputs, cotangent, segments, cos_in, sin_in, gain_attn, gain_ffn,
    wq_in, wk_in, wv_in, wo_in, wg_in, wu_in, wd_in,
    acts, n2_out, df_out, inner_out, attn_out, d_attn_out, d_pair_out, d_ffn_out,
    mid_out, q_out, kv_out, lse_out, bias_out, gain_out,
    wq, wk, wv, wo, wg, wu, wd, n2_t, df_t, inner, x_attn, d_attn, d_pair, d_ffn, gain_sums,
    cos_q, sin_q, columns, xin, cot, mid, q_t,
    kv, kv_send, kv_recv, lse, do_t, bias, accum, dmid, natural, scores, chances, grad_scores,
    sem_w, sem_k, sem_d, sem_e, sem_o,
):
    tokens, ctx_count, groups, group = size.tokens, size.ctx, size.kv_heads, size.group
    width, low_type, full = size.width, jnp.bfloat16, jnp.float32
    section, row, ctx = (lax.axis_index(name) for name in ("section", "dp", "ctx"))
    mate = (1 - section, row, ctx)
    own_rows = pl.ds(pl.multiple_of(ctx * tokens, tokens), tokens)
    env = types.SimpleNamespace(
        size=size, section=section, row=row, ctx=ctx, columns=columns, gain_sums=gain_sums,
        cos_q=cos_q, sin_q=sin_q, natural=natural, accum=accum, dmid=dmid, do_t=do_t,
        d_attn=d_attn, d_pair=d_pair, x_attn=x_attn, bias=bias, chances=chances,
        grad_scores=grad_scores, kv=kv.at[1], q_t=q_t.at[1], lse=lse.at[1], x=xin.at[1],
        kv_send=kv_send, kv_recv=kv_recv, sem_d=sem_d, wq=wq, wk=wk, wv=wv, wo=wo,
    )
    loads = [
        pltpu.make_async_copy(source, target, sem_w.at[number])
        for number, (source, target) in enumerate((
            (inputs.at[section], xin.at[0]), (cos_in.at[:, own_rows], cos_q),
            (sin_in.at[:, own_rows], sin_q), (wk_in, wk), (wv_in, wv), (wq_in, wq), (wo_in, wo),
            (wg_in, wg), (wu_in, wu), (wd_in, wd), (cotangent.at[section], cot),
        ))
    ]
    for load in loads:
        load.start()
    stores = []

    def store(source, target):
        copy = pltpu.make_async_copy(source, target, sem_o.at[len(stores)])
        copy.start()
        stores.append(copy)

    barrier = pltpu.get_barrier_semaphore()
    friends = [mate] + [(section, row, lax.rem(ctx + k, ctx_count)) for k in range(1, ctx_count)]
    for friend in friends:
        pl.semaphore_signal(barrier, 1, device_id=friend, device_id_type=MESH)
    spread_columns(size, (gain_attn, gain_ffn), columns)
    query_seg = segments[section, :, own_rows].astype(full)
    query_pos = lax.broadcasted_iota(jnp.int32, (1, tokens), 1) + ctx * tokens
    for start in range(0, size.length, LANES):
        key_seg = jnp.broadcast_to(
            segments[section, :, start : start + LANES].astype(full), (LANES, LANES)
        ).T
        key_pos = lax.broadcasted_iota(jnp.int32, (LANES, tokens), 0) + start
        key_seg = jnp.concatenate([key_seg] * (tokens // LANES), 1)
        allowed = (key_seg == query_seg) & (key_pos <= query_pos)
        bias[start : start + LANES, :] = jnp.where(allowed, 0.0, mask_floor)
    store(bias, bias_out)
    for k in range(1, ctx_count):
        @pl.when(ctx + k < ctx_count)
        def _():
            rows = pl.ds(pl.multiple_of((ctx + k) * tokens, tokens), tokens)
            for app in range(2):
                kv[app, :, rows, :] = jnp.zeros((groups, tokens, LANES), low_type)
    pl.semaphore_wait(barrier, len(friends))

    def kv_copy(app, g, k):
        return pltpu.make_async_remote_copy(
            kv.at[app, g, own_rows], kv.at[app, g, own_rows],
            sem_k.at[0, app, g, k - 1], sem_k.at[1, app, g, k - 1],
            device_id=(section, row, jnp.minimum(ctx + k, ctx_count - 1)), device_id_type=MESH,
        )

    def act_copy(app):
        return pltpu.make_async_remote_copy(
            xin.at[app + 1], acts.at[section], sem_e.at[0], sem_e.at[1],
            device_id=mate, device_id_type=MESH,
        )

    def act_store(app):
        return pltpu.make_async_copy(xin.at[app + 1], acts.at[section], sem_e.at[2])

    early = [
        pltpu.make_async_copy(source, target, sem_o.at[number])
        for number, (source, target) in enumerate((
            (q_t.at[0], q_out), (kv.at[0], kv_out), (lse.at[0], lse_out), (mid.at[0], mid_out)
        ))
    ]
    stores += early

    def forward(app, carry):
        at = pl.ds(pl.multiple_of(app * tokens, tokens), tokens)
        x = xin[app].astype(full)
        normed = (x * norm(x) * wide_gain(env, 0)).astype(low_type)
        x_attn[0, :, at] = normed

        @pl.when(app == 0)
        def _():
            for load in loads[1:6]:
                load.wait()

        keys = rope(env, dot(wk[...], normed), 1.0).astype(low_type)
        values = dot(wv[...], normed).astype(low_type)
        for g in range(groups):
            piece = slice(g * HEAD_DIM, (g + 1) * HEAD_DIM)
            kv[app, g, own_rows, :] = jnp.concatenate([keys[piece], values[piece]], 0).T
            for k in range(1, ctx_count):
                @pl.when(ctx + k < ctx_count)
                def _():
                    kv_copy(app, g, k).start()
        for start in range(0, width, 2 * LANES):
            stop = min(start + 2 * LANES, width)
            tile = dot(wq[:, start:stop], normed, (0, 0))
            q_t[app, start:stop, :] = rope(env, tile, 1.0).astype(low_type)

        def heads(g, carry):
            for k in range(1, ctx_count):
                @pl.when(ctx - k >= 0)
                def _():
                    kv_copy(app, g, k).wait_recv()
            v_t = kv[app, g].T[HEAD_DIM:]
            most, query = [None] * group, None
            for h in range(group + 1):
                if h < group:
                    query = q_t[app, head_rows(size, g, h), :]
                    query = jnp.concatenate([query, jnp.zeros_like(query)], 0)
                if h > 0:
                    largest = jnp.max(most[h - 1], 0, keepdims=True)
                    total = jnp.zeros((8, tokens), full)
                for start in range(0, size.length, LANES):
                    keys_at = slice(start, start + LANES)
                    if h < group:
                        part = dot(kv[app, g, keys_at, :], query) * score_unit + bias[keys_at, :]
                        scores[h, keys_at, :] = part
                        part = fold_rows(part, jnp.max)
                        most[h] = part if most[h] is None else jnp.maximum(most[h], part)
                    if h > 0:
                        for inside in range(start, start + LANES, 64):
                            at_once = slice(inside, inside + 64)
                            weights = jnp.exp2(scores[h - 1, at_once, :] - largest)
                            total = total + fold_rows(weights, jnp.sum)
                            chances[at_once, (h - 1) * tokens : h * tokens] = weights.astype(low_type)
                if h > 0:
                    total = jnp.sum(total, 0, keepdims=True)
                    out = dot(v_t, chances[:, (h - 1) * tokens : h * tokens]) / total
                    lse[app, g, h - 1 : h, :] = largest + jnp.log(total) * (1.0 / math.log(2.0))
                    x_attn[1, head_rows(size, g, h - 1), at] = out.astype(low_type)
            return carry

        lax.fori_loop(0, groups, heads, 0)

        @pl.when(app == 0)
        def _():
            for copy in early[:3]:
                copy.start()
            loads[6].wait()

        middle = xin[app].astype(full) + dot(wo[...], x_attn[1, :, at], (0, 0))
        mid[app] = middle
        ffn = (middle * norm(middle) * wide_gain(env, 1)).astype(low_type)
        n2_t[:, at] = ffn
        natural[...] = ffn.T

        @pl.when(app == 0)
        def _():
            early[3].start()
            for load in loads[7:10]:
                load.wait()

        accum[...] = middle

        def chunk(i, carry):
            cols = pl.ds(pl.multiple_of(i * size.front_step, size.front_step), size.front_step)
            gate = dot(natural[...], wg[:, cols])
            upward = dot(natural[...], wu[:, cols])
            hidden = (gate / (1.0 + jnp.exp(-gate)) * upward).astype(low_type)
            d_ffn[0, at, cols] = gate.astype(low_type)
            d_ffn[1, at, cols] = upward.astype(low_type)
            inner[at, cols] = hidden
            accum[...] += dot(wd[:, cols], hidden, (1, 1))
            return carry

        lax.fori_loop(0, size.hidden // size.front_step, chunk, 0)
        xin[app + 1] = accum[...].astype(low_type)

        @pl.when(section == app)
        def _():
            act_store(app).start()

        @pl.when(section != app)
        def _():
            act_copy(app).start()

        return carry

    gain_sums[...] = jnp.zeros_like(gain_sums)
    d_attn[:, :, width:] = jnp.zeros((2, tokens, d_attn.shape[2] - width), low_type)
    loads[0].wait()
    lax.fori_loop(0, 2, forward, 0)
    for source, target in ((x_attn, attn_out), (n2_t, n2_out), (inner, inner_out)):
        store(source, target)
    loads[10].wait()
    grad_low = cot[...]
    at = app_tokens(size, 1)
    df_t[:, at] = grad_low
    natural[...] = grad_low.T
    accum[...] = jnp.zeros_like(accum)

    def chunk(i, carry):
        cols = pl.ds(pl.multiple_of(i * size.front_step, size.front_step), size.front_step)
        ffn_back(env, d_ffn.at[0], d_ffn.at[1], at, cols, wd[:, cols], wg[:, cols], wu[:, cols])
        return carry

    lax.fori_loop(0, size.hidden // size.front_step, chunk, 0)
    store(d_ffn, d_ffn_out)
    middle_back(env, grad_low, mid[1])
    lax.fori_loop(0, groups, lambda g, carry: attend_back(env, at, g), None)
    df_t[:, app_tokens(size, 0)] = project_back(env).astype(low_type)
    for source, target in (
        (df_t, df_out), (d_attn, d_attn_out), (d_pair, d_pair_out), (gain_sums, gain_out)
    ):
        store(source, target)

    def drain(g, carry):
        for app in range(2):
            for k in range(1, ctx_count):
                @pl.when(ctx + k < ctx_count)
                def _():
                    kv_copy(app, g, k).wait_send()
        return carry

    lax.fori_loop(0, groups, drain, 0)
    drain_grad_copies(env)
    act_copy(0).wait()
    act_store(0).wait()
    for copy in stores:
        copy.wait()


def front_shapes(size, plan):
    tokens, width, hidden, groups = size.tokens, size.width, size.hidden, size.kv_heads
    low, full, both = jnp.bfloat16, jnp.float32, 2 * size.tokens
    return [
        ((width, both), low),
        ((width, both), low),
        ((both, hidden), low),
        ((2, width, both), low),
        ((2, tokens, plan.width_tiles * LANES), low),
        ((2, tokens, (plan.pair_tiles - plan.width_tiles + 1) * LANES), low),
        ((2, both, hidden), low),
        ((width, tokens), full),
        ((width, tokens), low),
        ((groups, size.length, LANES), low),
        ((groups, 8, tokens), full),
        ((size.length, tokens), full),
        ((8, plan.width_tiles * LANES), full),
    ]


def run_front(size, plan, *operands):
    tokens, width, hidden, groups = size.tokens, size.width, size.hidden, size.kv_heads
    low, full = jnp.bfloat16, jnp.float32
    vmem = pl.BlockSpec(memory_space=pltpu.VMEM)
    far = pl.BlockSpec(memory_space=pl.ANY)
    dma = pltpu.SemaphoreType.DMA
    others = max(size.ctx - 1, 1)
    kept = front_shapes(size, plan)
    shapes = [((2, width, tokens), low)] + kept
    scratch = [
        ((width, width), low),
        ((size.kv_width, width), low),
        ((size.kv_width, width), low),
        ((width, width), low),
        ((width, hidden), low),
        ((width, hidden), low),
        ((width, hidden), low),
        *kept[:7],
        kept[12],
        ((HEAD_DIM // 2, tokens), full),
        ((HEAD_DIM // 2, tokens), full),
        ((2, width, LANES), full),
        ((3, width, tokens), low),
        ((width, tokens), low),
        ((2, width, tokens), full),
        ((2, width, tokens), low),
        ((2, groups, size.length, LANES), low),
        ((groups, size.length, LANES), low),
        ((others, groups, tokens, LANES), low),
        ((2, groups, 8, tokens), full),
        ((width, tokens), low),
        ((size.length, tokens), full),
        ((width, tokens), full),
        ((width, tokens), full),
        ((tokens, width), low),
        ((size.group, size.length, tokens), full),
        ((size.length, size.group * tokens), low),
        ((size.length, size.group * tokens), low),
    ]
    return pl.pallas_call(
        functools.partial(front_kernel, size),
        out_shape=[jax.ShapeDtypeStruct(*shape) for shape in shapes],
        in_specs=[far, far, vmem, far, far, vmem, vmem] + [far] * 7,
        out_specs=[far] * len(shapes),
        scratch_shapes=[pltpu.VMEM(*shape) for shape in scratch] + [
            dma((11,)), dma((2, 2, groups, others)), dma((2, groups, others)), dma((3,)),
            dma((len(kept),)),
        ],
        compiler_params=pltpu.CompilerParams(
            collective_id=1, has_side_effects=True, vmem_limit_bytes=64 << 20
        ),
        cost_estimate=pl.CostEstimate(
            flops=3 * 10**10, bytes_accessed=40 * 10**6, transcendentals=3 * 10**7
        ),
    )(*operands)


def tail_kernel(
    size, plan, inputs, cos_in, sin_in, gain_attn, gain_ffn, n2_in, df_in, inner_in, attn_in, d_attn_in, d_pair_in,
    d_ffn_in, mid_in, q_in, kv_in, lse_in, bias_in, gain_in,
    wq_in, wk_in, wv_in, wo_in, wg_in, wu_in, wd_in,
    out, grads,
    n2_t, df_t, inner, x_attn, d_attn, d_pair, d_ffn, mid, q_t, kv, lse, bias, gain_sums,
    wq, wk, wv, wo, blocks, cos_q, sin_q, columns, xin, kv_send, kv_recv, do_t, accum, natural,
    chances, grad_scores, stage, extra, sem_l, sem_b, sem_d, sem_e, *refs,
):
    tokens, width, low_type, full = size.tokens, size.width, jnp.bfloat16, jnp.float32
    section, row, ctx = (lax.axis_index(name) for name in ("section", "dp", "ctx"))
    mate = (1 - section, row, ctx)
    own_rows = pl.ds(pl.multiple_of(ctx * tokens, tokens), tokens)
    first_ffn, ffn_count = plan.of("ffn")[0], len(plan.of("ffn"))
    env = types.SimpleNamespace(
        size=size, section=section, row=row, ctx=ctx, columns=columns, gain_sums=gain_sums,
        cos_q=cos_q, sin_q=sin_q, natural=natural, accum=accum, dmid=mid, do_t=do_t,
        d_attn=d_attn, d_pair=d_pair, x_attn=x_attn, bias=bias, chances=chances,
        grad_scores=grad_scores, kv=kv, q_t=q_t, lse=lse, x=xin,
        kv_send=kv_send, kv_recv=kv_recv, sem_d=sem_d, wq=wq, wk=wk, wv=wv, wo=wo,
    )
    sources = types.SimpleNamespace(
        ffn_x=n2_t, ffn_dy=lambda half, index, inside, cols: d_ffn[
            (index - first_ffn) % 3, half, :, inside : inside + cols.stop - cols.start
        ],
        down_x=df_t, down_dy=inner, attn_x=x_attn, attn_dy=d_attn, pair_dy=d_pair, extra=extra,
    )
    count = len(plan.chunks)
    turns = [step // 8 for step in TAIL_ORDER if step >= 0 and step % 8 == 0]
    reduction = Reduction(
        plan, lambda *place: shard_products(plan, *place, sources), out, refs, turns
    )

    def block_loads(i):
        cols = pl.ds(i * size.step, size.step)
        pairs = [(wd_in, 0), (wg_in, 1), (wu_in, 2)]
        return [
            pltpu.make_async_copy(weight.at[:, cols], blocks.at[i % 2, n], sem_b.at[i % 2, n])
            for weight, n in pairs
        ] + [pltpu.make_async_copy(d_ffn_in.at[:, :, cols], d_ffn.at[i % 3], sem_b.at[i % 2, 3])]

    later = pl.ds(tokens, tokens)
    names = (
        "df", "inner", "mid", "n2", "wo", "cos", "sin", "q", "kv", "lse", "bias", "attn", "d_attn",
        "d_pair", "x", "wq", "wk", "wv", "gain",
    )
    loads = dict(zip(names, (
        pltpu.make_async_copy(source, target, sem_l.at[number])
        for number, (source, target) in enumerate((
            (df_in, df_t), (inner_in, inner), (mid_in, mid), (n2_in, n2_t), (wo_in, wo),
            (cos_in.at[:, own_rows], cos_q), (sin_in.at[:, own_rows], sin_q),
            (q_in, q_t), (kv_in, kv), (lse_in, lse), (bias_in, bias), (attn_in, x_attn),
            (d_attn_in, d_attn.at[:, later]), (d_pair_in, d_pair.at[:, later]),
            (inputs.at[section], xin), (wq_in, wq), (wk_in, wk), (wv_in, wv), (gain_in, gain_sums),
        ))
    )))

    def ready(*names):
        for name in names:
            if name in loads:
                loads.pop(name).wait()

    for name in ("df", "inner"):
        loads[name].start()
    for load in block_loads(0):
        load.start()
    for name in names[2:]:
        loads[name].start()
    greet(reduction.friends())
    spread_columns(size, (gain_attn, gain_ffn), columns)
    d_attn[:, :tokens, width:] = jnp.zeros((2, tokens, d_attn.shape[2] - width), low_type)

    back_copy = pltpu.make_async_remote_copy(
        stage, grads.at[section], sem_e.at[0], sem_e.at[1], device_id=mate, device_id_type=MESH
    )
    back_store = pltpu.make_async_copy(stage, grads.at[section], sem_e.at[2])

    def keep(app, value):
        stage[...] = value

        @pl.when(section == app)
        def _():
            back_store.start()

        @pl.when(section != app)
        def _():
            back_copy.start()

    def kept(app):
        @pl.when(section == app)
        def _():
            back_store.wait()

        @pl.when(section != app)
        def _():
            back_copy.wait_send()

    ready("df", "inner")
    grad_low = df_t[:, :tokens]
    keep(1, grad_low.astype(full))
    natural[...] = grad_low.T
    accum[...] = jnp.zeros_like(accum)

    def ffn_step(i):
        for load in block_loads(i):
            load.wait()
        if i + 1 < ffn_count:
            assert i < 2 or reduction.done[first_ffn + i - 2] >= 2
            for load in block_loads(i + 1):
                load.start()
        ffn_back(
            env, d_ffn.at[i % 3, 0], d_ffn.at[i % 3, 1], slice(0, tokens), slice(0, size.step),
            blocks[i % 2, 0], blocks[i % 2, 1], blocks[i % 2, 2],
        )

    taken = {-1: 0, -2: 0, -3: 0, -4: 0}
    for step in TAIL_ORDER:
        if step >= 0:
            if plan.chunks[step // 8][0] == "ffn" and step % 8 < 2:
                ready("n2")
                assert taken[-1] > step // 8 - first_ffn
            assert reduction.done[step // 8] == step % 8
            reduction.advance(step // 8)
            continue
        number, taken[step] = taken[step], taken[step] + 1
        if step == -1:
            ffn_step(number)
        elif step == -2:
            assert taken[-1] == ffn_count
            ready("mid", "wo", "gain")
            middle_back(env, grad_low, mid[...])
        elif step == -3:
            ready("q", "kv", "lse", "bias", "attn")
            lax.fori_loop(
                0, size.kv_heads, lambda g, carry: attend_back(env, app_tokens(size, 0), g), None
            )
        else:
            assert taken[-3] == 1
            ready("cos", "sin", "d_attn", "d_pair", "x", "wq", "wk", "wv")
            grad_in = project_back(env)
            kept(1)
            keep(0, grad_in)
            spread_gains(plan, gain_sums, extra)
    reduction.drain()
    drain_grad_copies(env)
    kept(0)
    back_copy.wait_recv()


def run_tail(size, plan, *operands):
    tokens, width, groups = size.tokens, size.width, size.kv_heads
    low, full, both = jnp.bfloat16, jnp.float32, 2 * size.tokens
    vmem = pl.BlockSpec(memory_space=pltpu.VMEM)
    far = pl.BlockSpec(memory_space=pl.ANY)
    dma = pltpu.SemaphoreType.DMA
    others = max(size.ctx - 1, 1)
    kept = front_shapes(size, plan)
    scratch = kept[:4] + [
        ((2, both, kept[4][0][2]), low),
        ((2, both, kept[5][0][2]), low),
        ((3, 2, both, size.step), low),
        *kept[7:],
        ((width, width), low),
        ((size.kv_width, width), low),
        ((size.kv_width, width), low),
        ((width, width), low),
        ((2, 3, width, size.step), low),
        ((HEAD_DIM // 2, tokens), full),
        ((HEAD_DIM // 2, tokens), full),
        ((2, width, LANES), full),
        ((width, tokens), low),
        ((groups, size.length, LANES), low),
        ((others, groups, tokens, LANES), low),
        ((width, tokens), low),
        ((width, tokens), full),
        ((tokens, width), low),
        ((size.length, size.group * tokens), low),
        ((size.length, size.group * tokens), low),
        ((width, tokens), full),
        ((2, plan.dp, 16, LANES), full),
    ]
    return pl.pallas_call(
        functools.partial(tail_kernel, size, plan),
        out_shape=[
            jax.ShapeDtypeStruct((2, plan.cy, plan.cx, plan.total, LANES), low),
            jax.ShapeDtypeStruct((2, width, tokens), full),
        ],
        in_specs=[far, far, far, vmem, vmem] + [far] * (len(operands) - 5),
        out_specs=[far, far],
        scratch_shapes=[pltpu.VMEM(*shape) for shape in scratch] + [
            dma((19,)), dma((2, 4)), dma((2, groups, others)), dma((3,)), *plan.scratch(),
        ],
        compiler_params=pltpu.CompilerParams(
            collective_id=2, has_side_effects=True, vmem_limit_bytes=64 << 20
        ),
        cost_estimate=pl.CostEstimate(
            flops=3 * 10**10, bytes_accessed=40 * 10**6, transcendentals=10**7
        ),
    )(*operands)


def rotary(length):
    half = HEAD_DIM // 2
    frequency = 10000.0 ** (-2.0 * np.arange(half) / HEAD_DIM)
    angles = frequency[:, None] * np.arange(length)[None, :]
    return np.asarray(np.cos(angles), np.float32), np.asarray(np.sin(angles), np.float32)


def unpack_kernel(plan, sizes, *refs):
    width, hidden, kv_width, through = sizes
    summed, refs = refs[0], refs[1:]
    (query, key_t, value_t, out, gate, up, down_t, *gains), rest = refs[through : through + 9], refs[through + 9 :]
    for source, target in zip(refs[:through], rest):
        target[...] = source[...]
    full, rows, half_width = jnp.float32, width // plan.dp, width // 2

    def tile(half, index, first, count):
        parts = [
            summed[half, p // plan.cx, p % plan.cx, pl.ds(plan.offsets[index] + place, size), :]
            for p, place, inside, size in plan.spans(index, first, count)
        ]
        return (parts[0] if len(parts) == 1 else jnp.concatenate(parts, 0)).astype(full)

    def put(target, at, cols, value):
        count = min(LANES, target.shape[1] - cols)
        target[at : at + value.shape[0], cols : cols + count] = value[:, :count]

    for index, (kind, start, tiles, height, piece, mode) in enumerate(plan.chunks):
        for half in range(2):
            for number in range(tiles):
                value = tile(half, index, number * height, height)
                cols = (start + number) * LANES
                if kind == "ffn":
                    put((gate, up)[half], 0, cols, value[:rows])
                elif kind == "down":
                    put(down_t, half * half_width, cols, value[:half_width])
                elif kind == "attn":
                    put((query, out)[half], 0, cols, value[:rows])
                else:
                    spare = plan.width_tiles * LANES - width
                    if number == 0:
                        put((query, out)[half], 0, width + spare - LANES, value[:rows])
                    pair_t = value.T[:, :rows]
                    first = number * LANES - LANES + spare
                    if first < 0:
                        pair_t = pair_t[LANES - spare :]
                        first = 0
                    (key_t, value_t)[half][first : first + pair_t.shape[0], :] = pair_t
            if kind == "mixed":
                lines = tile(half, index, tiles * height, 16)
                for number in range(-(-rows // LANES)):
                    put(gains[half], 0, number * LANES, lines[number : number + 1])


def unpack(plan, sizes, summed, *through):
    width, hidden, kv_width = sizes
    rows, full = width // plan.dp, jnp.float32
    shapes = [
        (rows, width), (kv_width, rows), (kv_width, rows), (rows, width),
        (rows, hidden), (rows, hidden), (width, hidden // plan.dp), (1, rows), (1, rows),
    ]
    vmem = pl.BlockSpec(memory_space=pltpu.VMEM)
    return pl.pallas_call(
        functools.partial(unpack_kernel, plan, (*sizes, len(through))),
        out_shape=[jax.ShapeDtypeStruct(shape, full) for shape in shapes]
        + [jax.ShapeDtypeStruct(value.shape, value.dtype) for value in through],
        in_specs=[vmem] * (1 + len(through)),
        out_specs=[vmem] * (len(shapes) + len(through)),
        compiler_params=pltpu.CompilerParams(vmem_limit_bytes=60 << 20),
    )(summed, *through)


def plain_block(
    plan, inputs, segment_ids, cotangent,
    gain_attn, w_query, w_key, w_value, w_out, gain_ffn, w_gate, w_up, w_down,
):
    micro_count, row_count, tok_local, model_width = inputs.shape
    kv_width = w_key.shape[1]
    group_size = HEADS // KV_HEADS
    section_index = lax.axis_index("section")
    on_first = section_index == 0
    ctx_index = lax.axis_index("ctx")
    first_token = ctx_index * tok_local
    query_pos = first_token + jnp.arange(tok_local, dtype=jnp.int32)
    halfway = HEAD_DIM // 2
    frequency = 10000.0 ** (-2.0 * jnp.arange(halfway, dtype=jnp.float32) / HEAD_DIM)
    angles = query_pos.astype(jnp.float32)[:, None] * frequency[None, :]
    cos_table = jnp.cos(angles)
    sine_table = jnp.sin(angles)
    w_pair = jnp.concatenate([w_key, w_value], 1)
    head_shape = (row_count, tok_local, KV_HEADS, group_size, HEAD_DIM)
    state_shape = (row_count, KV_HEADS, group_size, tok_local)

    def front(hidden, segments):
        query_seg = lax.dynamic_slice_in_dim(segments, first_token, tok_local, 1)
        normed, inverse = rms_forward(hidden, gain_attn)
        normed_low = normed.astype(jnp.bfloat16)
        query_pre = jnp.einsum(
            "rcd,de->rce", normed_low, w_query, preferred_element_type=jnp.float32
        )
        pair_pre = jnp.einsum("rcd,de->rce", normed_low, w_pair, preferred_element_type=jnp.float32)
        queries = rotate(
            query_pre.reshape(row_count, tok_local, HEADS, HEAD_DIM), cos_table, sine_table
        )
        queries = queries.astype(jnp.bfloat16).reshape(head_shape)
        key_rot = rotate(
            pair_pre[..., :kv_width].reshape(row_count, tok_local, KV_HEADS, HEAD_DIM),
            cos_table,
            sine_table,
        )
        packed = jnp.concatenate(
            [key_rot.reshape(row_count, tok_local, kv_width), pair_pre[..., kv_width:]], -1
        )
        return (query_seg, inverse, normed_low, queries, packed.astype(jnp.bfloat16))

    def attend_forward(queries, arrived, segments, query_seg):
        start_state = (
            jnp.full(state_shape, mask_floor, jnp.float32),
            jnp.zeros(state_shape, jnp.float32),
            jnp.zeros(state_shape + (HEAD_DIM,), jnp.float32),
        )
        piece_rows = arrived.shape[1]
        block_rows = math.gcd(piece_rows, 512)

        def fold_inner_step(step_index, loop_state):
            run_max, run_sum, run_acc = loop_state
            offset = step_index * block_rows
            key_block = lax.dynamic_slice_in_dim(arrived, step_index * block_rows, block_rows, 1)
            key_part = key_block[..., :kv_width].reshape(row_count, block_rows, KV_HEADS, HEAD_DIM)
            value_part = key_block[..., kv_width:].reshape(
                row_count, block_rows, KV_HEADS, HEAD_DIM
            )
            key_seg = lax.dynamic_slice_in_dim(segments, offset, block_rows, 1)
            scores, allowed = block_scores(queries, key_part, query_seg, key_seg, query_pos, offset)
            masked = jnp.where(allowed, scores, mask_floor)
            new_max = jnp.maximum(run_max, jnp.max(masked, -1))
            weights = jnp.where(allowed, jnp.exp(masked - new_max[..., None]), 0.0)
            rescale = jnp.exp(run_max - new_max)
            run_sum = run_sum * rescale + jnp.sum(weights, -1)
            run_acc = run_acc * rescale[..., None] + jnp.einsum(
                "rkgcn,rnkd->rkgcd",
                weights.astype(jnp.bfloat16),
                value_part,
                preferred_element_type=jnp.float32,
            )
            return (new_max, run_sum, run_acc)

        run_max, run_sum, run_acc = lax.fori_loop(
            0, piece_rows // block_rows, fold_inner_step, start_state
        )
        return (run_acc / run_sum[..., None], run_max + jnp.log(run_sum))

    def rear(hidden, attended):
        attn_low = (
            attended.transpose(0, 3, 1, 2, 4)
            .reshape(row_count, tok_local, HEADS * HEAD_DIM)
            .astype(jnp.bfloat16)
        )
        middle = hidden + jnp.einsum(
            "rce,ed->rcd", attn_low, w_out, preferred_element_type=jnp.float32
        )
        normed_ffn, inverse_ffn = rms_forward(middle, gain_ffn)
        ffn_low = normed_ffn.astype(jnp.bfloat16)
        gate_pre = jnp.einsum("rcd,df->rcf", ffn_low, w_gate, preferred_element_type=jnp.float32)
        upward = jnp.einsum("rcd,df->rcf", ffn_low, w_up, preferred_element_type=jnp.float32)
        inner_act = (jax.nn.silu(gate_pre) * upward).astype(jnp.bfloat16)
        output = middle + jnp.einsum(
            "rcf,fd->rcd", inner_act, w_down, preferred_element_type=jnp.float32
        )
        return (output, (attn_low, middle, inverse_ffn, ffn_low, gate_pre, upward, inner_act))


    assert micro_count == lax.axis_size("section")

    def mine(stacked):
        return lax.dynamic_index_in_dim(stacked, section_index, 0, keepdims=False)

    segments = mine(segment_ids)

    def forward(hidden):
        query_seg, inverse, normed_low, queries, packed = front(hidden, segments)
        arrived = lax.all_gather(packed, "ctx", axis=1, tiled=True)
        attended, log_sum = attend_forward(queries, arrived, segments, query_seg)
        output, saved = rear(hidden, attended)
        return output.astype(jnp.bfloat16), (
            hidden, query_seg, inverse, normed_low, queries, arrived, attended, log_sum, saved
        )

    def backward(grad_out, kept):
        (
            hidden,
            backward_query_seg,
            backward_inverse,
            backward_normed_low,
            backward_queries,
            piece_arrived,
            backward_attended,
            log_sum,
            saved,
        ) = kept
        (
            backward_attn_low,
            backward_middle,
            backward_inverse_ffn,
            backward_ffn_low,
            backward_gate_pre,
            backward_upward,
            backward_inner_act,
        ) = saved
        grad_low = grad_out.astype(jnp.bfloat16)
        grad_inner = jnp.einsum("rcd,fd->rcf", grad_low, w_down, preferred_element_type=jnp.float32)
        sigmoid = jax.nn.sigmoid(backward_gate_pre)
        grad_gate = (
            grad_inner * backward_upward * sigmoid * (1.0 + backward_gate_pre * (1.0 - sigmoid))
        ).astype(jnp.bfloat16)
        grad_up = (grad_inner * backward_gate_pre * sigmoid).astype(jnp.bfloat16)
        grad_norm_ffn = jnp.einsum(
            "rcf,df->rcd", grad_gate, w_gate, preferred_element_type=jnp.float32
        ) + jnp.einsum("rcf,df->rcd", grad_up, w_up, preferred_element_type=jnp.float32)
        grad_mid_norm, backward_sum_gain_ffn = rms_backward(
            backward_middle, gain_ffn, backward_inverse_ffn, grad_norm_ffn
        )
        grad_middle = grad_out + grad_mid_norm
        grad_branch = grad_middle.astype(jnp.bfloat16)
        grad_attn = jnp.einsum(
            "rcd,ed->rce", grad_branch, w_out, preferred_element_type=jnp.float32
        ).astype(jnp.bfloat16)
        grad_heads = grad_attn.reshape(head_shape).transpose(0, 2, 3, 1, 4)
        row_delta = jnp.sum(grad_heads.astype(jnp.float32) * backward_attended, -1)
        query_start = jnp.zeros(state_shape + (HEAD_DIM,), jnp.float32)
        fold_grad_query = query_start
        grad_query = fold_grad_query
        piece_piece_rows = piece_arrived.shape[1]
        piece_block_rows = math.gcd(piece_piece_rows, 512)

        def piece_inner_step(step_index, loop_state):
            grad_query, local_pair = loop_state
            inside = step_index * piece_block_rows
            key_block = lax.dynamic_slice_in_dim(piece_arrived, inside, piece_block_rows, 1)
            key_part = key_block[..., :kv_width].reshape(
                row_count, piece_block_rows, KV_HEADS, HEAD_DIM
            )
            value_part = key_block[..., kv_width:].reshape(
                row_count, piece_block_rows, KV_HEADS, HEAD_DIM
            )
            key_seg = lax.dynamic_slice_in_dim(segments, inside, piece_block_rows, 1)
            scores, allowed = block_scores(
                backward_queries, key_part, backward_query_seg, key_seg, query_pos, inside
            )
            chances = jnp.where(
                allowed, jnp.exp(jnp.where(allowed, scores, mask_floor) - log_sum[..., None]), 0.0
            )
            grad_chance = jnp.einsum(
                "rkgcd,rnkd->rkgcn", grad_heads, value_part, preferred_element_type=jnp.float32
            )
            grad_scores = (chances * (grad_chance - row_delta[..., None])).astype(jnp.bfloat16)
            grad_query = grad_query + score_scale * jnp.einsum(
                "rkgcn,rnkd->rkgcd", grad_scores, key_part, preferred_element_type=jnp.float32
            )
            grad_key = score_scale * jnp.einsum(
                "rkgcn,rckgd->rnkd",
                grad_scores,
                backward_queries,
                preferred_element_type=jnp.float32,
            )
            grad_value = jnp.einsum(
                "rkgcn,rkgcd->rnkd",
                chances.astype(jnp.bfloat16),
                grad_heads,
                preferred_element_type=jnp.float32,
            )
            update = jnp.concatenate(
                [
                    grad_key.reshape(row_count, piece_block_rows, kv_width),
                    grad_value.reshape(row_count, piece_block_rows, kv_width),
                ],
                -1,
            )
            current = lax.dynamic_slice_in_dim(local_pair, inside, piece_block_rows, 1)
            local_pair = lax.dynamic_update_slice_in_dim(local_pair, current + update, inside, 1)
            return (grad_query, local_pair)

        local_start = jnp.zeros((row_count, piece_piece_rows, 2 * kv_width), jnp.float32)
        fold_grad_query, fold_local_pair = lax.fori_loop(
            0, piece_piece_rows // piece_block_rows, piece_inner_step, (grad_query, local_start)
        )
        grad_pair = fold_local_pair
        grad_query, grad_pair = (fold_grad_query, grad_pair)
        pair_share = lax.psum_scatter(
            grad_pair.astype(jnp.bfloat16), "ctx", scatter_dimension=1, tiled=True
        ).astype(jnp.float32)
        query_tok = grad_query.transpose(0, 3, 1, 2, 4).reshape(
            row_count, tok_local, HEADS, HEAD_DIM
        )
        query_back = rotate(query_tok, cos_table, -sine_table).reshape(
            row_count, tok_local, HEADS * HEAD_DIM
        )
        query_back = query_back.astype(jnp.bfloat16)
        key_back = rotate(
            pair_share[..., :kv_width].reshape(row_count, tok_local, KV_HEADS, HEAD_DIM),
            cos_table,
            -sine_table,
        )
        pair_low = jnp.concatenate(
            [key_back.reshape(row_count, tok_local, kv_width), pair_share[..., kv_width:]], -1
        )
        pair_low = pair_low.astype(jnp.bfloat16)
        grad_normed = jnp.einsum(
            "rce,de->rcd", query_back, w_query, preferred_element_type=jnp.float32
        ) + jnp.einsum("rce,de->rcd", pair_low, w_pair, preferred_element_type=jnp.float32)
        grad_front, backward_sum_gain_attn = rms_backward(
            hidden, gain_attn, backward_inverse, grad_normed
        )
        factors = (
            backward_normed_low, backward_attn_low, backward_ffn_low, backward_inner_act,
            query_back, pair_low, grad_branch, grad_gate, grad_up, grad_low,
        )
        tick_grads = (backward_sum_gain_attn, backward_sum_gain_ffn, factors)
        return grad_middle + grad_front, tick_grads

    first_low, first_kept = forward(mine(inputs).astype(jnp.float32))
    second_low, second_kept = forward(first_low.astype(jnp.float32))
    grad_mid, second_grads = backward(mine(cotangent).astype(jnp.float32), second_kept)
    grad_mid_low = grad_mid.astype(jnp.bfloat16)
    grad_in, first_grads = backward(grad_mid_low.astype(jnp.float32), first_kept)
    dp = plan.dp

    def stacked(one, other):
        return jnp.concatenate([one, other], 1).reshape(-1, one.shape[-1])

    normed, attn, ffn, inner, d_query, d_pair, d_branch, d_gate, d_up, d_out = (
        stacked(one, other) for one, other in zip(first_grads[2], second_grads[2])
    )
    tokens = normed.shape[0]

    def sides(values, rows):
        cut = values.reshape(tokens, dp, -1)
        cut = jnp.pad(cut, ((0, 0), (0, 0), (0, rows - cut.shape[2])))
        return cut.transpose(1, 2, 0).reshape(dp * rows, tokens)

    inner = inner.reshape(tokens, dp, -1)
    inner = jnp.pad(
        inner, ((0, 0), (0, 0), (0, plan.down_tiles * LANES - inner.shape[2]))
    ).reshape(tokens, -1)
    spare = plan.width_tiles * LANES - model_width
    gain_sums = jnp.stack([one + other for one, other in zip(first_grads[:2], second_grads[:2])])
    gain_sums = jnp.pad(gain_sums, ((0, 6), (0, plan.width_tiles * LANES - model_width)))
    factors = (
        sides(ffn, plan.rows),
        jnp.stack([d_gate, d_up]),
        d_out.T,
        inner,
        jnp.stack([sides(normed, plan.rows), sides(attn, plan.rows)]),
        jnp.pad(jnp.stack([d_query, d_branch]), ((0, 0), (0, 0), (0, spare))),
        jnp.pad(
            jnp.stack([d_pair[:, :kv_width], d_pair[:, kv_width:]]),
            ((0, 0), (0, 0), (LANES - spare, 0)),
        ),
    )
    acts = (first_low, second_low)
    return acts, (grad_in, grad_mid_low), gain_sums, factors


def fused_block(
    size, plan, inputs, segment_ids, cotangent,
    gain_attn, w_query, w_key, w_value, w_out, gain_ffn, w_gate, w_up, w_down,
):
    cos_in, sin_in = rotary(size.length)
    gains = (gain_attn, gain_ffn)
    hidden = inputs[:, 0].swapaxes(1, 2)
    weights = (w_query, w_key.T, w_value.T, w_out, w_gate, w_up, w_down.T)
    acts, *kept = run_front(
        size, plan, hidden, cotangent[:, 0].swapaxes(1, 2), segment_ids, cos_in, sin_in, *gains, *weights
    )
    summed, grads = run_tail(size, plan, hidden, cos_in, sin_in, *gains, *kept, *weights)
    return acts, grads, summed


def body(
    inputs,
    segment_ids,
    cotangent,
    gain_attn,
    w_query,
    w_key,
    w_value,
    w_out,
    gain_ffn,
    w_gate,
    w_up,
    w_down,
):
    micro_count, row_count, tok_local, model_width = inputs.shape
    kv_width, hidden = w_key.shape[1], w_gate.shape[1]
    assert micro_count == lax.axis_size("section")
    on_first = lax.axis_index("section") == 0
    plan = Plan(lax.axis_size("dp"), lax.axis_size("ctx"), model_width, hidden, kv_width)
    dp = plan.dp
    size = Block(tok_local, segment_ids.shape[2], model_width, hidden, kv_width, plan.ctx)
    fits = (
        row_count == 1
        and size.length <= 1024
        and tok_local % LANES == 0
        and plan.rows * dp == model_width
        and plan.down_tiles * LANES * dp == hidden
        and hidden % (2 * LANES) == 0
        and len(plan.chunks) == 11
    )
    params = (gain_attn, w_query, w_key, w_value, w_out, gain_ffn, w_gate, w_up, w_down)
    if fits:
        acts, grads, summed = fused_block(size, plan, inputs, segment_ids, cotangent, *params)
    else:
        acts, grads, gain_sums, factors = plain_block(
            plan, inputs, segment_ids, cotangent, *params
        )
        summed = reduce_grads(plan, *factors, gain_sums)
    sizes = (model_width, hidden, kv_width)

    def exchange(for_first, for_last):
        kept = jnp.where(on_first, for_first, for_last)
        sent = jnp.where(on_first, for_last, for_first)
        got = lax.ppermute(sent, "section", [(0, 1), (1, 0)])
        return jnp.where(
            on_first, jnp.stack([kept, got]), jnp.stack([got, kept])
        )

    def turned(values):
        return values[None, :, None].swapaxes(3, 4)

    if fits:
        *parts, acts, grads = unpack(plan, sizes, summed, acts, grads)
        activations, input_grads = turned(acts), turned(grads)
    else:
        parts = unpack(plan, sizes, summed)
        activations = exchange(*acts)[None]
        input_grads = exchange(grads[0].astype(jnp.bfloat16), grads[1]).astype(jnp.float32)[None]
    query, key_t, value_t, out, gate, up, down_t, gain_one, gain_two = parts
    return (
        activations,
        input_grads,
        gain_one.reshape(-1),
        query,
        key_t.T,
        value_t.T,
        out,
        gain_two.reshape(-1),
        gate,
        up,
        down_t.T,
    )


def solution(mesh):
    placed = (
        P(None, "dp", "ctx", None),
        P(None, "dp", None),
        P(None, "dp", "ctx", None),
        P(),
        P(),
        P(),
        P(),
        P(),
        P(),
        P(),
        P(),
        P(),
    )
    return jax.shard_map(
        body,
        mesh=mesh,
        in_specs=placed,
        out_specs=(
            P("section", None, "dp", "ctx", None),
            P("section", None, "dp", "ctx", None),
            P("dp"),
            P("dp", None),
            P("dp", None),
            P("dp", None),
            P("dp", None),
            P("dp"),
            P("dp", None),
            P("dp", None),
            P("dp", None),
        ),
        check_vma=False,
    )
```

```python
import functools
import math
import types

import jax
import jax.numpy as jnp
import numpy as np
from jax import lax
from jax.experimental import pallas as pl
from jax.experimental.pallas import tpu as pltpu
from jax.sharding import PartitionSpec as P

HEADS = 15
KV_HEADS = 5
HEAD_DIM = 64
LANES = 128
Z_CHUNKS = 3
Z_LAG = 2
OWN_SLOTS = 8
PARTNER_SLOTS = 3
MESH = pl.DeviceIdType.MESH


epsilon = 1e-05
score_scale = 0.125
score_unit = score_scale / math.log(2.0)
mask_floor = -1e30


def rms_forward(values, gain_vec):
    inverse = lax.rsqrt(jnp.mean(values * values, -1, keepdims=True) + epsilon)
    return (values * inverse * gain_vec, inverse)


def rms_backward(values, gain_vec, inverse, grad_normed):
    weighted = grad_normed * gain_vec
    grad_gain = jnp.sum(grad_normed * values * inverse, axis=(0, 1))
    cubed = inverse * inverse * inverse
    grad_values = inverse * weighted - values * cubed * jnp.mean(
        weighted * values, -1, keepdims=True
    )
    return (grad_values, grad_gain)


def rotate(values, cos_table, sine_table):
    halfway = values.shape[-1] // 2
    former = values[..., :halfway]
    latter = values[..., halfway:]
    cos_part = cos_table[None, :, None, :]
    sine_part = sine_table[None, :, None, :]
    return jnp.concatenate(
        [former * cos_part - latter * sine_part, latter * cos_part + former * sine_part], -1
    )


def block_scores(queries, key_part, query_seg, key_seg, query_pos, offset):
    block_rows = key_part.shape[1]
    scores = (
        jnp.einsum("rckgd,rnkd->rkgcn", queries, key_part, preferred_element_type=jnp.float32)
        * score_scale
    )
    key_pos = offset + jnp.arange(block_rows, dtype=jnp.int32)
    allowed = (query_seg[:, :, None] == key_seg[:, None, :]) & (
        key_pos[None, None, :] <= query_pos[None, :, None]
    )
    return (scores, allowed[:, None, None, :, :])


def up_to(value, step):
    return -(-value // step) * step


TAIL_ORDER = (
    0, 8, -1, 24, -1, 1, 16, 9, 25, 32, -1, 40, 17, 33, -1, 41, -1, -2, 26, -3,
    48, 2, 49, 56, -4, 3, 42, 4, 57, 64, 34, 58, 10, 72, 43, 27, 18, 65, 19, 11,
    59, 50, 20, 12, 35, 73, 66, 21, 51, 28, 44, 80, 81, 74, 5, 60, 67, 29, 75, 82,
    30, 52, 13, 36, 83, 61, 53, 22, 68, 45, 31, 76, 69, 84, 54, 62, 37, 46, 23, 77,
    6, 85, 70, 38, 63, 14, 78, 86, 39, 55, 71, 47, 15, 7, 79, 87,
)


class Plan:
    def __init__(self, dp, ctx, width, hidden, kv_width):
        self.dp, self.ctx = dp, ctx
        self.cx = 1 << (ctx.bit_length() // 2) if ctx & (ctx - 1) == 0 else ctx
        self.cy = ctx // self.cx
        self.low = max(dp // 2, 1)
        self.shard = width // dp
        self.rows = up_to(width // dp, 16)
        self.down_rows = up_to(width // 2, 16)
        self.down_tiles = up_to(hidden // dp, LANES) // LANES
        self.up_tiles = hidden // LANES
        self.width_tiles = up_to(width, LANES) // LANES
        self.pair_tiles = (width + kv_width) // LANES
        self.step = 4
        chunks = []
        for kind, count, rows, step in (
            ("down", self.down_tiles, self.down_rows, 2),
            ("ffn", self.up_tiles, self.rows, self.step),
            ("attn", self.width_tiles - 1, self.rows, 4),
            ("mixed", self.pair_tiles - self.width_tiles + 1, self.rows, 4),
        ):
            for start in range(0, count, step):
                tiles = min(step, count - start)
                extra = 16 if kind == "mixed" else 0
                piece = up_to(up_to(tiles * rows + extra, ctx) // ctx, 16)
                mode = "z" if len(chunks) < Z_CHUNKS else "xy"
                chunks.append((kind, start, tiles, rows, piece, mode))
        self.chunks = chunks
        self.offsets = [sum(c[4] for c in chunks[:i]) for i in range(len(chunks))]
        self.total = sum(c[4] for c in chunks)
        self.widest = max(c[4] for c in chunks)

    def of(self, kind):
        return [i for i, chunk in enumerate(self.chunks) if chunk[0] == kind]

    def spans(self, index, first, count):
        piece = self.chunks[index][4]
        out, done = [], 0
        while done < count:
            at = first + done
            size = min(count - done, piece - at % piece)
            out.append((at // piece, at % piece, done, size))
            done += size
        return out

    def scratch(self):
        dp, cy, cx, low = self.dp, self.cy, self.cx, self.low
        nx, ny, nz, high = max(cx - 1, 1), max(cy - 1, 1), max(dp - 1, 1), max(dp - low, 1)
        count = len(self.chunks)

        def buffer(*shape):
            return pltpu.VMEM((*shape, LANES), jnp.bfloat16)

        found = [
            buffer(2, dp, cy, cx, self.widest),
            buffer(PARTNER_SLOTS, dp, cy, cx, self.widest),
            buffer(OWN_SLOTS, dp, cy, cx, self.widest),
        ]
        for kind, start, tiles, rows, piece, mode in self.chunks:
            head = up_to(piece // 2, 16)
            rest = max(piece - head, 16)
            if mode == "xy":
                found += [
                    buffer(nz, piece), buffer(nx, low, cy, piece), buffer(ny, high, cx, piece),
                    buffer(nx, high, piece), buffer(ny, low, piece), buffer(piece),
                ]
            else:
                found += [
                    buffer(nz, cy, cx, piece), buffer(nx, cy, head), buffer(ny, cx, rest),
                    buffer(nx, rest), buffer(ny, head), buffer(piece),
                ]
        dma = pltpu.SemaphoreType.DMA
        return found + [
            dma((2, count)), dma((2, count, nx)), dma((2, count, ny)), dma((2, count, nx)),
            dma((2, count, ny)), dma((2, count, nz)), dma((2, count, nx)), dma((2, count, ny)),
            dma((2, count, nx)), dma((2, count, ny)), dma((2, count)), dma((count,)),
            pltpu.SemaphoreType.REGULAR,
        ]


class Reduction:
    def __init__(self, plan, products, out, refs, turns=None):
        self.plan, self.products, self.out = plan, products, out
        count = len(plan.chunks)
        self.turns = list(range(count)) if turns is None else turns
        self.sent, self.partner, self.own_ring = refs[:3]
        self.parts = [refs[3 + 6 * i : 9 + 6 * i] for i in range(count)]
        (
            self.sem_p, self.sem_x1, self.sem_y1, self.sem_x2, self.sem_y2, self.sem_z,
            self.sem_gx, self.sem_gy, self.sem_hx, self.sem_hy, self.sem_m, self.sem_o, self.credit,
        ) = refs[3 + 6 * count :]
        self.section, self.row, self.ctx = (
            lax.axis_index(name) for name in ("section", "dp", "ctx")
        )
        self.px, self.py = lax.rem(self.ctx, plan.cx), lax.div(self.ctx, plan.cx)
        self.mate = (1 - self.section, self.row, self.ctx)
        self.done = [0] * count

    def friends(self):
        plan = self.plan
        found = [self.mate]
        found += [(self.section, lax.rem(self.row + k, plan.dp), self.ctx) for k in range(1, plan.dp)]
        return found + [
            (self.section, self.row, lax.rem(self.ctx + k, plan.ctx)) for k in range(1, plan.ctx)
        ]

    def remote(self, source, target, sems, place, device):
        return pltpu.make_async_remote_copy(
            source, target, sems.at[(0, *place)], sems.at[(1, *place)],
            device_id=device, device_id_type=MESH,
        )

    def x_peers(self):
        for k in range(1, self.plan.cx):
            other = lax.rem(self.px + k, self.plan.cx)
            yield k - 1, other, (self.section, self.row, self.py * self.plan.cx + other)

    def y_peers(self):
        for k in range(1, self.plan.cy):
            other = lax.rem(self.py + k, self.plan.cy)
            yield k - 1, other, (self.section, self.row, other * self.plan.cx + self.px)

    def z_peers(self):
        for k in range(1, self.plan.dp):
            other = lax.rem(self.row + k, self.plan.dp)
            yield k - 1, other, (self.section, other, self.ctx)

    def turn(self, index):
        return self.turns.index(index)

    def own(self, index):
        return self.own_ring.at[self.turn(index) % OWN_SLOTS]

    def at(self, index):
        return pl.ds(self.plan.offsets[index], self.plan.chunks[index][4])

    def head(self, index):
        piece = self.plan.chunks[index][4]
        return up_to(piece // 2, 16)

    def partner_copy(self, index):
        rows = pl.ds(0, self.plan.chunks[index][4])
        return self.remote(
            self.sent.at[self.turn(index) % 2, :, :, :, rows],
            self.partner.at[self.turn(index) % PARTNER_SLOTS, :, :, :, rows],
            self.sem_p, (index,), self.mate,
        )

    def make_partner(self, index):
        turn, cx = self.turn(index), self.plan.cx
        if turn >= 2:
            self.partner_copy(self.turns[turn - 2]).wait_send()
        if turn >= PARTNER_SLOTS:
            pl.semaphore_wait(self.credit, 1)

        def finish(j, first, value):
            for p, place, inside, size in self.plan.spans(index, first, value.shape[0]):
                self.sent[turn % 2, j, p // cx, p % cx, place : place + size, :] = value[
                    inside : inside + size
                ].astype(jnp.bfloat16)

        self.products(index, 1 - self.section, finish)
        self.partner_copy(index).start()

    def make_own(self, index):
        turn = self.turn(index)
        assert turn < OWN_SLOTS or self.done[self.turns[turn - OWN_SLOTS]] > 4
        self.partner_copy(index).wait_recv()
        cx, slot, own = self.plan.cx, turn % PARTNER_SLOTS, self.own(index)

        def finish(j, first, value):
            for p, place, inside, size in self.plan.spans(index, first, value.shape[0]):
                rows = slice(place, place + size)
                other = self.partner[slot, j, p // cx, p % cx, rows, :].astype(jnp.float32)
                own[j, p // cx, p % cx, rows, :] = (
                    value[inside : inside + size] + other
                ).astype(jnp.bfloat16)

        self.products(index, self.section, finish)
        if turn + PARTNER_SLOTS < len(self.plan.chunks):
            pl.semaphore_signal(self.credit, 1, device_id=self.mate, device_id_type=MESH)
        self.start(self.z_copies(index) if self.is_z(index) else self.first_copies(index))

    def is_z(self, index):
        return self.plan.chunks[index][5] == "z"

    def start(self, copies):
        for copy in copies:
            copy.start()

    def wait(self, copies):
        for copy in copies:
            copy.wait()

    def z_copies(self, index):
        own, into = self.own(index), self.parts[index][0]
        piece = pl.ds(0, self.plan.chunks[index][4])
        found = []
        for slot, other, device in self.z_peers():
            if self.is_z(index):
                source = own.at[other, :, :, piece]
            else:
                source = own.at[other, self.py, self.px, piece]
            found.append(self.remote(source, into.at[slot], self.sem_z, (index, slot), device))
        return found

    def halves(self, index):
        plan, piece = self.plan, self.plan.chunks[index][4]
        if self.is_z(index):
            head = self.head(index)
            return (pl.ds(self.row, 1), pl.ds(0, head)), (pl.ds(self.row, 1), pl.ds(head, piece - head))
        rows = pl.ds(0, piece)
        return (pl.ds(0, plan.low), rows), (pl.ds(plan.low, plan.dp - plan.low), rows)

    def has_rest(self, index):
        if self.is_z(index):
            return self.plan.chunks[index][4] > self.head(index)
        return self.plan.dp > self.plan.low

    def first_copies(self, index):
        own = self.own(index)
        (j_x, rows_x), (j_y, rows_y) = self.halves(index)
        _, rx1, ry1, _, _, _ = self.parts[index]
        if self.is_z(index):
            j_x = j_y = self.row
        found = [
            self.remote(own.at[j_x, :, other, rows_x], rx1.at[slot], self.sem_x1, (index, slot), device)
            for slot, other, device in self.x_peers()
        ]
        if self.has_rest(index):
            found += [
                self.remote(
                    own.at[j_y, other, :, rows_y], ry1.at[slot], self.sem_y1, (index, slot), device
                )
                for slot, other, device in self.y_peers()
            ]
        return found

    def second_copies(self, index):
        own = self.own(index)
        (j_x, rows_x), (j_y, rows_y) = self.halves(index)
        _, _, _, rx2, ry2, _ = self.parts[index]
        if self.is_z(index):
            j_x = j_y = self.row
        found = [
            self.remote(
                own.at[j_x, other, self.px, rows_x], ry2.at[slot], self.sem_y2, (index, slot), device
            )
            for slot, other, device in self.y_peers()
        ]
        if self.has_rest(index):
            found += [
                self.remote(
                    own.at[j_y, self.py, other, rows_y], rx2.at[slot], self.sem_x2, (index, slot), device
                )
                for slot, other, device in self.x_peers()
            ]
        return found

    def add_all_z(self, index):
        plan, own, into = self.plan, self.own(index), self.parts[index][0]
        piece = slice(0, plan.chunks[index][4])
        self.wait(self.z_copies(index))
        for y in range(plan.cy):
            for x in range(plan.cx):
                total = own[self.row, y, x, piece, :].astype(jnp.float32)
                for k in range(plan.dp - 1):
                    total = total + into[k, y, x].astype(jnp.float32)
                own[self.row, y, x, piece, :] = total.astype(jnp.bfloat16)
        self.start(self.first_copies(index))

    def add_first(self, index):
        plan, own = self.plan, self.own(index)
        _, rx1, ry1, _, _, _ = self.parts[index]
        piece, is_z = plan.chunks[index][4], self.is_z(index)
        head = self.head(index)
        self.wait(self.first_copies(index))
        places = [(self.row, 0, 0)] if is_z else [(j, j, j - plan.low) for j in range(plan.dp)]
        for j, at_x, at_y in places:
            if is_z or at_x < plan.low:
                rows = slice(0, head) if is_z else slice(0, piece)
                for y in range(plan.cy):
                    total = own[j, y, self.px, rows, :].astype(jnp.float32)
                    for k in range(plan.cx - 1):
                        part = rx1[k, y] if is_z else rx1[k, at_x, y]
                        total = total + part.astype(jnp.float32)
                    own[j, y, self.px, rows, :] = total.astype(jnp.bfloat16)
            if (is_z and piece > head) or (not is_z and at_y >= 0):
                rows = slice(head, piece) if is_z else slice(0, piece)
                for x in range(plan.cx):
                    total = own[j, self.py, x, rows, :].astype(jnp.float32)
                    for k in range(plan.cy - 1):
                        part = ry1[k, x] if is_z else ry1[k, at_y, x]
                        total = total + part.astype(jnp.float32)
                    own[j, self.py, x, rows, :] = total.astype(jnp.bfloat16)
        self.start(self.second_copies(index))

    def add_second(self, index):
        plan, own = self.plan, self.own(index)
        _, _, _, rx2, ry2, _ = self.parts[index]
        piece = slice(0, plan.chunks[index][4])
        self.wait(self.second_copies(index))
        for j in range(plan.dp):
            total = own[j, self.py, self.px, piece, :].astype(jnp.float32)
            if j < plan.low:
                for k in range(plan.cy - 1):
                    total = total + ry2[k, j].astype(jnp.float32)
            else:
                for k in range(plan.cx - 1):
                    total = total + rx2[k, j - plan.low].astype(jnp.float32)
            own[j, self.py, self.px, piece, :] = total.astype(jnp.bfloat16)
        self.start(self.z_copies(index))

    def add_last(self, index):
        plan, own = self.plan, self.own(index)
        rz, _, _, rx2, ry2, final = self.parts[index]
        piece, head = plan.chunks[index][4], self.head(index)
        if self.is_z(index):
            self.wait(self.second_copies(index))
            total = own[self.row, self.py, self.px, 0:head, :].astype(jnp.float32)
            for k in range(plan.cy - 1):
                total = total + ry2[k].astype(jnp.float32)
            final[0:head, :] = total.astype(jnp.bfloat16)
            if piece > head:
                total = own[self.row, self.py, self.px, head:piece, :].astype(jnp.float32)
                for k in range(plan.cx - 1):
                    total = total + rx2[k].astype(jnp.float32)
                final[head:piece, :] = total.astype(jnp.bfloat16)
        else:
            self.wait(self.z_copies(index))
            total = own[self.row, self.py, self.px, 0:piece, :].astype(jnp.float32)
            for k in range(plan.dp - 1):
                total = total + rz[k].astype(jnp.float32)
            final[...] = total.astype(jnp.bfloat16)
        self.place_copy(index).start()
        self.start(self.gather_one(index))

    def place_copy(self, index):
        target = self.out.at[self.section, self.py, self.px, self.at(index)]
        return pltpu.make_async_copy(self.parts[index][5], target, self.sem_o.at[index])

    def gather_parts(self, index):
        offset, piece, head = self.plan.offsets[index], self.plan.chunks[index][4], self.head(index)
        return pl.ds(offset, head), pl.ds(offset + head, piece - head), piece > head

    def gather_one(self, index):
        final, out = self.parts[index][5], self.out
        rows_x, rows_y, rest = self.gather_parts(index)
        head, piece = self.head(index), self.plan.chunks[index][4]
        found = [
            self.remote(
                final.at[pl.ds(0, head)], out.at[self.section, self.py, self.px, rows_x],
                self.sem_gx, (index, slot), device,
            )
            for slot, other, device in self.x_peers()
        ]
        if rest:
            found += [
                self.remote(
                    final.at[pl.ds(head, piece - head)], out.at[self.section, self.py, self.px, rows_y],
                    self.sem_gy, (index, slot), device,
                )
                for slot, other, device in self.y_peers()
            ]
        return found

    def gather_two(self, index):
        out = self.out
        rows_x, rows_y, rest = self.gather_parts(index)
        found = []
        for slot, other, device in self.y_peers():
            region = out.at[self.section, self.py, :, rows_x]
            found.append(self.remote(region, region, self.sem_hy, (index, slot), device))
        if rest:
            for slot, other, device in self.x_peers():
                region = out.at[self.section, :, self.px, rows_y]
                found.append(self.remote(region, region, self.sem_hx, (index, slot), device))
        return found

    def gather_on(self, index):
        self.place_copy(index).wait()
        self.wait(self.gather_one(index))
        self.start(self.gather_two(index))

    def mate_copy(self, index):
        region = self.out.at[self.section, :, :, self.at(index)]
        return self.remote(region, region, self.sem_m, (index,), self.mate)

    def pass_on(self, index):
        self.wait(self.gather_two(index))
        self.mate_copy(index).start()

    def finish(self, index):
        self.mate_copy(index).wait()

    def stages(self, index):
        middle = (self.add_all_z, self.add_first) if self.is_z(index) else (self.add_first, self.add_second)
        return (
            self.make_partner, self.make_own, *middle, self.add_last, self.gather_on, self.pass_on, self.finish
        )

    def advance(self, index, upto=None):
        stages = self.stages(index)
        while self.done[index] < len(stages):
            if upto is not None and self.done[index] >= upto:
                return
            stages[self.done[index]](index)
            self.done[index] += 1
            if upto is None:
                return

    def drain(self):
        todo = []
        for index in range(len(self.done)):
            for stage in range(self.done[index], len(self.stages(index))):
                late = Z_LAG if self.is_z(index) and stage >= 2 else 0
                todo.append((index + stage + late, stage, index))
        for step, stage, index in sorted(todo):
            self.advance(index)
        for index in self.turns[-2:]:
            self.partner_copy(index).wait_send()


def greet(friends):
    barrier = pltpu.get_barrier_semaphore()
    for friend in friends:
        pl.semaphore_signal(barrier, 1, device_id=friend, device_id_type=MESH)
    pl.semaphore_wait(barrier, len(friends))


def shard_products(plan, index, half, finish, sources):
    kind, start, tiles, rows, piece, mode = plan.chunks[index]
    cols = slice(start * LANES, (start + tiles) * LANES)

    def shard(j, carry):
        own = pl.ds(pl.multiple_of(j * plan.rows, 16), plan.rows)
        if kind == "ffn":
            value = dot(sources.ffn_x[own, :], sources.ffn_dy(half, index, 0, cols))
        elif kind == "down":
            first = pl.multiple_of(j * (plan.down_tiles * LANES) + start * LANES, LANES)
            rows_of = pl.ds(pl.multiple_of(half * plan.down_rows, 16), plan.down_rows)
            value = dot(sources.down_x[rows_of, :], sources.down_dy[:, pl.ds(first, tiles * LANES)])
        elif kind == "attn":
            value = dot(sources.attn_x[half, own, :], sources.attn_dy[half, :, cols])
        else:
            value = dot(sources.attn_x[0, own, :], sources.pair_dy[half])
            last = plan.width_tiles - 1
            mixed = dot(sources.attn_x[half, own, :], sources.attn_dy[half, :, last * LANES :])
            value = jnp.concatenate([value[:, :LANES] + mixed, value[:, LANES:]], 1)
        for tile in range(tiles):
            finish(j, tile * rows, value[:, tile * LANES : (tile + 1) * LANES])
        if kind == "mixed":
            finish(j, tiles * rows, sources.extra[half, j])
        return carry

    lax.fori_loop(0, plan.dp, shard, 0)


def spread_gains(plan, gain_sums, extra):
    for half in range(2):
        for j in range(plan.dp):
            for number in range(-(-plan.shard // LANES)):
                start = j * plan.shard + number * LANES
                extra[half, j, number : number + 1, :] = gain_sums[
                    half : half + 1, start : start + LANES
                ]


def reduce_kernel(
    plan, ffn_x, ffn_dy, down_x, down_dy, attn_x, attn_dy, pair_dy, gain_sums, out, extra, *refs
):
    sources = types.SimpleNamespace(
        ffn_x=ffn_x, ffn_dy=lambda half, index, inside, cols: ffn_dy[half, :, cols],
        down_x=down_x, down_dy=down_dy,
        attn_x=attn_x, attn_dy=attn_dy, pair_dy=pair_dy, extra=extra,
    )
    reduction = Reduction(
        plan, lambda *place: shard_products(plan, *place, sources), out, refs
    )
    greet(reduction.friends())
    spread_gains(plan, gain_sums, extra)
    reduction.drain()


def reduce_grads(plan, *operands):
    return pl.pallas_call(
        functools.partial(reduce_kernel, plan),
        out_shape=jax.ShapeDtypeStruct((2, plan.cy, plan.cx, plan.total, LANES), jnp.bfloat16),
        in_specs=[pl.BlockSpec(memory_space=pltpu.VMEM)] * len(operands),
        out_specs=pl.BlockSpec(memory_space=pl.ANY),
        scratch_shapes=[pltpu.VMEM((2, plan.dp, 16, LANES), jnp.float32), *plan.scratch()],
        compiler_params=pltpu.CompilerParams(
            collective_id=0, has_side_effects=True, vmem_limit_bytes=64 << 20
        ),
        cost_estimate=pl.CostEstimate(flops=10**10, bytes_accessed=20 * 10**6, transcendentals=0),
    )(*operands)


class Block:
    def __init__(self, tokens, length, width, hidden, kv_width, ctx):
        self.tokens, self.length, self.width, self.hidden = tokens, length, width, hidden
        self.kv_width, self.ctx = kv_width, ctx
        self.kv_heads = kv_width // HEAD_DIM
        self.group = width // kv_width
        self.step, self.front_step = 512, hidden // 2


def dot(one, other, over=(1, 0)):
    return lax.dot_general(
        one, other, (((over[0],), (over[1],)), ((), ())), preferred_element_type=jnp.float32
    )


def fold_rows(values, combine):
    return combine(values.reshape(values.shape[0] // 8, 8, values.shape[1]), 0)


def norm(values):
    return lax.rsqrt(jnp.mean(values * values, 0, keepdims=True) + epsilon)


def app_tokens(size, app):
    return slice(app * size.tokens, (app + 1) * size.tokens)


def head_rows(size, g, h):
    return pl.ds(pl.multiple_of((g * size.group + h) * HEAD_DIM, HEAD_DIM), HEAD_DIM)


def wide_gain(env, which):
    return jnp.concatenate([env.columns[which]] * (env.size.tokens // LANES), 1)


def spread_columns(size, gains, columns):
    for which, gain in enumerate(gains):
        for start in range(0, size.width, LANES):
            stop = min(start + LANES, size.width)
            part = gain[start:stop].astype(jnp.float32)[None]
            if stop - start < LANES:
                part = jnp.concatenate([part, jnp.zeros((1, LANES - stop + start), jnp.float32)], 1)
            tile = jnp.broadcast_to(part, (LANES, LANES))
            columns[which, start:stop, :] = tile.T[: stop - start]


def norm_back(env, values, which, grad_normed):
    size = env.size
    inverse = norm(values)
    product = grad_normed * values * inverse
    folded = product[:, :LANES]
    for start in range(LANES, size.tokens, LANES):
        folded = folded + product[:, start : start + LANES]
    for start in range(0, size.width, LANES):
        stop = min(start + LANES, size.width)
        part = folded[start:stop]
        if stop - start < LANES:
            part = jnp.concatenate([part, jnp.zeros((LANES - stop + start, LANES), jnp.float32)], 0)
        env.gain_sums[which : which + 1, start : start + LANES] += jnp.sum(part.T, 0, keepdims=True)
    weighted = grad_normed * wide_gain(env, which)
    cubed = inverse * inverse * inverse
    return inverse * weighted - values * (cubed * jnp.mean(weighted * values, 0, keepdims=True))


def rope(env, values, sign):
    half = HEAD_DIM // 2
    cos, sine = env.cos_q[...], env.sin_q[...] * sign
    out = []
    for start in range(0, values.shape[0], HEAD_DIM):
        former = values[start : start + half]
        latter = values[start + half : start + HEAD_DIM]
        out += [former * cos - latter * sine, latter * cos + former * sine]
    return jnp.concatenate(out, 0)


def ffn_back(env, gate_ref, up_ref, rows, cols, wd, wg, wu):
    gate = gate_ref[rows, cols].astype(jnp.float32)
    upward = up_ref[rows, cols].astype(jnp.float32)
    sigmoid = 1.0 / (1.0 + jnp.exp(-gate))
    scaled = dot(env.natural[...], wd) * sigmoid
    grad_gate = (scaled * upward * (1.0 + gate * (1.0 - sigmoid))).astype(jnp.bfloat16)
    grad_up = (scaled * gate).astype(jnp.bfloat16)
    gate_ref[rows, cols] = grad_gate
    up_ref[rows, cols] = grad_up
    env.accum[...] += dot(wg, grad_gate, (1, 1)) + dot(wu, grad_up, (1, 1))


def middle_back(env, grad_low, mid):
    grad_middle = grad_low.astype(jnp.float32) + norm_back(env, mid, 1, env.accum[...])
    env.dmid[...] = grad_middle
    branch = grad_middle.astype(jnp.bfloat16)
    env.d_attn[1, : env.size.tokens, : env.size.width] = branch.T
    env.do_t[...] = dot(env.wo[...], branch).astype(jnp.bfloat16)


def grad_copy(env, g, k):
    owner = jnp.maximum(env.ctx - k, 0)
    rows = pl.ds(pl.multiple_of(owner * env.size.tokens, env.size.tokens), env.size.tokens)
    return pltpu.make_async_remote_copy(
        env.kv_send.at[g, rows], env.kv_recv.at[k - 1, g],
        env.sem_d.at[0, g, k - 1], env.sem_d.at[1, g, k - 1],
        device_id=(env.section, env.row, owner), device_id_type=MESH,
    )


def attend_back(env, at, g):
    size, low_type = env.size, jnp.bfloat16
    k_t = env.kv[g].T[:HEAD_DIM]
    sides = []
    for h in range(size.group):
        rows, cols = head_rows(size, g, h), slice(h * size.tokens, (h + 1) * size.tokens)
        query, grad_head = env.q_t[rows, :], env.do_t[rows, :]
        empty = jnp.zeros_like(query)
        query = jnp.concatenate([query, empty], 0)
        grad_pad = jnp.concatenate([empty, grad_head], 0)
        delta = jnp.sum(
            grad_head.astype(jnp.float32) * env.x_attn[1, rows, at].astype(jnp.float32),
            0, keepdims=True,
        )
        log_sum = env.lse[g, h : h + 1, :]
        for start in range(0, size.length, 256):
            keys_at = slice(start, start + 256)
            part = dot(env.kv[g, keys_at, :], query) * score_unit + env.bias[keys_at, :]
            chance = jnp.exp2(part - log_sum)
            env.chances[keys_at, cols] = chance.astype(low_type)
            change = dot(env.kv[g, keys_at, :], grad_pad) - delta
            env.grad_scores[keys_at, cols] = (chance * change).astype(low_type)
        sides.append(((query.astype(jnp.float32) * score_scale).astype(low_type), grad_pad))
        env.accum[rows, :] = dot(k_t, env.grad_scores[:, cols]) * score_scale
    small, grad_pad = (jnp.concatenate(side, 1) for side in zip(*sides))
    env.kv_send[g] = (
        dot(env.grad_scores[...], small, (1, 1)) + dot(env.chances[...], grad_pad, (1, 1))
    ).astype(low_type)
    for k in reversed(range(1, size.ctx)):
        @pl.when(env.ctx - k >= 0)
        def _():
            grad_copy(env, g, k).start()


def project_back(env):
    size, low_type = env.size, jnp.bfloat16
    tokens, width = size.tokens, size.width
    for start in range(0, width, 2 * LANES):
        stop = min(start + 2 * LANES, width)
        tile = rope(env, env.accum[start:stop, :], -1.0).astype(low_type)
        env.natural[:, start:stop] = tile.T
        env.do_t[start:stop, :] = tile
    env.d_attn[0, :tokens, :width] = env.natural[...]
    own_rows = pl.ds(pl.multiple_of(env.ctx * tokens, tokens), tokens)
    pairs = [[], []]
    for g in range(size.kv_heads):
        tile = env.kv_send[g, own_rows, :].astype(jnp.float32)
        for k in range(1, size.ctx):
            @pl.when(env.ctx + k < size.ctx)
            def _():
                grad_copy(env, g, k).wait_recv()
            tile = tile + jnp.where(
                env.ctx + k < size.ctx, env.kv_recv[k - 1, g].astype(jnp.float32), 0.0
            )
        tile = tile.T
        pairs[0].append(rope(env, tile[:HEAD_DIM], -1.0).astype(low_type))
        pairs[1].append(tile[HEAD_DIM:].astype(low_type))
    spare = env.d_pair.shape[2] - size.kv_width
    for half in range(2):
        pairs[half] = jnp.concatenate(pairs[half], 0)
        env.d_pair[half, :tokens, :] = jnp.concatenate(
            [jnp.zeros((spare, tokens), low_type), pairs[half]], 0
        ).T
    grad_normed = (
        dot(env.wq[...], env.do_t[...])
        + dot(env.wk[...], pairs[0], (0, 0))
        + dot(env.wv[...], pairs[1], (0, 0))
    )
    return env.dmid[...] + norm_back(env, env.x[...].astype(jnp.float32), 0, grad_normed)


def drain_grad_copies(env):
    def one(g, carry):
        for k in range(1, env.size.ctx):
            @pl.when(env.ctx - k >= 0)
            def _():
                grad_copy(env, g, k).wait_send()
        return carry

    lax.fori_loop(0, env.size.kv_heads, one, 0)


def front_kernel(
    size, inputs, cotangent, segments, cos_in, sin_in, gain_attn, gain_ffn,
    wq_in, wk_in, wv_in, wo_in, wg_in, wu_in, wd_in,
    acts, n2_out, df_out, inner_out, attn_out, d_attn_out, d_pair_out, d_ffn_out,
    mid_out, q_out, kv_out, lse_out, bias_out, gain_out,
    wq, wk, wv, wo, wg, wu, wd, n2_t, df_t, inner, x_attn, d_attn, d_pair, d_ffn, gain_sums,
    cos_q, sin_q, columns, xin, cot, mid, q_t,
    kv, kv_send, kv_recv, lse, do_t, bias, accum, dmid, natural, scores, chances, grad_scores,
    sem_w, sem_k, sem_d, sem_e, sem_o,
):
    tokens, ctx_count, groups, group = size.tokens, size.ctx, size.kv_heads, size.group
    width, low_type, full = size.width, jnp.bfloat16, jnp.float32
    section, row, ctx = (lax.axis_index(name) for name in ("section", "dp", "ctx"))
    mate = (1 - section, row, ctx)
    own_rows = pl.ds(pl.multiple_of(ctx * tokens, tokens), tokens)
    env = types.SimpleNamespace(
        size=size, section=section, row=row, ctx=ctx, columns=columns, gain_sums=gain_sums,
        cos_q=cos_q, sin_q=sin_q, natural=natural, accum=accum, dmid=dmid, do_t=do_t,
        d_attn=d_attn, d_pair=d_pair, x_attn=x_attn, bias=bias, chances=chances,
        grad_scores=grad_scores, kv=kv.at[1], q_t=q_t.at[1], lse=lse.at[1], x=xin.at[1],
        kv_send=kv_send, kv_recv=kv_recv, sem_d=sem_d, wq=wq, wk=wk, wv=wv, wo=wo,
    )
    loads = [
        pltpu.make_async_copy(source, target, sem_w.at[number])
        for number, (source, target) in enumerate((
            (inputs.at[section], xin.at[0]), (cos_in.at[:, own_rows], cos_q),
            (sin_in.at[:, own_rows], sin_q), (wk_in, wk), (wv_in, wv), (wq_in, wq), (wo_in, wo),
            (wg_in, wg), (wu_in, wu), (wd_in, wd), (cotangent.at[section], cot),
        ))
    ]
    for load in loads:
        load.start()
    stores = []

    def store(source, target):
        copy = pltpu.make_async_copy(source, target, sem_o.at[len(stores)])
        copy.start()
        stores.append(copy)

    barrier = pltpu.get_barrier_semaphore()
    friends = [mate] + [(section, row, lax.rem(ctx + k, ctx_count)) for k in range(1, ctx_count)]
    for friend in friends:
        pl.semaphore_signal(barrier, 1, device_id=friend, device_id_type=MESH)
    spread_columns(size, (gain_attn, gain_ffn), columns)
    query_seg = segments[section, :, own_rows].astype(full)
    query_pos = lax.broadcasted_iota(jnp.int32, (1, tokens), 1) + ctx * tokens
    for start in range(0, size.length, LANES):
        key_seg = jnp.broadcast_to(
            segments[section, :, start : start + LANES].astype(full), (LANES, LANES)
        ).T
        key_pos = lax.broadcasted_iota(jnp.int32, (LANES, tokens), 0) + start
        key_seg = jnp.concatenate([key_seg] * (tokens // LANES), 1)
        allowed = (key_seg == query_seg) & (key_pos <= query_pos)
        bias[start : start + LANES, :] = jnp.where(allowed, 0.0, mask_floor)
    store(bias, bias_out)
    for k in range(1, ctx_count):
        @pl.when(ctx + k < ctx_count)
        def _():
            rows = pl.ds(pl.multiple_of((ctx + k) * tokens, tokens), tokens)
            for app in range(2):
                kv[app, :, rows, :] = jnp.zeros((groups, tokens, LANES), low_type)
    pl.semaphore_wait(barrier, len(friends))

    def kv_copy(app, g, k):
        return pltpu.make_async_remote_copy(
            kv.at[app, g, own_rows], kv.at[app, g, own_rows],
            sem_k.at[0, app, g, k - 1], sem_k.at[1, app, g, k - 1],
            device_id=(section, row, jnp.minimum(ctx + k, ctx_count - 1)), device_id_type=MESH,
        )

    def act_copy(app):
        return pltpu.make_async_remote_copy(
            xin.at[app + 1], acts.at[section], sem_e.at[0], sem_e.at[1],
            device_id=mate, device_id_type=MESH,
        )

    def act_store(app):
        return pltpu.make_async_copy(xin.at[app + 1], acts.at[section], sem_e.at[2])

    early = [
        pltpu.make_async_copy(source, target, sem_o.at[number])
        for number, (source, target) in enumerate((
            (q_t.at[0], q_out), (kv.at[0], kv_out), (lse.at[0], lse_out), (mid.at[0], mid_out)
        ))
    ]
    stores += early

    def forward(app, carry):
        at = pl.ds(pl.multiple_of(app * tokens, tokens), tokens)
        x = xin[app].astype(full)
        normed = (x * norm(x) * wide_gain(env, 0)).astype(low_type)
        x_attn[0, :, at] = normed

        @pl.when(app == 0)
        def _():
            for load in loads[1:6]:
                load.wait()

        keys = rope(env, dot(wk[...], normed), 1.0).astype(low_type)
        values = dot(wv[...], normed).astype(low_type)
        for g in range(groups):
            piece = slice(g * HEAD_DIM, (g + 1) * HEAD_DIM)
            kv[app, g, own_rows, :] = jnp.concatenate([keys[piece], values[piece]], 0).T
            for k in reversed(range(1, ctx_count)):
                @pl.when(ctx + k < ctx_count)
                def _():
                    kv_copy(app, g, k).start()
        for start in range(0, width, 2 * LANES):
            stop = min(start + 2 * LANES, width)
            tile = dot(wq[:, start:stop], normed, (0, 0))
            q_t[app, start:stop, :] = rope(env, tile, 1.0).astype(low_type)

        def heads(g, carry):
            for k in range(1, ctx_count):
                @pl.when(ctx - k >= 0)
                def _():
                    kv_copy(app, g, k).wait_recv()
            v_t = kv[app, g].T[HEAD_DIM:]
            most, query = [None] * group, None
            for h in range(group + 1):
                if h < group:
                    query = q_t[app, head_rows(size, g, h), :]
                    query = jnp.concatenate([query, jnp.zeros_like(query)], 0)
                if h > 0:
                    largest = jnp.max(most[h - 1], 0, keepdims=True)
                    total = jnp.zeros((8, tokens), full)
                for start in range(0, size.length, LANES):
                    keys_at = slice(start, start + LANES)
                    if h < group:
                        part = dot(kv[app, g, keys_at, :], query) * score_unit + bias[keys_at, :]
                        scores[h, keys_at, :] = part
                        part = fold_rows(part, jnp.max)
                        most[h] = part if most[h] is None else jnp.maximum(most[h], part)
                    if h > 0:
                        for inside in range(start, start + LANES, 64):
                            at_once = slice(inside, inside + 64)
                            weights = jnp.exp2(scores[h - 1, at_once, :] - largest)
                            total = total + fold_rows(weights, jnp.sum)
                            chances[at_once, (h - 1) * tokens : h * tokens] = weights.astype(low_type)
                if h > 0:
                    total = jnp.sum(total, 0, keepdims=True)
                    out = dot(v_t, chances[:, (h - 1) * tokens : h * tokens]) / total
                    lse[app, g, h - 1 : h, :] = largest + jnp.log(total) * (1.0 / math.log(2.0))
                    x_attn[1, head_rows(size, g, h - 1), at] = out.astype(low_type)
            return carry

        lax.fori_loop(0, groups, heads, 0)

        @pl.when(app == 0)
        def _():
            for copy in early[:3]:
                copy.start()
            loads[6].wait()

        middle = xin[app].astype(full) + dot(wo[...], x_attn[1, :, at], (0, 0))
        mid[app] = middle
        ffn = (middle * norm(middle) * wide_gain(env, 1)).astype(low_type)
        n2_t[:, at] = ffn
        natural[...] = ffn.T

        @pl.when(app == 0)
        def _():
            early[3].start()
            for load in loads[7:10]:
                load.wait()

        accum[...] = middle

        def chunk(i, carry):
            cols = pl.ds(pl.multiple_of(i * size.front_step, size.front_step), size.front_step)
            gate = dot(natural[...], wg[:, cols])
            upward = dot(natural[...], wu[:, cols])
            hidden = (gate / (1.0 + jnp.exp(-gate)) * upward).astype(low_type)
            d_ffn[0, at, cols] = gate.astype(low_type)
            d_ffn[1, at, cols] = upward.astype(low_type)
            inner[at, cols] = hidden
            accum[...] += dot(wd[:, cols], hidden, (1, 1))
            return carry

        lax.fori_loop(0, size.hidden // size.front_step, chunk, 0)
        xin[app + 1] = accum[...].astype(low_type)

        @pl.when(section == app)
        def _():
            act_store(app).start()

        @pl.when(section != app)
        def _():
            act_copy(app).start()

        return carry

    gain_sums[...] = jnp.zeros_like(gain_sums)
    d_attn[:, :, width:] = jnp.zeros((2, tokens, d_attn.shape[2] - width), low_type)
    loads[0].wait()
    lax.fori_loop(0, 2, forward, 0)
    for source, target in ((x_attn, attn_out), (n2_t, n2_out), (inner, inner_out)):
        store(source, target)
    loads[10].wait()
    grad_low = cot[...]
    at = app_tokens(size, 1)
    df_t[:, at] = grad_low
    natural[...] = grad_low.T
    accum[...] = jnp.zeros_like(accum)

    def chunk(i, carry):
        cols = pl.ds(pl.multiple_of(i * size.front_step, size.front_step), size.front_step)
        ffn_back(env, d_ffn.at[0], d_ffn.at[1], at, cols, wd[:, cols], wg[:, cols], wu[:, cols])
        return carry

    lax.fori_loop(0, size.hidden // size.front_step, chunk, 0)
    store(d_ffn, d_ffn_out)
    middle_back(env, grad_low, mid[1])
    lax.fori_loop(0, groups, lambda g, carry: attend_back(env, at, g), None)
    df_t[:, app_tokens(size, 0)] = project_back(env).astype(low_type)
    for source, target in (
        (df_t, df_out), (d_attn, d_attn_out), (d_pair, d_pair_out), (gain_sums, gain_out)
    ):
        store(source, target)

    def drain(g, carry):
        for app in range(2):
            for k in range(1, ctx_count):
                @pl.when(ctx + k < ctx_count)
                def _():
                    kv_copy(app, g, k).wait_send()
        return carry

    lax.fori_loop(0, groups, drain, 0)
    drain_grad_copies(env)
    act_copy(0).wait()
    act_store(0).wait()
    for copy in stores:
        copy.wait()


def front_shapes(size, plan):
    tokens, width, hidden, groups = size.tokens, size.width, size.hidden, size.kv_heads
    low, full, both = jnp.bfloat16, jnp.float32, 2 * size.tokens
    return [
        ((width, both), low),
        ((width, both), low),
        ((both, hidden), low),
        ((2, width, both), low),
        ((2, tokens, plan.width_tiles * LANES), low),
        ((2, tokens, (plan.pair_tiles - plan.width_tiles + 1) * LANES), low),
        ((2, both, hidden), low),
        ((width, tokens), full),
        ((width, tokens), low),
        ((groups, size.length, LANES), low),
        ((groups, 8, tokens), full),
        ((size.length, tokens), full),
        ((8, plan.width_tiles * LANES), full),
    ]


def run_front(size, plan, *operands):
    tokens, width, hidden, groups = size.tokens, size.width, size.hidden, size.kv_heads
    low, full = jnp.bfloat16, jnp.float32
    vmem = pl.BlockSpec(memory_space=pltpu.VMEM)
    far = pl.BlockSpec(memory_space=pl.ANY)
    dma = pltpu.SemaphoreType.DMA
    others = max(size.ctx - 1, 1)
    kept = front_shapes(size, plan)
    shapes = [((2, width, tokens), low)] + kept
    scratch = [
        ((width, width), low),
        ((size.kv_width, width), low),
        ((size.kv_width, width), low),
        ((width, width), low),
        ((width, hidden), low),
        ((width, hidden), low),
        ((width, hidden), low),
        *kept[:7],
        kept[12],
        ((HEAD_DIM // 2, tokens), full),
        ((HEAD_DIM // 2, tokens), full),
        ((2, width, LANES), full),
        ((3, width, tokens), low),
        ((width, tokens), low),
        ((2, width, tokens), full),
        ((2, width, tokens), low),
        ((2, groups, size.length, LANES), low),
        ((groups, size.length, LANES), low),
        ((others, groups, tokens, LANES), low),
        ((2, groups, 8, tokens), full),
        ((width, tokens), low),
        ((size.length, tokens), full),
        ((width, tokens), full),
        ((width, tokens), full),
        ((tokens, width), low),
        ((size.group, size.length, tokens), full),
        ((size.length, size.group * tokens), low),
        ((size.length, size.group * tokens), low),
    ]
    return pl.pallas_call(
        functools.partial(front_kernel, size),
        out_shape=[jax.ShapeDtypeStruct(*shape) for shape in shapes],
        in_specs=[far, far, vmem, far, far, vmem, vmem] + [far] * 7,
        out_specs=[far] * len(shapes),
        scratch_shapes=[pltpu.VMEM(*shape) for shape in scratch] + [
            dma((11,)), dma((2, 2, groups, others)), dma((2, groups, others)), dma((3,)),
            dma((len(kept),)),
        ],
        compiler_params=pltpu.CompilerParams(
            collective_id=1, has_side_effects=True, vmem_limit_bytes=64 << 20
        ),
        cost_estimate=pl.CostEstimate(
            flops=3 * 10**10, bytes_accessed=40 * 10**6, transcendentals=3 * 10**7
        ),
    )(*operands)


def tail_kernel(
    size, plan, inputs, cos_in, sin_in, gain_attn, gain_ffn, n2_in, df_in, inner_in, attn_in, d_attn_in, d_pair_in,
    d_ffn_in, mid_in, q_in, kv_in, lse_in, bias_in, gain_in,
    wq_in, wk_in, wv_in, wo_in, wg_in, wu_in, wd_in,
    out, grads,
    n2_t, df_t, inner, x_attn, d_attn, d_pair, d_ffn, mid, q_t, kv, lse, bias, gain_sums,
    wq, wk, wv, wo, blocks, cos_q, sin_q, columns, xin, kv_send, kv_recv, do_t, accum, natural,
    chances, grad_scores, stage, extra, sem_l, sem_b, sem_d, sem_e, *refs,
):
    tokens, width, low_type, full = size.tokens, size.width, jnp.bfloat16, jnp.float32
    section, row, ctx = (lax.axis_index(name) for name in ("section", "dp", "ctx"))
    mate = (1 - section, row, ctx)
    own_rows = pl.ds(pl.multiple_of(ctx * tokens, tokens), tokens)
    first_ffn, ffn_count = plan.of("ffn")[0], len(plan.of("ffn"))
    env = types.SimpleNamespace(
        size=size, section=section, row=row, ctx=ctx, columns=columns, gain_sums=gain_sums,
        cos_q=cos_q, sin_q=sin_q, natural=natural, accum=accum, dmid=mid, do_t=do_t,
        d_attn=d_attn, d_pair=d_pair, x_attn=x_attn, bias=bias, chances=chances,
        grad_scores=grad_scores, kv=kv, q_t=q_t, lse=lse, x=xin,
        kv_send=kv_send, kv_recv=kv_recv, sem_d=sem_d, wq=wq, wk=wk, wv=wv, wo=wo,
    )
    sources = types.SimpleNamespace(
        ffn_x=n2_t, ffn_dy=lambda half, index, inside, cols: d_ffn[
            (index - first_ffn) % 3, half, :, inside : inside + cols.stop - cols.start
        ],
        down_x=df_t, down_dy=inner, attn_x=x_attn, attn_dy=d_attn, pair_dy=d_pair, extra=extra,
    )
    count = len(plan.chunks)
    turns = [step // 8 for step in TAIL_ORDER if step >= 0 and step % 8 == 0]
    reduction = Reduction(
        plan, lambda *place: shard_products(plan, *place, sources), out, refs, turns
    )

    def block_loads(i):
        cols = pl.ds(i * size.step, size.step)
        pairs = [(wd_in, 0), (wg_in, 1), (wu_in, 2)]
        return [
            pltpu.make_async_copy(weight.at[:, cols], blocks.at[i % 2, n], sem_b.at[i % 2, n])
            for weight, n in pairs
        ] + [pltpu.make_async_copy(d_ffn_in.at[:, :, cols], d_ffn.at[i % 3], sem_b.at[i % 2, 3])]

    later = pl.ds(tokens, tokens)
    names = (
        "df", "inner", "mid", "n2", "wo", "cos", "sin", "q", "kv", "lse", "bias", "attn", "d_attn",
        "d_pair", "x", "wq", "wk", "wv", "gain",
    )
    loads = dict(zip(names, (
        pltpu.make_async_copy(source, target, sem_l.at[number])
        for number, (source, target) in enumerate((
            (df_in, df_t), (inner_in, inner), (mid_in, mid), (n2_in, n2_t), (wo_in, wo),
            (cos_in.at[:, own_rows], cos_q), (sin_in.at[:, own_rows], sin_q),
            (q_in, q_t), (kv_in, kv), (lse_in, lse), (bias_in, bias), (attn_in, x_attn),
            (d_attn_in, d_attn.at[:, later]), (d_pair_in, d_pair.at[:, later]),
            (inputs.at[section], xin), (wq_in, wq), (wk_in, wk), (wv_in, wv), (gain_in, gain_sums),
        ))
    )))

    def ready(*names):
        for name in names:
            if name in loads:
                loads.pop(name).wait()

    for name in ("df", "inner"):
        loads[name].start()
    for load in block_loads(0):
        load.start()
    for name in names[2:]:
        loads[name].start()
    greet(reduction.friends())
    spread_columns(size, (gain_attn, gain_ffn), columns)
    d_attn[:, :tokens, width:] = jnp.zeros((2, tokens, d_attn.shape[2] - width), low_type)

    back_copy = pltpu.make_async_remote_copy(
        stage, grads.at[section], sem_e.at[0], sem_e.at[1], device_id=mate, device_id_type=MESH
    )
    back_store = pltpu.make_async_copy(stage, grads.at[section], sem_e.at[2])

    def keep(app, value):
        stage[...] = value

        @pl.when(section == app)
        def _():
            back_store.start()

        @pl.when(section != app)
        def _():
            back_copy.start()

    def kept(app):
        @pl.when(section == app)
        def _():
            back_store.wait()

        @pl.when(section != app)
        def _():
            back_copy.wait_send()

    ready("df", "inner")
    grad_low = df_t[:, :tokens]
    keep(1, grad_low.astype(full))
    natural[...] = grad_low.T
    accum[...] = jnp.zeros_like(accum)

    def ffn_step(i):
        for load in block_loads(i):
            load.wait()
        if i + 1 < ffn_count:
            assert i < 2 or reduction.done[first_ffn + i - 2] >= 2
            for load in block_loads(i + 1):
                load.start()
        ffn_back(
            env, d_ffn.at[i % 3, 0], d_ffn.at[i % 3, 1], slice(0, tokens), slice(0, size.step),
            blocks[i % 2, 0], blocks[i % 2, 1], blocks[i % 2, 2],
        )

    taken = {-1: 0, -2: 0, -3: 0, -4: 0}
    for step in TAIL_ORDER:
        if step >= 0:
            if plan.chunks[step // 8][0] == "ffn" and step % 8 < 2:
                ready("n2")
                assert taken[-1] > step // 8 - first_ffn
            assert reduction.done[step // 8] == step % 8
            reduction.advance(step // 8)
            continue
        number, taken[step] = taken[step], taken[step] + 1
        if step == -1:
            ffn_step(number)
        elif step == -2:
            assert taken[-1] == ffn_count
            ready("mid", "wo", "gain")
            middle_back(env, grad_low, mid[...])
        elif step == -3:
            ready("q", "kv", "lse", "bias", "attn")
            lax.fori_loop(
                0, size.kv_heads, lambda g, carry: attend_back(env, app_tokens(size, 0), g), None
            )
        else:
            assert taken[-3] == 1
            ready("cos", "sin", "d_attn", "d_pair", "x", "wq", "wk", "wv")
            grad_in = project_back(env)
            kept(1)
            keep(0, grad_in)
            spread_gains(plan, gain_sums, extra)
    reduction.drain()
    drain_grad_copies(env)
    kept(0)
    back_copy.wait_recv()


def run_tail(size, plan, *operands):
    tokens, width, groups = size.tokens, size.width, size.kv_heads
    low, full, both = jnp.bfloat16, jnp.float32, 2 * size.tokens
    vmem = pl.BlockSpec(memory_space=pltpu.VMEM)
    far = pl.BlockSpec(memory_space=pl.ANY)
    dma = pltpu.SemaphoreType.DMA
    others = max(size.ctx - 1, 1)
    kept = front_shapes(size, plan)
    scratch = kept[:4] + [
        ((2, both, kept[4][0][2]), low),
        ((2, both, kept[5][0][2]), low),
        ((3, 2, both, size.step), low),
        *kept[7:],
        ((width, width), low),
        ((size.kv_width, width), low),
        ((size.kv_width, width), low),
        ((width, width), low),
        ((2, 3, width, size.step), low),
        ((HEAD_DIM // 2, tokens), full),
        ((HEAD_DIM // 2, tokens), full),
        ((2, width, LANES), full),
        ((width, tokens), low),
        ((groups, size.length, LANES), low),
        ((others, groups, tokens, LANES), low),
        ((width, tokens), low),
        ((width, tokens), full),
        ((tokens, width), low),
        ((size.length, size.group * tokens), low),
        ((size.length, size.group * tokens), low),
        ((width, tokens), full),
        ((2, plan.dp, 16, LANES), full),
    ]
    return pl.pallas_call(
        functools.partial(tail_kernel, size, plan),
        out_shape=[
            jax.ShapeDtypeStruct((2, plan.cy, plan.cx, plan.total, LANES), low),
            jax.ShapeDtypeStruct((2, width, tokens), full),
        ],
        in_specs=[far, far, far, vmem, vmem] + [far] * (len(operands) - 5),
        out_specs=[far, far],
        scratch_shapes=[pltpu.VMEM(*shape) for shape in scratch] + [
            dma((19,)), dma((2, 4)), dma((2, groups, others)), dma((3,)), *plan.scratch(),
        ],
        compiler_params=pltpu.CompilerParams(
            collective_id=2, has_side_effects=True, vmem_limit_bytes=64 << 20
        ),
        cost_estimate=pl.CostEstimate(
            flops=3 * 10**10, bytes_accessed=40 * 10**6, transcendentals=10**7
        ),
    )(*operands)


def rotary(length):
    half = HEAD_DIM // 2
    frequency = 10000.0 ** (-2.0 * np.arange(half) / HEAD_DIM)
    angles = frequency[:, None] * np.arange(length)[None, :]
    return np.asarray(np.cos(angles), np.float32), np.asarray(np.sin(angles), np.float32)


def unpack_kernel(plan, sizes, *refs):
    width, hidden, kv_width, through = sizes
    summed, refs = refs[0], refs[1:]
    (query, key_t, value_t, out, gate, up, down_t, *gains), rest = refs[through : through + 9], refs[through + 9 :]
    for source, target in zip(refs[:through], rest):
        target[...] = source[...]
    full, rows, half_width = jnp.float32, width // plan.dp, width // 2

    def tile(half, index, first, count):
        parts = [
            summed[half, p // plan.cx, p % plan.cx, pl.ds(plan.offsets[index] + place, size), :]
            for p, place, inside, size in plan.spans(index, first, count)
        ]
        return (parts[0] if len(parts) == 1 else jnp.concatenate(parts, 0)).astype(full)

    def put(target, at, cols, value):
        count = min(LANES, target.shape[1] - cols)
        target[at : at + value.shape[0], cols : cols + count] = value[:, :count]

    for index, (kind, start, tiles, height, piece, mode) in enumerate(plan.chunks):
        for half in range(2):
            for number in range(tiles):
                value = tile(half, index, number * height, height)
                cols = (start + number) * LANES
                if kind == "ffn":
                    put((gate, up)[half], 0, cols, value[:rows])
                elif kind == "down":
                    put(down_t, half * half_width, cols, value[:half_width])
                elif kind == "attn":
                    put((query, out)[half], 0, cols, value[:rows])
                else:
                    spare = plan.width_tiles * LANES - width
                    if number == 0:
                        put((query, out)[half], 0, width + spare - LANES, value[:rows])
                    pair_t = value.T[:, :rows]
                    first = number * LANES - LANES + spare
                    if first < 0:
                        pair_t = pair_t[LANES - spare :]
                        first = 0
                    (key_t, value_t)[half][first : first + pair_t.shape[0], :] = pair_t
            if kind == "mixed":
                lines = tile(half, index, tiles * height, 16)
                for number in range(-(-rows // LANES)):
                    put(gains[half], 0, number * LANES, lines[number : number + 1])


def unpack(plan, sizes, summed, *through):
    width, hidden, kv_width = sizes
    rows, full = width // plan.dp, jnp.float32
    shapes = [
        (rows, width), (kv_width, rows), (kv_width, rows), (rows, width),
        (rows, hidden), (rows, hidden), (width, hidden // plan.dp), (1, rows), (1, rows),
    ]
    vmem = pl.BlockSpec(memory_space=pltpu.VMEM)
    return pl.pallas_call(
        functools.partial(unpack_kernel, plan, (*sizes, len(through))),
        out_shape=[jax.ShapeDtypeStruct(shape, full) for shape in shapes]
        + [jax.ShapeDtypeStruct(value.shape, value.dtype) for value in through],
        in_specs=[vmem] * (1 + len(through)),
        out_specs=[vmem] * (len(shapes) + len(through)),
        compiler_params=pltpu.CompilerParams(vmem_limit_bytes=60 << 20),
    )(summed, *through)


def plain_block(
    plan, inputs, segment_ids, cotangent,
    gain_attn, w_query, w_key, w_value, w_out, gain_ffn, w_gate, w_up, w_down,
):
    micro_count, row_count, tok_local, model_width = inputs.shape
    kv_width = w_key.shape[1]
    group_size = HEADS // KV_HEADS
    section_index = lax.axis_index("section")
    on_first = section_index == 0
    ctx_index = lax.axis_index("ctx")
    first_token = ctx_index * tok_local
    query_pos = first_token + jnp.arange(tok_local, dtype=jnp.int32)
    halfway = HEAD_DIM // 2
    frequency = 10000.0 ** (-2.0 * jnp.arange(halfway, dtype=jnp.float32) / HEAD_DIM)
    angles = query_pos.astype(jnp.float32)[:, None] * frequency[None, :]
    cos_table = jnp.cos(angles)
    sine_table = jnp.sin(angles)
    w_pair = jnp.concatenate([w_key, w_value], 1)
    head_shape = (row_count, tok_local, KV_HEADS, group_size, HEAD_DIM)
    state_shape = (row_count, KV_HEADS, group_size, tok_local)

    def front(hidden, segments):
        query_seg = lax.dynamic_slice_in_dim(segments, first_token, tok_local, 1)
        normed, inverse = rms_forward(hidden, gain_attn)
        normed_low = normed.astype(jnp.bfloat16)
        query_pre = jnp.einsum(
            "rcd,de->rce", normed_low, w_query, preferred_element_type=jnp.float32
        )
        pair_pre = jnp.einsum("rcd,de->rce", normed_low, w_pair, preferred_element_type=jnp.float32)
        queries = rotate(
            query_pre.reshape(row_count, tok_local, HEADS, HEAD_DIM), cos_table, sine_table
        )
        queries = queries.astype(jnp.bfloat16).reshape(head_shape)
        key_rot = rotate(
            pair_pre[..., :kv_width].reshape(row_count, tok_local, KV_HEADS, HEAD_DIM),
            cos_table,
            sine_table,
        )
        packed = jnp.concatenate(
            [key_rot.reshape(row_count, tok_local, kv_width), pair_pre[..., kv_width:]], -1
        )
        return (query_seg, inverse, normed_low, queries, packed.astype(jnp.bfloat16))

    def attend_forward(queries, arrived, segments, query_seg):
        start_state = (
            jnp.full(state_shape, mask_floor, jnp.float32),
            jnp.zeros(state_shape, jnp.float32),
            jnp.zeros(state_shape + (HEAD_DIM,), jnp.float32),
        )
        piece_rows = arrived.shape[1]
        block_rows = math.gcd(piece_rows, 512)

        def fold_inner_step(step_index, loop_state):
            run_max, run_sum, run_acc = loop_state
            offset = step_index * block_rows
            key_block = lax.dynamic_slice_in_dim(arrived, step_index * block_rows, block_rows, 1)
            key_part = key_block[..., :kv_width].reshape(row_count, block_rows, KV_HEADS, HEAD_DIM)
            value_part = key_block[..., kv_width:].reshape(
                row_count, block_rows, KV_HEADS, HEAD_DIM
            )
            key_seg = lax.dynamic_slice_in_dim(segments, offset, block_rows, 1)
            scores, allowed = block_scores(queries, key_part, query_seg, key_seg, query_pos, offset)
            masked = jnp.where(allowed, scores, mask_floor)
            new_max = jnp.maximum(run_max, jnp.max(masked, -1))
            weights = jnp.where(allowed, jnp.exp(masked - new_max[..., None]), 0.0)
            rescale = jnp.exp(run_max - new_max)
            run_sum = run_sum * rescale + jnp.sum(weights, -1)
            run_acc = run_acc * rescale[..., None] + jnp.einsum(
                "rkgcn,rnkd->rkgcd",
                weights.astype(jnp.bfloat16),
                value_part,
                preferred_element_type=jnp.float32,
            )
            return (new_max, run_sum, run_acc)

        run_max, run_sum, run_acc = lax.fori_loop(
            0, piece_rows // block_rows, fold_inner_step, start_state
        )
        return (run_acc / run_sum[..., None], run_max + jnp.log(run_sum))

    def rear(hidden, attended):
        attn_low = (
            attended.transpose(0, 3, 1, 2, 4)
            .reshape(row_count, tok_local, HEADS * HEAD_DIM)
            .astype(jnp.bfloat16)
        )
        middle = hidden + jnp.einsum(
            "rce,ed->rcd", attn_low, w_out, preferred_element_type=jnp.float32
        )
        normed_ffn, inverse_ffn = rms_forward(middle, gain_ffn)
        ffn_low = normed_ffn.astype(jnp.bfloat16)
        gate_pre = jnp.einsum("rcd,df->rcf", ffn_low, w_gate, preferred_element_type=jnp.float32)
        upward = jnp.einsum("rcd,df->rcf", ffn_low, w_up, preferred_element_type=jnp.float32)
        inner_act = (jax.nn.silu(gate_pre) * upward).astype(jnp.bfloat16)
        output = middle + jnp.einsum(
            "rcf,fd->rcd", inner_act, w_down, preferred_element_type=jnp.float32
        )
        return (output, (attn_low, middle, inverse_ffn, ffn_low, gate_pre, upward, inner_act))


    assert micro_count == lax.axis_size("section")

    def mine(stacked):
        return lax.dynamic_index_in_dim(stacked, section_index, 0, keepdims=False)

    segments = mine(segment_ids)

    def forward(hidden):
        query_seg, inverse, normed_low, queries, packed = front(hidden, segments)
        arrived = lax.all_gather(packed, "ctx", axis=1, tiled=True)
        attended, log_sum = attend_forward(queries, arrived, segments, query_seg)
        output, saved = rear(hidden, attended)
        return output.astype(jnp.bfloat16), (
            hidden, query_seg, inverse, normed_low, queries, arrived, attended, log_sum, saved
        )

    def backward(grad_out, kept):
        (
            hidden,
            backward_query_seg,
            backward_inverse,
            backward_normed_low,
            backward_queries,
            piece_arrived,
            backward_attended,
            log_sum,
            saved,
        ) = kept
        (
            backward_attn_low,
            backward_middle,
            backward_inverse_ffn,
            backward_ffn_low,
            backward_gate_pre,
            backward_upward,
            backward_inner_act,
        ) = saved
        grad_low = grad_out.astype(jnp.bfloat16)
        grad_inner = jnp.einsum("rcd,fd->rcf", grad_low, w_down, preferred_element_type=jnp.float32)
        sigmoid = jax.nn.sigmoid(backward_gate_pre)
        grad_gate = (
            grad_inner * backward_upward * sigmoid * (1.0 + backward_gate_pre * (1.0 - sigmoid))
        ).astype(jnp.bfloat16)
        grad_up = (grad_inner * backward_gate_pre * sigmoid).astype(jnp.bfloat16)
        grad_norm_ffn = jnp.einsum(
            "rcf,df->rcd", grad_gate, w_gate, preferred_element_type=jnp.float32
        ) + jnp.einsum("rcf,df->rcd", grad_up, w_up, preferred_element_type=jnp.float32)
        grad_mid_norm, backward_sum_gain_ffn = rms_backward(
            backward_middle, gain_ffn, backward_inverse_ffn, grad_norm_ffn
        )
        grad_middle = grad_out + grad_mid_norm
        grad_branch = grad_middle.astype(jnp.bfloat16)
        grad_attn = jnp.einsum(
            "rcd,ed->rce", grad_branch, w_out, preferred_element_type=jnp.float32
        ).astype(jnp.bfloat16)
        grad_heads = grad_attn.reshape(head_shape).transpose(0, 2, 3, 1, 4)
        row_delta = jnp.sum(grad_heads.astype(jnp.float32) * backward_attended, -1)
        query_start = jnp.zeros(state_shape + (HEAD_DIM,), jnp.float32)
        fold_grad_query = query_start
        grad_query = fold_grad_query
        piece_piece_rows = piece_arrived.shape[1]
        piece_block_rows = math.gcd(piece_piece_rows, 512)

        def piece_inner_step(step_index, loop_state):
            grad_query, local_pair = loop_state
            inside = step_index * piece_block_rows
            key_block = lax.dynamic_slice_in_dim(piece_arrived, inside, piece_block_rows, 1)
            key_part = key_block[..., :kv_width].reshape(
                row_count, piece_block_rows, KV_HEADS, HEAD_DIM
            )
            value_part = key_block[..., kv_width:].reshape(
                row_count, piece_block_rows, KV_HEADS, HEAD_DIM
            )
            key_seg = lax.dynamic_slice_in_dim(segments, inside, piece_block_rows, 1)
            scores, allowed = block_scores(
                backward_queries, key_part, backward_query_seg, key_seg, query_pos, inside
            )
            chances = jnp.where(
                allowed, jnp.exp(jnp.where(allowed, scores, mask_floor) - log_sum[..., None]), 0.0
            )
            grad_chance = jnp.einsum(
                "rkgcd,rnkd->rkgcn", grad_heads, value_part, preferred_element_type=jnp.float32
            )
            grad_scores = (chances * (grad_chance - row_delta[..., None])).astype(jnp.bfloat16)
            grad_query = grad_query + score_scale * jnp.einsum(
                "rkgcn,rnkd->rkgcd", grad_scores, key_part, preferred_element_type=jnp.float32
            )
            grad_key = score_scale * jnp.einsum(
                "rkgcn,rckgd->rnkd",
                grad_scores,
                backward_queries,
                preferred_element_type=jnp.float32,
            )
            grad_value = jnp.einsum(
                "rkgcn,rkgcd->rnkd",
                chances.astype(jnp.bfloat16),
                grad_heads,
                preferred_element_type=jnp.float32,
            )
            update = jnp.concatenate(
                [
                    grad_key.reshape(row_count, piece_block_rows, kv_width),
                    grad_value.reshape(row_count, piece_block_rows, kv_width),
                ],
                -1,
            )
            current = lax.dynamic_slice_in_dim(local_pair, inside, piece_block_rows, 1)
            local_pair = lax.dynamic_update_slice_in_dim(local_pair, current + update, inside, 1)
            return (grad_query, local_pair)

        local_start = jnp.zeros((row_count, piece_piece_rows, 2 * kv_width), jnp.float32)
        fold_grad_query, fold_local_pair = lax.fori_loop(
            0, piece_piece_rows // piece_block_rows, piece_inner_step, (grad_query, local_start)
        )
        grad_pair = fold_local_pair
        grad_query, grad_pair = (fold_grad_query, grad_pair)
        pair_share = lax.psum_scatter(
            grad_pair.astype(jnp.bfloat16), "ctx", scatter_dimension=1, tiled=True
        ).astype(jnp.float32)
        query_tok = grad_query.transpose(0, 3, 1, 2, 4).reshape(
            row_count, tok_local, HEADS, HEAD_DIM
        )
        query_back = rotate(query_tok, cos_table, -sine_table).reshape(
            row_count, tok_local, HEADS * HEAD_DIM
        )
        query_back = query_back.astype(jnp.bfloat16)
        key_back = rotate(
            pair_share[..., :kv_width].reshape(row_count, tok_local, KV_HEADS, HEAD_DIM),
            cos_table,
            -sine_table,
        )
        pair_low = jnp.concatenate(
            [key_back.reshape(row_count, tok_local, kv_width), pair_share[..., kv_width:]], -1
        )
        pair_low = pair_low.astype(jnp.bfloat16)
        grad_normed = jnp.einsum(
            "rce,de->rcd", query_back, w_query, preferred_element_type=jnp.float32
        ) + jnp.einsum("rce,de->rcd", pair_low, w_pair, preferred_element_type=jnp.float32)
        grad_front, backward_sum_gain_attn = rms_backward(
            hidden, gain_attn, backward_inverse, grad_normed
        )
        factors = (
            backward_normed_low, backward_attn_low, backward_ffn_low, backward_inner_act,
            query_back, pair_low, grad_branch, grad_gate, grad_up, grad_low,
        )
        tick_grads = (backward_sum_gain_attn, backward_sum_gain_ffn, factors)
        return grad_middle + grad_front, tick_grads

    first_low, first_kept = forward(mine(inputs).astype(jnp.float32))
    second_low, second_kept = forward(first_low.astype(jnp.float32))
    grad_mid, second_grads = backward(mine(cotangent).astype(jnp.float32), second_kept)
    grad_mid_low = grad_mid.astype(jnp.bfloat16)
    grad_in, first_grads = backward(grad_mid_low.astype(jnp.float32), first_kept)
    dp = plan.dp

    def stacked(one, other):
        return jnp.concatenate([one, other], 1).reshape(-1, one.shape[-1])

    normed, attn, ffn, inner, d_query, d_pair, d_branch, d_gate, d_up, d_out = (
        stacked(one, other) for one, other in zip(first_grads[2], second_grads[2])
    )
    tokens = normed.shape[0]

    def sides(values, rows):
        cut = values.reshape(tokens, dp, -1)
        cut = jnp.pad(cut, ((0, 0), (0, 0), (0, rows - cut.shape[2])))
        return cut.transpose(1, 2, 0).reshape(dp * rows, tokens)

    inner = inner.reshape(tokens, dp, -1)
    inner = jnp.pad(
        inner, ((0, 0), (0, 0), (0, plan.down_tiles * LANES - inner.shape[2]))
    ).reshape(tokens, -1)
    spare = plan.width_tiles * LANES - model_width
    gain_sums = jnp.stack([one + other for one, other in zip(first_grads[:2], second_grads[:2])])
    gain_sums = jnp.pad(gain_sums, ((0, 6), (0, plan.width_tiles * LANES - model_width)))
    factors = (
        sides(ffn, plan.rows),
        jnp.stack([d_gate, d_up]),
        d_out.T,
        inner,
        jnp.stack([sides(normed, plan.rows), sides(attn, plan.rows)]),
        jnp.pad(jnp.stack([d_query, d_branch]), ((0, 0), (0, 0), (0, spare))),
        jnp.pad(
            jnp.stack([d_pair[:, :kv_width], d_pair[:, kv_width:]]),
            ((0, 0), (0, 0), (LANES - spare, 0)),
        ),
    )
    acts = (first_low, second_low)
    return acts, (grad_in, grad_mid_low), gain_sums, factors


def fused_block(
    size, plan, inputs, segment_ids, cotangent,
    gain_attn, w_query, w_key, w_value, w_out, gain_ffn, w_gate, w_up, w_down,
):
    cos_in, sin_in = rotary(size.length)
    gains = (gain_attn, gain_ffn)
    hidden = inputs[:, 0].swapaxes(1, 2)
    weights = (w_query, w_key.T, w_value.T, w_out, w_gate, w_up, w_down.T)
    acts, *kept = run_front(
        size, plan, hidden, cotangent[:, 0].swapaxes(1, 2), segment_ids, cos_in, sin_in, *gains, *weights
    )
    summed, grads = run_tail(size, plan, hidden, cos_in, sin_in, *gains, *kept, *weights)
    return acts, grads, summed


def body(
    inputs,
    segment_ids,
    cotangent,
    gain_attn,
    w_query,
    w_key,
    w_value,
    w_out,
    gain_ffn,
    w_gate,
    w_up,
    w_down,
):
    micro_count, row_count, tok_local, model_width = inputs.shape
    kv_width, hidden = w_key.shape[1], w_gate.shape[1]
    assert micro_count == lax.axis_size("section")
    on_first = lax.axis_index("section") == 0
    plan = Plan(lax.axis_size("dp"), lax.axis_size("ctx"), model_width, hidden, kv_width)
    dp = plan.dp
    size = Block(tok_local, segment_ids.shape[2], model_width, hidden, kv_width, plan.ctx)
    fits = (
        row_count == 1
        and size.length <= 1024
        and tok_local % LANES == 0
        and plan.rows * dp == model_width
        and plan.down_tiles * LANES * dp == hidden
        and hidden % (2 * LANES) == 0
        and len(plan.chunks) == 11
    )
    params = (gain_attn, w_query, w_key, w_value, w_out, gain_ffn, w_gate, w_up, w_down)
    if fits:
        acts, grads, summed = fused_block(size, plan, inputs, segment_ids, cotangent, *params)
    else:
        acts, grads, gain_sums, factors = plain_block(
            plan, inputs, segment_ids, cotangent, *params
        )
        summed = reduce_grads(plan, *factors, gain_sums)
    sizes = (model_width, hidden, kv_width)

    def exchange(for_first, for_last):
        kept = jnp.where(on_first, for_first, for_last)
        sent = jnp.where(on_first, for_last, for_first)
        got = lax.ppermute(sent, "section", [(0, 1), (1, 0)])
        return jnp.where(
            on_first, jnp.stack([kept, got]), jnp.stack([got, kept])
        )

    def turned(values):
        return values[None, :, None].swapaxes(3, 4)

    if fits:
        *parts, acts, grads = unpack(plan, sizes, summed, acts, grads)
        activations, input_grads = turned(acts), turned(grads)
    else:
        parts = unpack(plan, sizes, summed)
        activations = exchange(*acts)[None]
        input_grads = exchange(grads[0].astype(jnp.bfloat16), grads[1]).astype(jnp.float32)[None]
    query, key_t, value_t, out, gate, up, down_t, gain_one, gain_two = parts
    return (
        activations,
        input_grads,
        gain_one.reshape(-1),
        query,
        key_t.T,
        value_t.T,
        out,
        gain_two.reshape(-1),
        gate,
        up,
        down_t.T,
    )


def solution(mesh):
    placed = (
        P(None, "dp", "ctx", None),
        P(None, "dp", None),
        P(None, "dp", "ctx", None),
        P(),
        P(),
        P(),
        P(),
        P(),
        P(),
        P(),
        P(),
        P(),
    )
    return jax.shard_map(
        body,
        mesh=mesh,
        in_specs=placed,
        out_specs=(
            P("section", None, "dp", "ctx", None),
            P("section", None, "dp", "ctx", None),
            P("dp"),
            P("dp", None),
            P("dp", None),
            P("dp", None),
            P("dp", None),
            P("dp"),
            P("dp", None),
            P("dp", None),
            P("dp", None),
        ),
        check_vma=False,
    )
```
